32 devices in a mesh: groups: 2 (over x), gx: 16 (over z, y, core).
Axes of the slice: x: 2, y: 2, z: 4, core: 2. Of those that a mesh axis runs over, the one named last changes fastest.
Arguments:
- inputs: bfloat16 [2, 32, 12288], P(None, 'groups', 'gx'), parts along dimension 1
- norm_gain: float32 [12288], replicated, may hold values from 0.1 to 1.9
- qkv_weight: bfloat16 [12288, 18432], P(None, 'gx'), may hold values from -0.0546875 to 0.0546875
- head_lambda: float32 [24], replicated, may hold values from 0.2 to 0.8
- head_gain: float32 [6144], replicated, may hold values from 0.1 to 1.9
- out_weight: bfloat16 [6144, 12288], P(None, 'gx'), may hold values from -0.078125 to 0.078125
- key_one_pages: bfloat16 [192, 16, 3072], P(('groups', 'gx')), parts along dimension 0, may hold values from -110 to 110
- key_two_pages: bfloat16 [192, 16, 3072], P(('groups', 'gx')), parts along dimension 0, may hold values from -110 to 110
- value_pages: bfloat16 [192, 16, 6144], P(('groups', 'gx')), parts along dimension 0, may hold values from -6 to 6
- page_table: int32 [32, 6], P(('groups', 'gx')), parts along dimension 0, may hold values from 0 to 5, as said below
- context_len: int32 [32], P(('groups', 'gx')), parts along dimension 0, may hold values from 1 to 96, as said below
- positions: int32 [32], P(('groups', 'gx')), parts along dimension 0, may hold values from 1 to 4191, as said below
Outputs:
- outputs: bfloat16 [2, 32, 12288], P(None, 'groups', 'gx'), parts along dimension 1
The draws below stay inside these ranges and needn't reach their ends.
There are 2 independent parts, one for each index of `groups`. The reference program is written for one: setup_inputs(seed, part) draws one part's arguments, and reference() takes and returns one part's arrays. A program takes and returns all parts, laid end to end along the dimension named above; an argument that names none is the same for every part. Nothing has to cross between parts.
Inputs may be any that keep to these rules, and one draw needn't show every extreme that they name: `page_table`: each device's 1 x 6 entries are all its 6 pages, each once, counted from the start of that device's block of the pools. `context_len`: some sequence fills all of its pages. `positions`: at least the sequence's context length.
All inputs are finite; a program needn't handle non-finite values.
Results may differ from the reference program's by a relative error of at most 0.0077.
Values may be sent and summed in bfloat16 or wider, within the bound.
No kernel may reach another device: no remote copies, remote signals or barrier semaphores. Data moves between devices by JAX's collectives and lax.ppermute only.
A program may use at most 128 MiB of HBM per device.

```python
import math
import jax
import jax.numpy as jnp
from jax import lax

D = 12288
H = 24
HD = 128
SEQ_DEV = 1
MAXP = 6
PAGE = 16
STEPS = 2
SEQS = 16
PAGES_DEV = 6
PAGES = 96


def context_draw(key):
    capacity = MAXP * PAGE
    lengths = jax.random.randint(jax.random.fold_in(key, 21), (SEQS,), 1, capacity + 1)
    longest = jax.random.randint(jax.random.fold_in(key, 22), (), 0, SEQS)
    shortest = (longest + 1) % SEQS
    indices = jnp.arange(SEQS)
    lengths = jnp.where(indices == longest, capacity, lengths)
    lengths = jnp.where(indices == shortest, 1, lengths)
    offsets = jax.random.randint(jax.random.fold_in(key, 23), (SEQS,), 0, 4096)
    offsets = jnp.where(indices == longest, 4095, offsets)
    offsets = jnp.where(indices == shortest, 0, offsets)
    return (lengths.astype(jnp.int32), (lengths + offsets).astype(jnp.int32))


def draw_inputs(key, part):
    key = jax.random.fold_in(key, 1)
    split_keys = jax.random.split(key, 3)
    noise = jax.random.normal(split_keys[0], (STEPS, SEQS, D), jnp.float32)
    row_scale = jnp.exp(jax.random.uniform(split_keys[1], (STEPS, SEQS, 1), jnp.float32, math.log(0.3), math.log(3.0)))
    col_scale = jnp.exp(jax.random.uniform(split_keys[2], (D,), jnp.float32, math.log(0.5), math.log(2.0)))
    rising = jnp.exp(math.log(3.0) * jnp.arange(D, dtype=jnp.float32) / D)
    return (noise * row_scale * col_scale * rising / 1.5).astype(jnp.bfloat16)


def draw_key_one_pages(key, part):
    key = jax.random.fold_in(key, 2)
    base_key = jax.random.fold_in(key, 0)
    pool_shape = (PAGES, PAGE, H * HD)
    return jnp.clip(jax.random.normal(base_key, pool_shape, jnp.float32), -6.0, 6.0).astype(jnp.bfloat16)


def draw_key_two_pages(key, part):
    key = jax.random.fold_in(key, 3)
    base_key = jax.random.fold_in(key, 0)
    pool_shape = (PAGES, PAGE, H * HD)
    return jnp.clip(jax.random.normal(base_key, pool_shape, jnp.float32), -6.0, 6.0).astype(jnp.bfloat16)


def draw_page_table(key, part):
    key = jax.random.fold_in(key, 4)
    blocks = SEQS // SEQ_DEV
    split_keys = jax.random.split(key, blocks)
    orders = jax.vmap(lambda single: jax.random.permutation(single, PAGES_DEV))(split_keys)
    return orders.reshape(SEQS, MAXP).astype(jnp.int32)


def draw_context_len(key, part):
    lengths, starts = context_draw(key)
    return lengths


def draw_positions(key, part):
    lengths, starts = context_draw(key)
    return starts


def shard_levels(own_key, extent, shards, least, high):
    gain, own = 1.0, jax.random.fold_in(own_key, 6)
    for position, blocks in shards:
        steps = jnp.exp(jax.random.uniform(jax.random.fold_in(own, position), (blocks,), jnp.float32, least / len(shards), high / len(shards)))
        gain = gain * jnp.repeat(steps, extent[position] // blocks).reshape([-1 if axis == position else 1 for axis in range(len(extent))])
    return gain


def normal_values(rng, shape, scale, bound, shards=(), kind=jnp.bfloat16):
    drawn = jax.random.normal(rng, shape, jnp.float32) * scale
    if len(shards) > 0:
        drawn = shard_levels(rng, shape, shards, -0.22, 0.18) * drawn
    return jnp.clip(drawn, min=-bound, max=bound).astype(kind)


def setup_inputs(seed: int = 0, part: int = 0) -> dict:
    splits = jax.random.split(jax.random.key(seed), 13)
    part_keys = jax.random.split(jax.random.fold_in(splits[12], part), 13)
    return {
        "inputs": draw_inputs(jax.random.fold_in(jax.random.fold_in(splits[12], part), 71), part),
        "norm_gain": jnp.clip(1.0 + 0.18 * jax.random.normal(splits[1], (D,), jnp.float32), 0.1, 1.9),
        "qkv_weight": normal_values(splits[2], (D, 6 * H * HD), D ** -0.5, 0.0546875, ((1, 16),)),
        "head_lambda": jnp.clip(jax.random.uniform(splits[3], (H,), jnp.float32, 0.2, 0.8), 0.2, 0.8),
        "head_gain": jnp.clip(1.0 + 0.18 * jax.random.normal(splits[4], (H * 2 * HD,), jnp.float32), 0.1, 1.9),
        "out_weight": normal_values(splits[5], (H * 2 * HD, D), (2 * H * HD) ** -0.5, 0.078125, ((1, 16),)),
        "key_one_pages": draw_key_one_pages(jax.random.fold_in(jax.random.fold_in(splits[12], part), 71), part),
        "key_two_pages": draw_key_two_pages(jax.random.fold_in(jax.random.fold_in(splits[12], part), 71), part),
        "value_pages": normal_values(part_keys[8], (PAGES, PAGE, H * 2 * HD), 1.0, 6.0, ((0, 16),)),
        "page_table": draw_page_table(jax.random.fold_in(jax.random.fold_in(splits[12], part), 71), part),
        "context_len": draw_context_len(jax.random.fold_in(jax.random.fold_in(splits[12], part), 71), part),
        "positions": draw_positions(jax.random.fold_in(jax.random.fold_in(splits[12], part), 71), part),
    }


epsilon = 1e-05
rope_base = 10000.0

def rotary(vectors, places):
    half_dim = vectors.shape[-1] // 2
    frequency = jnp.exp(-math.log(rope_base) * 2.0 * jnp.arange(half_dim, dtype=jnp.float32) / vectors.shape[-1])
    angles = places[:, None] * frequency[None, :]
    cosine = jnp.cos(angles)[:, None, :]
    sine_values = jnp.sin(angles)[:, None, :]
    lower_half = vectors[..., :half_dim]
    upper_half = vectors[..., half_dim:]
    return jnp.concatenate([lower_half * cosine - upper_half * sine_values, upper_half * cosine + lower_half * sine_values], axis=-1)

def split_heads(qkv_rows):
    head_width = H * HD
    row_count = qkv_rows.shape[0]
    query_one = qkv_rows[:, :head_width].reshape(row_count, H, HD)
    query_two = qkv_rows[:, head_width:2 * head_width].reshape(row_count, H, HD)
    key_one = qkv_rows[:, 2 * head_width:3 * head_width].reshape(row_count, H, HD)
    key_two = qkv_rows[:, 3 * head_width:4 * head_width].reshape(row_count, H, HD)
    value_rows = qkv_rows[:, 4 * head_width:].reshape(row_count, H, 2 * HD)
    return (query_one, query_two, key_one, key_two, value_rows)

def attend(step_rows, step_index, fresh, cached, allowed, starts, head_lambda, head_gain):
    query_one, query_two, key_one, key_two, value_rows = split_heads(step_rows)
    places = (starts + step_index).astype(jnp.float32)
    query_one = rotary(query_one.astype(jnp.float32), places).astype(jnp.bfloat16)
    query_two = rotary(query_two.astype(jnp.float32), places).astype(jnp.bfloat16)
    key_one = rotary(key_one.astype(jnp.float32), places).astype(jnp.bfloat16)
    key_two = rotary(key_two.astype(jnp.float32), places).astype(jnp.bfloat16)
    fresh.append((key_one, key_two, value_rows))
    fresh_one = jnp.stack([entry[0] for entry in fresh])
    fresh_two = jnp.stack([entry[1] for entry in fresh])
    fresh_value = jnp.stack([entry[2] for entry in fresh])
    capacity = cached[0].shape[1]
    newest = fresh_one.shape[0]
    allowed_all = jnp.concatenate([allowed, jnp.ones((allowed.shape[0], newest), dtype=bool)], axis=1)[:, None, :]
    factor = 1.0 / math.sqrt(HD)

    def softmax_map(query, cache_keys, new_keys):
        older = jnp.einsum('shd,sjhd->shj', query.astype(jnp.float32), cache_keys.astype(jnp.float32))
        newer = jnp.einsum('shd,eshd->she', query.astype(jnp.float32), new_keys.astype(jnp.float32))
        scores = jnp.concatenate([older, newer], axis=-1) * factor
        return jax.nn.softmax(jnp.where(allowed_all, scores, -jnp.inf), axis=-1)
    first_map = softmax_map(query_one, cached[0], fresh_one)
    second_map = softmax_map(query_two, cached[1], fresh_two)
    mix = (first_map - head_lambda[None, :, None] * second_map).astype(jnp.bfloat16)
    mixed_out = jnp.einsum('shj,sjhf->shf', mix[..., :capacity].astype(jnp.float32), cached[2].astype(jnp.float32))
    mixed_out = mixed_out + jnp.einsum('she,eshf->shf', mix[..., capacity:].astype(jnp.float32), fresh_value.astype(jnp.float32))
    norms = lax.rsqrt(lax.optimization_barrier(jnp.mean(mixed_out * mixed_out, axis=-1, keepdims=True)) + epsilon)
    grouped = (mixed_out * norms * head_gain.reshape(H, 2 * HD)).astype(jnp.bfloat16)
    return grouped.reshape(grouped.shape[0], H * 2 * HD)

def reference(inputs, norm_gain, qkv_weight, head_lambda, head_gain, out_weight, key_one_pages, key_two_pages, value_pages, page_table, context_len, positions):
    values = inputs.astype(jnp.float32)
    factor_rows = lax.rsqrt(lax.optimization_barrier(jnp.mean(values * values, axis=-1, keepdims=True)) + epsilon)
    normed = (values * factor_rows * norm_gain).astype(jnp.bfloat16)
    projected = jnp.stack([jnp.dot(normed[step_index], qkv_weight, preferred_element_type=jnp.float32) for step_index in range(STEPS)]).astype(jnp.bfloat16)
    device_count = SEQS // SEQ_DEV
    block_qkv = projected.reshape(STEPS, device_count, SEQ_DEV, -1).transpose(1, 0, 2, 3)
    tables = page_table.reshape(device_count, SEQ_DEV, MAXP)
    lengths = context_len.reshape(device_count, SEQ_DEV)
    starts = positions.reshape(device_count, SEQ_DEV)
    pools_one = key_one_pages.reshape(device_count, PAGES_DEV, PAGE, -1)
    pools_two = key_two_pages.reshape(device_count, PAGES_DEV, PAGE, -1)
    pools_value = value_pages.reshape(device_count, PAGES_DEV, PAGE, -1)

    def one_device(operands):
        step_rows, table_rows, length_rows, start_rows, pool_one, pool_two, pool_value = operands
        cached = tuple((page_pool[table_rows].reshape(SEQ_DEV, MAXP * PAGE, H, -1) for page_pool in (pool_one, pool_two, pool_value)))
        allowed = jnp.arange(MAXP * PAGE, dtype=jnp.int32)[None, :] < length_rows[:, None]
        fresh = []
        results = []
        for step_index in range(STEPS):
            results.append(attend(step_rows[step_index], step_index, fresh, cached, allowed, start_rows, head_lambda, head_gain))
        return jnp.stack(results)
    attended = lax.map(one_device, (block_qkv, tables, lengths, starts, pools_one, pools_two, pools_value))
    attended = attended.transpose(1, 0, 2, 3).reshape(STEPS, SEQS, -1)
    produced = [(values[step_index] + jnp.dot(attended[step_index], out_weight, preferred_element_type=jnp.float32)).astype(jnp.bfloat16) for step_index in range(STEPS)]
    return jnp.stack(produced)
```

```python
import functools
import math

import jax
import jax.numpy as jnp
from jax import lax
from jax.experimental import pallas as pl
from jax.experimental.pallas import tpu as pltpu
from jax.sharding import PartitionSpec as P

H = 24
HD = 128
EPS = 1e-05
ROPE_BASE = 10000.0
F32 = jnp.float32
BF16 = jnp.bfloat16
VMEM_LIMIT = 16 * 1024 * 1024


def radices(n):
    rest = n // 2
    middle = 1
    while middle * middle * 4 <= rest:
        middle *= 2
    return rest // middle, middle


def swap(block, n, mask):
    return lax.ppermute(block, "gx", [(i, i ^ mask) for i in range(n)])


def gather_blocks(block, n):
    outer, middle = radices(n)
    rows = jnp.stack([block] + [swap(block, n, o * 2 * middle) for o in range(1, outer)])
    mine = jnp.concatenate([rows] + [swap(rows, n, m * 2) for m in range(1, middle)])
    return mine, swap(mine, n, 1)


def owner(me, entry, core, n):
    outer, middle = radices(n)
    mask = (entry % outer) * (2 * middle) + (entry // outer) * 2 + core
    return jnp.bitwise_xor(me, mask)


def project_kernel(n, me_ref, mine_ref, other_ref, gain_ref, weight_ref, out_ref, total, spread):
    me = me_ref[0]
    half, rows, part = mine_ref.shape
    columns = weight_ref.shape[1]
    blocks = columns // 128
    squares = jnp.zeros((rows, part), F32)
    for entry in range(half):
        for ref in (mine_ref, other_ref):
            values = ref[entry].astype(F32)
            squares = squares + values * values
    mean = jnp.sum(squares, axis=1, keepdims=True) * (1.0 / (n * part))
    factor = lax.rsqrt(mean + EPS)
    total[...] = jnp.zeros_like(total)

    @pl.loop(0, half)
    def _(entry):
        for core, ref in ((0, mine_ref), (1, other_ref)):
            shard = owner(me, entry, core, n)
            normed = (ref[entry].astype(F32) * factor * gain_ref[shard]).astype(BF16)
            start = pl.multiple_of(shard * part, part)
            total[...] += jnp.dot(
                normed, weight_ref[pl.ds(start, part), :], preferred_element_type=F32
            )

    steps = rows // n
    for step in range(steps):
        for block in range(blocks):
            spread[:, step * blocks + block, :] = total[
                step * n : (step + 1) * n, block * 128 : (block + 1) * 128
            ]
    for target in range(n):
        out_ref[target] = spread[target, : steps * blocks, :].astype(BF16)


def project(me, mine, other, gain, weight, n):
    half, rows, part = mine.shape
    columns = weight.shape[1]
    pieces = rows // n * (columns // 128)
    vmem = pl.BlockSpec(memory_space=pltpu.VMEM)
    return pl.pallas_call(
        functools.partial(project_kernel, n),
        out_shape=jax.ShapeDtypeStruct((n, pieces, 128), BF16),
        in_specs=[pl.BlockSpec(memory_space=pltpu.SMEM), vmem, vmem, vmem, vmem],
        out_specs=vmem,
        scratch_shapes=[
            pltpu.VMEM((rows, columns), F32),
            pltpu.VMEM((n, -(-pieces // 8) * 8, 128), F32),
        ],
        compiler_params=pltpu.CompilerParams(vmem_limit_bytes=VMEM_LIMIT),
        cost_estimate=pl.CostEstimate(
            flops=2 * rows * weight.shape[0] * columns, bytes_accessed=0, transcendentals=0
        ),
    )(me, mine, other, gain, pltpu.with_memory_space_constraint(weight, pltpu.VMEM))


def attend_kernel(
    table_ref, length_ref, received_ref, cos_ref, sin_ref, lambda_ref, gain_ref,
    keys_one_ref, keys_two_ref, values_ref, out_ref, fresh,
):
    sources, pieces, _ = received_ref.shape
    steps = cos_ref.shape[0]
    blocks = pieces // steps
    pages, page, _ = keys_one_ref.shape
    capacity = pages * page
    for source in range(sources):
        piece = received_ref[source].astype(F32)
        for step in range(steps):
            fresh[step, source * blocks : (source + 1) * blocks, :] = piece[
                step * blocks : (step + 1) * blocks
            ]

    def heads(step, kind):
        return fresh[step, kind * H : (kind + 1) * H, :]

    def rotated(step, kind):
        values = heads(step, kind)
        turned = values * cos_ref[step] + pltpu.roll(values, HD // 2, 1) * sin_ref[step]
        return turned.astype(BF16).astype(F32)

    row = lax.broadcasted_iota(jnp.int32, (1, capacity), 1)
    place = jnp.zeros((1, capacity), jnp.int32)
    for index in range(pages):
        first = table_ref[0, index] * page
        inside = (row >= first) & (row < first + page)
        place = jnp.where(inside, row - first + index * page, place)
    allowed = place < length_ref[0]

    scale = 1.0 / math.sqrt(HD)
    head_row = lax.rem(lax.broadcasted_iota(jnp.int32, (steps * H, HD), 0), H)

    def softmax_map(kind, keys_ref):
        queries = [rotated(step, kind) for step in range(steps)]
        news = [rotated(step, kind + 2) for step in range(steps)]
        stacked = jnp.concatenate(queries, axis=0)
        apart = jnp.concatenate(
            [jnp.where(head_row == h, stacked, 0.0).astype(BF16) for h in range(H)], axis=1
        )
        older = lax.dot_general(
            apart, keys_ref[...].reshape(capacity, H * HD), (((1,), (1,)), ((), ())),
            preferred_element_type=F32,
        )
        older = jnp.where(allowed, older * scale, -1e38)
        parts = []
        for step in range(steps):
            cached = older[step * H : (step + 1) * H]
            newer = [
                jnp.sum(queries[step] * news[e], axis=1, keepdims=True) * scale
                for e in range(step + 1)
            ]
            top = jnp.max(cached, axis=1, keepdims=True)
            for value in newer:
                top = jnp.maximum(top, value)
            cached = jnp.exp(cached - top)
            newer = [jnp.exp(value - top) for value in newer]
            whole = jnp.sum(cached, axis=1, keepdims=True)
            for value in newer:
                whole = whole + value
            parts.append((cached / whole, [value / whole for value in newer]))
        return parts

    first = softmax_map(0, keys_one_ref)
    second = softmax_map(1, keys_two_ref)
    weight = lambda_ref[...]
    mix = jnp.concatenate(
        [first[step][0] - weight * second[step][0] for step in range(steps)], axis=0
    ).astype(BF16)
    spread = jnp.dot(mix, values_ref[...].reshape(capacity, -1), preferred_element_type=F32)
    wide_row = lax.broadcasted_iota(jnp.int32, (H, 2 * HD), 0)
    fresh_values = [
        jnp.concatenate(
            [fresh[e, pl.ds(4 * H + half, H, stride=2), :] for half in range(2)], axis=1
        )
        for e in range(steps)
    ]
    for step in range(steps):
        mixed = jnp.zeros((H, 2 * HD), F32)
        for h in range(H):
            block = spread[step * H : (step + 1) * H, h * 2 * HD : (h + 1) * 2 * HD]
            mixed = jnp.where(wide_row == h, block, mixed)
        for e in range(step + 1):
            share = first[step][1][e] - weight * second[step][1][e]
            mixed = mixed + share.astype(BF16).astype(F32) * fresh_values[e]
        norm = lax.rsqrt(jnp.mean(mixed * mixed, axis=1, keepdims=True) + EPS)
        out_ref[step * H : (step + 1) * H, :] = (mixed * norm * gain_ref[...]).astype(BF16)


def attend(table, length, received, cos, sin, weights, gain, keys_one, keys_two, values):
    steps = cos.shape[0]
    sources, pieces, _ = received.shape
    vmem = pl.BlockSpec(memory_space=pltpu.VMEM)
    smem = pl.BlockSpec(memory_space=pltpu.SMEM)
    held = [pltpu.with_memory_space_constraint(x, pltpu.VMEM) for x in (keys_one, keys_two, values)]
    return pl.pallas_call(
        attend_kernel,
        out_shape=jax.ShapeDtypeStruct((steps * H, 2 * HD), BF16),
        in_specs=[smem, smem] + [vmem] * 8,
        out_specs=vmem,
        scratch_shapes=[pltpu.VMEM((steps, sources * (pieces // steps), 128), F32)],
        compiler_params=pltpu.CompilerParams(vmem_limit_bytes=VMEM_LIMIT),
    )(table, length, received, cos, sin, weights, gain, *held)


def output_kernel(n, me_ref, mine_ref, other_ref, inputs_ref, weight_ref, out_ref, rows_ref, total):
    me = me_ref[0]
    half, heads, width = mine_ref.shape
    steps = heads // H
    lanes = width // 128
    for entry in range(half):
        for core, ref in ((0, mine_ref), (1, other_ref)):
            start = pl.multiple_of(owner(me, entry, core, n) * heads, 8)
            block = ref[entry].astype(F32)
            for lane in range(lanes):
                rows_ref[lane, pl.ds(start, heads), :] = block[:, lane * 128 : (lane + 1) * 128]
    total[...] = jnp.zeros_like(total)
    for h in range(H):
        left = jnp.concatenate(
            [
                jnp.concatenate(
                    [rows_ref[lane, pl.ds(step * H + h, n, stride=heads), :] for lane in range(lanes)],
                    axis=1,
                )
                for step in range(steps)
            ],
            axis=0,
        ).astype(BF16)
        total[...] += jnp.dot(
            left, weight_ref[h * width : (h + 1) * width, :], preferred_element_type=F32
        )
    for step in range(steps):
        out_ref[step] = (
            inputs_ref[step].astype(F32) + total[step * n : (step + 1) * n]
        ).astype(BF16)


def output(me, mine, other, inputs, weight, n):
    half, heads, width = mine.shape
    vmem = pl.BlockSpec(memory_space=pltpu.VMEM)
    steps, rows, columns = inputs.shape
    return pl.pallas_call(
        functools.partial(output_kernel, n),
        out_shape=jax.ShapeDtypeStruct(inputs.shape, BF16),
        in_specs=[pl.BlockSpec(memory_space=pltpu.SMEM), vmem, vmem, vmem, vmem],
        out_specs=vmem,
        scratch_shapes=[
            pltpu.VMEM((width // 128, n * heads, 128), F32),
            pltpu.VMEM((steps * rows, columns), F32),
        ],
        compiler_params=pltpu.CompilerParams(vmem_limit_bytes=VMEM_LIMIT),
    )(me, mine, other, inputs, pltpu.with_memory_space_constraint(weight, pltpu.VMEM))


def angles(positions, steps):
    half = HD // 2
    frequency = jnp.exp(-math.log(ROPE_BASE) * 2.0 * jnp.arange(half, dtype=F32) / HD)
    places = (positions + jnp.arange(steps, dtype=jnp.int32)).astype(F32)
    turns = places[:, None] * frequency[None, :]
    cosine, sine = jnp.cos(turns), jnp.sin(turns)
    cos = jnp.concatenate([cosine, cosine], axis=-1)
    sin = jnp.concatenate([-sine, sine], axis=-1)
    return cos[:, None, :], sin[:, None, :]


def local(
    n, inputs, norm_gain, qkv_weight, head_lambda, head_gain, out_weight,
    key_one_pages, key_two_pages, value_pages, page_table, context_len, positions,
):
    steps, rows, part = inputs.shape
    me = lax.axis_index("gx").astype(jnp.int32).reshape(1)
    mine, other = gather_blocks(inputs.reshape(steps * rows, part), n)
    sent = project(me, mine, other, norm_gain.reshape(n, 1, part), qkv_weight, n)
    received = lax.all_to_all(sent, "gx", 0, 0)
    cos, sin = angles(positions, steps)
    attended = attend(
        page_table, context_len, received, cos, sin, head_lambda.reshape(H, 1),
        head_gain.reshape(H, 2 * HD), key_one_pages, key_two_pages, value_pages,
    )
    mine, other = gather_blocks(attended, n)
    return output(me, mine, other, inputs, out_weight, n)


def rotary(vectors, cos, sin):
    return vectors * cos + jnp.roll(vectors, HD // 2, axis=-1) * sin


def local_any(
    n, inputs, norm_gain, qkv_weight, head_lambda, head_gain, out_weight,
    key_one_pages, key_two_pages, value_pages, page_table, context_len, positions,
):
    steps = inputs.shape[0]
    own = page_table.shape[0]
    capacity = page_table.shape[1] * key_one_pages.shape[1]
    values = lax.all_gather(inputs, "gx", axis=2, tiled=True).astype(F32)
    factor = lax.rsqrt(jnp.mean(values * values, axis=-1, keepdims=True) + EPS)
    normed = (values * factor * norm_gain).astype(BF16)
    projected = jnp.einsum("sbd,dc->sbc", normed, qkv_weight, preferred_element_type=F32)
    received = lax.all_to_all(
        projected.astype(BF16), "gx", split_axis=1, concat_axis=2, tiled=True
    )
    cached = tuple(
        pool[page_table].reshape(own, capacity, H, -1)
        for pool in (key_one_pages, key_two_pages, value_pages)
    )
    both = received[..., : 4 * H * HD].reshape(steps, own, 4, H, HD).astype(F32)
    new_values = received[..., 4 * H * HD :].reshape(steps, own, H, 2 * HD)
    cos, sin = jax.vmap(lambda p: angles(p, steps))(positions.reshape(own, 1))
    cos, sin = (jnp.moveaxis(x, 0, 1)[:, :, None] for x in (cos, sin))
    turned = rotary(both, cos, sin).astype(BF16)
    place = jnp.arange(capacity, dtype=jnp.int32)
    allowed = (place[None, :] < context_len[:, None])[None, :, None, :]
    step = jnp.arange(steps)
    newer_allowed = (step[None, :] <= step[:, None])[:, None, None, :]

    def softmax_map(query, keys, news):
        older = jnp.einsum("tshd,sjhd->tshj", query, keys, preferred_element_type=F32)
        newer = jnp.einsum("tshd,eshd->tshe", query, news, preferred_element_type=F32)
        scores = jnp.concatenate(
            [jnp.where(allowed, older, -jnp.inf), jnp.where(newer_allowed, newer, -jnp.inf)], axis=-1
        )
        return jax.nn.softmax(scores * (1.0 / math.sqrt(HD)), axis=-1)

    first = softmax_map(turned[:, :, 0], cached[0], turned[:, :, 2])
    second = softmax_map(turned[:, :, 1], cached[1], turned[:, :, 3])
    mix = (first - head_lambda[:, None] * second).astype(BF16)
    mixed = jnp.einsum(
        "tshj,sjhf->tshf", mix[..., :capacity], cached[2], preferred_element_type=F32
    ) + jnp.einsum("tshe,eshf->tshf", mix[..., capacity:], new_values, preferred_element_type=F32)
    norm = lax.rsqrt(jnp.mean(mixed * mixed, axis=-1, keepdims=True) + EPS)
    grouped = (mixed * norm * head_gain.reshape(H, 2 * HD)).astype(BF16)
    whole = lax.all_gather(grouped.reshape(steps, own, -1), "gx", axis=1, tiled=True)
    branch = jnp.einsum("sbf,fd->sbd", whole, out_weight, preferred_element_type=F32)
    return (inputs.astype(F32) + branch).astype(BF16)


def solution(mesh):
    n = mesh.shape["gx"]
    placed = (
        P(None, "groups", "gx"),
        P(),
        P(None, "gx"),
        P(),
        P(),
        P(None, "gx"),
        P(("groups", "gx"), None, None),
        P(("groups", "gx"), None, None),
        P(("groups", "gx"), None, None),
        P(("groups", "gx"), None),
        P(("groups", "gx")),
        P(("groups", "gx")),
    )

    def chosen(inputs, norm_gain, qkv_weight, *rest):
        aligned = inputs.shape[2] % 128 == 0 and qkv_weight.shape[1] % 128 == 0
        single = rest[6].shape[0] == 1
        power = n >= 2 and n & (n - 1) == 0
        body = local if aligned and single and power else local_any
        return body(n, inputs, norm_gain, qkv_weight, *rest)

    return jax.shard_map(
        chosen, mesh=mesh, in_specs=placed, out_specs=P(None, "groups", "gx"), check_vma=False
    )
```

```python
import functools
import math

import jax
import jax.numpy as jnp
from jax import lax
from jax.experimental import pallas as pl
from jax.experimental.pallas import tpu as pltpu
from jax.sharding import PartitionSpec as P

H = 24
HD = 128
EPS = 1e-05
ROPE_BASE = 10000.0
F32 = jnp.float32
BF16 = jnp.bfloat16
VMEM_LIMIT = 16 * 1024 * 1024


def radices(n):
    rest = n // 2
    middle = 1
    while middle * middle * 4 <= rest:
        middle *= 2
    return rest // middle, middle


def swap(block, n, mask):
    return lax.ppermute(block, "gx", [(i, i ^ mask) for i in range(n)])


def outer_row(block, n, held=None):
    outer, middle = radices(n)
    arrived = [swap(block, n, o * 2 * middle) for o in range(1, outer)]
    return jnp.stack([block if held is None else held] + arrived)


def gather_blocks(block, n, held=None):
    _, middle = radices(n)
    rows = outer_row(block, n, held)
    mine = jnp.concatenate([rows] + [swap(rows, n, m * 2) for m in range(1, middle)])
    return mine, swap(mine, n, 1)


def owner(me, entry, core, n):
    outer, middle = radices(n)
    mask = (entry % outer) * (2 * middle) + (entry // outer) * 2 + core
    return jnp.bitwise_xor(me, mask)


def far(x):
    return pltpu.with_memory_space_constraint(x, pltpu.HBM)


def hint(us):
    return pl.CostEstimate(flops=0, bytes_accessed=int(us * 3_000_000), transcendentals=0)


def fetches(n, first, count, cores, me, from_ref, to_ref, sems):
    part = from_ref.shape[0] // n
    copies = []
    for index, core in enumerate(cores):
        for entry in range(count):
            slot = index * count + entry
            start = pl.multiple_of(owner(me, first + entry, core, n) * part, part)
            copies.append(
                pltpu.make_async_copy(
                    from_ref.at[pl.ds(start, part), :],
                    to_ref.at[slot],
                    sems.at[slot],
                )
            )
    return copies


def fetch_kernel(
    n, count, me_ref, block_ref, gain_ref, weight_ref, held, gain_out, weight_out, sems, other_sems
):
    copies = fetches(n, 0, count, (0, 1), me_ref[0], weight_ref, weight_out, sems)
    copies = [
        pltpu.make_async_copy(block_ref, held, other_sems.at[0]),
        pltpu.make_async_copy(gain_ref, gain_out, other_sems.at[1]),
    ] + copies
    for copy in copies:
        copy.start()
    for copy in copies:
        copy.wait()


def add_products(n, first, base, core, me, ref, gain_ref, weight_ref, total, squares):
    @pl.loop(0, ref.shape[0])
    def _(entry):
        shard = owner(me, first + entry, core, n)
        values = ref[entry].astype(F32)
        squares[...] += values * values
        scaled = (values * gain_ref[shard]).astype(BF16)
        total[...] += jnp.dot(scaled, weight_ref[base + entry], preferred_element_type=F32)


def open_kernel(
    n, me_ref, mine_ref, other_ref, gain_ref, held_ref, weight_ref, total, squares, later_ref, sems
):
    me = me_ref[0]
    outer = mine_ref.shape[0]
    copies = fetches(n, outer, n // 2 - outer, (0, 1), me, weight_ref, later_ref, sems)
    for copy in copies:
        copy.start()
    total[...] = jnp.zeros_like(total)
    squares[...] = jnp.zeros_like(squares)
    for core, ref in ((0, mine_ref), (1, other_ref)):
        add_products(n, 0, core * outer, core, me, ref, gain_ref, held_ref, total, squares)
    for copy in copies:
        copy.wait()


def more_kernel(
    n, first, base, core, me_ref, block_ref, gain_ref, weight_ref, total_in, squares_in, total, squares
):
    total[...] = total_in[...]
    squares[...] = squares_in[...]
    add_products(
        n, first, base, core, me_ref[0], block_ref, gain_ref, weight_ref, total, squares
    )


def close_kernel(
    n, first, base, core, me_ref, block_ref, gain_ref, weight_ref, total_in, squares_in, out_ref,
    total, squares, spread,
):
    more_kernel(
        n, first, base, core, me_ref, block_ref, gain_ref, weight_ref, total_in, squares_in,
        total, squares,
    )
    rows, part = squares.shape
    mean = jnp.sum(squares[...], axis=1, keepdims=True) * (1.0 / (n * part))
    factor = lax.rsqrt(mean + EPS)
    blocks = total.shape[1] // 128
    steps = rows // n
    for block in range(blocks):
        scaled = total[:, block * 128 : (block + 1) * 128] * factor
        for step in range(steps):
            spread[:, step * blocks + block, :] = scaled[step * n : (step + 1) * n]
    for target in range(n):
        out_ref[target] = spread[target, : steps * blocks, :].astype(BF16)


def project(me, block, gain, weight, n):
    rows, part = block.shape
    columns = weight.shape[1]
    pieces = rows // n * (columns // 128)
    outer, middle = radices(n)
    vmem = pl.BlockSpec(memory_space=pltpu.VMEM)
    smem = pl.BlockSpec(memory_space=pltpu.SMEM)
    hbm = pl.BlockSpec(memory_space=pltpu.HBM)
    params = pltpu.CompilerParams(vmem_limit_bytes=VMEM_LIMIT)
    sums = (jax.ShapeDtypeStruct((rows, columns), F32), jax.ShapeDtypeStruct((rows, part), F32))
    now, later_count = 2 * outer, n - 2 * outer

    held, gain, weight_now = pl.pallas_call(
        functools.partial(fetch_kernel, n, outer),
        out_shape=(
            pltpu.VMEM(block.shape, BF16),
            pltpu.VMEM(gain.shape, F32),
            pltpu.VMEM((now, part, columns), BF16),
        ),
        in_specs=[smem, hbm, hbm, hbm],
        out_specs=(vmem,) * 3,
        scratch_shapes=[pltpu.SemaphoreType.DMA((now,)), pltpu.SemaphoreType.DMA((2,))],
        compiler_params=params,
        cost_estimate=hint(5),
    )(me, far(block), far(gain), far(weight))
    row = outer_row(block, n, held)
    later = [swap(row, n, m * 2) for m in range(1, middle)]
    *partial, weight_later = pl.pallas_call(
        functools.partial(open_kernel, n),
        out_shape=sums + (pltpu.VMEM((later_count, part, columns), BF16),),
        in_specs=[smem] + [vmem] * 4 + [hbm],
        out_specs=(vmem,) * 3,
        scratch_shapes=[pltpu.SemaphoreType.DMA((later_count,))],
        compiler_params=params,
        cost_estimate=hint(5),
    )(
        me, row, swap(row, n, 1), gain, pltpu.with_memory_space_constraint(weight_now, pltpu.VMEM),
        far(weight),
    )
    later, partial = lax.optimization_barrier((later, partial))
    weight_later = pltpu.with_memory_space_constraint(weight_later, pltpu.VMEM)
    for m in range(1, middle):
        across = swap(later[m - 1], n, 1)
        for core, blocks in ((0, later[m - 1]), (1, across)):
            last = m == middle - 1 and core == 1
            spread = pltpu.VMEM((n, -(-pieces // 8) * 8, 128), F32)
            base = core * (later_count // 2) + (m - 1) * outer
            partial = pl.pallas_call(
                functools.partial(close_kernel if last else more_kernel, n, m * outer, base, core),
                out_shape=jax.ShapeDtypeStruct((n, pieces, 128), BF16) if last else sums,
                in_specs=[smem] + [vmem] * 5,
                out_specs=vmem if last else (vmem, vmem),
                scratch_shapes=[pltpu.VMEM(x.shape, F32) for x in sums] + [spread] if last else (),
                compiler_params=params,
                cost_estimate=hint(2),
            )(me, blocks, gain, weight_later, *partial)
    return partial


def attend_kernel(
    table_ref, length_ref, received_ref, cos_ref, sin_ref, lambda_ref, gain_ref,
    keys_one_ref, keys_two_ref, values_ref, out_ref, fresh,
):
    sources, pieces, _ = received_ref.shape
    steps = cos_ref.shape[0]
    blocks = pieces // steps
    pages, page, _ = keys_one_ref.shape
    capacity = pages * page
    for source in range(sources):
        piece = received_ref[source].astype(F32)
        for step in range(steps):
            fresh[step, source * blocks : (source + 1) * blocks, :] = piece[
                step * blocks : (step + 1) * blocks
            ]

    def heads(step, kind):
        return fresh[step, kind * H : (kind + 1) * H, :]

    def rotated(step, kind):
        values = heads(step, kind)
        turned = values * cos_ref[step] + pltpu.roll(values, HD // 2, 1) * sin_ref[step]
        return turned.astype(BF16).astype(F32)

    row = lax.broadcasted_iota(jnp.int32, (1, capacity), 1)
    place = jnp.zeros((1, capacity), jnp.int32)
    for index in range(pages):
        first = table_ref[0, index] * page
        inside = (row >= first) & (row < first + page)
        place = jnp.where(inside, row - first + index * page, place)
    allowed = place < length_ref[0]

    scale = 1.0 / math.sqrt(HD)
    head_row = lax.rem(lax.broadcasted_iota(jnp.int32, (steps * H, HD), 0), H)

    def softmax_map(kind, keys_ref):
        queries = [rotated(step, kind) for step in range(steps)]
        news = [rotated(step, kind + 2) for step in range(steps)]
        stacked = jnp.concatenate(queries, axis=0)
        apart = jnp.concatenate(
            [jnp.where(head_row == h, stacked, 0.0).astype(BF16) for h in range(H)], axis=1
        )
        older = lax.dot_general(
            apart, keys_ref[...].reshape(capacity, H * HD), (((1,), (1,)), ((), ())),
            preferred_element_type=F32,
        )
        older = jnp.where(allowed, older * scale, -1e38)
        parts = []
        for step in range(steps):
            cached = older[step * H : (step + 1) * H]
            newer = [
                jnp.sum(queries[step] * news[e], axis=1, keepdims=True) * scale
                for e in range(step + 1)
            ]
            top = jnp.max(cached, axis=1, keepdims=True)
            for value in newer:
                top = jnp.maximum(top, value)
            cached = jnp.exp(cached - top)
            newer = [jnp.exp(value - top) for value in newer]
            whole = jnp.sum(cached, axis=1, keepdims=True)
            for value in newer:
                whole = whole + value
            parts.append((cached / whole, [value / whole for value in newer]))
        return parts

    first = softmax_map(0, keys_one_ref)
    second = softmax_map(1, keys_two_ref)
    weight = lambda_ref[...]
    mix = jnp.concatenate(
        [first[step][0] - weight * second[step][0] for step in range(steps)], axis=0
    ).astype(BF16)
    spread = jnp.dot(mix, values_ref[...].reshape(capacity, -1), preferred_element_type=F32)
    wide_row = lax.broadcasted_iota(jnp.int32, (H, 2 * HD), 0)
    fresh_values = [
        jnp.concatenate(
            [fresh[e, pl.ds(4 * H + half, H, stride=2), :] for half in range(2)], axis=1
        )
        for e in range(steps)
    ]
    for step in range(steps):
        mixed = jnp.zeros((H, 2 * HD), F32)
        for h in range(H):
            block = spread[step * H : (step + 1) * H, h * 2 * HD : (h + 1) * 2 * HD]
            mixed = jnp.where(wide_row == h, block, mixed)
        for e in range(step + 1):
            share = first[step][1][e] - weight * second[step][1][e]
            mixed = mixed + share.astype(BF16).astype(F32) * fresh_values[e]
        norm = lax.rsqrt(jnp.mean(mixed * mixed, axis=1, keepdims=True) + EPS)
        out_ref[step * H : (step + 1) * H, :] = (mixed * norm * gain_ref[...]).astype(BF16)


def attend(table, length, received, cos, sin, weights, gain, keys_one, keys_two, values):
    steps = cos.shape[0]
    sources, pieces, _ = received.shape
    vmem = pl.BlockSpec(memory_space=pltpu.VMEM)
    smem = pl.BlockSpec(memory_space=pltpu.SMEM)
    held = [pltpu.with_memory_space_constraint(x, pltpu.VMEM) for x in (keys_one, keys_two, values)]
    return pl.pallas_call(
        attend_kernel,
        out_shape=jax.ShapeDtypeStruct((steps * H, 2 * HD), BF16),
        in_specs=[smem, smem] + [vmem] * 8,
        out_specs=vmem,
        scratch_shapes=[pltpu.VMEM((steps, sources * (pieces // steps), 128), F32)],
        compiler_params=pltpu.CompilerParams(vmem_limit_bytes=VMEM_LIMIT),
        cost_estimate=hint(10),
    )(table, length, received, cos, sin, weights, gain, *held)


def output_kernel(n, me_ref, mine_ref, other_ref, inputs_ref, weight_ref, out_ref, rows_ref, total):
    me = me_ref[0]
    half, heads, width = mine_ref.shape
    steps = heads // H
    lanes = width // 128
    for entry in range(half):
        for core, ref in ((0, mine_ref), (1, other_ref)):
            start = pl.multiple_of(owner(me, entry, core, n) * heads, 8)
            block = ref[entry].astype(F32)
            for lane in range(lanes):
                rows_ref[lane, pl.ds(start, heads), :] = block[:, lane * 128 : (lane + 1) * 128]
    total[...] = jnp.zeros_like(total)
    for h in range(H):
        left = jnp.concatenate(
            [
                jnp.concatenate(
                    [rows_ref[lane, pl.ds(step * H + h, n, stride=heads), :] for lane in range(lanes)],
                    axis=1,
                )
                for step in range(steps)
            ],
            axis=0,
        ).astype(BF16)
        total[...] += jnp.dot(
            left, weight_ref[h * width : (h + 1) * width, :], preferred_element_type=F32
        )
    for step in range(steps):
        out_ref[step] = (
            inputs_ref[step].astype(F32) + total[step * n : (step + 1) * n]
        ).astype(BF16)


def keep_kernel(block_ref, from_ref, held, to_ref, sem):
    copy = pltpu.make_async_copy(from_ref, to_ref, sem)
    copy.start()
    held[...] = block_ref[...]
    copy.wait()


def keep(block, weight):
    vmem = pl.BlockSpec(memory_space=pltpu.VMEM)
    return pl.pallas_call(
        keep_kernel,
        out_shape=(
            jax.ShapeDtypeStruct(block.shape, block.dtype),
            pltpu.VMEM(weight.shape, weight.dtype),
        ),
        in_specs=[vmem, pl.BlockSpec(memory_space=pltpu.HBM)],
        out_specs=(vmem, vmem),
        scratch_shapes=[pltpu.SemaphoreType.DMA],
        compiler_params=pltpu.CompilerParams(vmem_limit_bytes=4 * 1024 * 1024),
        cost_estimate=hint(3),
    )(block, far(weight))


def output(me, mine, other, inputs, weight, n):
    half, heads, width = mine.shape
    vmem = pl.BlockSpec(memory_space=pltpu.VMEM)
    steps, rows, columns = inputs.shape
    return pl.pallas_call(
        functools.partial(output_kernel, n),
        out_shape=jax.ShapeDtypeStruct(inputs.shape, BF16),
        in_specs=[pl.BlockSpec(memory_space=pltpu.SMEM), vmem, vmem, vmem, vmem],
        out_specs=vmem,
        scratch_shapes=[
            pltpu.VMEM((width // 128, n * heads, 128), F32),
            pltpu.VMEM((steps * rows, columns), F32),
        ],
        compiler_params=pltpu.CompilerParams(vmem_limit_bytes=VMEM_LIMIT),
    )(me, mine, other, inputs, pltpu.with_memory_space_constraint(weight, pltpu.VMEM))


def angles(positions, steps):
    half = HD // 2
    frequency = jnp.exp(-math.log(ROPE_BASE) * 2.0 * jnp.arange(half, dtype=F32) / HD)
    places = (positions + jnp.arange(steps, dtype=jnp.int32)).astype(F32)
    turns = places[:, None] * frequency[None, :]
    cosine, sine = jnp.cos(turns), jnp.sin(turns)
    cos = jnp.concatenate([cosine, cosine], axis=-1)
    sin = jnp.concatenate([-sine, sine], axis=-1)
    return cos[:, None, :], sin[:, None, :]


def local(
    n, inputs, norm_gain, qkv_weight, head_lambda, head_gain, out_weight,
    key_one_pages, key_two_pages, value_pages, page_table, context_len, positions,
):
    steps, rows, part = inputs.shape
    me = lax.axis_index("gx").astype(jnp.int32).reshape(1)
    block = inputs.reshape(steps * rows, part)
    sent = project(me, block, norm_gain.reshape(n, 1, part), qkv_weight, n)
    received = lax.all_to_all(sent, "gx", 0, 0)
    cos, sin = angles(positions, steps)
    attended = attend(
        page_table, context_len, received, cos, sin, head_lambda.reshape(H, 1),
        head_gain.reshape(H, 2 * HD), key_one_pages, key_two_pages, value_pages,
    )
    held, weight = keep(attended, out_weight)
    mine, other = gather_blocks(attended, n, held)
    return output(me, mine, other, inputs, weight, n)


def rotary(vectors, cos, sin):
    return vectors * cos + jnp.roll(vectors, HD // 2, axis=-1) * sin


def local_any(
    n, inputs, norm_gain, qkv_weight, head_lambda, head_gain, out_weight,
    key_one_pages, key_two_pages, value_pages, page_table, context_len, positions,
):
    steps = inputs.shape[0]
    own = page_table.shape[0]
    capacity = page_table.shape[1] * key_one_pages.shape[1]
    values = lax.all_gather(inputs, "gx", axis=2, tiled=True).astype(F32)
    factor = lax.rsqrt(jnp.mean(values * values, axis=-1, keepdims=True) + EPS)
    normed = (values * factor * norm_gain).astype(BF16)
    projected = jnp.einsum("sbd,dc->sbc", normed, qkv_weight, preferred_element_type=F32)
    received = lax.all_to_all(
        projected.astype(BF16), "gx", split_axis=1, concat_axis=2, tiled=True
    )
    cached = tuple(
        pool[page_table].reshape(own, capacity, H, -1)
        for pool in (key_one_pages, key_two_pages, value_pages)
    )
    both = received[..., : 4 * H * HD].reshape(steps, own, 4, H, HD).astype(F32)
    new_values = received[..., 4 * H * HD :].reshape(steps, own, H, 2 * HD)
    cos, sin = jax.vmap(lambda p: angles(p, steps))(positions.reshape(own, 1))
    cos, sin = (jnp.moveaxis(x, 0, 1)[:, :, None] for x in (cos, sin))
    turned = rotary(both, cos, sin).astype(BF16)
    place = jnp.arange(capacity, dtype=jnp.int32)
    allowed = (place[None, :] < context_len[:, None])[None, :, None, :]
    step = jnp.arange(steps)
    newer_allowed = (step[None, :] <= step[:, None])[:, None, None, :]

    def softmax_map(query, keys, news):
        older = jnp.einsum("tshd,sjhd->tshj", query, keys, preferred_element_type=F32)
        newer = jnp.einsum("tshd,eshd->tshe", query, news, preferred_element_type=F32)
        scores = jnp.concatenate(
            [jnp.where(allowed, older, -jnp.inf), jnp.where(newer_allowed, newer, -jnp.inf)], axis=-1
        )
        return jax.nn.softmax(scores * (1.0 / math.sqrt(HD)), axis=-1)

    first = softmax_map(turned[:, :, 0], cached[0], turned[:, :, 2])
    second = softmax_map(turned[:, :, 1], cached[1], turned[:, :, 3])
    mix = (first - head_lambda[:, None] * second).astype(BF16)
    mixed = jnp.einsum(
        "tshj,sjhf->tshf", mix[..., :capacity], cached[2], preferred_element_type=F32
    ) + jnp.einsum("tshe,eshf->tshf", mix[..., capacity:], new_values, preferred_element_type=F32)
    norm = lax.rsqrt(jnp.mean(mixed * mixed, axis=-1, keepdims=True) + EPS)
    grouped = (mixed * norm * head_gain.reshape(H, 2 * HD)).astype(BF16)
    whole = lax.all_gather(grouped.reshape(steps, own, -1), "gx", axis=1, tiled=True)
    branch = jnp.einsum("sbf,fd->sbd", whole, out_weight, preferred_element_type=F32)
    return (inputs.astype(F32) + branch).astype(BF16)


def solution(mesh):
    n = mesh.shape["gx"]
    placed = (
        P(None, "groups", "gx"),
        P(),
        P(None, "gx"),
        P(),
        P(),
        P(None, "gx"),
        P(("groups", "gx"), None, None),
        P(("groups", "gx"), None, None),
        P(("groups", "gx"), None, None),
        P(("groups", "gx"), None),
        P(("groups", "gx")),
        P(("groups", "gx")),
    )

    def chosen(inputs, norm_gain, qkv_weight, *rest):
        aligned = inputs.shape[2] % 128 == 0 and qkv_weight.shape[1] % 128 == 0
        single = rest[6].shape[0] == 1
        power = n >= 4 and n & (n - 1) == 0
        body = local if aligned and single and power else local_any
        return body(n, inputs, norm_gain, qkv_weight, *rest)

    return jax.shard_map(
        chosen, mesh=mesh, in_specs=placed, out_specs=P(None, "groups", "gx"), check_vma=False
    )
```

```python
import functools
import math

import jax
import jax.numpy as jnp
from jax import lax
from jax.experimental import pallas as pl
from jax.experimental.pallas import tpu as pltpu
from jax.sharding import PartitionSpec as P

H = 24
HD = 128
EPS = 1e-05
ROPE_BASE = 10000.0
F32 = jnp.float32
BF16 = jnp.bfloat16
VMEM_LIMIT = 16 * 1024 * 1024


def radices(n):
    rest = n // 2
    middle = 1
    while middle * middle * 4 <= rest:
        middle *= 2
    return rest // middle, middle


def swap(block, n, mask):
    return lax.ppermute(block, "gx", [(i, i ^ mask) for i in range(n)])


def gather_blocks(block, n, first_aside, second_aside):
    outer, middle = radices(n)
    arrived = [swap(block, n, o * 2 * middle) for o in range(1, outer)]
    rows = jnp.stack([first_aside(block)] + arrived)
    others = [swap(rows, n, m * 2) for m in range(1, middle)]
    rows, others = lax.optimization_barrier((second_aside(rows), others))
    mine = jnp.concatenate([rows] + others)
    return mine, swap(mine, n, 1)


def owner(me, entry, core, n):
    outer, middle = radices(n)
    mask = (entry % outer) * (2 * middle) + (entry // outer) * 2 + core
    return jnp.bitwise_xor(me, mask)


def far(x):
    return pltpu.with_memory_space_constraint(x, pltpu.HBM)


def hint(us):
    return pl.CostEstimate(flops=0, bytes_accessed=int(us * 3_000_000), transcendentals=0)


def fetches(n, first, count, cores, me, from_ref, to_ref, sems):
    part = from_ref.shape[0] // n
    copies = []
    for index, core in enumerate(cores):
        for entry in range(count):
            slot = index * count + entry
            start = pl.multiple_of(owner(me, first + entry, core, n) * part, part)
            copies.append(
                pltpu.make_async_copy(
                    from_ref.at[pl.ds(start, part), :],
                    to_ref.at[slot],
                    sems.at[slot],
                )
            )
    return copies


def slots(n):
    outer, middle = radices(n)
    return [
        (m * outer + entry, core) for m in range(middle) for core in range(2) for entry in range(outer)
    ]


def fetches(n, order, me, from_ref, to_ref, sems):
    part = from_ref.shape[0] // n
    copies = []
    for slot, (entry, core) in enumerate(order):
        start = pl.multiple_of(owner(me, entry, core, n) * part, part)
        copies.append(
            pltpu.make_async_copy(
                from_ref.at[pl.ds(start, part), :], to_ref.at[slot], sems.at[slot]
            )
        )
    return copies


def fetch_kernel(
    n, order, me_ref, block_ref, gain_ref, weight_ref, held, gain_out, weight_out, sems, other_sems
):
    copies = [
        pltpu.make_async_copy(block_ref, held, other_sems.at[0]),
        pltpu.make_async_copy(gain_ref, gain_out, other_sems.at[1]),
    ] + fetches(n, order, me_ref[0], weight_ref, weight_out, sems)
    for copy in copies:
        copy.start()
    for copy in copies:
        copy.wait()


def fetch(me, block, gain, weight, n, order):
    part, columns = weight.shape[0] // n, weight.shape[1]
    vmem = pl.BlockSpec(memory_space=pltpu.VMEM)
    hbm = pl.BlockSpec(memory_space=pltpu.HBM)
    return pl.pallas_call(
        functools.partial(fetch_kernel, n, order),
        out_shape=(
            pltpu.VMEM(block.shape, BF16),
            pltpu.VMEM(gain.shape, F32),
            pltpu.VMEM((len(order), part, columns), BF16),
        ),
        in_specs=[pl.BlockSpec(memory_space=pltpu.SMEM), hbm, hbm, hbm],
        out_specs=(vmem,) * 3,
        scratch_shapes=[
            pltpu.SemaphoreType.DMA((len(order),)),
            pltpu.SemaphoreType.DMA((2,)),
        ],
        compiler_params=pltpu.CompilerParams(vmem_limit_bytes=4 * 1024 * 1024),
        cost_estimate=hint(5),
    )(me, far(block), far(gain), far(weight))


def near(x):
    return pltpu.with_memory_space_constraint(x, pltpu.VMEM)


def add_products(n, order, me, refs, gain_ref, weights, total, squares):
    rows = total.shape[0]
    sums = None
    square = squares[...]
    for (entry, core), ref, (held, slot) in zip(order, refs, weights, strict=True):
        values = ref[...].astype(F32)
        square = square + values * values
        scaled = values * gain_ref[owner(me, entry, core, n)]
        high = scaled.astype(BF16)
        low = (scaled - high.astype(F32)).astype(BF16)
        product = jnp.dot(
            jnp.concatenate([high, low], axis=0), held[slot], preferred_element_type=F32
        )
        sums = product if sums is None else sums + product
    squares[...] = square
    total[...] += sums[:rows] + sums[rows:]


def open_kernel(n, cuts, me_ref, mine_ref, other_ref, gain_ref, weight_ref, *rest):
    *helds, total, squares, later_ref, sems = rest
    me = me_ref[0]
    outer = mine_ref.shape[0]
    order = slots(n)
    copies = fetches(n, order[cuts[-1] :], me, weight_ref, later_ref, sems)
    for copy in copies:
        copy.start()
    total[...] = jnp.zeros_like(total)
    squares[...] = jnp.zeros_like(squares)
    refs = [mine_ref.at[e] for e in range(outer)] + [other_ref.at[e] for e in range(outer)]
    add_products(
        n, order[: 2 * outer], me, refs, gain_ref, places(helds, cuts)[: 2 * outer], total, squares
    )
    for copy in copies:
        copy.wait()


def places(helds, cuts):
    found = []
    for held, start, stop in zip(helds, (0,) + cuts[:-1], cuts, strict=True):
        found += [(held, slot) for slot in range(stop - start)]
    return found


def more_kernel(
    n, cuts, first, me_ref, block_ref, gain_ref, *rest,
):
    *helds, total_in, squares_in, total, squares = rest
    total[...] = total_in[...]
    squares[...] = squares_in[...]
    outer = block_ref.shape[0]
    picked = slice(first, first + outer)
    add_products(
        n, slots(n)[picked], me_ref[0], [block_ref.at[e] for e in range(outer)], gain_ref,
        places(helds, cuts)[picked], total, squares,
    )


def close_kernel(n, cuts, first, me_ref, block_ref, gain_ref, *rest):
    *refs, out_ref, total, squares, spread = rest
    more_kernel(n, cuts, first, me_ref, block_ref, gain_ref, *refs, total, squares)
    rows, part = squares.shape
    mean = jnp.sum(squares[...], axis=1, keepdims=True) * (1.0 / (n * part))
    factor = lax.rsqrt(mean + EPS)
    blocks = total.shape[1] // 128
    steps = rows // n
    for block in range(blocks):
        scaled = total[:, block * 128 : (block + 1) * 128] * factor
        for step in range(steps):
            spread[:, step * blocks + block, :] = scaled[step * n : (step + 1) * n]
    for target in range(n):
        out_ref[target] = spread[target, : steps * blocks, :].astype(BF16)


def project(me, block, gain, weight, n):
    rows, part = block.shape
    columns = weight.shape[1]
    pieces = rows // n * (columns // 128)
    outer, middle = radices(n)
    vmem = pl.BlockSpec(memory_space=pltpu.VMEM)
    smem = pl.BlockSpec(memory_space=pltpu.SMEM)
    hbm = pl.BlockSpec(memory_space=pltpu.HBM)
    params = pltpu.CompilerParams(vmem_limit_bytes=VMEM_LIMIT)
    sums = (jax.ShapeDtypeStruct((rows, columns), F32), jax.ShapeDtypeStruct((rows, part), F32))
    order = slots(n)
    cut = 2 * outer
    cuts = (cut,)

    arrived = [swap(block, n, o * 2 * middle) for o in range(1, outer)]
    held, gain_held, weight_now = fetch(me, block, gain, weight, n, order[:cut])
    row = jnp.stack([held] + arrived)
    later = [swap(row, n, m * 2) for m in range(1, middle)]
    helds = (near(weight_now),)
    *partial, weight_later = pl.pallas_call(
        functools.partial(open_kernel, n, cuts),
        out_shape=sums + (pltpu.VMEM((n - cut, part, columns), BF16),),
        in_specs=[smem] + [vmem] * 3 + [hbm, vmem],
        out_specs=(vmem,) * 3,
        scratch_shapes=[pltpu.SemaphoreType.DMA((n - cut,))],
        compiler_params=params,
        cost_estimate=hint(5),
    )(me, row, swap(row, n, 1), gain_held, far(weight), *helds)
    later, partial = lax.optimization_barrier((later, partial))
    helds += (near(weight_later),)
    cuts += (n,)
    for m in range(1, middle):
        across = swap(later[m - 1], n, 1)
        for core, blocks in ((0, later[m - 1]), (1, across)):
            last = m == middle - 1 and core == 1
            spread = pltpu.VMEM((n, -(-pieces // 8) * 8, 128), F32)
            first = (2 * m + core) * outer
            partial = pl.pallas_call(
                functools.partial(close_kernel if last else more_kernel, n, cuts, first),
                out_shape=jax.ShapeDtypeStruct((n, pieces, 128), BF16) if last else sums,
                in_specs=[smem] + [vmem] * 6,
                out_specs=vmem if last else (vmem, vmem),
                scratch_shapes=[pltpu.VMEM(x.shape, F32) for x in sums] + [spread] if last else (),
                compiler_params=params,
                cost_estimate=hint(2),
            )(me, blocks, gain_held, *helds, *partial)
    return partial


def attend_kernel(
    table_ref, length_ref, received_ref, cos_ref, sin_ref, lambda_ref, gain_ref,
    keys_one_ref, keys_two_ref, values_ref, out_ref, fresh,
):
    sources, pieces, _ = received_ref.shape
    steps = cos_ref.shape[0]
    blocks = pieces // steps
    pages, page, _ = keys_one_ref.shape
    capacity = pages * page
    for source in range(sources):
        piece = received_ref[source].astype(F32)
        for step in range(steps):
            fresh[step, source * blocks : (source + 1) * blocks, :] = piece[
                step * blocks : (step + 1) * blocks
            ]

    def heads(step, kind):
        return fresh[step, kind * H : (kind + 1) * H, :]

    def rotated(step, kind):
        values = heads(step, kind)
        turned = values * cos_ref[step] + pltpu.roll(values, HD // 2, 1) * sin_ref[step]
        return turned.astype(BF16).astype(F32)

    row = lax.broadcasted_iota(jnp.int32, (1, capacity), 1)
    place = jnp.zeros((1, capacity), jnp.int32)
    for index in range(pages):
        first = table_ref[0, index] * page
        inside = (row >= first) & (row < first + page)
        place = jnp.where(inside, row - first + index * page, place)
    allowed = place < length_ref[0]

    scale = 1.0 / math.sqrt(HD)
    head_row = lax.rem(lax.broadcasted_iota(jnp.int32, (steps * H, HD), 0), H)

    def softmax_map(kind, keys_ref):
        queries = [rotated(step, kind) for step in range(steps)]
        news = [rotated(step, kind + 2) for step in range(steps)]
        stacked = jnp.concatenate(queries, axis=0)
        apart = jnp.concatenate(
            [jnp.where(head_row == h, stacked, 0.0).astype(BF16) for h in range(H)], axis=1
        )
        older = lax.dot_general(
            apart, keys_ref[...].reshape(capacity, H * HD), (((1,), (1,)), ((), ())),
            preferred_element_type=F32,
        )
        older = jnp.where(allowed, older * scale, -1e38)
        parts = []
        for step in range(steps):
            cached = older[step * H : (step + 1) * H]
            newer = [
                jnp.sum(queries[step] * news[e], axis=1, keepdims=True) * scale
                for e in range(step + 1)
            ]
            top = jnp.max(cached, axis=1, keepdims=True)
            for value in newer:
                top = jnp.maximum(top, value)
            cached = jnp.exp(cached - top)
            newer = [jnp.exp(value - top) for value in newer]
            whole = jnp.sum(cached, axis=1, keepdims=True)
            for value in newer:
                whole = whole + value
            parts.append((cached / whole, [value / whole for value in newer]))
        return parts

    first = softmax_map(0, keys_one_ref)
    second = softmax_map(1, keys_two_ref)
    weight = lambda_ref[...]
    mix = jnp.concatenate(
        [first[step][0] - weight * second[step][0] for step in range(steps)], axis=0
    ).astype(BF16)
    spread = jnp.dot(mix, values_ref[...].reshape(capacity, -1), preferred_element_type=F32)
    wide_row = lax.broadcasted_iota(jnp.int32, (H, 2 * HD), 0)
    fresh_values = [
        jnp.concatenate(
            [fresh[e, pl.ds(4 * H + half, H, stride=2), :] for half in range(2)], axis=1
        )
        for e in range(steps)
    ]
    for step in range(steps):
        mixed = jnp.zeros((H, 2 * HD), F32)
        for h in range(H):
            block = spread[step * H : (step + 1) * H, h * 2 * HD : (h + 1) * 2 * HD]
            mixed = jnp.where(wide_row == h, block, mixed)
        for e in range(step + 1):
            share = first[step][1][e] - weight * second[step][1][e]
            mixed = mixed + share.astype(BF16).astype(F32) * fresh_values[e]
        norm = lax.rsqrt(jnp.mean(mixed * mixed, axis=1, keepdims=True) + EPS)
        out_ref[step * H : (step + 1) * H, :] = (mixed * norm * gain_ref[...]).astype(BF16)


def attend(table, length, received, cos, sin, weights, gain, keys_one, keys_two, values):
    steps = cos.shape[0]
    sources, pieces, _ = received.shape
    vmem = pl.BlockSpec(memory_space=pltpu.VMEM)
    smem = pl.BlockSpec(memory_space=pltpu.SMEM)
    held = [near(x) for x in (keys_one, keys_two, values)]
    return pl.pallas_call(
        attend_kernel,
        out_shape=jax.ShapeDtypeStruct((steps * H, 2 * HD), BF16),
        in_specs=[smem, smem] + [vmem] * 8,
        out_specs=vmem,
        scratch_shapes=[pltpu.VMEM((steps, sources * (pieces // steps), 128), F32)],
        compiler_params=pltpu.CompilerParams(vmem_limit_bytes=VMEM_LIMIT),
        cost_estimate=hint(10),
    )(table, length, received, cos, sin, weights, gain, *held)


def output_kernel(n, me_ref, mine_ref, other_ref, inputs_ref, *rest):
    *weights, out_ref, rows_ref = rest
    me = me_ref[0]
    half, heads, width = mine_ref.shape
    steps = heads // H
    lanes = width // 128
    for entry in range(half):
        for core, ref in ((0, mine_ref), (1, other_ref)):
            start = pl.multiple_of(owner(me, entry, core, n) * heads, 8)
            block = ref[entry].astype(F32)
            for lane in range(lanes):
                rows_ref[lane, pl.ds(start, heads), :] = block[:, lane * 128 : (lane + 1) * 128]
    total = None
    for h in range(H):
        left = jnp.concatenate(
            [
                jnp.concatenate(
                    [rows_ref[lane, pl.ds(step * H + h, n, stride=heads), :] for lane in range(lanes)],
                    axis=1,
                )
                for step in range(steps)
            ],
            axis=0,
        ).astype(BF16)
        held = weights[h * len(weights) // H]
        at = h * width % held.shape[0]
        product = jnp.dot(left, held[at : at + width, :], preferred_element_type=F32)
        total = product if total is None else total + product
    for step in range(steps):
        out_ref[step] = (
            inputs_ref[step].astype(F32) + total[step * n : (step + 1) * n]
        ).astype(BF16)


def keep_kernel(half, block_ref, from_ref, held, to_ref, sem):
    rows = to_ref.shape[0]
    copy = pltpu.make_async_copy(from_ref.at[pl.ds(half * rows, rows), :], to_ref, sem)
    copy.start()
    held[...] = block_ref[...]
    copy.wait()


def keep(block, weight, half, us):
    vmem = pl.BlockSpec(memory_space=pltpu.VMEM)
    return pl.pallas_call(
        functools.partial(keep_kernel, half),
        out_shape=(
            jax.ShapeDtypeStruct(block.shape, block.dtype),
            pltpu.VMEM((weight.shape[0] // 2, weight.shape[1]), weight.dtype),
        ),
        in_specs=[vmem, pl.BlockSpec(memory_space=pltpu.HBM)],
        out_specs=(vmem, vmem),
        scratch_shapes=[pltpu.SemaphoreType.DMA],
        compiler_params=pltpu.CompilerParams(vmem_limit_bytes=4 * 1024 * 1024),
        cost_estimate=hint(us),
    )(block, far(weight))


def output(me, attended, inputs, weight, n):
    kept = []

    def aside(half, block):
        block, part = keep(block, weight, half, 2)
        kept.append(near(part))
        return block

    mine, other = gather_blocks(
        attended, n, functools.partial(aside, 0), functools.partial(aside, 1)
    )
    half, heads, width = mine.shape
    vmem = pl.BlockSpec(memory_space=pltpu.VMEM)
    return pl.pallas_call(
        functools.partial(output_kernel, n),
        out_shape=jax.ShapeDtypeStruct(inputs.shape, BF16),
        in_specs=[pl.BlockSpec(memory_space=pltpu.SMEM)] + [vmem] * 5,
        out_specs=vmem,
        scratch_shapes=[pltpu.VMEM((width // 128, n * heads, 128), F32)],
        compiler_params=pltpu.CompilerParams(vmem_limit_bytes=VMEM_LIMIT),
    )(me, mine, other, inputs, *kept)


def angles(positions, steps):
    half = HD // 2
    frequency = jnp.exp(-math.log(ROPE_BASE) * 2.0 * jnp.arange(half, dtype=F32) / HD)
    places = (positions + jnp.arange(steps, dtype=jnp.int32)).astype(F32)
    turns = places[:, None] * frequency[None, :]
    cosine, sine = jnp.cos(turns), jnp.sin(turns)
    cos = jnp.concatenate([cosine, cosine], axis=-1)
    sin = jnp.concatenate([-sine, sine], axis=-1)
    return cos[:, None, :], sin[:, None, :]


def turn_kernel(positions_ref, after_ref, cos_ref, sin_ref):
    steps = cos_ref.shape[0]
    lane = lax.broadcasted_iota(jnp.int32, (8, HD), 1)
    step = lax.broadcasted_iota(jnp.int32, (8, HD), 0)
    pair = lax.rem(lane, HD // 2).astype(F32)
    frequency = jnp.exp(-math.log(ROPE_BASE) * 2.0 * pair / HD)
    turns = (positions_ref[0] + step).astype(F32) * frequency
    cos = jnp.cos(turns)
    sin = jnp.where(lane < HD // 2, -1.0, 1.0) * jnp.sin(turns)
    for index in range(steps):
        cos_ref[index] = cos[index : index + 1]
        sin_ref[index] = sin[index : index + 1]


def turn(positions, after, steps):
    vmem = pl.BlockSpec(memory_space=pltpu.VMEM)
    return pl.pallas_call(
        turn_kernel,
        out_shape=(jax.ShapeDtypeStruct((steps, 1, HD), F32),) * 2,
        in_specs=[pl.BlockSpec(memory_space=pltpu.SMEM), pl.BlockSpec(memory_space=pl.ANY)],
        out_specs=(vmem, vmem),
        compiler_params=pltpu.CompilerParams(vmem_limit_bytes=4 * 1024 * 1024),
        cost_estimate=hint(1),
    )(positions, after)


def local(
    n, inputs, norm_gain, qkv_weight, head_lambda, head_gain, out_weight,
    key_one_pages, key_two_pages, value_pages, page_table, context_len, positions,
):
    steps, rows, part = inputs.shape
    me = lax.axis_index("gx").astype(jnp.int32).reshape(1)
    block = inputs.reshape(steps * rows, part)
    sent = project(me, block, norm_gain.reshape(n, 1, part), qkv_weight, n)
    received = lax.all_to_all(sent, "gx", 0, 0)
    cos, sin = turn(positions, sent, steps)
    attended = attend(
        page_table, context_len, received, cos, sin, head_lambda.reshape(H, 1),
        head_gain.reshape(H, 2 * HD), key_one_pages, key_two_pages, value_pages,
    )
    return output(me, attended, inputs, out_weight, n)


def rotary(vectors, cos, sin):
    return vectors * cos + jnp.roll(vectors, HD // 2, axis=-1) * sin


def local_any(
    n, inputs, norm_gain, qkv_weight, head_lambda, head_gain, out_weight,
    key_one_pages, key_two_pages, value_pages, page_table, context_len, positions,
):
    steps = inputs.shape[0]
    own = page_table.shape[0]
    capacity = page_table.shape[1] * key_one_pages.shape[1]
    values = lax.all_gather(inputs, "gx", axis=2, tiled=True).astype(F32)
    factor = lax.rsqrt(jnp.mean(values * values, axis=-1, keepdims=True) + EPS)
    normed = (values * factor * norm_gain).astype(BF16)
    projected = jnp.einsum("sbd,dc->sbc", normed, qkv_weight, preferred_element_type=F32)
    received = lax.all_to_all(
        projected.astype(BF16), "gx", split_axis=1, concat_axis=2, tiled=True
    )
    cached = tuple(
        pool[page_table].reshape(own, capacity, H, -1)
        for pool in (key_one_pages, key_two_pages, value_pages)
    )
    both = received[..., : 4 * H * HD].reshape(steps, own, 4, H, HD).astype(F32)
    new_values = received[..., 4 * H * HD :].reshape(steps, own, H, 2 * HD)
    cos, sin = jax.vmap(lambda p: angles(p, steps))(positions.reshape(own, 1))
    cos, sin = (jnp.moveaxis(x, 0, 1)[:, :, None] for x in (cos, sin))
    turned = rotary(both, cos, sin).astype(BF16)
    place = jnp.arange(capacity, dtype=jnp.int32)
    allowed = (place[None, :] < context_len[:, None])[None, :, None, :]
    step = jnp.arange(steps)
    newer_allowed = (step[None, :] <= step[:, None])[:, None, None, :]

    def softmax_map(query, keys, news):
        older = jnp.einsum("tshd,sjhd->tshj", query, keys, preferred_element_type=F32)
        newer = jnp.einsum("tshd,eshd->tshe", query, news, preferred_element_type=F32)
        scores = jnp.concatenate(
            [jnp.where(allowed, older, -jnp.inf), jnp.where(newer_allowed, newer, -jnp.inf)], axis=-1
        )
        return jax.nn.softmax(scores * (1.0 / math.sqrt(HD)), axis=-1)

    first = softmax_map(turned[:, :, 0], cached[0], turned[:, :, 2])
    second = softmax_map(turned[:, :, 1], cached[1], turned[:, :, 3])
    mix = (first - head_lambda[:, None] * second).astype(BF16)
    mixed = jnp.einsum(
        "tshj,sjhf->tshf", mix[..., :capacity], cached[2], preferred_element_type=F32
    ) + jnp.einsum("tshe,eshf->tshf", mix[..., capacity:], new_values, preferred_element_type=F32)
    norm = lax.rsqrt(jnp.mean(mixed * mixed, axis=-1, keepdims=True) + EPS)
    grouped = (mixed * norm * head_gain.reshape(H, 2 * HD)).astype(BF16)
    whole = lax.all_gather(grouped.reshape(steps, own, -1), "gx", axis=1, tiled=True)
    branch = jnp.einsum("sbf,fd->sbd", whole, out_weight, preferred_element_type=F32)
    return (inputs.astype(F32) + branch).astype(BF16)


def solution(mesh):
    n = mesh.shape["gx"]
    placed = (
        P(None, "groups", "gx"),
        P(),
        P(None, "gx"),
        P(),
        P(),
        P(None, "gx"),
        P(("groups", "gx"), None, None),
        P(("groups", "gx"), None, None),
        P(("groups", "gx"), None, None),
        P(("groups", "gx"), None),
        P(("groups", "gx")),
        P(("groups", "gx")),
    )

    def chosen(inputs, norm_gain, qkv_weight, *rest):
        aligned = inputs.shape[2] % 128 == 0 and qkv_weight.shape[1] % 128 == 0
        single = rest[6].shape[0] == 1
        power = n >= 4 and n & (n - 1) == 0
        body = local if aligned and single and power else local_any
        return body(n, inputs, norm_gain, qkv_weight, *rest)

    return jax.shard_map(
        chosen, mesh=mesh, in_specs=placed, out_specs=P(None, "groups", "gx"), check_vma=False
    )
```

```python
import functools
import math

import jax
import jax.numpy as jnp
from jax import lax
from jax.experimental import pallas as pl
from jax.experimental.pallas import tpu as pltpu
from jax.sharding import PartitionSpec as P

H = 24
HD = 128
EPS = 1e-05
ROPE_BASE = 10000.0
F32 = jnp.float32
BF16 = jnp.bfloat16
VMEM_LIMIT = 16 * 1024 * 1024


def radices(n):
    rest = n // 2
    middle = 1
    while middle * middle * 4 <= rest:
        middle *= 2
    return rest // middle, middle


def swap(block, n, mask):
    return lax.ppermute(block, "gx", [(i, i ^ mask) for i in range(n)])


def gather_blocks(block, n, first_aside, second_aside):
    outer, middle = radices(n)
    arrived = [swap(block, n, o * 2 * middle) for o in range(1, outer)]
    rows = jnp.stack([first_aside(block)] + arrived)
    others = [swap(rows, n, m * 2) for m in range(1, middle)]
    rows, others = lax.optimization_barrier((second_aside(rows), others))
    mine = jnp.concatenate([rows] + others)
    return mine, swap(mine, n, 1)


def owner(me, entry, core, n):
    outer, middle = radices(n)
    mask = (entry % outer) * (2 * middle) + (entry // outer) * 2 + core
    return jnp.bitwise_xor(me, mask)


def far(x):
    return pltpu.with_memory_space_constraint(x, pltpu.HBM)


def hint(us):
    return pl.CostEstimate(flops=0, bytes_accessed=int(us * 3_000_000), transcendentals=0)


def fetches(n, first, count, cores, me, from_ref, to_ref, sems):
    part = from_ref.shape[0] // n
    copies = []
    for index, core in enumerate(cores):
        for entry in range(count):
            slot = index * count + entry
            start = pl.multiple_of(owner(me, first + entry, core, n) * part, part)
            copies.append(
                pltpu.make_async_copy(
                    from_ref.at[pl.ds(start, part), :],
                    to_ref.at[slot],
                    sems.at[slot],
                )
            )
    return copies


def slots(n):
    outer, middle = radices(n)
    return [
        (m * outer + entry, core) for m in range(middle) for core in range(2) for entry in range(outer)
    ]


def fetches(n, order, me, from_ref, to_ref, sems):
    part = from_ref.shape[0] // n
    copies = []
    for slot, (entry, core) in enumerate(order):
        start = pl.multiple_of(owner(me, entry, core, n) * part, part)
        copies.append(
            pltpu.make_async_copy(
                from_ref.at[pl.ds(start, part), :], to_ref.at[slot], sems.at[slot]
            )
        )
    return copies


def fetch_kernel(
    n, order, me_ref, block_ref, gain_ref, weight_ref, held, gain_out, weight_out, sems, other_sems
):
    copies = [
        pltpu.make_async_copy(block_ref, held, other_sems.at[0]),
        pltpu.make_async_copy(gain_ref, gain_out, other_sems.at[1]),
    ] + fetches(n, order, me_ref[0], weight_ref, weight_out, sems)
    for copy in copies:
        copy.start()
    for copy in copies:
        copy.wait()


def fetch(me, block, gain, weight, n, order):
    part, columns = weight.shape[0] // n, weight.shape[1]
    vmem = pl.BlockSpec(memory_space=pltpu.VMEM)
    hbm = pl.BlockSpec(memory_space=pltpu.HBM)
    return pl.pallas_call(
        functools.partial(fetch_kernel, n, order),
        out_shape=(
            pltpu.VMEM(block.shape, BF16),
            pltpu.VMEM(gain.shape, F32),
            pltpu.VMEM((len(order), part, columns), BF16),
        ),
        in_specs=[pl.BlockSpec(memory_space=pltpu.SMEM), hbm, hbm, hbm],
        out_specs=(vmem,) * 3,
        scratch_shapes=[
            pltpu.SemaphoreType.DMA((len(order),)),
            pltpu.SemaphoreType.DMA((2,)),
        ],
        compiler_params=pltpu.CompilerParams(vmem_limit_bytes=4 * 1024 * 1024),
        cost_estimate=hint(5),
    )(me, far(block), far(gain), far(weight))


def near(x):
    return pltpu.with_memory_space_constraint(x, pltpu.VMEM)


def add_squares(refs, square):
    for ref in refs:
        for entry in range(ref.shape[0]):
            values = ref[entry].astype(F32)
            square = square + values * values
    return square


def squares_kernel(n, order, count, me_ref, weight_ref, *rest):
    blocks, (before, squares, weight_out, sems) = rest[:count], rest[count:]
    copies = fetches(n, order, me_ref[0], weight_ref, weight_out, sems)
    for copy in copies:
        copy.start()
    squares[...] = add_squares(blocks, before[...])
    for copy in copies:
        copy.wait()


def squares_beside(me, weight, blocks, before, n, order):
    part, columns = weight.shape[0] // n, weight.shape[1]
    vmem = pl.BlockSpec(memory_space=pltpu.VMEM)
    return pl.pallas_call(
        functools.partial(squares_kernel, n, order, len(blocks)),
        out_shape=(
            jax.ShapeDtypeStruct(before.shape, F32),
            pltpu.VMEM((len(order), part, columns), BF16),
        ),
        in_specs=[
            pl.BlockSpec(memory_space=pltpu.SMEM),
            pl.BlockSpec(memory_space=pltpu.HBM),
        ]
        + [vmem] * (len(blocks) + 1),
        out_specs=(vmem, vmem),
        scratch_shapes=[pltpu.SemaphoreType.DMA((len(order),))],
        compiler_params=pltpu.CompilerParams(vmem_limit_bytes=4 * 1024 * 1024),
        cost_estimate=hint(len(order) * 0.7),
    )(me, far(weight), *blocks, before)


def project_kernel(n, count, me_ref, gain_ref, before_ref, *rest):
    blocks, (*helds, out_ref, spread) = rest[:count], rest[count:]
    me = me_ref[0]
    rows, part = before_ref.shape
    square = add_squares(blocks[-1:], before_ref[...])
    mean = jnp.sum(square, axis=1, keepdims=True) * (1.0 / (n * part))
    factor = lax.rsqrt(mean + EPS)
    refs = [(ref, entry) for ref in blocks for entry in range(ref.shape[0])]
    places = [(held, slot) for held in helds for slot in range(held.shape[0])]
    total = None
    for (entry, core), (ref, at), (held, slot) in zip(slots(n), refs, places, strict=True):
        gain = gain_ref[owner(me, entry, core, n)]
        normed = (ref[at].astype(F32) * factor * gain).astype(BF16)
        product = jnp.dot(normed, held[slot], preferred_element_type=F32)
        total = product if total is None else total + product
    columns = total.shape[1] // 128
    steps = rows // n
    for block in range(columns):
        for step in range(steps):
            spread[:, step * columns + block, :] = total[
                step * n : (step + 1) * n, block * 128 : (block + 1) * 128
            ]
    for target in range(n):
        out_ref[target] = spread[target, : steps * columns, :].astype(BF16)


def project(me, block, gain, weight, n):
    rows, part = block.shape
    columns = weight.shape[1]
    pieces = rows // n * (columns // 128)
    outer, middle = radices(n)
    order = slots(n)
    first, second = 2 * outer, n - max(1, outer // 2)

    arrived = [swap(block, n, o * 2 * middle) for o in range(1, outer)]
    held, gain, weight_a = fetch(me, block, gain, weight, n, order[:first])
    row = jnp.stack([held] + arrived)
    later = [swap(row, n, m * 2) for m in range(1, middle)]
    blocks = [row, swap(row, n, 1)]
    squares = jnp.zeros((rows, part), F32)
    squares, weight_b = squares_beside(me, weight, blocks, squares, n, order[first:second])
    later, squares = lax.optimization_barrier((later, squares))
    across = [swap(each, n, 1) for each in later]
    for each, other in zip(later, across, strict=True):
        blocks += [each, other]
    squares, weight_c = squares_beside(me, weight, blocks[2:-1], squares, n, order[second:])
    vmem = pl.BlockSpec(memory_space=pltpu.VMEM)
    return pl.pallas_call(
        functools.partial(project_kernel, n, len(blocks)),
        out_shape=jax.ShapeDtypeStruct((n, pieces, 128), BF16),
        in_specs=[pl.BlockSpec(memory_space=pltpu.SMEM)] + [vmem] * (len(blocks) + 5),
        out_specs=vmem,
        scratch_shapes=[pltpu.VMEM((n, -(-pieces // 8) * 8, 128), F32)],
        compiler_params=pltpu.CompilerParams(vmem_limit_bytes=VMEM_LIMIT),
        cost_estimate=hint(6),
    )(me, gain, squares, *blocks, near(weight_a), near(weight_b), near(weight_c))


def attend_kernel(
    table_ref, length_ref, received_ref, cos_ref, sin_ref, lambda_ref, gain_ref,
    keys_one_ref, keys_two_ref, values_ref, out_ref, fresh,
):
    sources, pieces, _ = received_ref.shape
    steps = cos_ref.shape[0]
    blocks = pieces // steps
    pages, page, _ = keys_one_ref.shape
    capacity = pages * page
    for source in range(sources):
        piece = received_ref[source].astype(F32)
        for step in range(steps):
            fresh[step, source * blocks : (source + 1) * blocks, :] = piece[
                step * blocks : (step + 1) * blocks
            ]

    def heads(step, kind):
        return fresh[step, kind * H : (kind + 1) * H, :]

    def rotated(step, kind):
        values = heads(step, kind)
        turned = values * cos_ref[step] + pltpu.roll(values, HD // 2, 1) * sin_ref[step]
        return turned.astype(BF16).astype(F32)

    row = lax.broadcasted_iota(jnp.int32, (1, capacity), 1)
    place = jnp.zeros((1, capacity), jnp.int32)
    for index in range(pages):
        first = table_ref[0, index] * page
        inside = (row >= first) & (row < first + page)
        place = jnp.where(inside, row - first + index * page, place)
    allowed = place < length_ref[0]

    scale = 1.0 / math.sqrt(HD)
    head_row = lax.rem(lax.broadcasted_iota(jnp.int32, (steps * H, HD), 0), H)

    def softmax_map(kind, keys_ref):
        queries = [rotated(step, kind) for step in range(steps)]
        news = [rotated(step, kind + 2) for step in range(steps)]
        stacked = jnp.concatenate(queries, axis=0)
        apart = jnp.concatenate(
            [jnp.where(head_row == h, stacked, 0.0).astype(BF16) for h in range(H)], axis=1
        )
        older = lax.dot_general(
            apart, keys_ref[...].reshape(capacity, H * HD), (((1,), (1,)), ((), ())),
            preferred_element_type=F32,
        )
        older = jnp.where(allowed, older * scale, -1e38)
        parts = []
        for step in range(steps):
            cached = older[step * H : (step + 1) * H]
            newer = [
                jnp.sum(queries[step] * news[e], axis=1, keepdims=True) * scale
                for e in range(step + 1)
            ]
            top = jnp.max(cached, axis=1, keepdims=True)
            for value in newer:
                top = jnp.maximum(top, value)
            cached = jnp.exp(cached - top)
            newer = [jnp.exp(value - top) for value in newer]
            whole = jnp.sum(cached, axis=1, keepdims=True)
            for value in newer:
                whole = whole + value
            parts.append((cached / whole, [value / whole for value in newer]))
        return parts

    first = softmax_map(0, keys_one_ref)
    second = softmax_map(1, keys_two_ref)
    weight = lambda_ref[...]
    mix = jnp.concatenate(
        [first[step][0] - weight * second[step][0] for step in range(steps)], axis=0
    ).astype(BF16)
    spread = jnp.dot(mix, values_ref[...].reshape(capacity, -1), preferred_element_type=F32)
    wide_row = lax.broadcasted_iota(jnp.int32, (H, 2 * HD), 0)
    fresh_values = [
        jnp.concatenate(
            [fresh[e, pl.ds(4 * H + half, H, stride=2), :] for half in range(2)], axis=1
        )
        for e in range(steps)
    ]
    for step in range(steps):
        mixed = jnp.zeros((H, 2 * HD), F32)
        for h in range(H):
            block = spread[step * H : (step + 1) * H, h * 2 * HD : (h + 1) * 2 * HD]
            mixed = jnp.where(wide_row == h, block, mixed)
        for e in range(step + 1):
            share = first[step][1][e] - weight * second[step][1][e]
            mixed = mixed + share.astype(BF16).astype(F32) * fresh_values[e]
        norm = lax.rsqrt(jnp.mean(mixed * mixed, axis=1, keepdims=True) + EPS)
        out_ref[step * H : (step + 1) * H, :] = (mixed * norm * gain_ref[...]).astype(BF16)


def attend(table, length, received, cos, sin, weights, gain, keys_one, keys_two, values):
    steps = cos.shape[0]
    sources, pieces, _ = received.shape
    vmem = pl.BlockSpec(memory_space=pltpu.VMEM)
    smem = pl.BlockSpec(memory_space=pltpu.SMEM)
    held = [near(x) for x in (keys_one, keys_two, values)]
    return pl.pallas_call(
        attend_kernel,
        out_shape=jax.ShapeDtypeStruct((steps * H, 2 * HD), BF16),
        in_specs=[smem, smem] + [vmem] * 8,
        out_specs=vmem,
        scratch_shapes=[pltpu.VMEM((steps, sources * (pieces // steps), 128), F32)],
        compiler_params=pltpu.CompilerParams(vmem_limit_bytes=VMEM_LIMIT),
        cost_estimate=hint(10),
    )(table, length, received, cos, sin, weights, gain, *held)


def output_kernel(n, me_ref, mine_ref, other_ref, inputs_ref, *rest):
    *weights, out_ref, rows_ref = rest
    me = me_ref[0]
    half, heads, width = mine_ref.shape
    steps = heads // H
    lanes = width // 128
    for entry in range(half):
        for core, ref in ((0, mine_ref), (1, other_ref)):
            start = pl.multiple_of(owner(me, entry, core, n) * heads, 8)
            block = ref[entry].astype(F32)
            for lane in range(lanes):
                rows_ref[lane, pl.ds(start, heads), :] = block[:, lane * 128 : (lane + 1) * 128]
    total = None
    for h in range(H):
        left = jnp.concatenate(
            [
                jnp.concatenate(
                    [rows_ref[lane, pl.ds(step * H + h, n, stride=heads), :] for lane in range(lanes)],
                    axis=1,
                )
                for step in range(steps)
            ],
            axis=0,
        ).astype(BF16)
        held = weights[h * len(weights) // H]
        at = h * width % held.shape[0]
        product = jnp.dot(left, held[at : at + width, :], preferred_element_type=F32)
        total = product if total is None else total + product
    for step in range(steps):
        out_ref[step] = (
            inputs_ref[step].astype(F32) + total[step * n : (step + 1) * n]
        ).astype(BF16)


def keep_kernel(half, block_ref, from_ref, held, to_ref, sem):
    rows = to_ref.shape[0]
    copy = pltpu.make_async_copy(from_ref.at[pl.ds(half * rows, rows), :], to_ref, sem)
    copy.start()
    held[...] = block_ref[...]
    copy.wait()


def keep(block, weight, half, us):
    vmem = pl.BlockSpec(memory_space=pltpu.VMEM)
    return pl.pallas_call(
        functools.partial(keep_kernel, half),
        out_shape=(
            jax.ShapeDtypeStruct(block.shape, block.dtype),
            pltpu.VMEM((weight.shape[0] // 2, weight.shape[1]), weight.dtype),
        ),
        in_specs=[vmem, pl.BlockSpec(memory_space=pltpu.HBM)],
        out_specs=(vmem, vmem),
        scratch_shapes=[pltpu.SemaphoreType.DMA],
        compiler_params=pltpu.CompilerParams(vmem_limit_bytes=4 * 1024 * 1024),
        cost_estimate=hint(us),
    )(block, far(weight))


def output(me, attended, inputs, weight, n):
    kept = []

    def aside(half, block):
        block, part = keep(block, weight, half, 2)
        kept.append(near(part))
        return block

    mine, other = gather_blocks(
        attended, n, functools.partial(aside, 0), functools.partial(aside, 1)
    )
    half, heads, width = mine.shape
    vmem = pl.BlockSpec(memory_space=pltpu.VMEM)
    return pl.pallas_call(
        functools.partial(output_kernel, n),
        out_shape=jax.ShapeDtypeStruct(inputs.shape, BF16),
        in_specs=[pl.BlockSpec(memory_space=pltpu.SMEM)] + [vmem] * 5,
        out_specs=vmem,
        scratch_shapes=[pltpu.VMEM((width // 128, n * heads, 128), F32)],
        compiler_params=pltpu.CompilerParams(vmem_limit_bytes=VMEM_LIMIT),
    )(me, mine, other, inputs, *kept)


def angles(positions, steps):
    half = HD // 2
    frequency = jnp.exp(-math.log(ROPE_BASE) * 2.0 * jnp.arange(half, dtype=F32) / HD)
    places = (positions + jnp.arange(steps, dtype=jnp.int32)).astype(F32)
    turns = places[:, None] * frequency[None, :]
    cosine, sine = jnp.cos(turns), jnp.sin(turns)
    cos = jnp.concatenate([cosine, cosine], axis=-1)
    sin = jnp.concatenate([-sine, sine], axis=-1)
    return cos[:, None, :], sin[:, None, :]


def turn_kernel(positions_ref, after_ref, cos_ref, sin_ref):
    steps = cos_ref.shape[0]
    lane = lax.broadcasted_iota(jnp.int32, (8, HD), 1)
    step = lax.broadcasted_iota(jnp.int32, (8, HD), 0)
    pair = lax.rem(lane, HD // 2).astype(F32)
    frequency = jnp.exp(-math.log(ROPE_BASE) * 2.0 * pair / HD)
    turns = (positions_ref[0] + step).astype(F32) * frequency
    cos = jnp.cos(turns)
    sin = jnp.where(lane < HD // 2, -1.0, 1.0) * jnp.sin(turns)
    for index in range(steps):
        cos_ref[index] = cos[index : index + 1]
        sin_ref[index] = sin[index : index + 1]


def turn(positions, after, steps):
    vmem = pl.BlockSpec(memory_space=pltpu.VMEM)
    return pl.pallas_call(
        turn_kernel,
        out_shape=(jax.ShapeDtypeStruct((steps, 1, HD), F32),) * 2,
        in_specs=[pl.BlockSpec(memory_space=pltpu.SMEM), pl.BlockSpec(memory_space=pl.ANY)],
        out_specs=(vmem, vmem),
        compiler_params=pltpu.CompilerParams(vmem_limit_bytes=4 * 1024 * 1024),
        cost_estimate=hint(1),
    )(positions, after)


def local(
    n, inputs, norm_gain, qkv_weight, head_lambda, head_gain, out_weight,
    key_one_pages, key_two_pages, value_pages, page_table, context_len, positions,
):
    steps, rows, part = inputs.shape
    me = lax.axis_index("gx").astype(jnp.int32).reshape(1)
    block = inputs.reshape(steps * rows, part)
    sent = project(me, block, norm_gain.reshape(n, 1, part), qkv_weight, n)
    received = lax.all_to_all(sent, "gx", 0, 0)
    cos, sin = turn(positions, sent, steps)
    attended = attend(
        page_table, context_len, received, cos, sin, head_lambda.reshape(H, 1),
        head_gain.reshape(H, 2 * HD), key_one_pages, key_two_pages, value_pages,
    )
    return output(me, attended, inputs, out_weight, n)


def rotary(vectors, cos, sin):
    return vectors * cos + jnp.roll(vectors, HD // 2, axis=-1) * sin


def local_any(
    n, inputs, norm_gain, qkv_weight, head_lambda, head_gain, out_weight,
    key_one_pages, key_two_pages, value_pages, page_table, context_len, positions,
):
    steps = inputs.shape[0]
    own = page_table.shape[0]
    capacity = page_table.shape[1] * key_one_pages.shape[1]
    values = lax.all_gather(inputs, "gx", axis=2, tiled=True).astype(F32)
    factor = lax.rsqrt(jnp.mean(values * values, axis=-1, keepdims=True) + EPS)
    normed = (values * factor * norm_gain).astype(BF16)
    projected = jnp.einsum("sbd,dc->sbc", normed, qkv_weight, preferred_element_type=F32)
    received = lax.all_to_all(
        projected.astype(BF16), "gx", split_axis=1, concat_axis=2, tiled=True
    )
    cached = tuple(
        pool[page_table].reshape(own, capacity, H, -1)
        for pool in (key_one_pages, key_two_pages, value_pages)
    )
    both = received[..., : 4 * H * HD].reshape(steps, own, 4, H, HD).astype(F32)
    new_values = received[..., 4 * H * HD :].reshape(steps, own, H, 2 * HD)
    cos, sin = jax.vmap(lambda p: angles(p, steps))(positions.reshape(own, 1))
    cos, sin = (jnp.moveaxis(x, 0, 1)[:, :, None] for x in (cos, sin))
    turned = rotary(both, cos, sin).astype(BF16)
    place = jnp.arange(capacity, dtype=jnp.int32)
    allowed = (place[None, :] < context_len[:, None])[None, :, None, :]
    step = jnp.arange(steps)
    newer_allowed = (step[None, :] <= step[:, None])[:, None, None, :]

    def softmax_map(query, keys, news):
        older = jnp.einsum("tshd,sjhd->tshj", query, keys, preferred_element_type=F32)
        newer = jnp.einsum("tshd,eshd->tshe", query, news, preferred_element_type=F32)
        scores = jnp.concatenate(
            [jnp.where(allowed, older, -jnp.inf), jnp.where(newer_allowed, newer, -jnp.inf)], axis=-1
        )
        return jax.nn.softmax(scores * (1.0 / math.sqrt(HD)), axis=-1)

    first = softmax_map(turned[:, :, 0], cached[0], turned[:, :, 2])
    second = softmax_map(turned[:, :, 1], cached[1], turned[:, :, 3])
    mix = (first - head_lambda[:, None] * second).astype(BF16)
    mixed = jnp.einsum(
        "tshj,sjhf->tshf", mix[..., :capacity], cached[2], preferred_element_type=F32
    ) + jnp.einsum("tshe,eshf->tshf", mix[..., capacity:], new_values, preferred_element_type=F32)
    norm = lax.rsqrt(jnp.mean(mixed * mixed, axis=-1, keepdims=True) + EPS)
    grouped = (mixed * norm * head_gain.reshape(H, 2 * HD)).astype(BF16)
    whole = lax.all_gather(grouped.reshape(steps, own, -1), "gx", axis=1, tiled=True)
    branch = jnp.einsum("sbf,fd->sbd", whole, out_weight, preferred_element_type=F32)
    return (inputs.astype(F32) + branch).astype(BF16)


def solution(mesh):
    n = mesh.shape["gx"]
    placed = (
        P(None, "groups", "gx"),
        P(),
        P(None, "gx"),
        P(),
        P(),
        P(None, "gx"),
        P(("groups", "gx"), None, None),
        P(("groups", "gx"), None, None),
        P(("groups", "gx"), None, None),
        P(("groups", "gx"), None),
        P(("groups", "gx")),
        P(("groups", "gx")),
    )

    def chosen(inputs, norm_gain, qkv_weight, *rest):
        aligned = inputs.shape[2] % 128 == 0 and qkv_weight.shape[1] % 128 == 0
        single = rest[6].shape[0] == 1
        power = n >= 4 and n & (n - 1) == 0
        body = local if aligned and single and power else local_any
        return body(n, inputs, norm_gain, qkv_weight, *rest)

    return jax.shard_map(
        chosen, mesh=mesh, in_specs=placed, out_specs=P(None, "groups", "gx"), check_vma=False
    )
```

```python
import functools
import math

import jax
import jax.numpy as jnp
from jax import lax
from jax.experimental import pallas as pl
from jax.experimental.pallas import tpu as pltpu
from jax.sharding import PartitionSpec as P

H = 24
HD = 128
EPS = 1e-05
ROPE_BASE = 10000.0
F32 = jnp.float32
BF16 = jnp.bfloat16
VMEM_LIMIT = 16 * 1024 * 1024


def radices(n):
    rest = n // 2
    middle = 1
    while middle * middle * 4 <= rest:
        middle *= 2
    return rest // middle, middle


def swap(block, n, mask):
    return lax.ppermute(block, "gx", [(i, i ^ mask) for i in range(n)])


def gather_blocks(block, n, first_aside, second_aside):
    outer, middle = radices(n)
    arrived = [swap(block, n, o * 2 * middle) for o in range(1, outer)]
    rows = jnp.stack([first_aside(block)] + arrived)
    others = [swap(rows, n, m * 2) for m in range(1, middle)]
    rows, others = lax.optimization_barrier((second_aside(rows), others))
    mine = jnp.concatenate([rows] + others)
    return mine, swap(mine, n, 1)


def owner(me, entry, core, n):
    outer, middle = radices(n)
    mask = (entry % outer) * (2 * middle) + (entry // outer) * 2 + core
    return jnp.bitwise_xor(me, mask)


def far(x):
    return pltpu.with_memory_space_constraint(x, pltpu.HBM)


def hint(us):
    return pl.CostEstimate(flops=0, bytes_accessed=int(us * 3_000_000), transcendentals=0)


def fetches(n, first, count, cores, me, from_ref, to_ref, sems):
    part = from_ref.shape[0] // n
    copies = []
    for index, core in enumerate(cores):
        for entry in range(count):
            slot = index * count + entry
            start = pl.multiple_of(owner(me, first + entry, core, n) * part, part)
            copies.append(
                pltpu.make_async_copy(
                    from_ref.at[pl.ds(start, part), :],
                    to_ref.at[slot],
                    sems.at[slot],
                )
            )
    return copies


def slots(n):
    return [(entry, core) for core in range(2) for entry in range(n // 2)]


def fetches(n, order, me, from_ref, to_ref, sems):
    part = from_ref.shape[0] // n
    copies = []
    for slot, (entry, core) in enumerate(order):
        start = pl.multiple_of(owner(me, entry, core, n) * part, part)
        copies.append(
            pltpu.make_async_copy(
                from_ref.at[pl.ds(start, part), :], to_ref.at[slot], sems.at[slot]
            )
        )
    return copies


def fetch_kernel(
    n, order, me_ref, block_ref, gain_ref, weight_ref, held, gain_out, weight_out, sems, other_sems
):
    copies = [
        pltpu.make_async_copy(block_ref, held, other_sems.at[0]),
        pltpu.make_async_copy(gain_ref, gain_out, other_sems.at[1]),
    ] + fetches(n, order, me_ref[0], weight_ref, weight_out, sems)
    for copy in copies:
        copy.start()
    for copy in copies:
        copy.wait()


def fetch(me, block, gain, weight, n, order):
    part, columns = weight.shape[0] // n, weight.shape[1]
    vmem = pl.BlockSpec(memory_space=pltpu.VMEM)
    hbm = pl.BlockSpec(memory_space=pltpu.HBM)
    return pl.pallas_call(
        functools.partial(fetch_kernel, n, order),
        out_shape=(
            pltpu.VMEM(block.shape, BF16),
            pltpu.VMEM(gain.shape, F32),
            pltpu.VMEM((len(order), part, columns), BF16),
        ),
        in_specs=[pl.BlockSpec(memory_space=pltpu.SMEM), hbm, hbm, hbm],
        out_specs=(vmem,) * 3,
        scratch_shapes=[
            pltpu.SemaphoreType.DMA((len(order),)),
            pltpu.SemaphoreType.DMA((2,)),
        ],
        compiler_params=pltpu.CompilerParams(vmem_limit_bytes=4 * 1024 * 1024),
        cost_estimate=hint(5),
    )(me, far(block), far(gain), far(weight))


def near(x):
    return pltpu.with_memory_space_constraint(x, pltpu.VMEM)


def add_squares(refs, square):
    for ref in refs:
        for entry in range(ref.shape[0]):
            values = ref[entry].astype(F32)
            square = square + values * values
    return square


def squares_kernel(n, order, count, me_ref, weight_ref, *rest):
    blocks, (before, squares, weight_out, sems) = rest[:count], rest[count:]
    copies = fetches(n, order, me_ref[0], weight_ref, weight_out, sems)
    for copy in copies:
        copy.start()
    squares[...] = add_squares(blocks, before[...])
    for copy in copies:
        copy.wait()


def squares_beside(me, weight, blocks, before, n, order):
    part, columns = weight.shape[0] // n, weight.shape[1]
    vmem = pl.BlockSpec(memory_space=pltpu.VMEM)
    return pl.pallas_call(
        functools.partial(squares_kernel, n, order, len(blocks)),
        out_shape=(
            jax.ShapeDtypeStruct(before.shape, F32),
            pltpu.VMEM((len(order), part, columns), BF16),
        ),
        in_specs=[
            pl.BlockSpec(memory_space=pltpu.SMEM),
            pl.BlockSpec(memory_space=pltpu.HBM),
        ]
        + [vmem] * (len(blocks) + 1),
        out_specs=(vmem, vmem),
        scratch_shapes=[pltpu.SemaphoreType.DMA((len(order),))],
        compiler_params=pltpu.CompilerParams(vmem_limit_bytes=4 * 1024 * 1024),
        cost_estimate=hint(len(order) * 0.7),
    )(me, far(weight), *blocks, before)


def project_kernel(n, count, me_ref, gain_ref, before_ref, *rest):
    blocks, (*helds, out_ref, spread) = rest[:count], rest[count:]
    me = me_ref[0]
    rows, part = before_ref.shape
    square = add_squares(blocks[-1:], before_ref[...])
    mean = jnp.sum(square, axis=1, keepdims=True) * (1.0 / (n * part))
    factor = lax.rsqrt(mean + EPS)
    refs = [(ref, entry) for ref in blocks for entry in range(ref.shape[0])]
    places = [(held, slot) for held in helds for slot in range(held.shape[0])]
    total = None
    for (entry, core), (ref, at), (held, slot) in zip(slots(n), refs, places, strict=True):
        gain = gain_ref[owner(me, entry, core, n)]
        normed = (ref[at].astype(F32) * factor * gain).astype(BF16)
        product = jnp.dot(normed, held[slot], preferred_element_type=F32)
        total = product if total is None else total + product
    columns = total.shape[1] // 128
    steps = rows // n
    for block in range(columns):
        for step in range(steps):
            spread[:, step * columns + block, :] = total[
                step * n : (step + 1) * n, block * 128 : (block + 1) * 128
            ]
    for target in range(n):
        out_ref[target] = spread[target, : steps * columns, :].astype(BF16)


def project(me, block, gain, weight, n):
    rows, part = block.shape
    columns = weight.shape[1]
    pieces = rows // n * (columns // 128)
    outer, middle = radices(n)
    order = slots(n)
    first, second = 2 * outer, n - max(1, outer // 2)

    arrived = [swap(block, n, o * 2 * middle) for o in range(1, outer)]
    held, gain, weight_a = fetch(me, block, gain, weight, n, order[:first])
    row = jnp.stack([held] + arrived)
    later = [swap(row, n, m * 2) for m in range(1, middle)]
    squares = jnp.zeros((rows, part), F32)
    squares, weight_b = squares_beside(me, weight, [row], squares, n, order[first:second])
    later, squares = lax.optimization_barrier((later, squares))
    mine = jnp.concatenate([row] + later)
    blocks = [mine, swap(mine, n, 1)]
    squares, weight_c = squares_beside(me, weight, later, squares, n, order[second:])
    vmem = pl.BlockSpec(memory_space=pltpu.VMEM)
    return pl.pallas_call(
        functools.partial(project_kernel, n, len(blocks)),
        out_shape=jax.ShapeDtypeStruct((n, pieces, 128), BF16),
        in_specs=[pl.BlockSpec(memory_space=pltpu.SMEM)] + [vmem] * (len(blocks) + 5),
        out_specs=vmem,
        scratch_shapes=[pltpu.VMEM((n, -(-pieces // 8) * 8, 128), F32)],
        compiler_params=pltpu.CompilerParams(vmem_limit_bytes=VMEM_LIMIT),
        cost_estimate=hint(6),
    )(me, gain, squares, *blocks, near(weight_a), near(weight_b), near(weight_c))


def attend_kernel(
    table_ref, length_ref, received_ref, cos_ref, sin_ref, lambda_ref, gain_ref,
    keys_one_ref, keys_two_ref, values_ref, out_ref, fresh,
):
    sources, pieces, _ = received_ref.shape
    steps = cos_ref.shape[0]
    blocks = pieces // steps
    pages, page, _ = keys_one_ref.shape
    capacity = pages * page
    for source in range(sources):
        piece = received_ref[source].astype(F32)
        for step in range(steps):
            fresh[step, source * blocks : (source + 1) * blocks, :] = piece[
                step * blocks : (step + 1) * blocks
            ]

    def heads(step, kind):
        return fresh[step, kind * H : (kind + 1) * H, :]

    def rotated(step, kind):
        values = heads(step, kind)
        turned = values * cos_ref[step] + pltpu.roll(values, HD // 2, 1) * sin_ref[step]
        return turned.astype(BF16).astype(F32)

    row = lax.broadcasted_iota(jnp.int32, (1, capacity), 1)
    place = jnp.zeros((1, capacity), jnp.int32)
    for index in range(pages):
        first = table_ref[0, index] * page
        inside = (row >= first) & (row < first + page)
        place = jnp.where(inside, row - first + index * page, place)
    allowed = place < length_ref[0]

    scale = 1.0 / math.sqrt(HD)
    head_row = lax.rem(lax.broadcasted_iota(jnp.int32, (steps * H, HD), 0), H)

    def softmax_map(kind, keys_ref):
        queries = [rotated(step, kind) for step in range(steps)]
        news = [rotated(step, kind + 2) for step in range(steps)]
        stacked = jnp.concatenate(queries, axis=0)
        apart = jnp.concatenate(
            [jnp.where(head_row == h, stacked, 0.0).astype(BF16) for h in range(H)], axis=1
        )
        older = lax.dot_general(
            apart, keys_ref[...].reshape(capacity, H * HD), (((1,), (1,)), ((), ())),
            preferred_element_type=F32,
        )
        older = jnp.where(allowed, older * scale, -1e38)
        parts = []
        for step in range(steps):
            cached = older[step * H : (step + 1) * H]
            newer = [
                jnp.sum(queries[step] * news[e], axis=1, keepdims=True) * scale
                for e in range(step + 1)
            ]
            top = jnp.max(cached, axis=1, keepdims=True)
            for value in newer:
                top = jnp.maximum(top, value)
            cached = jnp.exp(cached - top)
            newer = [jnp.exp(value - top) for value in newer]
            whole = jnp.sum(cached, axis=1, keepdims=True)
            for value in newer:
                whole = whole + value
            parts.append((cached / whole, [value / whole for value in newer]))
        return parts

    first = softmax_map(0, keys_one_ref)
    second = softmax_map(1, keys_two_ref)
    weight = lambda_ref[...]
    mix = jnp.concatenate(
        [first[step][0] - weight * second[step][0] for step in range(steps)], axis=0
    ).astype(BF16)
    spread = jnp.dot(mix, values_ref[...].reshape(capacity, -1), preferred_element_type=F32)
    wide_row = lax.broadcasted_iota(jnp.int32, (H, 2 * HD), 0)
    fresh_values = [
        jnp.concatenate(
            [fresh[e, pl.ds(4 * H + half, H, stride=2), :] for half in range(2)], axis=1
        )
        for e in range(steps)
    ]
    for step in range(steps):
        mixed = jnp.zeros((H, 2 * HD), F32)
        for h in range(H):
            block = spread[step * H : (step + 1) * H, h * 2 * HD : (h + 1) * 2 * HD]
            mixed = jnp.where(wide_row == h, block, mixed)
        for e in range(step + 1):
            share = first[step][1][e] - weight * second[step][1][e]
            mixed = mixed + share.astype(BF16).astype(F32) * fresh_values[e]
        norm = lax.rsqrt(jnp.mean(mixed * mixed, axis=1, keepdims=True) + EPS)
        out_ref[step * H : (step + 1) * H, :] = (mixed * norm * gain_ref[...]).astype(BF16)


def attend(table, length, received, cos, sin, weights, gain, keys_one, keys_two, values):
    steps = cos.shape[0]
    sources, pieces, _ = received.shape
    vmem = pl.BlockSpec(memory_space=pltpu.VMEM)
    smem = pl.BlockSpec(memory_space=pltpu.SMEM)
    held = [near(x) for x in (keys_one, keys_two, values)]
    return pl.pallas_call(
        attend_kernel,
        out_shape=jax.ShapeDtypeStruct((steps * H, 2 * HD), BF16),
        in_specs=[smem, smem] + [vmem] * 8,
        out_specs=vmem,
        scratch_shapes=[pltpu.VMEM((steps, sources * (pieces // steps), 128), F32)],
        compiler_params=pltpu.CompilerParams(vmem_limit_bytes=VMEM_LIMIT),
        cost_estimate=hint(10),
    )(table, length, received, cos, sin, weights, gain, *held)


def output_kernel(n, me_ref, mine_ref, other_ref, inputs_ref, *rest):
    *weights, out_ref, rows_ref = rest
    me = me_ref[0]
    half, heads, width = mine_ref.shape
    steps = heads // H
    lanes = width // 128
    for entry in range(half):
        for core, ref in ((0, mine_ref), (1, other_ref)):
            start = pl.multiple_of(owner(me, entry, core, n) * heads, 8)
            block = ref[entry].astype(F32)
            for lane in range(lanes):
                rows_ref[lane, pl.ds(start, heads), :] = block[:, lane * 128 : (lane + 1) * 128]
    total = None
    for h in range(H):
        left = jnp.concatenate(
            [
                jnp.concatenate(
                    [rows_ref[lane, pl.ds(step * H + h, n, stride=heads), :] for lane in range(lanes)],
                    axis=1,
                )
                for step in range(steps)
            ],
            axis=0,
        ).astype(BF16)
        held = weights[h * len(weights) // H]
        at = h * width % held.shape[0]
        product = jnp.dot(left, held[at : at + width, :], preferred_element_type=F32)
        total = product if total is None else total + product
    for step in range(steps):
        out_ref[step] = (
            inputs_ref[step].astype(F32) + total[step * n : (step + 1) * n]
        ).astype(BF16)


def keep_kernel(half, block_ref, from_ref, held, to_ref, sem):
    rows = to_ref.shape[0]
    copy = pltpu.make_async_copy(from_ref.at[pl.ds(half * rows, rows), :], to_ref, sem)
    copy.start()
    held[...] = block_ref[...]
    copy.wait()


def keep(block, weight, half, us):
    vmem = pl.BlockSpec(memory_space=pltpu.VMEM)
    return pl.pallas_call(
        functools.partial(keep_kernel, half),
        out_shape=(
            jax.ShapeDtypeStruct(block.shape, block.dtype),
            pltpu.VMEM((weight.shape[0] // 2, weight.shape[1]), weight.dtype),
        ),
        in_specs=[vmem, pl.BlockSpec(memory_space=pltpu.HBM)],
        out_specs=(vmem, vmem),
        scratch_shapes=[pltpu.SemaphoreType.DMA],
        compiler_params=pltpu.CompilerParams(vmem_limit_bytes=4 * 1024 * 1024),
        cost_estimate=hint(us),
    )(block, far(weight))


def output(me, attended, inputs, weight, n):
    kept = []

    def aside(half, block):
        block, part = keep(block, weight, half, 2)
        kept.append(near(part))
        return block

    mine, other = gather_blocks(
        attended, n, functools.partial(aside, 0), functools.partial(aside, 1)
    )
    half, heads, width = mine.shape
    vmem = pl.BlockSpec(memory_space=pltpu.VMEM)
    return pl.pallas_call(
        functools.partial(output_kernel, n),
        out_shape=jax.ShapeDtypeStruct(inputs.shape, BF16),
        in_specs=[pl.BlockSpec(memory_space=pltpu.SMEM)] + [vmem] * 5,
        out_specs=vmem,
        scratch_shapes=[pltpu.VMEM((width // 128, n * heads, 128), F32)],
        compiler_params=pltpu.CompilerParams(vmem_limit_bytes=VMEM_LIMIT),
    )(me, mine, other, inputs, *kept)


def angles(positions, steps):
    half = HD // 2
    frequency = jnp.exp(-math.log(ROPE_BASE) * 2.0 * jnp.arange(half, dtype=F32) / HD)
    places = (positions + jnp.arange(steps, dtype=jnp.int32)).astype(F32)
    turns = places[:, None] * frequency[None, :]
    cosine, sine = jnp.cos(turns), jnp.sin(turns)
    cos = jnp.concatenate([cosine, cosine], axis=-1)
    sin = jnp.concatenate([-sine, sine], axis=-1)
    return cos[:, None, :], sin[:, None, :]


def turn_kernel(positions_ref, after_ref, cos_ref, sin_ref):
    steps = cos_ref.shape[0]
    lane = lax.broadcasted_iota(jnp.int32, (8, HD), 1)
    step = lax.broadcasted_iota(jnp.int32, (8, HD), 0)
    pair = lax.rem(lane, HD // 2).astype(F32)
    frequency = jnp.exp(-math.log(ROPE_BASE) * 2.0 * pair / HD)
    turns = (positions_ref[0] + step).astype(F32) * frequency
    cos = jnp.cos(turns)
    sin = jnp.where(lane < HD // 2, -1.0, 1.0) * jnp.sin(turns)
    for index in range(steps):
        cos_ref[index] = cos[index : index + 1]
        sin_ref[index] = sin[index : index + 1]


def turn(positions, after, steps):
    vmem = pl.BlockSpec(memory_space=pltpu.VMEM)
    return pl.pallas_call(
        turn_kernel,
        out_shape=(jax.ShapeDtypeStruct((steps, 1, HD), F32),) * 2,
        in_specs=[pl.BlockSpec(memory_space=pltpu.SMEM), pl.BlockSpec(memory_space=pl.ANY)],
        out_specs=(vmem, vmem),
        compiler_params=pltpu.CompilerParams(vmem_limit_bytes=4 * 1024 * 1024),
        cost_estimate=hint(1),
    )(positions, after)


def local(
    n, inputs, norm_gain, qkv_weight, head_lambda, head_gain, out_weight,
    key_one_pages, key_two_pages, value_pages, page_table, context_len, positions,
):
    steps, rows, part = inputs.shape
    me = lax.axis_index("gx").astype(jnp.int32).reshape(1)
    block = inputs.reshape(steps * rows, part)
    sent = project(me, block, norm_gain.reshape(n, 1, part), qkv_weight, n)
    received = lax.all_to_all(sent, "gx", 0, 0)
    cos, sin = turn(positions, sent, steps)
    attended = attend(
        page_table, context_len, received, cos, sin, head_lambda.reshape(H, 1),
        head_gain.reshape(H, 2 * HD), key_one_pages, key_two_pages, value_pages,
    )
    return output(me, attended, inputs, out_weight, n)


def rotary(vectors, cos, sin):
    return vectors * cos + jnp.roll(vectors, HD // 2, axis=-1) * sin


def local_any(
    n, inputs, norm_gain, qkv_weight, head_lambda, head_gain, out_weight,
    key_one_pages, key_two_pages, value_pages, page_table, context_len, positions,
):
    steps = inputs.shape[0]
    own = page_table.shape[0]
    capacity = page_table.shape[1] * key_one_pages.shape[1]
    values = lax.all_gather(inputs, "gx", axis=2, tiled=True).astype(F32)
    factor = lax.rsqrt(jnp.mean(values * values, axis=-1, keepdims=True) + EPS)
    normed = (values * factor * norm_gain).astype(BF16)
    projected = jnp.einsum("sbd,dc->sbc", normed, qkv_weight, preferred_element_type=F32)
    received = lax.all_to_all(
        projected.astype(BF16), "gx", split_axis=1, concat_axis=2, tiled=True
    )
    cached = tuple(
        pool[page_table].reshape(own, capacity, H, -1)
        for pool in (key_one_pages, key_two_pages, value_pages)
    )
    both = received[..., : 4 * H * HD].reshape(steps, own, 4, H, HD).astype(F32)
    new_values = received[..., 4 * H * HD :].reshape(steps, own, H, 2 * HD)
    cos, sin = jax.vmap(lambda p: angles(p, steps))(positions.reshape(own, 1))
    cos, sin = (jnp.moveaxis(x, 0, 1)[:, :, None] for x in (cos, sin))
    turned = rotary(both, cos, sin).astype(BF16)
    place = jnp.arange(capacity, dtype=jnp.int32)
    allowed = (place[None, :] < context_len[:, None])[None, :, None, :]
    step = jnp.arange(steps)
    newer_allowed = (step[None, :] <= step[:, None])[:, None, None, :]

    def softmax_map(query, keys, news):
        older = jnp.einsum("tshd,sjhd->tshj", query, keys, preferred_element_type=F32)
        newer = jnp.einsum("tshd,eshd->tshe", query, news, preferred_element_type=F32)
        scores = jnp.concatenate(
            [jnp.where(allowed, older, -jnp.inf), jnp.where(newer_allowed, newer, -jnp.inf)], axis=-1
        )
        return jax.nn.softmax(scores * (1.0 / math.sqrt(HD)), axis=-1)

    first = softmax_map(turned[:, :, 0], cached[0], turned[:, :, 2])
    second = softmax_map(turned[:, :, 1], cached[1], turned[:, :, 3])
    mix = (first - head_lambda[:, None] * second).astype(BF16)
    mixed = jnp.einsum(
        "tshj,sjhf->tshf", mix[..., :capacity], cached[2], preferred_element_type=F32
    ) + jnp.einsum("tshe,eshf->tshf", mix[..., capacity:], new_values, preferred_element_type=F32)
    norm = lax.rsqrt(jnp.mean(mixed * mixed, axis=-1, keepdims=True) + EPS)
    grouped = (mixed * norm * head_gain.reshape(H, 2 * HD)).astype(BF16)
    whole = lax.all_gather(grouped.reshape(steps, own, -1), "gx", axis=1, tiled=True)
    branch = jnp.einsum("sbf,fd->sbd", whole, out_weight, preferred_element_type=F32)
    return (inputs.astype(F32) + branch).astype(BF16)


def solution(mesh):
    n = mesh.shape["gx"]
    placed = (
        P(None, "groups", "gx"),
        P(),
        P(None, "gx"),
        P(),
        P(),
        P(None, "gx"),
        P(("groups", "gx"), None, None),
        P(("groups", "gx"), None, None),
        P(("groups", "gx"), None, None),
        P(("groups", "gx"), None),
        P(("groups", "gx")),
        P(("groups", "gx")),
    )

    def chosen(inputs, norm_gain, qkv_weight, *rest):
        aligned = inputs.shape[2] % 128 == 0 and qkv_weight.shape[1] % 128 == 0
        single = rest[6].shape[0] == 1
        power = n >= 4 and n & (n - 1) == 0
        body = local if aligned and single and power else local_any
        return body(n, inputs, norm_gain, qkv_weight, *rest)

    return jax.shard_map(
        chosen, mesh=mesh, in_specs=placed, out_specs=P(None, "groups", "gx"), check_vma=False
    )
```

```python
import functools
import math

import jax
import jax.numpy as jnp
from jax import lax
from jax.experimental import pallas as pl
from jax.experimental.pallas import tpu as pltpu
from jax.sharding import PartitionSpec as P

H = 24
HD = 128
EPS = 1e-05
ROPE_BASE = 10000.0
F32 = jnp.float32
BF16 = jnp.bfloat16
VMEM_LIMIT = 16 * 1024 * 1024


def radices(n):
    rest = n // 2
    middle = 1
    while middle * middle * 4 <= rest:
        middle *= 2
    return rest // middle, middle


def swap(block, n, mask):
    return lax.ppermute(block, "gx", [(i, i ^ mask) for i in range(n)])


def gather_blocks(block, n, first_aside, second_aside):
    outer, middle = radices(n)
    arrived = [swap(block, n, o * 2 * middle) for o in range(1, outer)]
    rows = jnp.stack([first_aside(block)] + arrived)
    others = [swap(rows, n, m * 2) for m in range(1, middle)]
    rows, others = lax.optimization_barrier((second_aside(rows), others))
    mine = jnp.concatenate([rows] + others)
    return mine, swap(mine, n, 1)


def owner(me, entry, core, n):
    outer, middle = radices(n)
    mask = (entry % outer) * (2 * middle) + (entry // outer) * 2 + core
    return jnp.bitwise_xor(me, mask)


def far(x):
    return pltpu.with_memory_space_constraint(x, pltpu.HBM)


def hint(us):
    return pl.CostEstimate(flops=0, bytes_accessed=int(us * 3_000_000), transcendentals=0)


def fetches(n, first, count, cores, me, from_ref, to_ref, sems):
    part = from_ref.shape[0] // n
    copies = []
    for index, core in enumerate(cores):
        for entry in range(count):
            slot = index * count + entry
            start = pl.multiple_of(owner(me, first + entry, core, n) * part, part)
            copies.append(
                pltpu.make_async_copy(
                    from_ref.at[pl.ds(start, part), :],
                    to_ref.at[slot],
                    sems.at[slot],
                )
            )
    return copies


def slots(n):
    return [(entry, core) for core in range(2) for entry in range(n // 2)]


def fetches(n, order, me, from_ref, to_ref, sems):
    part = from_ref.shape[0] // n
    copies = []
    for slot, (entry, core) in enumerate(order):
        start = pl.multiple_of(owner(me, entry, core, n) * part, part)
        copies.append(
            pltpu.make_async_copy(
                from_ref.at[pl.ds(start, part), :], to_ref.at[slot], sems.at[slot]
            )
        )
    return copies


def fetch_kernel(
    n, order, me_ref, block_ref, gain_ref, weight_ref, held, gain_out, weight_out, sems, other_sems
):
    copies = [
        pltpu.make_async_copy(block_ref, held, other_sems.at[0]),
        pltpu.make_async_copy(gain_ref, gain_out, other_sems.at[1]),
    ] + fetches(n, order, me_ref[0], weight_ref, weight_out, sems)
    for copy in copies:
        copy.start()
    for copy in copies:
        copy.wait()


def fetch(me, block, gain, weight, n, order):
    part, columns = weight.shape[0] // n, weight.shape[1]
    vmem = pl.BlockSpec(memory_space=pltpu.VMEM)
    hbm = pl.BlockSpec(memory_space=pltpu.HBM)
    return pl.pallas_call(
        functools.partial(fetch_kernel, n, order),
        out_shape=(
            pltpu.VMEM(block.shape, BF16),
            pltpu.VMEM(gain.shape, F32),
            pltpu.VMEM((len(order), part, columns), BF16),
        ),
        in_specs=[pl.BlockSpec(memory_space=pltpu.SMEM), hbm, hbm, hbm],
        out_specs=(vmem,) * 3,
        scratch_shapes=[
            pltpu.SemaphoreType.DMA((len(order),)),
            pltpu.SemaphoreType.DMA((2,)),
        ],
        compiler_params=pltpu.CompilerParams(vmem_limit_bytes=4 * 1024 * 1024),
        cost_estimate=hint(5),
    )(me, far(block), far(gain), far(weight))


def near(x):
    return pltpu.with_memory_space_constraint(x, pltpu.VMEM)


def add_squares(refs, square):
    for ref in refs:
        for entry in range(ref.shape[0]):
            values = ref[entry].astype(F32)
            square = square + values * values
    return square


def squares_kernel(n, order, count, me_ref, weight_ref, *rest):
    blocks, (squares, weight_out, sems) = rest[:count], rest[count:]
    copies = fetches(n, order, me_ref[0], weight_ref, weight_out, sems)
    for copy in copies:
        copy.start()
    squares[...] = add_squares(blocks, jnp.zeros(squares.shape, F32))
    for copy in copies:
        copy.wait()


def squares_beside(me, weight, blocks, n, order):
    part, columns = weight.shape[0] // n, weight.shape[1]
    vmem = pl.BlockSpec(memory_space=pltpu.VMEM)
    return pl.pallas_call(
        functools.partial(squares_kernel, n, order, len(blocks)),
        out_shape=(
            jax.ShapeDtypeStruct(blocks[0].shape[1:], F32),
            pltpu.VMEM((len(order), part, columns), BF16),
        ),
        in_specs=[
            pl.BlockSpec(memory_space=pltpu.SMEM),
            pl.BlockSpec(memory_space=pltpu.HBM),
        ]
        + [vmem] * len(blocks),
        out_specs=(vmem, vmem),
        scratch_shapes=[pltpu.SemaphoreType.DMA((len(order),))],
        compiler_params=pltpu.CompilerParams(vmem_limit_bytes=4 * 1024 * 1024),
        cost_estimate=hint(len(order) * 0.7),
    )(me, far(weight), *blocks)


def more_squares_kernel(count, before, *rest):
    *blocks, squares = rest
    squares[...] = add_squares(blocks, before[...])


def more_squares(blocks, before):
    vmem = pl.BlockSpec(memory_space=pltpu.VMEM)
    return pl.pallas_call(
        functools.partial(more_squares_kernel, len(blocks)),
        out_shape=jax.ShapeDtypeStruct(before.shape, F32),
        in_specs=[vmem] * (len(blocks) + 1),
        out_specs=vmem,
        compiler_params=pltpu.CompilerParams(vmem_limit_bytes=4 * 1024 * 1024),
        cost_estimate=hint(1),
    )(before, *blocks)


def project_kernel(n, order, me_ref, gain_ref, before_ref, mine_ref, other_ref, weight_ref, *rest):
    *helds, out_ref, last, spread, total, kept, sems = rest
    me = me_ref[0]
    rows, part = before_ref.shape
    copies = fetches(n, order, me, weight_ref, last, sems)
    for copy in copies:
        copy.start()
    places = [(held, slot) for held in helds for slot in range(held.shape[0])]
    early = len(places)
    places += [(last, slot) for slot in range(len(order))]
    blocks = list(zip(slots(n), places, strict=True))

    def products(picked, factor):
        summed = None
        for (entry, core), (held, slot) in picked:
            values = (mine_ref, other_ref)[core][entry].astype(F32)
            normed = (values * factor * gain_ref[owner(me, entry, core, n)]).astype(BF16)
            product = jnp.dot(normed, held[slot], preferred_element_type=F32)
            summed = product if summed is None else summed + product
        return summed

    def row_factor():
        square = add_squares([other_ref], before_ref[...])
        mean = jnp.sum(square, axis=1, keepdims=True) * (1.0 / (n * part))
        return lax.rsqrt(mean + EPS)

    @pl.when(me >= 0)
    def _():
        factor = row_factor()
        total[...] = products(blocks[:early], factor)
        kept[...] = jnp.broadcast_to(factor, kept.shape)

    for copy in copies:
        copy.wait()
    factor = kept[:, :1]
    summed = total[...] + products(blocks[early:], factor)
    columns = summed.shape[1] // 128
    steps = rows // n
    for block in range(columns):
        for step in range(steps):
            spread[:, step * columns + block, :] = summed[
                step * n : (step + 1) * n, block * 128 : (block + 1) * 128
            ]
    for target in range(n):
        out_ref[target] = spread[target, : steps * columns, :].astype(BF16)


def project(me, block, gain, weight, n):
    rows, part = block.shape
    columns = weight.shape[1]
    pieces = rows // n * (columns // 128)
    outer, middle = radices(n)
    order = slots(n)
    first, second = 3 * n // 8, 3 * n // 4

    arrived = [swap(block, n, o * 2 * middle) for o in range(1, outer)]
    held, gain, weight_a = fetch(me, block, gain, weight, n, order[:first])
    row = jnp.stack([held] + arrived)
    later = [swap(row, n, m * 2) for m in range(1, middle)]
    squares, weight_b = squares_beside(me, weight, [row], n, order[first:second])
    later, squares = lax.optimization_barrier((later, squares))
    mine = jnp.concatenate([row] + later)
    other = swap(mine, n, 1)
    squares = more_squares(later, squares)
    vmem = pl.BlockSpec(memory_space=pltpu.VMEM)
    hbm = pl.BlockSpec(memory_space=pltpu.HBM)
    return pl.pallas_call(
        functools.partial(project_kernel, n, order[second:]),
        out_shape=jax.ShapeDtypeStruct((n, pieces, 128), BF16),
        in_specs=[pl.BlockSpec(memory_space=pltpu.SMEM)] + [vmem] * 4 + [hbm] + [vmem] * 2,
        out_specs=vmem,
        scratch_shapes=[
            pltpu.VMEM((n - second, part, columns), BF16),
            pltpu.VMEM((n, -(-pieces // 8) * 8, 128), F32),
            pltpu.VMEM((rows, columns), F32),
            pltpu.VMEM((rows, 128), F32),
            pltpu.SemaphoreType.DMA((n - second,)),
        ],
        compiler_params=pltpu.CompilerParams(vmem_limit_bytes=VMEM_LIMIT),
        cost_estimate=hint(6),
    )(me, gain, squares, mine, other, far(weight), near(weight_a), near(weight_b))


def attend_kernel(
    table_ref, length_ref, received_ref, cos_ref, sin_ref, lambda_ref, gain_ref,
    keys_one_ref, keys_two_ref, values_ref, out_ref, fresh,
):
    sources, pieces, _ = received_ref.shape
    steps = cos_ref.shape[0]
    blocks = pieces // steps
    pages, page, _ = keys_one_ref.shape
    capacity = pages * page
    for source in range(sources):
        piece = received_ref[source].astype(F32)
        for step in range(steps):
            fresh[step, source * blocks : (source + 1) * blocks, :] = piece[
                step * blocks : (step + 1) * blocks
            ]

    def heads(step, kind):
        return fresh[step, kind * H : (kind + 1) * H, :]

    def rotated(step, kind):
        values = heads(step, kind)
        turned = values * cos_ref[step] + pltpu.roll(values, HD // 2, 1) * sin_ref[step]
        return turned.astype(BF16).astype(F32)

    row = lax.broadcasted_iota(jnp.int32, (1, capacity), 1)
    place = jnp.zeros((1, capacity), jnp.int32)
    for index in range(pages):
        first = table_ref[0, index] * page
        inside = (row >= first) & (row < first + page)
        place = jnp.where(inside, row - first + index * page, place)
    allowed = place < length_ref[0]

    scale = 1.0 / math.sqrt(HD)
    head_row = lax.rem(lax.broadcasted_iota(jnp.int32, (steps * H, HD), 0), H)

    def softmax_map(kind, keys_ref):
        queries = [rotated(step, kind) for step in range(steps)]
        news = [rotated(step, kind + 2) for step in range(steps)]
        stacked = jnp.concatenate(queries, axis=0)
        apart = jnp.concatenate(
            [jnp.where(head_row == h, stacked, 0.0).astype(BF16) for h in range(H)], axis=1
        )
        older = lax.dot_general(
            apart, keys_ref[...].reshape(capacity, H * HD), (((1,), (1,)), ((), ())),
            preferred_element_type=F32,
        )
        older = jnp.where(allowed, older * scale, -1e38)
        parts = []
        for step in range(steps):
            cached = older[step * H : (step + 1) * H]
            newer = [
                jnp.sum(queries[step] * news[e], axis=1, keepdims=True) * scale
                for e in range(step + 1)
            ]
            top = jnp.max(cached, axis=1, keepdims=True)
            for value in newer:
                top = jnp.maximum(top, value)
            cached = jnp.exp(cached - top)
            newer = [jnp.exp(value - top) for value in newer]
            whole = jnp.sum(cached, axis=1, keepdims=True)
            for value in newer:
                whole = whole + value
            parts.append((cached / whole, [value / whole for value in newer]))
        return parts

    first = softmax_map(0, keys_one_ref)
    second = softmax_map(1, keys_two_ref)
    weight = lambda_ref[...]
    mix = jnp.concatenate(
        [first[step][0] - weight * second[step][0] for step in range(steps)], axis=0
    ).astype(BF16)
    spread = jnp.dot(mix, values_ref[...].reshape(capacity, -1), preferred_element_type=F32)
    wide_row = lax.broadcasted_iota(jnp.int32, (H, 2 * HD), 0)
    fresh_values = [
        jnp.concatenate(
            [fresh[e, pl.ds(4 * H + half, H, stride=2), :] for half in range(2)], axis=1
        )
        for e in range(steps)
    ]
    for step in range(steps):
        mixed = jnp.zeros((H, 2 * HD), F32)
        for h in range(H):
            block = spread[step * H : (step + 1) * H, h * 2 * HD : (h + 1) * 2 * HD]
            mixed = jnp.where(wide_row == h, block, mixed)
        for e in range(step + 1):
            share = first[step][1][e] - weight * second[step][1][e]
            mixed = mixed + share.astype(BF16).astype(F32) * fresh_values[e]
        norm = lax.rsqrt(jnp.mean(mixed * mixed, axis=1, keepdims=True) + EPS)
        out_ref[step * H : (step + 1) * H, :] = (mixed * norm * gain_ref[...]).astype(BF16)


def attend(table, length, received, cos, sin, weights, gain, keys_one, keys_two, values):
    steps = cos.shape[0]
    sources, pieces, _ = received.shape
    vmem = pl.BlockSpec(memory_space=pltpu.VMEM)
    smem = pl.BlockSpec(memory_space=pltpu.SMEM)
    held = [near(x) for x in (keys_one, keys_two, values)]
    return pl.pallas_call(
        attend_kernel,
        out_shape=jax.ShapeDtypeStruct((steps * H, 2 * HD), BF16),
        in_specs=[smem, smem] + [vmem] * 8,
        out_specs=vmem,
        scratch_shapes=[pltpu.VMEM((steps, sources * (pieces // steps), 128), F32)],
        compiler_params=pltpu.CompilerParams(vmem_limit_bytes=VMEM_LIMIT),
        cost_estimate=hint(10),
    )(table, length, received, cos, sin, weights, gain, *held)


def output_kernel(n, me_ref, mine_ref, other_ref, inputs_ref, *rest):
    *weights, out_ref, rows_ref = rest
    me = me_ref[0]
    half, heads, width = mine_ref.shape
    steps = heads // H
    lanes = width // 128
    for entry in range(half):
        for core, ref in ((0, mine_ref), (1, other_ref)):
            start = pl.multiple_of(owner(me, entry, core, n) * heads, 8)
            block = ref[entry].astype(F32)
            for lane in range(lanes):
                rows_ref[lane, pl.ds(start, heads), :] = block[:, lane * 128 : (lane + 1) * 128]
    total = None
    for h in range(H):
        left = jnp.concatenate(
            [
                jnp.concatenate(
                    [rows_ref[lane, pl.ds(step * H + h, n, stride=heads), :] for lane in range(lanes)],
                    axis=1,
                )
                for step in range(steps)
            ],
            axis=0,
        ).astype(BF16)
        held = weights[h * len(weights) // H]
        at = h * width % held.shape[0]
        product = jnp.dot(left, held[at : at + width, :], preferred_element_type=F32)
        total = product if total is None else total + product
    for step in range(steps):
        out_ref[step] = (
            inputs_ref[step].astype(F32) + total[step * n : (step + 1) * n]
        ).astype(BF16)


def keep_kernel(half, block_ref, from_ref, held, to_ref, sem):
    rows = to_ref.shape[0]
    copy = pltpu.make_async_copy(from_ref.at[pl.ds(half * rows, rows), :], to_ref, sem)
    copy.start()
    held[...] = block_ref[...]
    copy.wait()


def keep(block, weight, half, us):
    vmem = pl.BlockSpec(memory_space=pltpu.VMEM)
    return pl.pallas_call(
        functools.partial(keep_kernel, half),
        out_shape=(
            jax.ShapeDtypeStruct(block.shape, block.dtype),
            pltpu.VMEM((weight.shape[0] // 2, weight.shape[1]), weight.dtype),
        ),
        in_specs=[vmem, pl.BlockSpec(memory_space=pltpu.HBM)],
        out_specs=(vmem, vmem),
        scratch_shapes=[pltpu.SemaphoreType.DMA],
        compiler_params=pltpu.CompilerParams(vmem_limit_bytes=4 * 1024 * 1024),
        cost_estimate=hint(us),
    )(block, far(weight))


def output(me, attended, inputs, weight, n):
    kept = []

    def aside(half, block):
        block, part = keep(block, weight, half, 2)
        kept.append(near(part))
        return block

    mine, other = gather_blocks(
        attended, n, functools.partial(aside, 0), functools.partial(aside, 1)
    )
    half, heads, width = mine.shape
    vmem = pl.BlockSpec(memory_space=pltpu.VMEM)
    return pl.pallas_call(
        functools.partial(output_kernel, n),
        out_shape=jax.ShapeDtypeStruct(inputs.shape, BF16),
        in_specs=[pl.BlockSpec(memory_space=pltpu.SMEM)] + [vmem] * 5,
        out_specs=vmem,
        scratch_shapes=[pltpu.VMEM((width // 128, n * heads, 128), F32)],
        compiler_params=pltpu.CompilerParams(vmem_limit_bytes=VMEM_LIMIT),
    )(me, mine, other, inputs, *kept)


def angles(positions, steps):
    half = HD // 2
    frequency = jnp.exp(-math.log(ROPE_BASE) * 2.0 * jnp.arange(half, dtype=F32) / HD)
    places = (positions + jnp.arange(steps, dtype=jnp.int32)).astype(F32)
    turns = places[:, None] * frequency[None, :]
    cosine, sine = jnp.cos(turns), jnp.sin(turns)
    cos = jnp.concatenate([cosine, cosine], axis=-1)
    sin = jnp.concatenate([-sine, sine], axis=-1)
    return cos[:, None, :], sin[:, None, :]


def turn_kernel(positions_ref, after_ref, cos_ref, sin_ref):
    steps = cos_ref.shape[0]
    lane = lax.broadcasted_iota(jnp.int32, (8, HD), 1)
    step = lax.broadcasted_iota(jnp.int32, (8, HD), 0)
    pair = lax.rem(lane, HD // 2).astype(F32)
    frequency = jnp.exp(-math.log(ROPE_BASE) * 2.0 * pair / HD)
    turns = (positions_ref[0] + step).astype(F32) * frequency
    cos = jnp.cos(turns)
    sin = jnp.where(lane < HD // 2, -1.0, 1.0) * jnp.sin(turns)
    for index in range(steps):
        cos_ref[index] = cos[index : index + 1]
        sin_ref[index] = sin[index : index + 1]


def turn(positions, after, steps):
    vmem = pl.BlockSpec(memory_space=pltpu.VMEM)
    return pl.pallas_call(
        turn_kernel,
        out_shape=(jax.ShapeDtypeStruct((steps, 1, HD), F32),) * 2,
        in_specs=[pl.BlockSpec(memory_space=pltpu.SMEM), pl.BlockSpec(memory_space=pl.ANY)],
        out_specs=(vmem, vmem),
        compiler_params=pltpu.CompilerParams(vmem_limit_bytes=4 * 1024 * 1024),
        cost_estimate=hint(1),
    )(positions, after)


def local(
    n, inputs, norm_gain, qkv_weight, head_lambda, head_gain, out_weight,
    key_one_pages, key_two_pages, value_pages, page_table, context_len, positions,
):
    steps, rows, part = inputs.shape
    me = lax.axis_index("gx").astype(jnp.int32).reshape(1)
    block = inputs.reshape(steps * rows, part)
    sent = project(me, block, norm_gain.reshape(n, 1, part), qkv_weight, n)
    received = lax.all_to_all(sent, "gx", 0, 0)
    cos, sin = turn(positions, sent, steps)
    attended = attend(
        page_table, context_len, received, cos, sin, head_lambda.reshape(H, 1),
        head_gain.reshape(H, 2 * HD), key_one_pages, key_two_pages, value_pages,
    )
    return output(me, attended, inputs, out_weight, n)


def rotary(vectors, cos, sin):
    return vectors * cos + jnp.roll(vectors, HD // 2, axis=-1) * sin


def local_any(
    n, inputs, norm_gain, qkv_weight, head_lambda, head_gain, out_weight,
    key_one_pages, key_two_pages, value_pages, page_table, context_len, positions,
):
    steps = inputs.shape[0]
    own = page_table.shape[0]
    capacity = page_table.shape[1] * key_one_pages.shape[1]
    values = lax.all_gather(inputs, "gx", axis=2, tiled=True).astype(F32)
    factor = lax.rsqrt(jnp.mean(values * values, axis=-1, keepdims=True) + EPS)
    normed = (values * factor * norm_gain).astype(BF16)
    projected = jnp.einsum("sbd,dc->sbc", normed, qkv_weight, preferred_element_type=F32)
    received = lax.all_to_all(
        projected.astype(BF16), "gx", split_axis=1, concat_axis=2, tiled=True
    )
    cached = tuple(
        pool[page_table].reshape(own, capacity, H, -1)
        for pool in (key_one_pages, key_two_pages, value_pages)
    )
    both = received[..., : 4 * H * HD].reshape(steps, own, 4, H, HD).astype(F32)
    new_values = received[..., 4 * H * HD :].reshape(steps, own, H, 2 * HD)
    cos, sin = jax.vmap(lambda p: angles(p, steps))(positions.reshape(own, 1))
    cos, sin = (jnp.moveaxis(x, 0, 1)[:, :, None] for x in (cos, sin))
    turned = rotary(both, cos, sin).astype(BF16)
    place = jnp.arange(capacity, dtype=jnp.int32)
    allowed = (place[None, :] < context_len[:, None])[None, :, None, :]
    step = jnp.arange(steps)
    newer_allowed = (step[None, :] <= step[:, None])[:, None, None, :]

    def softmax_map(query, keys, news):
        older = jnp.einsum("tshd,sjhd->tshj", query, keys, preferred_element_type=F32)
        newer = jnp.einsum("tshd,eshd->tshe", query, news, preferred_element_type=F32)
        scores = jnp.concatenate(
            [jnp.where(allowed, older, -jnp.inf), jnp.where(newer_allowed, newer, -jnp.inf)], axis=-1
        )
        return jax.nn.softmax(scores * (1.0 / math.sqrt(HD)), axis=-1)

    first = softmax_map(turned[:, :, 0], cached[0], turned[:, :, 2])
    second = softmax_map(turned[:, :, 1], cached[1], turned[:, :, 3])
    mix = (first - head_lambda[:, None] * second).astype(BF16)
    mixed = jnp.einsum(
        "tshj,sjhf->tshf", mix[..., :capacity], cached[2], preferred_element_type=F32
    ) + jnp.einsum("tshe,eshf->tshf", mix[..., capacity:], new_values, preferred_element_type=F32)
    norm = lax.rsqrt(jnp.mean(mixed * mixed, axis=-1, keepdims=True) + EPS)
    grouped = (mixed * norm * head_gain.reshape(H, 2 * HD)).astype(BF16)
    whole = lax.all_gather(grouped.reshape(steps, own, -1), "gx", axis=1, tiled=True)
    branch = jnp.einsum("sbf,fd->sbd", whole, out_weight, preferred_element_type=F32)
    return (inputs.astype(F32) + branch).astype(BF16)


def solution(mesh):
    n = mesh.shape["gx"]
    placed = (
        P(None, "groups", "gx"),
        P(),
        P(None, "gx"),
        P(),
        P(),
        P(None, "gx"),
        P(("groups", "gx"), None, None),
        P(("groups", "gx"), None, None),
        P(("groups", "gx"), None, None),
        P(("groups", "gx"), None),
        P(("groups", "gx")),
        P(("groups", "gx")),
    )

    def chosen(inputs, norm_gain, qkv_weight, *rest):
        aligned = inputs.shape[2] % 128 == 0 and qkv_weight.shape[1] % 128 == 0
        single = rest[6].shape[0] == 1
        power = n >= 4 and n & (n - 1) == 0
        body = local if aligned and single and power else local_any
        return body(n, inputs, norm_gain, qkv_weight, *rest)

    return jax.shard_map(
        chosen, mesh=mesh, in_specs=placed, out_specs=P(None, "groups", "gx"), check_vma=False
    )
```

```python
import functools
import math

import jax
import jax.numpy as jnp
from jax import lax
from jax.experimental import pallas as pl
from jax.experimental.pallas import tpu as pltpu
from jax.sharding import PartitionSpec as P

H = 24
HD = 128
EPS = 1e-05
ROPE_BASE = 10000.0
F32 = jnp.float32
BF16 = jnp.bfloat16
VMEM_LIMIT = 16 * 1024 * 1024


def radices(n):
    rest = n // 2
    middle = 1
    while middle * middle * 4 <= rest:
        middle *= 2
    return rest // middle, middle


def swap(block, n, mask):
    return lax.ppermute(block, "gx", [(i, i ^ mask) for i in range(n)])


def gather_blocks(block, n, first_aside, second_aside):
    outer, middle = radices(n)
    arrived = [swap(block, n, o * 2 * middle) for o in range(1, outer)]
    rows = jnp.stack([first_aside(block)] + arrived)
    others = [swap(rows, n, m * 2) for m in range(1, middle)]
    rows, others = lax.optimization_barrier((second_aside(rows), others))
    mine = jnp.concatenate([rows] + others)
    return mine, swap(mine, n, 1)


def owner(me, entry, core, n):
    outer, middle = radices(n)
    mask = (entry % outer) * (2 * middle) + (entry // outer) * 2 + core
    return jnp.bitwise_xor(me, mask)


def far(x):
    return pltpu.with_memory_space_constraint(x, pltpu.HBM)


def hint(us):
    return pl.CostEstimate(flops=0, bytes_accessed=int(us * 3_000_000), transcendentals=0)


def fetches(n, first, count, cores, me, from_ref, to_ref, sems):
    part = from_ref.shape[0] // n
    copies = []
    for index, core in enumerate(cores):
        for entry in range(count):
            slot = index * count + entry
            start = pl.multiple_of(owner(me, first + entry, core, n) * part, part)
            copies.append(
                pltpu.make_async_copy(
                    from_ref.at[pl.ds(start, part), :],
                    to_ref.at[slot],
                    sems.at[slot],
                )
            )
    return copies


def slots(n):
    return [(entry, core) for core in range(2) for entry in range(n // 2)]


def fetches(n, order, me, from_ref, to_ref, sems):
    part = from_ref.shape[0] // n
    copies = []
    for slot, (entry, core) in enumerate(order):
        start = pl.multiple_of(owner(me, entry, core, n) * part, part)
        copies.append(
            pltpu.make_async_copy(
                from_ref.at[pl.ds(start, part), :], to_ref.at[slot], sems.at[slot]
            )
        )
    return copies


def fetch_kernel(
    n, order, me_ref, block_ref, gain_ref, weight_ref, held, gain_out, weight_out, sems, other_sems
):
    copies = [
        pltpu.make_async_copy(block_ref, held, other_sems.at[0]),
        pltpu.make_async_copy(gain_ref, gain_out, other_sems.at[1]),
    ] + fetches(n, order, me_ref[0], weight_ref, weight_out, sems)
    for copy in copies:
        copy.start()
    for copy in copies:
        copy.wait()


def fetch(me, block, gain, weight, n, order):
    part, columns = weight.shape[0] // n, weight.shape[1]
    vmem = pl.BlockSpec(memory_space=pltpu.VMEM)
    hbm = pl.BlockSpec(memory_space=pltpu.HBM)
    return pl.pallas_call(
        functools.partial(fetch_kernel, n, order),
        out_shape=(
            pltpu.VMEM(block.shape, BF16),
            pltpu.VMEM(gain.shape, F32),
            pltpu.VMEM((len(order), part, columns), BF16),
        ),
        in_specs=[pl.BlockSpec(memory_space=pltpu.SMEM), hbm, hbm, hbm],
        out_specs=(vmem,) * 3,
        scratch_shapes=[
            pltpu.SemaphoreType.DMA((len(order),)),
            pltpu.SemaphoreType.DMA((2,)),
        ],
        compiler_params=pltpu.CompilerParams(vmem_limit_bytes=4 * 1024 * 1024),
        cost_estimate=hint(5),
    )(me, far(block), far(gain), far(weight))


def near(x):
    return pltpu.with_memory_space_constraint(x, pltpu.VMEM)


def add_squares(refs, square):
    for ref in refs:
        for entry in range(ref.shape[0]):
            values = ref[entry].astype(F32)
            square = square + values * values
    return square


def squares_kernel(n, order, count, me_ref, weight_ref, *rest):
    blocks, (squares, weight_out, sems) = rest[:count], rest[count:]
    copies = fetches(n, order, me_ref[0], weight_ref, weight_out, sems)
    for copy in copies:
        copy.start()
    squares[...] = add_squares(blocks, jnp.zeros(squares.shape, F32))
    for copy in copies:
        copy.wait()


def squares_beside(me, weight, blocks, n, order):
    part, columns = weight.shape[0] // n, weight.shape[1]
    vmem = pl.BlockSpec(memory_space=pltpu.VMEM)
    return pl.pallas_call(
        functools.partial(squares_kernel, n, order, len(blocks)),
        out_shape=(
            jax.ShapeDtypeStruct(blocks[0].shape[1:], F32),
            pltpu.VMEM((len(order), part, columns), BF16),
        ),
        in_specs=[
            pl.BlockSpec(memory_space=pltpu.SMEM),
            pl.BlockSpec(memory_space=pltpu.HBM),
        ]
        + [vmem] * len(blocks),
        out_specs=(vmem, vmem),
        scratch_shapes=[pltpu.SemaphoreType.DMA((len(order),))],
        compiler_params=pltpu.CompilerParams(vmem_limit_bytes=4 * 1024 * 1024),
        cost_estimate=hint(len(order) * 0.7),
    )(me, far(weight), *blocks)


def more_squares_kernel(count, before, *rest):
    *blocks, squares = rest
    squares[...] = add_squares(blocks, before[...])


def more_squares(blocks, before):
    vmem = pl.BlockSpec(memory_space=pltpu.VMEM)
    return pl.pallas_call(
        functools.partial(more_squares_kernel, len(blocks)),
        out_shape=jax.ShapeDtypeStruct(before.shape, F32),
        in_specs=[vmem] * (len(blocks) + 1),
        out_specs=vmem,
        compiler_params=pltpu.CompilerParams(vmem_limit_bytes=4 * 1024 * 1024),
        cost_estimate=hint(1),
    )(before, *blocks)


def project_kernel(n, order, me_ref, gain_ref, before_ref, mine_ref, other_ref, weight_ref, *rest):
    *helds, out_ref, last, spread, total, kept, sems = rest
    me = me_ref[0]
    rows, part = before_ref.shape
    copies = fetches(n, order, me, weight_ref, last, sems)
    for copy in copies:
        copy.start()
    places = [(held, slot) for held in helds for slot in range(held.shape[0])]
    early = len(places)
    places += [(last, slot) for slot in range(len(order))]
    blocks = list(zip(slots(n), places, strict=True))

    def products(picked, factor):
        summed = None
        for (entry, core), (held, slot) in picked:
            values = (mine_ref, other_ref)[core][entry].astype(F32)
            normed = (values * factor * gain_ref[owner(me, entry, core, n)]).astype(BF16)
            product = jnp.dot(normed, held[slot], preferred_element_type=F32)
            summed = product if summed is None else summed + product
        return summed

    def row_factor():
        square = add_squares([other_ref], before_ref[...])
        mean = jnp.sum(square, axis=1, keepdims=True) * (1.0 / (n * part))
        return lax.rsqrt(mean + EPS)

    @pl.when(me >= 0)
    def _():
        factor = row_factor()
        total[...] = products(blocks[:early], factor)
        kept[...] = jnp.broadcast_to(factor, kept.shape)

    for copy in copies:
        copy.wait()
    factor = kept[:, :1]
    summed = total[...] + products(blocks[early:], factor)
    columns = summed.shape[1] // 128
    steps = rows // n
    for block in range(columns):
        for step in range(steps):
            spread[:, step * columns + block, :] = summed[
                step * n : (step + 1) * n, block * 128 : (block + 1) * 128
            ]
    for target in range(n):
        out_ref[target] = spread[target, : steps * columns, :].astype(BF16)


def project(me, block, gain, weight, n):
    rows, part = block.shape
    columns = weight.shape[1]
    pieces = rows // n * (columns // 128)
    outer, middle = radices(n)
    order = slots(n)
    first, second = 5 * n // 16, 11 * n // 16

    arrived = [swap(block, n, o * 2 * middle) for o in range(1, outer)]
    own = [swap(block, n, m * 2) for m in range(1, middle)]
    held, gain, weight_a = fetch(me, block, gain, weight, n, order[:first])
    arrived = jnp.stack(arrived)
    row = jnp.concatenate([held[None], arrived])
    later = [swap(arrived, n, m * 2) for m in range(1, middle)]
    squares, weight_b = squares_beside(me, weight, [row], n, order[first:second])
    later, squares = lax.optimization_barrier((later, squares))
    later = [part for pair in zip([each[None] for each in own], later) for part in pair]
    mine = jnp.concatenate([row] + later)
    other = swap(mine, n, 1)
    squares = more_squares(later, squares)
    vmem = pl.BlockSpec(memory_space=pltpu.VMEM)
    hbm = pl.BlockSpec(memory_space=pltpu.HBM)
    return pl.pallas_call(
        functools.partial(project_kernel, n, order[second:]),
        out_shape=jax.ShapeDtypeStruct((n, pieces, 128), BF16),
        in_specs=[pl.BlockSpec(memory_space=pltpu.SMEM)] + [vmem] * 4 + [hbm] + [vmem] * 2,
        out_specs=vmem,
        scratch_shapes=[
            pltpu.VMEM((n - second, part, columns), BF16),
            pltpu.VMEM((n, -(-pieces // 8) * 8, 128), F32),
            pltpu.VMEM((rows, columns), F32),
            pltpu.VMEM((rows, 128), F32),
            pltpu.SemaphoreType.DMA((n - second,)),
        ],
        compiler_params=pltpu.CompilerParams(vmem_limit_bytes=VMEM_LIMIT),
        cost_estimate=hint(6),
    )(me, gain, squares, mine, other, far(weight), near(weight_a), near(weight_b))


def attend_kernel(
    table_ref, length_ref, received_ref, cos_ref, sin_ref, lambda_ref, gain_ref,
    keys_one_ref, keys_two_ref, values_ref, out_ref, fresh,
):
    sources, pieces, _ = received_ref.shape
    steps = cos_ref.shape[0]
    blocks = pieces // steps
    pages, page, _ = keys_one_ref.shape
    capacity = pages * page
    for source in range(sources):
        piece = received_ref[source].astype(F32)
        for step in range(steps):
            fresh[step, source * blocks : (source + 1) * blocks, :] = piece[
                step * blocks : (step + 1) * blocks
            ]

    def heads(step, kind):
        return fresh[step, kind * H : (kind + 1) * H, :]

    def rotated(step, kind):
        values = heads(step, kind)
        turned = values * cos_ref[step] + pltpu.roll(values, HD // 2, 1) * sin_ref[step]
        return turned.astype(BF16).astype(F32)

    row = lax.broadcasted_iota(jnp.int32, (1, capacity), 1)
    place = jnp.zeros((1, capacity), jnp.int32)
    for index in range(pages):
        first = table_ref[0, index] * page
        inside = (row >= first) & (row < first + page)
        place = jnp.where(inside, row - first + index * page, place)
    allowed = place < length_ref[0]

    scale = 1.0 / math.sqrt(HD)
    head_row = lax.rem(lax.broadcasted_iota(jnp.int32, (steps * H, HD), 0), H)

    def softmax_map(kind, keys_ref):
        queries = [rotated(step, kind) for step in range(steps)]
        news = [rotated(step, kind + 2) for step in range(steps)]
        stacked = jnp.concatenate(queries, axis=0)
        apart = jnp.concatenate(
            [jnp.where(head_row == h, stacked, 0.0).astype(BF16) for h in range(H)], axis=1
        )
        older = lax.dot_general(
            apart, keys_ref[...].reshape(capacity, H * HD), (((1,), (1,)), ((), ())),
            preferred_element_type=F32,
        )
        older = jnp.where(allowed, older * scale, -1e38)
        parts = []
        for step in range(steps):
            cached = older[step * H : (step + 1) * H]
            newer = [
                jnp.sum(queries[step] * news[e], axis=1, keepdims=True) * scale
                for e in range(step + 1)
            ]
            top = jnp.max(cached, axis=1, keepdims=True)
            for value in newer:
                top = jnp.maximum(top, value)
            cached = jnp.exp(cached - top)
            newer = [jnp.exp(value - top) for value in newer]
            whole = jnp.sum(cached, axis=1, keepdims=True)
            for value in newer:
                whole = whole + value
            parts.append((cached / whole, [value / whole for value in newer]))
        return parts

    first = softmax_map(0, keys_one_ref)
    second = softmax_map(1, keys_two_ref)
    weight = lambda_ref[...]
    mix = jnp.concatenate(
        [first[step][0] - weight * second[step][0] for step in range(steps)], axis=0
    ).astype(BF16)
    spread = jnp.dot(mix, values_ref[...].reshape(capacity, -1), preferred_element_type=F32)
    wide_row = lax.broadcasted_iota(jnp.int32, (H, 2 * HD), 0)
    fresh_values = [
        jnp.concatenate(
            [fresh[e, pl.ds(4 * H + half, H, stride=2), :] for half in range(2)], axis=1
        )
        for e in range(steps)
    ]
    for step in range(steps):
        mixed = jnp.zeros((H, 2 * HD), F32)
        for h in range(H):
            block = spread[step * H : (step + 1) * H, h * 2 * HD : (h + 1) * 2 * HD]
            mixed = jnp.where(wide_row == h, block, mixed)
        for e in range(step + 1):
            share = first[step][1][e] - weight * second[step][1][e]
            mixed = mixed + share.astype(BF16).astype(F32) * fresh_values[e]
        norm = lax.rsqrt(jnp.mean(mixed * mixed, axis=1, keepdims=True) + EPS)
        out_ref[step * H : (step + 1) * H, :] = (mixed * norm * gain_ref[...]).astype(BF16)


def attend(table, length, received, cos, sin, weights, gain, keys_one, keys_two, values):
    steps = cos.shape[0]
    sources, pieces, _ = received.shape
    vmem = pl.BlockSpec(memory_space=pltpu.VMEM)
    smem = pl.BlockSpec(memory_space=pltpu.SMEM)
    held = [near(x) for x in (keys_one, keys_two, values)]
    return pl.pallas_call(
        attend_kernel,
        out_shape=jax.ShapeDtypeStruct((steps * H, 2 * HD), BF16),
        in_specs=[smem, smem] + [vmem] * 8,
        out_specs=vmem,
        scratch_shapes=[pltpu.VMEM((steps, sources * (pieces // steps), 128), F32)],
        compiler_params=pltpu.CompilerParams(vmem_limit_bytes=VMEM_LIMIT),
        cost_estimate=hint(10),
    )(table, length, received, cos, sin, weights, gain, *held)


def output_kernel(n, me_ref, mine_ref, other_ref, inputs_ref, *rest):
    *weights, out_ref, rows_ref = rest
    me = me_ref[0]
    half, heads, width = mine_ref.shape
    steps = heads // H
    lanes = width // 128
    for entry in range(half):
        for core, ref in ((0, mine_ref), (1, other_ref)):
            start = pl.multiple_of(owner(me, entry, core, n) * heads, 8)
            block = ref[entry].astype(F32)
            for lane in range(lanes):
                rows_ref[lane, pl.ds(start, heads), :] = block[:, lane * 128 : (lane + 1) * 128]
    total = None
    for h in range(H):
        left = jnp.concatenate(
            [
                jnp.concatenate(
                    [rows_ref[lane, pl.ds(step * H + h, n, stride=heads), :] for lane in range(lanes)],
                    axis=1,
                )
                for step in range(steps)
            ],
            axis=0,
        ).astype(BF16)
        held = weights[h * len(weights) // H]
        at = h * width % held.shape[0]
        product = jnp.dot(left, held[at : at + width, :], preferred_element_type=F32)
        total = product if total is None else total + product
    for step in range(steps):
        out_ref[step] = (
            inputs_ref[step].astype(F32) + total[step * n : (step + 1) * n]
        ).astype(BF16)


def keep_kernel(half, block_ref, from_ref, held, to_ref, sem):
    rows = to_ref.shape[0]
    copy = pltpu.make_async_copy(from_ref.at[pl.ds(half * rows, rows), :], to_ref, sem)
    copy.start()
    held[...] = block_ref[...]
    copy.wait()


def keep(block, weight, half, us):
    vmem = pl.BlockSpec(memory_space=pltpu.VMEM)
    return pl.pallas_call(
        functools.partial(keep_kernel, half),
        out_shape=(
            jax.ShapeDtypeStruct(block.shape, block.dtype),
            pltpu.VMEM((weight.shape[0] // 2, weight.shape[1]), weight.dtype),
        ),
        in_specs=[vmem, pl.BlockSpec(memory_space=pltpu.HBM)],
        out_specs=(vmem, vmem),
        scratch_shapes=[pltpu.SemaphoreType.DMA],
        compiler_params=pltpu.CompilerParams(vmem_limit_bytes=4 * 1024 * 1024),
        cost_estimate=hint(us),
    )(block, far(weight))


def output(me, attended, inputs, weight, n):
    kept = []

    def aside(half, block):
        block, part = keep(block, weight, half, 2)
        kept.append(near(part))
        return block

    mine, other = gather_blocks(
        attended, n, functools.partial(aside, 0), functools.partial(aside, 1)
    )
    half, heads, width = mine.shape
    vmem = pl.BlockSpec(memory_space=pltpu.VMEM)
    return pl.pallas_call(
        functools.partial(output_kernel, n),
        out_shape=jax.ShapeDtypeStruct(inputs.shape, BF16),
        in_specs=[pl.BlockSpec(memory_space=pltpu.SMEM)] + [vmem] * 5,
        out_specs=vmem,
        scratch_shapes=[pltpu.VMEM((width // 128, n * heads, 128), F32)],
        compiler_params=pltpu.CompilerParams(vmem_limit_bytes=VMEM_LIMIT),
    )(me, mine, other, inputs, *kept)


def angles(positions, steps):
    half = HD // 2
    frequency = jnp.exp(-math.log(ROPE_BASE) * 2.0 * jnp.arange(half, dtype=F32) / HD)
    places = (positions + jnp.arange(steps, dtype=jnp.int32)).astype(F32)
    turns = places[:, None] * frequency[None, :]
    cosine, sine = jnp.cos(turns), jnp.sin(turns)
    cos = jnp.concatenate([cosine, cosine], axis=-1)
    sin = jnp.concatenate([-sine, sine], axis=-1)
    return cos[:, None, :], sin[:, None, :]


def turn_kernel(positions_ref, after_ref, cos_ref, sin_ref):
    steps = cos_ref.shape[0]
    lane = lax.broadcasted_iota(jnp.int32, (8, HD), 1)
    step = lax.broadcasted_iota(jnp.int32, (8, HD), 0)
    pair = lax.rem(lane, HD // 2).astype(F32)
    frequency = jnp.exp(-math.log(ROPE_BASE) * 2.0 * pair / HD)
    turns = (positions_ref[0] + step).astype(F32) * frequency
    cos = jnp.cos(turns)
    sin = jnp.where(lane < HD // 2, -1.0, 1.0) * jnp.sin(turns)
    for index in range(steps):
        cos_ref[index] = cos[index : index + 1]
        sin_ref[index] = sin[index : index + 1]


def turn(positions, after, steps):
    vmem = pl.BlockSpec(memory_space=pltpu.VMEM)
    return pl.pallas_call(
        turn_kernel,
        out_shape=(jax.ShapeDtypeStruct((steps, 1, HD), F32),) * 2,
        in_specs=[pl.BlockSpec(memory_space=pltpu.SMEM), pl.BlockSpec(memory_space=pl.ANY)],
        out_specs=(vmem, vmem),
        compiler_params=pltpu.CompilerParams(vmem_limit_bytes=4 * 1024 * 1024),
        cost_estimate=hint(1),
    )(positions, after)


def local(
    n, inputs, norm_gain, qkv_weight, head_lambda, head_gain, out_weight,
    key_one_pages, key_two_pages, value_pages, page_table, context_len, positions,
):
    steps, rows, part = inputs.shape
    me = lax.axis_index("gx").astype(jnp.int32).reshape(1)
    block = inputs.reshape(steps * rows, part)
    sent = project(me, block, norm_gain.reshape(n, 1, part), qkv_weight, n)
    received = lax.all_to_all(sent, "gx", 0, 0)
    cos, sin = turn(positions, sent, steps)
    attended = attend(
        page_table, context_len, received, cos, sin, head_lambda.reshape(H, 1),
        head_gain.reshape(H, 2 * HD), key_one_pages, key_two_pages, value_pages,
    )
    return output(me, attended, inputs, out_weight, n)


def rotary(vectors, cos, sin):
    return vectors * cos + jnp.roll(vectors, HD // 2, axis=-1) * sin


def local_any(
    n, inputs, norm_gain, qkv_weight, head_lambda, head_gain, out_weight,
    key_one_pages, key_two_pages, value_pages, page_table, context_len, positions,
):
    steps = inputs.shape[0]
    own = page_table.shape[0]
    capacity = page_table.shape[1] * key_one_pages.shape[1]
    values = lax.all_gather(inputs, "gx", axis=2, tiled=True).astype(F32)
    factor = lax.rsqrt(jnp.mean(values * values, axis=-1, keepdims=True) + EPS)
    normed = (values * factor * norm_gain).astype(BF16)
    projected = jnp.einsum("sbd,dc->sbc", normed, qkv_weight, preferred_element_type=F32)
    received = lax.all_to_all(
        projected.astype(BF16), "gx", split_axis=1, concat_axis=2, tiled=True
    )
    cached = tuple(
        pool[page_table].reshape(own, capacity, H, -1)
        for pool in (key_one_pages, key_two_pages, value_pages)
    )
    both = received[..., : 4 * H * HD].reshape(steps, own, 4, H, HD).astype(F32)
    new_values = received[..., 4 * H * HD :].reshape(steps, own, H, 2 * HD)
    cos, sin = jax.vmap(lambda p: angles(p, steps))(positions.reshape(own, 1))
    cos, sin = (jnp.moveaxis(x, 0, 1)[:, :, None] for x in (cos, sin))
    turned = rotary(both, cos, sin).astype(BF16)
    place = jnp.arange(capacity, dtype=jnp.int32)
    allowed = (place[None, :] < context_len[:, None])[None, :, None, :]
    step = jnp.arange(steps)
    newer_allowed = (step[None, :] <= step[:, None])[:, None, None, :]

    def softmax_map(query, keys, news):
        older = jnp.einsum("tshd,sjhd->tshj", query, keys, preferred_element_type=F32)
        newer = jnp.einsum("tshd,eshd->tshe", query, news, preferred_element_type=F32)
        scores = jnp.concatenate(
            [jnp.where(allowed, older, -jnp.inf), jnp.where(newer_allowed, newer, -jnp.inf)], axis=-1
        )
        return jax.nn.softmax(scores * (1.0 / math.sqrt(HD)), axis=-1)

    first = softmax_map(turned[:, :, 0], cached[0], turned[:, :, 2])
    second = softmax_map(turned[:, :, 1], cached[1], turned[:, :, 3])
    mix = (first - head_lambda[:, None] * second).astype(BF16)
    mixed = jnp.einsum(
        "tshj,sjhf->tshf", mix[..., :capacity], cached[2], preferred_element_type=F32
    ) + jnp.einsum("tshe,eshf->tshf", mix[..., capacity:], new_values, preferred_element_type=F32)
    norm = lax.rsqrt(jnp.mean(mixed * mixed, axis=-1, keepdims=True) + EPS)
    grouped = (mixed * norm * head_gain.reshape(H, 2 * HD)).astype(BF16)
    whole = lax.all_gather(grouped.reshape(steps, own, -1), "gx", axis=1, tiled=True)
    branch = jnp.einsum("sbf,fd->sbd", whole, out_weight, preferred_element_type=F32)
    return (inputs.astype(F32) + branch).astype(BF16)


def solution(mesh):
    n = mesh.shape["gx"]
    placed = (
        P(None, "groups", "gx"),
        P(),
        P(None, "gx"),
        P(),
        P(),
        P(None, "gx"),
        P(("groups", "gx"), None, None),
        P(("groups", "gx"), None, None),
        P(("groups", "gx"), None, None),
        P(("groups", "gx"), None),
        P(("groups", "gx")),
        P(("groups", "gx")),
    )

    def chosen(inputs, norm_gain, qkv_weight, *rest):
        aligned = inputs.shape[2] % 128 == 0 and qkv_weight.shape[1] % 128 == 0
        single = rest[6].shape[0] == 1
        power = n >= 4 and n & (n - 1) == 0
        body = local if aligned and single and power else local_any
        return body(n, inputs, norm_gain, qkv_weight, *rest)

    return jax.shard_map(
        chosen, mesh=mesh, in_specs=placed, out_specs=P(None, "groups", "gx"), check_vma=False
    )
```

```python
import functools
import math

import jax
import jax.numpy as jnp
from jax import lax
from jax.experimental import pallas as pl
from jax.experimental.pallas import tpu as pltpu
from jax.sharding import PartitionSpec as P

H = 24
HD = 128
EPS = 1e-05
ROPE_BASE = 10000.0
F32 = jnp.float32
BF16 = jnp.bfloat16
VMEM_LIMIT = 16 * 1024 * 1024


def radices(n):
    rest = n // 2
    middle = 1
    while middle * middle * 4 <= rest:
        middle *= 2
    return rest // middle, middle


def swap(block, n, mask):
    return lax.ppermute(block, "gx", [(i, i ^ mask) for i in range(n)])


def gather_blocks(block, n, first_aside, second_aside):
    outer, middle = radices(n)
    arrived = [swap(block, n, o * 2 * middle) for o in range(1, outer)]
    rows = jnp.stack([first_aside(block)] + arrived)
    others = [swap(rows, n, m * 2) for m in range(1, middle)]
    rows, others = lax.optimization_barrier((second_aside(rows), others))
    mine = jnp.concatenate([rows] + others)
    return mine, swap(mine, n, 1)


def owner(me, entry, core, n):
    outer, middle = radices(n)
    mask = (entry % outer) * (2 * middle) + (entry // outer) * 2 + core
    return jnp.bitwise_xor(me, mask)


def far(x):
    return pltpu.with_memory_space_constraint(x, pltpu.HBM)


def hint(us):
    return pl.CostEstimate(flops=0, bytes_accessed=int(us * 3_000_000), transcendentals=0)


def fetches(n, first, count, cores, me, from_ref, to_ref, sems):
    part = from_ref.shape[0] // n
    copies = []
    for index, core in enumerate(cores):
        for entry in range(count):
            slot = index * count + entry
            start = pl.multiple_of(owner(me, first + entry, core, n) * part, part)
            copies.append(
                pltpu.make_async_copy(
                    from_ref.at[pl.ds(start, part), :],
                    to_ref.at[slot],
                    sems.at[slot],
                )
            )
    return copies


def slots(n):
    return [(entry, core) for core in range(2) for entry in range(n // 2)]


def fetches(n, order, me, from_ref, to_ref, sems):
    part = from_ref.shape[0] // n
    copies = []
    for slot, (entry, core) in enumerate(order):
        start = pl.multiple_of(owner(me, entry, core, n) * part, part)
        copies.append(
            pltpu.make_async_copy(
                from_ref.at[pl.ds(start, part), :], to_ref.at[slot], sems.at[slot]
            )
        )
    return copies


def fetch_kernel(n, order, *rest):
    (
        me_ref, block_ref, gain_ref, weight_ref, table_ref, lambda_ref, head_gain_ref,
        held, gain_out, weight_out, place_ref, lambda_out, head_gain_out,
        table, row_ref, wide_ref, sems, other_sems,
    ) = rest
    small = [
        pltpu.make_async_copy(start, end, other_sems.at[index])
        for index, (start, end) in enumerate(
            (
                (table_ref, table),
                (lambda_ref, row_ref),
                (head_gain_ref, wide_ref),
                (block_ref, held),
                (gain_ref, gain_out),
            )
        )
    ]
    large = fetches(n, order, me_ref[0], weight_ref, weight_out, sems)
    for copy in small + large:
        copy.start()
    for copy in small:
        copy.wait()

    capacity = place_ref.shape[1]
    pages = table_ref.shape[1]
    page = capacity // pages
    row = lax.broadcasted_iota(jnp.int32, (1, capacity), 1)
    place = jnp.zeros((1, capacity), jnp.int32)
    for index in range(pages):
        first = table[0, index] * page
        inside = (row >= first) & (row < first + page)
        place = jnp.where(inside, row - first + index * page, place)
    place_ref[...] = place
    across = lax.broadcasted_iota(jnp.int32, (H, H), 1) == lax.broadcasted_iota(jnp.int32, (H, H), 0)
    lambda_out[...] = jnp.sum(jnp.where(across, row_ref[...], 0.0), axis=1, keepdims=True)
    for h in range(H):
        head_gain_out[h : h + 1, :] = wide_ref[:, h * 2 * HD : (h + 1) * 2 * HD]

    for copy in large:
        copy.wait()


def fetch(me, block, gain, weight, n, order, small, capacity):
    part, columns = weight.shape[0] // n, weight.shape[1]
    vmem = pl.BlockSpec(memory_space=pltpu.VMEM)
    hbm = pl.BlockSpec(memory_space=pltpu.HBM)
    table, weights, head_gain = small
    return pl.pallas_call(
        functools.partial(fetch_kernel, n, order),
        out_shape=(
            pltpu.VMEM(block.shape, BF16),
            pltpu.VMEM(gain.shape, F32),
            pltpu.VMEM((len(order), part, columns), BF16),
            jax.ShapeDtypeStruct((1, capacity), jnp.int32),
            jax.ShapeDtypeStruct((H, 1), F32),
            jax.ShapeDtypeStruct((H, 2 * HD), F32),
        ),
        in_specs=[pl.BlockSpec(memory_space=pltpu.SMEM)] + [hbm] * 6,
        out_specs=(vmem,) * 6,
        scratch_shapes=[
            pltpu.SMEM(table.shape, table.dtype),
            pltpu.VMEM(weights.shape, F32),
            pltpu.VMEM(head_gain.shape, F32),
            pltpu.SemaphoreType.DMA((len(order),)),
            pltpu.SemaphoreType.DMA((5,)),
        ],
        compiler_params=pltpu.CompilerParams(vmem_limit_bytes=4 * 1024 * 1024),
        cost_estimate=hint(5),
    )(me, far(block), far(gain), far(weight), *map(far, small))


def near(x):
    return pltpu.with_memory_space_constraint(x, pltpu.VMEM)


def add_squares(refs, square):
    for ref in refs:
        for entry in range(ref.shape[0]):
            values = ref[entry].astype(F32)
            square = square + values * values
    return square


def squares_kernel(n, order, count, me_ref, weight_ref, *rest):
    blocks, (squares, weight_out, sems) = rest[:count], rest[count:]
    copies = fetches(n, order, me_ref[0], weight_ref, weight_out, sems)
    for copy in copies:
        copy.start()
    squares[...] = add_squares(blocks, jnp.zeros(squares.shape, F32))
    for copy in copies:
        copy.wait()


def squares_beside(me, weight, blocks, n, order):
    part, columns = weight.shape[0] // n, weight.shape[1]
    vmem = pl.BlockSpec(memory_space=pltpu.VMEM)
    return pl.pallas_call(
        functools.partial(squares_kernel, n, order, len(blocks)),
        out_shape=(
            jax.ShapeDtypeStruct(blocks[0].shape[1:], F32),
            pltpu.VMEM((len(order), part, columns), BF16),
        ),
        in_specs=[
            pl.BlockSpec(memory_space=pltpu.SMEM),
            pl.BlockSpec(memory_space=pltpu.HBM),
        ]
        + [vmem] * len(blocks),
        out_specs=(vmem, vmem),
        scratch_shapes=[pltpu.SemaphoreType.DMA((len(order),))],
        compiler_params=pltpu.CompilerParams(vmem_limit_bytes=4 * 1024 * 1024),
        cost_estimate=hint(len(order) * 0.7),
    )(me, far(weight), *blocks)


def more_squares_kernel(positions_ref, length_ref, place_ref, before, *rest):
    *blocks, squares, cos_ref, sin_ref, allowed_ref = rest
    squares[...] = add_squares(blocks, before[...])
    steps = cos_ref.shape[0]
    lane = lax.broadcasted_iota(jnp.int32, (8, HD), 1)
    step = lax.broadcasted_iota(jnp.int32, (8, HD), 0)
    pair = lax.rem(lane, HD // 2).astype(F32)
    frequency = jnp.exp(-math.log(ROPE_BASE) * 2.0 * pair / HD)
    turns = (positions_ref[0] + step).astype(F32) * frequency
    cos = jnp.cos(turns)
    sin = jnp.where(lane < HD // 2, -1.0, 1.0) * jnp.sin(turns)
    for index in range(steps):
        cos_ref[index] = cos[index : index + 1]
        sin_ref[index] = sin[index : index + 1]
    allowed_ref[...] = jnp.where(place_ref[...] < length_ref[0], 1.0, 0.0)


def more_squares(blocks, before, positions, length, place, steps):
    vmem = pl.BlockSpec(memory_space=pltpu.VMEM)
    smem = pl.BlockSpec(memory_space=pltpu.SMEM)
    turns = jax.ShapeDtypeStruct((steps, 1, HD), F32)
    return pl.pallas_call(
        more_squares_kernel,
        out_shape=(
            jax.ShapeDtypeStruct(before.shape, F32),
            turns,
            turns,
            jax.ShapeDtypeStruct(place.shape, F32),
        ),
        in_specs=[smem, smem] + [vmem] * (len(blocks) + 2),
        out_specs=(vmem,) * 4,
        compiler_params=pltpu.CompilerParams(vmem_limit_bytes=4 * 1024 * 1024),
        cost_estimate=hint(1),
    )(positions, length, place, before, *blocks)


def project_kernel(n, order, me_ref, gain_ref, before_ref, mine_ref, other_ref, weight_ref, *rest):
    *helds, out_ref, last, spread, total, kept, sems = rest
    me = me_ref[0]
    rows, part = before_ref.shape
    copies = fetches(n, order, me, weight_ref, last, sems)
    for copy in copies:
        copy.start()
    places = [(held, slot) for held in helds for slot in range(held.shape[0])]
    early = len(places)
    places += [(last, slot) for slot in range(len(order))]
    blocks = list(zip(slots(n), places, strict=True))

    def products(picked, factor):
        summed = None
        for (entry, core), (held, slot) in picked:
            values = (mine_ref, other_ref)[core][entry].astype(F32)
            normed = (values * factor * gain_ref[owner(me, entry, core, n)]).astype(BF16)
            product = jnp.dot(normed, held[slot], preferred_element_type=F32)
            summed = product if summed is None else summed + product
        return summed

    def row_factor():
        square = add_squares([other_ref], before_ref[...])
        mean = jnp.sum(square, axis=1, keepdims=True) * (1.0 / (n * part))
        return lax.rsqrt(mean + EPS)

    @pl.when(me >= 0)
    def _():
        factor = row_factor()
        total[...] = products(blocks[:early], factor)
        kept[...] = jnp.broadcast_to(factor, kept.shape)

    for copy in copies:
        copy.wait()
    factor = kept[:, :1]
    summed = total[...] + products(blocks[early:], factor)
    columns = summed.shape[1] // 128
    steps = rows // n
    for block in range(columns):
        for step in range(steps):
            spread[:, step * columns + block, :] = summed[
                step * n : (step + 1) * n, block * 128 : (block + 1) * 128
            ]
    for target in range(n):
        out_ref[target] = spread[target, : steps * columns, :].astype(BF16)


def project(me, block, gain, weight, n, scalars, small, capacity):
    rows, part = block.shape
    columns = weight.shape[1]
    pieces = rows // n * (columns // 128)
    outer, middle = radices(n)
    order = slots(n)
    first, second = 3 * n // 8, 3 * n // 4

    arrived = [swap(block, n, o * 2 * middle) for o in range(1, outer)]
    held, gain, weight_a, place, weights, head_gain = fetch(
        me, block, gain, weight, n, order[:first], small, capacity
    )
    row = jnp.stack([held] + arrived)
    later = [swap(row, n, m * 2) for m in range(1, middle)]
    squares, weight_b = squares_beside(me, weight, [row], n, order[first:second])
    later, squares = lax.optimization_barrier((later, squares))
    mine = jnp.concatenate([row] + later)
    other = swap(mine, n, 1)
    squares, cos, sin, allowed = more_squares(later, squares, *scalars, place, rows // n)
    vmem = pl.BlockSpec(memory_space=pltpu.VMEM)
    hbm = pl.BlockSpec(memory_space=pltpu.HBM)
    sent = pl.pallas_call(
        functools.partial(project_kernel, n, order[second:]),
        out_shape=jax.ShapeDtypeStruct((n, pieces, 128), BF16),
        in_specs=[pl.BlockSpec(memory_space=pltpu.SMEM)] + [vmem] * 4 + [hbm] + [vmem] * 2,
        out_specs=vmem,
        scratch_shapes=[
            pltpu.VMEM((n - second, part, columns), BF16),
            pltpu.VMEM((n, -(-pieces // 8) * 8, 128), F32),
            pltpu.VMEM((rows, columns), F32),
            pltpu.VMEM((rows, 128), F32),
            pltpu.SemaphoreType.DMA((n - second,)),
        ],
        compiler_params=pltpu.CompilerParams(vmem_limit_bytes=VMEM_LIMIT),
        cost_estimate=hint(6),
    )(me, gain, squares, mine, other, far(weight), near(weight_a), near(weight_b))
    return sent, (cos, sin, allowed, weights, head_gain)


def attend_kernel(
    received_ref, cos_ref, sin_ref, allowed_ref, lambda_ref, gain_ref,
    keys_one_ref, keys_two_ref, values_ref, out_ref, fresh,
):
    sources, pieces, _ = received_ref.shape
    steps = cos_ref.shape[0]
    blocks = pieces // steps
    pages, page, _ = keys_one_ref.shape
    capacity = pages * page
    for source in range(sources):
        piece = received_ref[source].astype(F32)
        for step in range(steps):
            fresh[step, source * blocks : (source + 1) * blocks, :] = piece[
                step * blocks : (step + 1) * blocks
            ]

    def heads(step, kind):
        return fresh[step, kind * H : (kind + 1) * H, :]

    def rotated(step, kind):
        values = heads(step, kind)
        turned = values * cos_ref[step] + pltpu.roll(values, HD // 2, 1) * sin_ref[step]
        return turned.astype(BF16).astype(F32)

    allowed = allowed_ref[...] > 0.0
    scale = 1.0 / math.sqrt(HD)
    head_row = lax.rem(lax.broadcasted_iota(jnp.int32, (steps * H, HD), 0), H)

    def softmax_map(kind, keys_ref):
        queries = [rotated(step, kind) for step in range(steps)]
        news = [rotated(step, kind + 2) for step in range(steps)]
        stacked = jnp.concatenate(queries, axis=0)
        apart = jnp.concatenate(
            [jnp.where(head_row == h, stacked, 0.0).astype(BF16) for h in range(H)], axis=1
        )
        older = lax.dot_general(
            apart, keys_ref[...].reshape(capacity, H * HD), (((1,), (1,)), ((), ())),
            preferred_element_type=F32,
        )
        older = jnp.where(allowed, older * scale, -1e38)
        parts = []
        for step in range(steps):
            cached = older[step * H : (step + 1) * H]
            newer = [
                jnp.sum(queries[step] * news[e], axis=1, keepdims=True) * scale
                for e in range(step + 1)
            ]
            top = jnp.max(cached, axis=1, keepdims=True)
            for value in newer:
                top = jnp.maximum(top, value)
            cached = jnp.exp(cached - top)
            newer = [jnp.exp(value - top) for value in newer]
            whole = jnp.sum(cached, axis=1, keepdims=True)
            for value in newer:
                whole = whole + value
            parts.append((cached / whole, [value / whole for value in newer]))
        return parts

    first = softmax_map(0, keys_one_ref)
    second = softmax_map(1, keys_two_ref)
    weight = lambda_ref[...]
    mix = jnp.concatenate(
        [first[step][0] - weight * second[step][0] for step in range(steps)], axis=0
    ).astype(BF16)
    spread = jnp.dot(mix, values_ref[...].reshape(capacity, -1), preferred_element_type=F32)
    wide_row = lax.broadcasted_iota(jnp.int32, (H, 2 * HD), 0)
    fresh_values = [
        jnp.concatenate(
            [fresh[e, pl.ds(4 * H + half, H, stride=2), :] for half in range(2)], axis=1
        )
        for e in range(steps)
    ]
    for step in range(steps):
        mixed = jnp.zeros((H, 2 * HD), F32)
        for h in range(H):
            block = spread[step * H : (step + 1) * H, h * 2 * HD : (h + 1) * 2 * HD]
            mixed = jnp.where(wide_row == h, block, mixed)
        for e in range(step + 1):
            share = first[step][1][e] - weight * second[step][1][e]
            mixed = mixed + share.astype(BF16).astype(F32) * fresh_values[e]
        norm = lax.rsqrt(jnp.mean(mixed * mixed, axis=1, keepdims=True) + EPS)
        out_ref[step * H : (step + 1) * H, :] = (mixed * norm * gain_ref[...]).astype(BF16)


def attend(received, cos, sin, allowed, weights, gain, keys_one, keys_two, values):
    steps = cos.shape[0]
    sources, pieces, _ = received.shape
    vmem = pl.BlockSpec(memory_space=pltpu.VMEM)
    held = [near(x) for x in (keys_one, keys_two, values)]
    return pl.pallas_call(
        attend_kernel,
        out_shape=jax.ShapeDtypeStruct((steps * H, 2 * HD), BF16),
        in_specs=[vmem] * 9,
        out_specs=vmem,
        scratch_shapes=[pltpu.VMEM((steps, sources * (pieces // steps), 128), F32)],
        compiler_params=pltpu.CompilerParams(vmem_limit_bytes=VMEM_LIMIT),
        cost_estimate=hint(10),
    )(received, cos, sin, allowed, weights, gain, *held)


def output_kernel(n, me_ref, mine_ref, other_ref, inputs_ref, *rest):
    *weights, out_ref, rows_ref = rest
    me = me_ref[0]
    half, heads, width = mine_ref.shape
    steps = heads // H
    lanes = width // 128
    for entry in range(half):
        for core, ref in ((0, mine_ref), (1, other_ref)):
            start = pl.multiple_of(owner(me, entry, core, n) * heads, 8)
            block = ref[entry].astype(F32)
            for lane in range(lanes):
                rows_ref[lane, pl.ds(start, heads), :] = block[:, lane * 128 : (lane + 1) * 128]
    total = None
    for h in range(H):
        left = jnp.concatenate(
            [
                jnp.concatenate(
                    [rows_ref[lane, pl.ds(step * H + h, n, stride=heads), :] for lane in range(lanes)],
                    axis=1,
                )
                for step in range(steps)
            ],
            axis=0,
        ).astype(BF16)
        held = weights[h * len(weights) // H]
        at = h * width % held.shape[0]
        product = jnp.dot(left, held[at : at + width, :], preferred_element_type=F32)
        total = product if total is None else total + product
    for step in range(steps):
        out_ref[step] = (
            inputs_ref[step].astype(F32) + total[step * n : (step + 1) * n]
        ).astype(BF16)


def keep_kernel(half, block_ref, from_ref, held, to_ref, sem):
    rows = to_ref.shape[0]
    copy = pltpu.make_async_copy(from_ref.at[pl.ds(half * rows, rows), :], to_ref, sem)
    copy.start()
    held[...] = block_ref[...]
    copy.wait()


def keep(block, weight, half, us):
    vmem = pl.BlockSpec(memory_space=pltpu.VMEM)
    return pl.pallas_call(
        functools.partial(keep_kernel, half),
        out_shape=(
            jax.ShapeDtypeStruct(block.shape, block.dtype),
            pltpu.VMEM((weight.shape[0] // 2, weight.shape[1]), weight.dtype),
        ),
        in_specs=[vmem, pl.BlockSpec(memory_space=pltpu.HBM)],
        out_specs=(vmem, vmem),
        scratch_shapes=[pltpu.SemaphoreType.DMA],
        compiler_params=pltpu.CompilerParams(vmem_limit_bytes=4 * 1024 * 1024),
        cost_estimate=hint(us),
    )(block, far(weight))


def output(me, attended, inputs, weight, n):
    kept = []

    def aside(half, block):
        block, part = keep(block, weight, half, 2)
        kept.append(near(part))
        return block

    mine, other = gather_blocks(
        attended, n, functools.partial(aside, 0), functools.partial(aside, 1)
    )
    half, heads, width = mine.shape
    vmem = pl.BlockSpec(memory_space=pltpu.VMEM)
    return pl.pallas_call(
        functools.partial(output_kernel, n),
        out_shape=jax.ShapeDtypeStruct(inputs.shape, BF16),
        in_specs=[pl.BlockSpec(memory_space=pltpu.SMEM)] + [vmem] * 5,
        out_specs=vmem,
        scratch_shapes=[pltpu.VMEM((width // 128, n * heads, 128), F32)],
        compiler_params=pltpu.CompilerParams(vmem_limit_bytes=VMEM_LIMIT),
    )(me, mine, other, inputs, *kept)


def angles(positions, steps):
    half = HD // 2
    frequency = jnp.exp(-math.log(ROPE_BASE) * 2.0 * jnp.arange(half, dtype=F32) / HD)
    places = (positions + jnp.arange(steps, dtype=jnp.int32)).astype(F32)
    turns = places[:, None] * frequency[None, :]
    cosine, sine = jnp.cos(turns), jnp.sin(turns)
    cos = jnp.concatenate([cosine, cosine], axis=-1)
    sin = jnp.concatenate([-sine, sine], axis=-1)
    return cos[:, None, :], sin[:, None, :]


def local(
    n, inputs, norm_gain, qkv_weight, head_lambda, head_gain, out_weight,
    key_one_pages, key_two_pages, value_pages, page_table, context_len, positions,
):
    steps, rows, part = inputs.shape
    me = lax.axis_index("gx").astype(jnp.int32).reshape(1)
    block = inputs.reshape(steps * rows, part)
    capacity = page_table.shape[1] * key_one_pages.shape[1]
    small = (page_table, head_lambda.reshape(1, H), head_gain.reshape(1, H * 2 * HD))
    sent, aside = project(
        me, block, norm_gain.reshape(n, 1, part), qkv_weight, n, (positions, context_len), small,
        capacity,
    )
    received = lax.all_to_all(sent, "gx", 0, 0)
    attended = attend(received, *aside, key_one_pages, key_two_pages, value_pages)
    return output(me, attended, inputs, out_weight, n)


def rotary(vectors, cos, sin):
    return vectors * cos + jnp.roll(vectors, HD // 2, axis=-1) * sin


def local_any(
    n, inputs, norm_gain, qkv_weight, head_lambda, head_gain, out_weight,
    key_one_pages, key_two_pages, value_pages, page_table, context_len, positions,
):
    steps = inputs.shape[0]
    own = page_table.shape[0]
    capacity = page_table.shape[1] * key_one_pages.shape[1]
    values = lax.all_gather(inputs, "gx", axis=2, tiled=True).astype(F32)
    factor = lax.rsqrt(jnp.mean(values * values, axis=-1, keepdims=True) + EPS)
    normed = (values * factor * norm_gain).astype(BF16)
    projected = jnp.einsum("sbd,dc->sbc", normed, qkv_weight, preferred_element_type=F32)
    received = lax.all_to_all(
        projected.astype(BF16), "gx", split_axis=1, concat_axis=2, tiled=True
    )
    cached = tuple(
        pool[page_table].reshape(own, capacity, H, -1)
        for pool in (key_one_pages, key_two_pages, value_pages)
    )
    both = received[..., : 4 * H * HD].reshape(steps, own, 4, H, HD).astype(F32)
    new_values = received[..., 4 * H * HD :].reshape(steps, own, H, 2 * HD)
    cos, sin = jax.vmap(lambda p: angles(p, steps))(positions.reshape(own, 1))
    cos, sin = (jnp.moveaxis(x, 0, 1)[:, :, None] for x in (cos, sin))
    turned = rotary(both, cos, sin).astype(BF16)
    place = jnp.arange(capacity, dtype=jnp.int32)
    allowed = (place[None, :] < context_len[:, None])[None, :, None, :]
    step = jnp.arange(steps)
    newer_allowed = (step[None, :] <= step[:, None])[:, None, None, :]

    def softmax_map(query, keys, news):
        older = jnp.einsum("tshd,sjhd->tshj", query, keys, preferred_element_type=F32)
        newer = jnp.einsum("tshd,eshd->tshe", query, news, preferred_element_type=F32)
        scores = jnp.concatenate(
            [jnp.where(allowed, older, -jnp.inf), jnp.where(newer_allowed, newer, -jnp.inf)], axis=-1
        )
        return jax.nn.softmax(scores * (1.0 / math.sqrt(HD)), axis=-1)

    first = softmax_map(turned[:, :, 0], cached[0], turned[:, :, 2])
    second = softmax_map(turned[:, :, 1], cached[1], turned[:, :, 3])
    mix = (first - head_lambda[:, None] * second).astype(BF16)
    mixed = jnp.einsum(
        "tshj,sjhf->tshf", mix[..., :capacity], cached[2], preferred_element_type=F32
    ) + jnp.einsum("tshe,eshf->tshf", mix[..., capacity:], new_values, preferred_element_type=F32)
    norm = lax.rsqrt(jnp.mean(mixed * mixed, axis=-1, keepdims=True) + EPS)
    grouped = (mixed * norm * head_gain.reshape(H, 2 * HD)).astype(BF16)
    whole = lax.all_gather(grouped.reshape(steps, own, -1), "gx", axis=1, tiled=True)
    branch = jnp.einsum("sbf,fd->sbd", whole, out_weight, preferred_element_type=F32)
    return (inputs.astype(F32) + branch).astype(BF16)


def solution(mesh):
    n = mesh.shape["gx"]
    placed = (
        P(None, "groups", "gx"),
        P(),
        P(None, "gx"),
        P(),
        P(),
        P(None, "gx"),
        P(("groups", "gx"), None, None),
        P(("groups", "gx"), None, None),
        P(("groups", "gx"), None, None),
        P(("groups", "gx"), None),
        P(("groups", "gx")),
        P(("groups", "gx")),
    )

    def chosen(inputs, norm_gain, qkv_weight, *rest):
        aligned = inputs.shape[2] % 128 == 0 and qkv_weight.shape[1] % 128 == 0
        single = rest[6].shape[0] == 1
        power = n >= 4 and n & (n - 1) == 0
        body = local if aligned and single and power else local_any
        return body(n, inputs, norm_gain, qkv_weight, *rest)

    return jax.shard_map(
        chosen, mesh=mesh, in_specs=placed, out_specs=P(None, "groups", "gx"), check_vma=False
    )
```

```python
import functools
import math

import jax
import jax.numpy as jnp
from jax import lax
from jax.experimental import pallas as pl
from jax.experimental.pallas import tpu as pltpu
from jax.sharding import PartitionSpec as P

H = 24
HD = 128
EPS = 1e-05
ROPE_BASE = 10000.0
F32 = jnp.float32
BF16 = jnp.bfloat16
VMEM_LIMIT = 16 * 1024 * 1024


def radices(n):
    rest = n // 2
    middle = 1
    while middle * middle * 4 <= rest:
        middle *= 2
    return rest // middle, middle


def swap(block, n, mask):
    return lax.ppermute(block, "gx", [(i, i ^ mask) for i in range(n)])


def gather_blocks(block, n, first_aside, second_aside):
    outer, middle = radices(n)
    arrived = [swap(block, n, o * 2 * middle) for o in range(1, outer)]
    rows = jnp.stack([first_aside(block)] + arrived)
    others = [swap(rows, n, m * 2) for m in range(1, middle)]
    rows, others = lax.optimization_barrier((second_aside(rows), others))
    mine = jnp.concatenate([rows] + others)
    return mine, swap(mine, n, 1)


def owner(me, entry, core, n):
    outer, middle = radices(n)
    mask = (entry % outer) * (2 * middle) + (entry // outer) * 2 + core
    return jnp.bitwise_xor(me, mask)


def far(x):
    return pltpu.with_memory_space_constraint(x, pltpu.HBM)


def hint(us):
    return pl.CostEstimate(flops=0, bytes_accessed=int(us * 3_000_000), transcendentals=0)


def fetches(n, first, count, cores, me, from_ref, to_ref, sems):
    part = from_ref.shape[0] // n
    copies = []
    for index, core in enumerate(cores):
        for entry in range(count):
            slot = index * count + entry
            start = pl.multiple_of(owner(me, first + entry, core, n) * part, part)
            copies.append(
                pltpu.make_async_copy(
                    from_ref.at[pl.ds(start, part), :],
                    to_ref.at[slot],
                    sems.at[slot],
                )
            )
    return copies


def slots(n):
    return [(entry, core) for core in range(2) for entry in range(n // 2)]


def fetches(n, order, me, from_ref, to_ref, sems):
    part = from_ref.shape[0] // n
    copies = []
    for slot, (entry, core) in enumerate(order):
        start = pl.multiple_of(owner(me, entry, core, n) * part, part)
        copies.append(
            pltpu.make_async_copy(
                from_ref.at[pl.ds(start, part), :], to_ref.at[slot], sems.at[slot]
            )
        )
    return copies


def fetch_kernel(n, order, *rest):
    (
        me_ref, block_ref, gain_ref, weight_ref, table_ref, lambda_ref, head_gain_ref,
        held, gain_out, weight_out, place_ref, lambda_out, head_gain_out,
        table, row_ref, wide_ref, sems, other_sems,
    ) = rest
    small = [
        pltpu.make_async_copy(start, end, other_sems.at[index])
        for index, (start, end) in enumerate(
            (
                (table_ref, table),
                (lambda_ref, row_ref),
                (head_gain_ref, wide_ref),
                (block_ref, held),
                (gain_ref, gain_out),
            )
        )
    ]
    large = fetches(n, order, me_ref[0], weight_ref, weight_out, sems)
    for copy in small + large:
        copy.start()
    for copy in small:
        copy.wait()

    capacity = place_ref.shape[1]
    pages = table_ref.shape[1]
    page = capacity // pages
    row = lax.broadcasted_iota(jnp.int32, (1, capacity), 1)
    place = jnp.zeros((1, capacity), jnp.int32)
    for index in range(pages):
        first = table[0, index] * page
        inside = (row >= first) & (row < first + page)
        place = jnp.where(inside, row - first + index * page, place)
    place_ref[...] = place
    across = lax.broadcasted_iota(jnp.int32, (H, H), 1) == lax.broadcasted_iota(jnp.int32, (H, H), 0)
    lambda_out[...] = jnp.sum(jnp.where(across, row_ref[...], 0.0), axis=1, keepdims=True)
    for h in range(H):
        head_gain_out[h : h + 1, :] = wide_ref[:, h * 2 * HD : (h + 1) * 2 * HD]

    for copy in large:
        copy.wait()


def fetch(me, block, gain, weight, n, order, small, capacity):
    part, columns = weight.shape[0] // n, weight.shape[1]
    vmem = pl.BlockSpec(memory_space=pltpu.VMEM)
    hbm = pl.BlockSpec(memory_space=pltpu.HBM)
    table, weights, head_gain = small
    return pl.pallas_call(
        functools.partial(fetch_kernel, n, order),
        out_shape=(
            pltpu.VMEM(block.shape, BF16),
            pltpu.VMEM(gain.shape, F32),
            pltpu.VMEM((len(order), part, columns), BF16),
            jax.ShapeDtypeStruct((1, capacity), jnp.int32),
            jax.ShapeDtypeStruct((H, 1), F32),
            jax.ShapeDtypeStruct((H, 2 * HD), F32),
        ),
        in_specs=[pl.BlockSpec(memory_space=pltpu.SMEM)] + [hbm] * 6,
        out_specs=(vmem,) * 6,
        scratch_shapes=[
            pltpu.SMEM(table.shape, table.dtype),
            pltpu.VMEM(weights.shape, F32),
            pltpu.VMEM(head_gain.shape, F32),
            pltpu.SemaphoreType.DMA((len(order),)),
            pltpu.SemaphoreType.DMA((5,)),
        ],
        compiler_params=pltpu.CompilerParams(vmem_limit_bytes=4 * 1024 * 1024),
        cost_estimate=hint(5),
    )(me, far(block), far(gain), far(weight), *map(far, small))


def near(x):
    return pltpu.with_memory_space_constraint(x, pltpu.VMEM)


def add_squares(refs, square):
    for ref in refs:
        for entry in range(ref.shape[0]):
            values = ref[entry].astype(F32)
            square = square + values * values
    return square


def squares_kernel(n, order, count, me_ref, weight_ref, *rest):
    blocks, (squares, weight_out, sems) = rest[:count], rest[count:]
    copies = fetches(n, order, me_ref[0], weight_ref, weight_out, sems)
    for copy in copies:
        copy.start()
    squares[...] = add_squares(blocks, jnp.zeros(squares.shape, F32))
    for copy in copies:
        copy.wait()


def squares_beside(me, weight, blocks, n, order):
    part, columns = weight.shape[0] // n, weight.shape[1]
    vmem = pl.BlockSpec(memory_space=pltpu.VMEM)
    return pl.pallas_call(
        functools.partial(squares_kernel, n, order, len(blocks)),
        out_shape=(
            jax.ShapeDtypeStruct(blocks[0].shape[1:], F32),
            pltpu.VMEM((len(order), part, columns), BF16),
        ),
        in_specs=[
            pl.BlockSpec(memory_space=pltpu.SMEM),
            pl.BlockSpec(memory_space=pltpu.HBM),
        ]
        + [vmem] * len(blocks),
        out_specs=(vmem, vmem),
        scratch_shapes=[pltpu.SemaphoreType.DMA((len(order),))],
        compiler_params=pltpu.CompilerParams(vmem_limit_bytes=4 * 1024 * 1024),
        cost_estimate=hint(len(order) * 0.7),
    )(me, far(weight), *blocks)


def more_squares_kernel(positions_ref, length_ref, place_ref, before, *rest):
    *blocks, squares, cos_ref, sin_ref, allowed_ref = rest
    squares[...] = add_squares(blocks, before[...])
    steps = cos_ref.shape[0]
    lane = lax.broadcasted_iota(jnp.int32, (8, HD), 1)
    step = lax.broadcasted_iota(jnp.int32, (8, HD), 0)
    pair = lax.rem(lane, HD // 2).astype(F32)
    frequency = jnp.exp(-math.log(ROPE_BASE) * 2.0 * pair / HD)
    turns = (positions_ref[0] + step).astype(F32) * frequency
    cos = jnp.cos(turns)
    sin = jnp.where(lane < HD // 2, -1.0, 1.0) * jnp.sin(turns)
    for index in range(steps):
        cos_ref[index] = cos[index : index + 1]
        sin_ref[index] = sin[index : index + 1]
    allowed_ref[...] = jnp.where(place_ref[...] < length_ref[0], 1.0, 0.0)


def more_squares(blocks, before, positions, length, place, steps):
    vmem = pl.BlockSpec(memory_space=pltpu.VMEM)
    smem = pl.BlockSpec(memory_space=pltpu.SMEM)
    turns = jax.ShapeDtypeStruct((steps, 1, HD), F32)
    return pl.pallas_call(
        more_squares_kernel,
        out_shape=(
            jax.ShapeDtypeStruct(before.shape, F32),
            turns,
            turns,
            jax.ShapeDtypeStruct(place.shape, F32),
        ),
        in_specs=[smem, smem] + [vmem] * (len(blocks) + 2),
        out_specs=(vmem,) * 4,
        compiler_params=pltpu.CompilerParams(vmem_limit_bytes=4 * 1024 * 1024),
        cost_estimate=hint(1),
    )(positions, length, place, before, *blocks)


def project_kernel(n, order, me_ref, gain_ref, before_ref, mine_ref, other_ref, weight_ref, *rest):
    *helds, out_ref, last, spread, total, kept, sems = rest
    me = me_ref[0]
    rows, part = before_ref.shape
    copies = fetches(n, order, me, weight_ref, last, sems)
    for copy in copies:
        copy.start()
    places = [(held, slot) for held in helds for slot in range(held.shape[0])]
    early = len(places)
    places += [(last, slot) for slot in range(len(order))]
    blocks = list(zip(slots(n), places, strict=True))

    def products(picked, factor):
        summed = None
        for (entry, core), (held, slot) in picked:
            values = (mine_ref, other_ref)[core][entry].astype(F32)
            normed = (values * factor * gain_ref[owner(me, entry, core, n)]).astype(BF16)
            product = jnp.dot(normed, held[slot], preferred_element_type=F32)
            summed = product if summed is None else summed + product
        return summed

    def row_factor():
        square = add_squares([other_ref], before_ref[...])
        mean = jnp.sum(square, axis=1, keepdims=True) * (1.0 / (n * part))
        return lax.rsqrt(mean + EPS)

    @pl.when(me >= 0)
    def _():
        factor = row_factor()
        total[...] = products(blocks[:early], factor)
        kept[...] = jnp.broadcast_to(factor, kept.shape)

    for copy in copies:
        copy.wait()
    factor = kept[:, :1]
    summed = total[...] + products(blocks[early:], factor)
    columns = summed.shape[1] // 128
    steps = rows // n
    for block in range(columns):
        for step in range(steps):
            spread[:, step * columns + block, :] = summed[
                step * n : (step + 1) * n, block * 128 : (block + 1) * 128
            ]
    for target in range(n):
        out_ref[target] = spread[target, : steps * columns, :].astype(BF16)


def project(me, block, gain, weight, n, scalars, small, capacity):
    rows, part = block.shape
    columns = weight.shape[1]
    pieces = rows // n * (columns // 128)
    outer, middle = radices(n)
    order = slots(n)
    first, second = 5 * n // 16, 3 * n // 4

    arrived = [swap(block, n, o * 2 * middle) for o in range(1, outer)]
    held, gain, weight_a, place, weights, head_gain = fetch(
        me, block, gain, weight, n, order[:first], small, capacity
    )
    row = jnp.stack([held] + arrived)
    later = [swap(row, n, m * 2) for m in range(1, middle)]
    squares, weight_b = squares_beside(me, weight, [row], n, order[first:second])
    later, squares = lax.optimization_barrier((later, squares))
    mine = jnp.concatenate([row] + later)
    other = swap(mine, n, 1)
    squares, cos, sin, allowed = more_squares(later, squares, *scalars, place, rows // n)
    vmem = pl.BlockSpec(memory_space=pltpu.VMEM)
    hbm = pl.BlockSpec(memory_space=pltpu.HBM)
    sent = pl.pallas_call(
        functools.partial(project_kernel, n, order[second:]),
        out_shape=jax.ShapeDtypeStruct((n, pieces, 128), BF16),
        in_specs=[pl.BlockSpec(memory_space=pltpu.SMEM)] + [vmem] * 4 + [hbm] + [vmem] * 2,
        out_specs=vmem,
        scratch_shapes=[
            pltpu.VMEM((n - second, part, columns), BF16),
            pltpu.VMEM((n, -(-pieces // 8) * 8, 128), F32),
            pltpu.VMEM((rows, columns), F32),
            pltpu.VMEM((rows, 128), F32),
            pltpu.SemaphoreType.DMA((n - second,)),
        ],
        compiler_params=pltpu.CompilerParams(vmem_limit_bytes=VMEM_LIMIT),
        cost_estimate=hint(6),
    )(me, gain, squares, mine, other, far(weight), near(weight_a), near(weight_b))
    return sent, (cos, sin, allowed, weights, head_gain)


def attend_kernel(
    received_ref, cos_ref, sin_ref, allowed_ref, lambda_ref, gain_ref,
    keys_one_ref, keys_two_ref, values_ref, out_ref, fresh,
):
    sources, pieces, _ = received_ref.shape
    steps = cos_ref.shape[0]
    blocks = pieces // steps
    pages, page, _ = keys_one_ref.shape
    capacity = pages * page
    for source in range(sources):
        piece = received_ref[source].astype(F32)
        for step in range(steps):
            fresh[step, source * blocks : (source + 1) * blocks, :] = piece[
                step * blocks : (step + 1) * blocks
            ]

    def heads(step, kind):
        return fresh[step, kind * H : (kind + 1) * H, :]

    def rotated(step, kind):
        values = heads(step, kind)
        turned = values * cos_ref[step] + pltpu.roll(values, HD // 2, 1) * sin_ref[step]
        return turned.astype(BF16).astype(F32)

    allowed = allowed_ref[...] > 0.0
    scale = 1.0 / math.sqrt(HD)
    head_row = lax.rem(lax.broadcasted_iota(jnp.int32, (steps * H, HD), 0), H)

    def softmax_map(kind, keys_ref):
        queries = [rotated(step, kind) for step in range(steps)]
        news = [rotated(step, kind + 2) for step in range(steps)]
        stacked = jnp.concatenate(queries, axis=0)
        apart = jnp.concatenate(
            [jnp.where(head_row == h, stacked, 0.0).astype(BF16) for h in range(H)], axis=1
        )
        older = lax.dot_general(
            apart, keys_ref[...].reshape(capacity, H * HD), (((1,), (1,)), ((), ())),
            preferred_element_type=F32,
        )
        older = jnp.where(allowed, older * scale, -1e38)
        parts = []
        for step in range(steps):
            cached = older[step * H : (step + 1) * H]
            newer = [
                jnp.sum(queries[step] * news[e], axis=1, keepdims=True) * scale
                for e in range(step + 1)
            ]
            top = jnp.max(cached, axis=1, keepdims=True)
            for value in newer:
                top = jnp.maximum(top, value)
            cached = jnp.exp(cached - top)
            newer = [jnp.exp(value - top) for value in newer]
            whole = jnp.sum(cached, axis=1, keepdims=True)
            for value in newer:
                whole = whole + value
            parts.append((cached / whole, [value / whole for value in newer]))
        return parts

    first = softmax_map(0, keys_one_ref)
    second = softmax_map(1, keys_two_ref)
    weight = lambda_ref[...]
    mix = jnp.concatenate(
        [first[step][0] - weight * second[step][0] for step in range(steps)], axis=0
    ).astype(BF16)
    spread = jnp.dot(mix, values_ref[...].reshape(capacity, -1), preferred_element_type=F32)
    wide_row = lax.broadcasted_iota(jnp.int32, (H, 2 * HD), 0)
    fresh_values = [
        jnp.concatenate(
            [fresh[e, pl.ds(4 * H + half, H, stride=2), :] for half in range(2)], axis=1
        )
        for e in range(steps)
    ]
    for step in range(steps):
        mixed = jnp.zeros((H, 2 * HD), F32)
        for h in range(H):
            block = spread[step * H : (step + 1) * H, h * 2 * HD : (h + 1) * 2 * HD]
            mixed = jnp.where(wide_row == h, block, mixed)
        for e in range(step + 1):
            share = first[step][1][e] - weight * second[step][1][e]
            mixed = mixed + share.astype(BF16).astype(F32) * fresh_values[e]
        norm = lax.rsqrt(jnp.mean(mixed * mixed, axis=1, keepdims=True) + EPS)
        out_ref[step * H : (step + 1) * H, :] = (mixed * norm * gain_ref[...]).astype(BF16)


def attend(received, cos, sin, allowed, weights, gain, keys_one, keys_two, values):
    steps = cos.shape[0]
    sources, pieces, _ = received.shape
    vmem = pl.BlockSpec(memory_space=pltpu.VMEM)
    held = [near(x) for x in (keys_one, keys_two, values)]
    return pl.pallas_call(
        attend_kernel,
        out_shape=jax.ShapeDtypeStruct((steps * H, 2 * HD), BF16),
        in_specs=[vmem] * 9,
        out_specs=vmem,
        scratch_shapes=[pltpu.VMEM((steps, sources * (pieces // steps), 128), F32)],
        compiler_params=pltpu.CompilerParams(vmem_limit_bytes=VMEM_LIMIT),
        cost_estimate=hint(10),
    )(received, cos, sin, allowed, weights, gain, *held)


def output_kernel(n, me_ref, mine_ref, other_ref, inputs_ref, *rest):
    *weights, out_ref, rows_ref = rest
    me = me_ref[0]
    half, heads, width = mine_ref.shape
    steps = heads // H
    lanes = width // 128
    for entry in range(half):
        for core, ref in ((0, mine_ref), (1, other_ref)):
            start = pl.multiple_of(owner(me, entry, core, n) * heads, 8)
            block = ref[entry].astype(F32)
            for lane in range(lanes):
                rows_ref[lane, pl.ds(start, heads), :] = block[:, lane * 128 : (lane + 1) * 128]
    total = None
    for h in range(H):
        left = jnp.concatenate(
            [
                jnp.concatenate(
                    [rows_ref[lane, pl.ds(step * H + h, n, stride=heads), :] for lane in range(lanes)],
                    axis=1,
                )
                for step in range(steps)
            ],
            axis=0,
        ).astype(BF16)
        held = weights[h * len(weights) // H]
        at = h * width % held.shape[0]
        product = jnp.dot(left, held[at : at + width, :], preferred_element_type=F32)
        total = product if total is None else total + product
    for step in range(steps):
        out_ref[step] = (
            inputs_ref[step].astype(F32) + total[step * n : (step + 1) * n]
        ).astype(BF16)


def keep_kernel(half, block_ref, from_ref, held, to_ref, sem):
    rows = to_ref.shape[0]
    copy = pltpu.make_async_copy(from_ref.at[pl.ds(half * rows, rows), :], to_ref, sem)
    copy.start()
    held[...] = block_ref[...]
    copy.wait()


def keep(block, weight, half, us):
    vmem = pl.BlockSpec(memory_space=pltpu.VMEM)
    return pl.pallas_call(
        functools.partial(keep_kernel, half),
        out_shape=(
            jax.ShapeDtypeStruct(block.shape, block.dtype),
            pltpu.VMEM((weight.shape[0] // 2, weight.shape[1]), weight.dtype),
        ),
        in_specs=[vmem, pl.BlockSpec(memory_space=pltpu.HBM)],
        out_specs=(vmem, vmem),
        scratch_shapes=[pltpu.SemaphoreType.DMA],
        compiler_params=pltpu.CompilerParams(vmem_limit_bytes=4 * 1024 * 1024),
        cost_estimate=hint(us),
    )(block, far(weight))


def output(me, attended, inputs, weight, n):
    kept = []

    def aside(half, block):
        block, part = keep(block, weight, half, 2)
        kept.append(near(part))
        return block

    mine, other = gather_blocks(
        attended, n, functools.partial(aside, 0), functools.partial(aside, 1)
    )
    half, heads, width = mine.shape
    vmem = pl.BlockSpec(memory_space=pltpu.VMEM)
    return pl.pallas_call(
        functools.partial(output_kernel, n),
        out_shape=jax.ShapeDtypeStruct(inputs.shape, BF16),
        in_specs=[pl.BlockSpec(memory_space=pltpu.SMEM)] + [vmem] * 5,
        out_specs=vmem,
        scratch_shapes=[pltpu.VMEM((width // 128, n * heads, 128), F32)],
        compiler_params=pltpu.CompilerParams(vmem_limit_bytes=VMEM_LIMIT),
    )(me, mine, other, inputs, *kept)


def angles(positions, steps):
    half = HD // 2
    frequency = jnp.exp(-math.log(ROPE_BASE) * 2.0 * jnp.arange(half, dtype=F32) / HD)
    places = (positions + jnp.arange(steps, dtype=jnp.int32)).astype(F32)
    turns = places[:, None] * frequency[None, :]
    cosine, sine = jnp.cos(turns), jnp.sin(turns)
    cos = jnp.concatenate([cosine, cosine], axis=-1)
    sin = jnp.concatenate([-sine, sine], axis=-1)
    return cos[:, None, :], sin[:, None, :]


def local(
    n, inputs, norm_gain, qkv_weight, head_lambda, head_gain, out_weight,
    key_one_pages, key_two_pages, value_pages, page_table, context_len, positions,
):
    steps, rows, part = inputs.shape
    me = lax.axis_index("gx").astype(jnp.int32).reshape(1)
    block = inputs.reshape(steps * rows, part)
    capacity = page_table.shape[1] * key_one_pages.shape[1]
    small = (page_table, head_lambda.reshape(1, H), head_gain.reshape(1, H * 2 * HD))
    sent, aside = project(
        me, block, norm_gain.reshape(n, 1, part), qkv_weight, n, (positions, context_len), small,
        capacity,
    )
    received = lax.all_to_all(sent, "gx", 0, 0)
    attended = attend(received, *aside, key_one_pages, key_two_pages, value_pages)
    return output(me, attended, inputs, out_weight, n)


def rotary(vectors, cos, sin):
    return vectors * cos + jnp.roll(vectors, HD // 2, axis=-1) * sin


def local_any(
    n, inputs, norm_gain, qkv_weight, head_lambda, head_gain, out_weight,
    key_one_pages, key_two_pages, value_pages, page_table, context_len, positions,
):
    steps = inputs.shape[0]
    own = page_table.shape[0]
    capacity = page_table.shape[1] * key_one_pages.shape[1]
    values = lax.all_gather(inputs, "gx", axis=2, tiled=True).astype(F32)
    factor = lax.rsqrt(jnp.mean(values * values, axis=-1, keepdims=True) + EPS)
    normed = (values * factor * norm_gain).astype(BF16)
    projected = jnp.einsum("sbd,dc->sbc", normed, qkv_weight, preferred_element_type=F32)
    received = lax.all_to_all(
        projected.astype(BF16), "gx", split_axis=1, concat_axis=2, tiled=True
    )
    cached = tuple(
        pool[page_table].reshape(own, capacity, H, -1)
        for pool in (key_one_pages, key_two_pages, value_pages)
    )
    both = received[..., : 4 * H * HD].reshape(steps, own, 4, H, HD).astype(F32)
    new_values = received[..., 4 * H * HD :].reshape(steps, own, H, 2 * HD)
    cos, sin = jax.vmap(lambda p: angles(p, steps))(positions.reshape(own, 1))
    cos, sin = (jnp.moveaxis(x, 0, 1)[:, :, None] for x in (cos, sin))
    turned = rotary(both, cos, sin).astype(BF16)
    place = jnp.arange(capacity, dtype=jnp.int32)
    allowed = (place[None, :] < context_len[:, None])[None, :, None, :]
    step = jnp.arange(steps)
    newer_allowed = (step[None, :] <= step[:, None])[:, None, None, :]

    def softmax_map(query, keys, news):
        older = jnp.einsum("tshd,sjhd->tshj", query, keys, preferred_element_type=F32)
        newer = jnp.einsum("tshd,eshd->tshe", query, news, preferred_element_type=F32)
        scores = jnp.concatenate(
            [jnp.where(allowed, older, -jnp.inf), jnp.where(newer_allowed, newer, -jnp.inf)], axis=-1
        )
        return jax.nn.softmax(scores * (1.0 / math.sqrt(HD)), axis=-1)

    first = softmax_map(turned[:, :, 0], cached[0], turned[:, :, 2])
    second = softmax_map(turned[:, :, 1], cached[1], turned[:, :, 3])
    mix = (first - head_lambda[:, None] * second).astype(BF16)
    mixed = jnp.einsum(
        "tshj,sjhf->tshf", mix[..., :capacity], cached[2], preferred_element_type=F32
    ) + jnp.einsum("tshe,eshf->tshf", mix[..., capacity:], new_values, preferred_element_type=F32)
    norm = lax.rsqrt(jnp.mean(mixed * mixed, axis=-1, keepdims=True) + EPS)
    grouped = (mixed * norm * head_gain.reshape(H, 2 * HD)).astype(BF16)
    whole = lax.all_gather(grouped.reshape(steps, own, -1), "gx", axis=1, tiled=True)
    branch = jnp.einsum("sbf,fd->sbd", whole, out_weight, preferred_element_type=F32)
    return (inputs.astype(F32) + branch).astype(BF16)


def solution(mesh):
    n = mesh.shape["gx"]
    placed = (
        P(None, "groups", "gx"),
        P(),
        P(None, "gx"),
        P(),
        P(),
        P(None, "gx"),
        P(("groups", "gx"), None, None),
        P(("groups", "gx"), None, None),
        P(("groups", "gx"), None, None),
        P(("groups", "gx"), None),
        P(("groups", "gx")),
        P(("groups", "gx")),
    )

    def chosen(inputs, norm_gain, qkv_weight, *rest):
        aligned = inputs.shape[2] % 128 == 0 and qkv_weight.shape[1] % 128 == 0
        single = rest[6].shape[0] == 1
        power = n >= 4 and n & (n - 1) == 0
        body = local if aligned and single and power else local_any
        return body(n, inputs, norm_gain, qkv_weight, *rest)

    return jax.shard_map(
        chosen, mesh=mesh, in_specs=placed, out_specs=P(None, "groups", "gx"), check_vma=False
    )
```

```python
import functools
import math

import jax
import jax.numpy as jnp
from jax import lax
from jax.experimental import pallas as pl
from jax.experimental.pallas import tpu as pltpu
from jax.sharding import PartitionSpec as P

H = 24
HD = 128
EPS = 1e-05
ROPE_BASE = 10000.0
F32 = jnp.float32
BF16 = jnp.bfloat16
VMEM_LIMIT = 16 * 1024 * 1024


def radices(n):
    rest = n // 2
    middle = 1
    while middle * middle * 4 <= rest:
        middle *= 2
    return rest // middle, middle


def swap(block, n, mask):
    return lax.ppermute(block, "gx", [(i, i ^ mask) for i in range(n)])


def gather_blocks(block, n, first_aside, second_aside):
    outer, middle = radices(n)
    arrived = [swap(block, n, o * 2 * middle) for o in range(1, outer)]
    rows = jnp.stack([first_aside(block)] + arrived)
    others = [swap(rows, n, m * 2) for m in range(1, middle)]
    rows, others = lax.optimization_barrier((second_aside(rows), others))
    mine = jnp.concatenate([rows] + others)
    return mine, swap(mine, n, 1)


def owner(me, entry, core, n, far_first=False):
    outer, middle = radices(n)
    place = entry % outer
    if far_first:
        place = (outer - place) % outer
    mask = place * (2 * middle) + (entry // outer) * 2 + core
    return jnp.bitwise_xor(me, mask)


def far(x):
    return pltpu.with_memory_space_constraint(x, pltpu.HBM)


def hint(us):
    return pl.CostEstimate(flops=0, bytes_accessed=int(us * 3_000_000), transcendentals=0)


def fetches(n, first, count, cores, me, from_ref, to_ref, sems):
    part = from_ref.shape[0] // n
    copies = []
    for index, core in enumerate(cores):
        for entry in range(count):
            slot = index * count + entry
            start = pl.multiple_of(owner(me, first + entry, core, n) * part, part)
            copies.append(
                pltpu.make_async_copy(
                    from_ref.at[pl.ds(start, part), :],
                    to_ref.at[slot],
                    sems.at[slot],
                )
            )
    return copies


def slots(n):
    return [(entry, core) for core in range(2) for entry in range(n // 2)]


def fetches(n, order, me, from_ref, to_ref, sems):
    part = from_ref.shape[0] // n
    copies = []
    for slot, (entry, core) in enumerate(order):
        start = pl.multiple_of(owner(me, entry, core, n, True) * part, part)
        copies.append(
            pltpu.make_async_copy(
                from_ref.at[pl.ds(start, part), :], to_ref.at[slot], sems.at[slot]
            )
        )
    return copies


def fetch_kernel(n, order, *rest):
    (
        me_ref, block_ref, gain_ref, weight_ref, table_ref, lambda_ref, head_gain_ref,
        held, gain_out, weight_out, place_ref, lambda_out, head_gain_out,
        table, row_ref, wide_ref, sems, other_sems,
    ) = rest
    small = [
        pltpu.make_async_copy(start, end, other_sems.at[index])
        for index, (start, end) in enumerate(
            (
                (table_ref, table),
                (lambda_ref, row_ref),
                (head_gain_ref, wide_ref),
                (block_ref, held),
                (gain_ref, gain_out),
            )
        )
    ]
    large = fetches(n, order, me_ref[0], weight_ref, weight_out, sems)
    for copy in small + large:
        copy.start()
    for copy in small:
        copy.wait()

    capacity = place_ref.shape[1]
    pages = table_ref.shape[1]
    page = capacity // pages
    row = lax.broadcasted_iota(jnp.int32, (1, capacity), 1)
    place = jnp.zeros((1, capacity), jnp.int32)
    for index in range(pages):
        first = table[0, index] * page
        inside = (row >= first) & (row < first + page)
        place = jnp.where(inside, row - first + index * page, place)
    place_ref[...] = place
    across = lax.broadcasted_iota(jnp.int32, (H, H), 1) == lax.broadcasted_iota(jnp.int32, (H, H), 0)
    lambda_out[...] = jnp.sum(jnp.where(across, row_ref[...], 0.0), axis=1, keepdims=True)
    for h in range(H):
        head_gain_out[h : h + 1, :] = wide_ref[:, h * 2 * HD : (h + 1) * 2 * HD]

    for copy in large:
        copy.wait()


def fetch(me, block, gain, weight, n, order, small, capacity):
    part, columns = weight.shape[0] // n, weight.shape[1]
    vmem = pl.BlockSpec(memory_space=pltpu.VMEM)
    hbm = pl.BlockSpec(memory_space=pltpu.HBM)
    table, weights, head_gain = small
    return pl.pallas_call(
        functools.partial(fetch_kernel, n, order),
        out_shape=(
            pltpu.VMEM(block.shape, BF16),
            pltpu.VMEM(gain.shape, F32),
            pltpu.VMEM((len(order), part, columns), BF16),
            jax.ShapeDtypeStruct((1, capacity), jnp.int32),
            jax.ShapeDtypeStruct((H, 1), F32),
            jax.ShapeDtypeStruct((H, 2 * HD), F32),
        ),
        in_specs=[pl.BlockSpec(memory_space=pltpu.SMEM)] + [hbm] * 6,
        out_specs=(vmem,) * 6,
        scratch_shapes=[
            pltpu.SMEM(table.shape, table.dtype),
            pltpu.VMEM(weights.shape, F32),
            pltpu.VMEM(head_gain.shape, F32),
            pltpu.SemaphoreType.DMA((len(order),)),
            pltpu.SemaphoreType.DMA((5,)),
        ],
        compiler_params=pltpu.CompilerParams(vmem_limit_bytes=4 * 1024 * 1024),
        cost_estimate=hint(5),
    )(me, far(block), far(gain), far(weight), *map(far, small))


def near(x):
    return pltpu.with_memory_space_constraint(x, pltpu.VMEM)


def add_squares(refs, square):
    for ref in refs:
        for entry in range(ref.shape[0]):
            values = ref[entry].astype(F32)
            square = square + values * values
    return square


def squares_kernel(n, order, count, me_ref, weight_ref, *rest):
    blocks, (squares, weight_out, sems) = rest[:count], rest[count:]
    copies = fetches(n, order, me_ref[0], weight_ref, weight_out, sems)
    for copy in copies:
        copy.start()
    squares[...] = add_squares(blocks, jnp.zeros(squares.shape, F32))
    for copy in copies:
        copy.wait()


def squares_beside(me, weight, blocks, n, order):
    part, columns = weight.shape[0] // n, weight.shape[1]
    vmem = pl.BlockSpec(memory_space=pltpu.VMEM)
    return pl.pallas_call(
        functools.partial(squares_kernel, n, order, len(blocks)),
        out_shape=(
            jax.ShapeDtypeStruct(blocks[0].shape[1:], F32),
            pltpu.VMEM((len(order), part, columns), BF16),
        ),
        in_specs=[
            pl.BlockSpec(memory_space=pltpu.SMEM),
            pl.BlockSpec(memory_space=pltpu.HBM),
        ]
        + [vmem] * len(blocks),
        out_specs=(vmem, vmem),
        scratch_shapes=[pltpu.SemaphoreType.DMA((len(order),))],
        compiler_params=pltpu.CompilerParams(vmem_limit_bytes=4 * 1024 * 1024),
        cost_estimate=hint(len(order) * 0.7),
    )(me, far(weight), *blocks)


def more_squares_kernel(positions_ref, length_ref, place_ref, before, *rest):
    *blocks, squares, cos_ref, sin_ref, allowed_ref = rest
    squares[...] = add_squares(blocks, before[...])
    steps = cos_ref.shape[0]
    lane = lax.broadcasted_iota(jnp.int32, (8, HD), 1)
    step = lax.broadcasted_iota(jnp.int32, (8, HD), 0)
    pair = lax.rem(lane, HD // 2).astype(F32)
    frequency = jnp.exp(-math.log(ROPE_BASE) * 2.0 * pair / HD)
    turns = (positions_ref[0] + step).astype(F32) * frequency
    cos = jnp.cos(turns)
    sin = jnp.where(lane < HD // 2, -1.0, 1.0) * jnp.sin(turns)
    for index in range(steps):
        cos_ref[index] = cos[index : index + 1]
        sin_ref[index] = sin[index : index + 1]
    allowed_ref[...] = jnp.where(place_ref[...] < length_ref[0], 1.0, 0.0)


def more_squares(blocks, before, positions, length, place, steps):
    vmem = pl.BlockSpec(memory_space=pltpu.VMEM)
    smem = pl.BlockSpec(memory_space=pltpu.SMEM)
    turns = jax.ShapeDtypeStruct((steps, 1, HD), F32)
    return pl.pallas_call(
        more_squares_kernel,
        out_shape=(
            jax.ShapeDtypeStruct(before.shape, F32),
            turns,
            turns,
            jax.ShapeDtypeStruct(place.shape, F32),
        ),
        in_specs=[smem, smem] + [vmem] * (len(blocks) + 2),
        out_specs=(vmem,) * 4,
        compiler_params=pltpu.CompilerParams(vmem_limit_bytes=4 * 1024 * 1024),
        cost_estimate=hint(1),
    )(positions, length, place, before, *blocks)


def project_kernel(n, order, me_ref, gain_ref, before_ref, mine_ref, other_ref, weight_ref, *rest):
    *helds, out_ref, last, spread, total, kept, sems = rest
    me = me_ref[0]
    rows, part = before_ref.shape
    copies = fetches(n, order, me, weight_ref, last, sems)
    for copy in copies:
        copy.start()
    places = [(held, slot) for held in helds for slot in range(held.shape[0])]
    early = len(places)
    places += [(last, slot) for slot in range(len(order))]
    blocks = list(zip(slots(n), places, strict=True))

    def products(picked, factor):
        summed = None
        for (entry, core), (held, slot) in picked:
            values = (mine_ref, other_ref)[core][entry].astype(F32)
            normed = (values * factor * gain_ref[owner(me, entry, core, n, True)]).astype(BF16)
            product = jnp.dot(normed, held[slot], preferred_element_type=F32)
            summed = product if summed is None else summed + product
        return summed

    def row_factor():
        square = add_squares([other_ref], before_ref[...])
        mean = jnp.sum(square, axis=1, keepdims=True) * (1.0 / (n * part))
        return lax.rsqrt(mean + EPS)

    @pl.when(me >= 0)
    def _():
        factor = row_factor()
        total[...] = products(blocks[:early], factor)
        kept[...] = jnp.broadcast_to(factor, kept.shape)

    for copy in copies:
        copy.wait()
    factor = kept[:, :1]
    summed = total[...] + products(blocks[early:], factor)
    columns = summed.shape[1] // 128
    steps = rows // n
    for block in range(columns):
        for step in range(steps):
            spread[:, step * columns + block, :] = summed[
                step * n : (step + 1) * n, block * 128 : (block + 1) * 128
            ]
    for target in range(n):
        out_ref[target] = spread[target, : steps * columns, :].astype(BF16)


def project(me, block, gain, weight, n, scalars, small, capacity):
    rows, part = block.shape
    columns = weight.shape[1]
    pieces = rows // n * (columns // 128)
    outer, middle = radices(n)
    order = slots(n)
    first, second = 5 * n // 16, 3 * n // 4

    arrived = [swap(block, n, o * 2 * middle) for o in range(outer - 1, 0, -1)]
    held, gain, weight_a, place, weights, head_gain = fetch(
        me, block, gain, weight, n, order[:first], small, capacity
    )
    row = jnp.stack([held] + arrived)
    later = [swap(row, n, m * 2) for m in range(1, middle)]
    squares, weight_b = squares_beside(me, weight, [row], n, order[first:second])
    later, squares = lax.optimization_barrier((later, squares))
    mine = jnp.concatenate([row] + later)
    other = swap(mine, n, 1)
    squares, cos, sin, allowed = more_squares(later, squares, *scalars, place, rows // n)
    vmem = pl.BlockSpec(memory_space=pltpu.VMEM)
    hbm = pl.BlockSpec(memory_space=pltpu.HBM)
    sent = pl.pallas_call(
        functools.partial(project_kernel, n, order[second:]),
        out_shape=jax.ShapeDtypeStruct((n, pieces, 128), BF16),
        in_specs=[pl.BlockSpec(memory_space=pltpu.SMEM)] + [vmem] * 4 + [hbm] + [vmem] * 2,
        out_specs=vmem,
        scratch_shapes=[
            pltpu.VMEM((n - second, part, columns), BF16),
            pltpu.VMEM((n, -(-pieces // 8) * 8, 128), F32),
            pltpu.VMEM((rows, columns), F32),
            pltpu.VMEM((rows, 128), F32),
            pltpu.SemaphoreType.DMA((n - second,)),
        ],
        compiler_params=pltpu.CompilerParams(vmem_limit_bytes=VMEM_LIMIT),
        cost_estimate=hint(6),
    )(me, gain, squares, mine, other, far(weight), near(weight_a), near(weight_b))
    return sent, (cos, sin, allowed, weights, head_gain)


def attend_kernel(
    received_ref, cos_ref, sin_ref, allowed_ref, lambda_ref, gain_ref,
    keys_one_ref, keys_two_ref, values_ref, out_ref, fresh,
):
    sources, pieces, _ = received_ref.shape
    steps = cos_ref.shape[0]
    blocks = pieces // steps
    pages, page, _ = keys_one_ref.shape
    capacity = pages * page
    for source in range(sources):
        piece = received_ref[source].astype(F32)
        for step in range(steps):
            fresh[step, source * blocks : (source + 1) * blocks, :] = piece[
                step * blocks : (step + 1) * blocks
            ]

    def heads(step, kind):
        return fresh[step, kind * H : (kind + 1) * H, :]

    def rotated(step, kind):
        values = heads(step, kind)
        turned = values * cos_ref[step] + pltpu.roll(values, HD // 2, 1) * sin_ref[step]
        return turned.astype(BF16).astype(F32)

    allowed = allowed_ref[...] > 0.0
    scale = 1.0 / math.sqrt(HD)
    head_row = lax.rem(lax.broadcasted_iota(jnp.int32, (steps * H, HD), 0), H)

    def softmax_map(kind, keys_ref):
        queries = [rotated(step, kind) for step in range(steps)]
        news = [rotated(step, kind + 2) for step in range(steps)]
        stacked = jnp.concatenate(queries, axis=0)
        apart = jnp.concatenate(
            [jnp.where(head_row == h, stacked, 0.0).astype(BF16) for h in range(H)], axis=1
        )
        older = lax.dot_general(
            apart, keys_ref[...].reshape(capacity, H * HD), (((1,), (1,)), ((), ())),
            preferred_element_type=F32,
        )
        older = jnp.where(allowed, older * scale, -1e38)
        parts = []
        for step in range(steps):
            cached = older[step * H : (step + 1) * H]
            newer = [
                jnp.sum(queries[step] * news[e], axis=1, keepdims=True) * scale
                for e in range(step + 1)
            ]
            top = jnp.max(cached, axis=1, keepdims=True)
            for value in newer:
                top = jnp.maximum(top, value)
            cached = jnp.exp(cached - top)
            newer = [jnp.exp(value - top) for value in newer]
            whole = jnp.sum(cached, axis=1, keepdims=True)
            for value in newer:
                whole = whole + value
            parts.append((cached / whole, [value / whole for value in newer]))
        return parts

    first = softmax_map(0, keys_one_ref)
    second = softmax_map(1, keys_two_ref)
    weight = lambda_ref[...]
    mix = jnp.concatenate(
        [first[step][0] - weight * second[step][0] for step in range(steps)], axis=0
    ).astype(BF16)
    spread = jnp.dot(mix, values_ref[...].reshape(capacity, -1), preferred_element_type=F32)
    wide_row = lax.broadcasted_iota(jnp.int32, (H, 2 * HD), 0)
    fresh_values = [
        jnp.concatenate(
            [fresh[e, pl.ds(4 * H + half, H, stride=2), :] for half in range(2)], axis=1
        )
        for e in range(steps)
    ]
    for step in range(steps):
        mixed = jnp.zeros((H, 2 * HD), F32)
        for h in range(H):
            block = spread[step * H : (step + 1) * H, h * 2 * HD : (h + 1) * 2 * HD]
            mixed = jnp.where(wide_row == h, block, mixed)
        for e in range(step + 1):
            share = first[step][1][e] - weight * second[step][1][e]
            mixed = mixed + share.astype(BF16).astype(F32) * fresh_values[e]
        norm = lax.rsqrt(jnp.mean(mixed * mixed, axis=1, keepdims=True) + EPS)
        out_ref[step * H : (step + 1) * H, :] = (mixed * norm * gain_ref[...]).astype(BF16)


def attend(received, cos, sin, allowed, weights, gain, keys_one, keys_two, values):
    steps = cos.shape[0]
    sources, pieces, _ = received.shape
    vmem = pl.BlockSpec(memory_space=pltpu.VMEM)
    held = [near(x) for x in (keys_one, keys_two, values)]
    return pl.pallas_call(
        attend_kernel,
        out_shape=jax.ShapeDtypeStruct((steps * H, 2 * HD), BF16),
        in_specs=[vmem] * 9,
        out_specs=vmem,
        scratch_shapes=[pltpu.VMEM((steps, sources * (pieces // steps), 128), F32)],
        compiler_params=pltpu.CompilerParams(vmem_limit_bytes=VMEM_LIMIT),
        cost_estimate=hint(10),
    )(received, cos, sin, allowed, weights, gain, *held)


def output_kernel(n, me_ref, mine_ref, other_ref, inputs_ref, *rest):
    *weights, out_ref, rows_ref = rest
    me = me_ref[0]
    half, heads, width = mine_ref.shape
    steps = heads // H
    lanes = width // 128
    for entry in range(half):
        for core, ref in ((0, mine_ref), (1, other_ref)):
            start = pl.multiple_of(owner(me, entry, core, n) * heads, 8)
            block = ref[entry].astype(F32)
            for lane in range(lanes):
                rows_ref[lane, pl.ds(start, heads), :] = block[:, lane * 128 : (lane + 1) * 128]
    total = None
    for h in range(H):
        left = jnp.concatenate(
            [
                jnp.concatenate(
                    [rows_ref[lane, pl.ds(step * H + h, n, stride=heads), :] for lane in range(lanes)],
                    axis=1,
                )
                for step in range(steps)
            ],
            axis=0,
        ).astype(BF16)
        held = weights[h * len(weights) // H]
        at = h * width % held.shape[0]
        product = jnp.dot(left, held[at : at + width, :], preferred_element_type=F32)
        total = product if total is None else total + product
    for step in range(steps):
        out_ref[step] = (
            inputs_ref[step].astype(F32) + total[step * n : (step + 1) * n]
        ).astype(BF16)


def keep_kernel(half, block_ref, from_ref, held, to_ref, sem):
    rows = to_ref.shape[0]
    copy = pltpu.make_async_copy(from_ref.at[pl.ds(half * rows, rows), :], to_ref, sem)
    copy.start()
    held[...] = block_ref[...]
    copy.wait()


def keep(block, weight, half, us):
    vmem = pl.BlockSpec(memory_space=pltpu.VMEM)
    return pl.pallas_call(
        functools.partial(keep_kernel, half),
        out_shape=(
            jax.ShapeDtypeStruct(block.shape, block.dtype),
            pltpu.VMEM((weight.shape[0] // 2, weight.shape[1]), weight.dtype),
        ),
        in_specs=[vmem, pl.BlockSpec(memory_space=pltpu.HBM)],
        out_specs=(vmem, vmem),
        scratch_shapes=[pltpu.SemaphoreType.DMA],
        compiler_params=pltpu.CompilerParams(vmem_limit_bytes=4 * 1024 * 1024),
        cost_estimate=hint(us),
    )(block, far(weight))


def output(me, attended, inputs, weight, n):
    kept = []

    def aside(half, block):
        block, part = keep(block, weight, half, 2)
        kept.append(near(part))
        return block

    mine, other = gather_blocks(
        attended, n, functools.partial(aside, 0), functools.partial(aside, 1)
    )
    half, heads, width = mine.shape
    vmem = pl.BlockSpec(memory_space=pltpu.VMEM)
    return pl.pallas_call(
        functools.partial(output_kernel, n),
        out_shape=jax.ShapeDtypeStruct(inputs.shape, BF16),
        in_specs=[pl.BlockSpec(memory_space=pltpu.SMEM)] + [vmem] * 5,
        out_specs=vmem,
        scratch_shapes=[pltpu.VMEM((width // 128, n * heads, 128), F32)],
        compiler_params=pltpu.CompilerParams(vmem_limit_bytes=VMEM_LIMIT),
    )(me, mine, other, inputs, *kept)


def angles(positions, steps):
    half = HD // 2
    frequency = jnp.exp(-math.log(ROPE_BASE) * 2.0 * jnp.arange(half, dtype=F32) / HD)
    places = (positions + jnp.arange(steps, dtype=jnp.int32)).astype(F32)
    turns = places[:, None] * frequency[None, :]
    cosine, sine = jnp.cos(turns), jnp.sin(turns)
    cos = jnp.concatenate([cosine, cosine], axis=-1)
    sin = jnp.concatenate([-sine, sine], axis=-1)
    return cos[:, None, :], sin[:, None, :]


def local(
    n, inputs, norm_gain, qkv_weight, head_lambda, head_gain, out_weight,
    key_one_pages, key_two_pages, value_pages, page_table, context_len, positions,
):
    steps, rows, part = inputs.shape
    me = lax.axis_index("gx").astype(jnp.int32).reshape(1)
    block = inputs.reshape(steps * rows, part)
    capacity = page_table.shape[1] * key_one_pages.shape[1]
    small = (page_table, head_lambda.reshape(1, H), head_gain.reshape(1, H * 2 * HD))
    sent, aside = project(
        me, block, norm_gain.reshape(n, 1, part), qkv_weight, n, (positions, context_len), small,
        capacity,
    )
    received = lax.all_to_all(sent, "gx", 0, 0)
    attended = attend(received, *aside, key_one_pages, key_two_pages, value_pages)
    return output(me, attended, inputs, out_weight, n)


def rotary(vectors, cos, sin):
    return vectors * cos + jnp.roll(vectors, HD // 2, axis=-1) * sin


def local_any(
    n, inputs, norm_gain, qkv_weight, head_lambda, head_gain, out_weight,
    key_one_pages, key_two_pages, value_pages, page_table, context_len, positions,
):
    steps = inputs.shape[0]
    own = page_table.shape[0]
    capacity = page_table.shape[1] * key_one_pages.shape[1]
    values = lax.all_gather(inputs, "gx", axis=2, tiled=True).astype(F32)
    factor = lax.rsqrt(jnp.mean(values * values, axis=-1, keepdims=True) + EPS)
    normed = (values * factor * norm_gain).astype(BF16)
    projected = jnp.einsum("sbd,dc->sbc", normed, qkv_weight, preferred_element_type=F32)
    received = lax.all_to_all(
        projected.astype(BF16), "gx", split_axis=1, concat_axis=2, tiled=True
    )
    cached = tuple(
        pool[page_table].reshape(own, capacity, H, -1)
        for pool in (key_one_pages, key_two_pages, value_pages)
    )
    both = received[..., : 4 * H * HD].reshape(steps, own, 4, H, HD).astype(F32)
    new_values = received[..., 4 * H * HD :].reshape(steps, own, H, 2 * HD)
    cos, sin = jax.vmap(lambda p: angles(p, steps))(positions.reshape(own, 1))
    cos, sin = (jnp.moveaxis(x, 0, 1)[:, :, None] for x in (cos, sin))
    turned = rotary(both, cos, sin).astype(BF16)
    place = jnp.arange(capacity, dtype=jnp.int32)
    allowed = (place[None, :] < context_len[:, None])[None, :, None, :]
    step = jnp.arange(steps)
    newer_allowed = (step[None, :] <= step[:, None])[:, None, None, :]

    def softmax_map(query, keys, news):
        older = jnp.einsum("tshd,sjhd->tshj", query, keys, preferred_element_type=F32)
        newer = jnp.einsum("tshd,eshd->tshe", query, news, preferred_element_type=F32)
        scores = jnp.concatenate(
            [jnp.where(allowed, older, -jnp.inf), jnp.where(newer_allowed, newer, -jnp.inf)], axis=-1
        )
        return jax.nn.softmax(scores * (1.0 / math.sqrt(HD)), axis=-1)

    first = softmax_map(turned[:, :, 0], cached[0], turned[:, :, 2])
    second = softmax_map(turned[:, :, 1], cached[1], turned[:, :, 3])
    mix = (first - head_lambda[:, None] * second).astype(BF16)
    mixed = jnp.einsum(
        "tshj,sjhf->tshf", mix[..., :capacity], cached[2], preferred_element_type=F32
    ) + jnp.einsum("tshe,eshf->tshf", mix[..., capacity:], new_values, preferred_element_type=F32)
    norm = lax.rsqrt(jnp.mean(mixed * mixed, axis=-1, keepdims=True) + EPS)
    grouped = (mixed * norm * head_gain.reshape(H, 2 * HD)).astype(BF16)
    whole = lax.all_gather(grouped.reshape(steps, own, -1), "gx", axis=1, tiled=True)
    branch = jnp.einsum("sbf,fd->sbd", whole, out_weight, preferred_element_type=F32)
    return (inputs.astype(F32) + branch).astype(BF16)


def solution(mesh):
    n = mesh.shape["gx"]
    placed = (
        P(None, "groups", "gx"),
        P(),
        P(None, "gx"),
        P(),
        P(),
        P(None, "gx"),
        P(("groups", "gx"), None, None),
        P(("groups", "gx"), None, None),
        P(("groups", "gx"), None, None),
        P(("groups", "gx"), None),
        P(("groups", "gx")),
        P(("groups", "gx")),
    )

    def chosen(inputs, norm_gain, qkv_weight, *rest):
        aligned = inputs.shape[2] % 128 == 0 and qkv_weight.shape[1] % 128 == 0
        single = rest[6].shape[0] == 1
        power = n >= 4 and n & (n - 1) == 0
        body = local if aligned and single and power else local_any
        return body(n, inputs, norm_gain, qkv_weight, *rest)

    return jax.shard_map(
        chosen, mesh=mesh, in_specs=placed, out_specs=P(None, "groups", "gx"), check_vma=False
    )
```

```python
import functools
import math

import jax
import jax.numpy as jnp
from jax import lax
from jax.experimental import pallas as pl
from jax.experimental.pallas import tpu as pltpu
from jax.sharding import PartitionSpec as P

H = 24
HD = 128
EPS = 1e-05
ROPE_BASE = 10000.0
F32 = jnp.float32
BF16 = jnp.bfloat16
VMEM_LIMIT = 16 * 1024 * 1024


def radices(n):
    rest = n // 2
    middle = 1
    while middle * middle * 4 <= rest:
        middle *= 2
    return rest // middle, middle


def swap(block, n, mask):
    return lax.ppermute(block, "gx", [(i, i ^ mask) for i in range(n)])


def gather_blocks(block, n, first_aside, second_aside):
    outer, middle = radices(n)
    arrived = [swap(block, n, o * 2 * middle) for o in range(1, outer)]
    rows = jnp.stack([first_aside(block)] + arrived)
    others = [swap(rows, n, m * 2) for m in range(1, middle)]
    rows, others = lax.optimization_barrier((second_aside(rows), others))
    mine = jnp.concatenate([rows] + others)
    return mine, swap(mine, n, 1)


def owner(me, entry, core, n, far_first=False):
    outer, middle = radices(n)
    place = entry % outer
    if far_first:
        place = (outer - place) % outer
    mask = place * (2 * middle) + (entry // outer) * 2 + core
    return jnp.bitwise_xor(me, mask)


def far(x):
    return pltpu.with_memory_space_constraint(x, pltpu.HBM)


def hint(us):
    return pl.CostEstimate(flops=0, bytes_accessed=int(us * 3_000_000), transcendentals=0)


def slots(n):
    return [(entry, core) for core in range(2) for entry in range(n // 2)]


def fetches(n, order, me, from_ref, to_ref, sems):
    part = from_ref.shape[0] // n
    copies = []
    for slot, (entry, core) in enumerate(order):
        start = pl.multiple_of(owner(me, entry, core, n, True) * part, part)
        copies.append(
            pltpu.make_async_copy(
                from_ref.at[pl.ds(start, part), :], to_ref.at[slot], sems.at[slot]
            )
        )
    return copies


def fetch_kernel(n, order, *rest):
    (
        me_ref, block_ref, gain_ref, weight_ref, table_ref, lambda_ref, head_gain_ref,
        held, gain_out, weight_out, place_ref, lambda_out, head_gain_out,
        table, row_ref, wide_ref, sems, other_sems,
    ) = rest
    small = [
        pltpu.make_async_copy(start, end, other_sems.at[index])
        for index, (start, end) in enumerate(
            (
                (table_ref, table),
                (lambda_ref, row_ref),
                (head_gain_ref, wide_ref),
                (block_ref, held),
                (gain_ref, gain_out),
            )
        )
    ]
    large = fetches(n, order, me_ref[0], weight_ref, weight_out, sems)
    for copy in small + large:
        copy.start()
    for copy in small:
        copy.wait()

    capacity = place_ref.shape[1]
    pages = table_ref.shape[1]
    page = capacity // pages
    row = lax.broadcasted_iota(jnp.int32, (1, capacity), 1)
    place = jnp.zeros((1, capacity), jnp.int32)
    for index in range(pages):
        first = table[0, index] * page
        inside = (row >= first) & (row < first + page)
        place = jnp.where(inside, row - first + index * page, place)
    place_ref[...] = place
    across = lax.broadcasted_iota(jnp.int32, (H, H), 1) == lax.broadcasted_iota(jnp.int32, (H, H), 0)
    lambda_out[...] = jnp.sum(jnp.where(across, row_ref[...], 0.0), axis=1, keepdims=True)
    for h in range(H):
        head_gain_out[h : h + 1, :] = wide_ref[:, h * 2 * HD : (h + 1) * 2 * HD]

    for copy in large:
        copy.wait()


def fetch(me, block, gain, weight, n, order, small, capacity):
    part, columns = weight.shape[0] // n, weight.shape[1]
    vmem = pl.BlockSpec(memory_space=pltpu.VMEM)
    hbm = pl.BlockSpec(memory_space=pltpu.HBM)
    table, weights, head_gain = small
    return pl.pallas_call(
        functools.partial(fetch_kernel, n, order),
        out_shape=(
            pltpu.VMEM(block.shape, BF16),
            pltpu.VMEM(gain.shape, F32),
            pltpu.VMEM((len(order), part, columns), BF16),
            jax.ShapeDtypeStruct((1, capacity), jnp.int32),
            jax.ShapeDtypeStruct((H, 1), F32),
            jax.ShapeDtypeStruct((H, 2 * HD), F32),
        ),
        in_specs=[pl.BlockSpec(memory_space=pltpu.SMEM)] + [hbm] * 6,
        out_specs=(vmem,) * 6,
        scratch_shapes=[
            pltpu.SMEM(table.shape, table.dtype),
            pltpu.VMEM(weights.shape, F32),
            pltpu.VMEM(head_gain.shape, F32),
            pltpu.SemaphoreType.DMA((len(order),)),
            pltpu.SemaphoreType.DMA((5,)),
        ],
        compiler_params=pltpu.CompilerParams(vmem_limit_bytes=4 * 1024 * 1024),
        cost_estimate=hint(5),
    )(me, far(block), far(gain), far(weight), *map(far, small))


def near(x):
    return pltpu.with_memory_space_constraint(x, pltpu.VMEM)


def add_squares(refs, square):
    for ref in refs:
        for entry in range(ref.shape[0]):
            values = ref[entry].astype(F32)
            square = square + values * values
    return square


def squares_kernel(n, order, count, me_ref, weight_ref, *rest):
    blocks, (squares, weight_out, sems) = rest[:count], rest[count:]
    copies = fetches(n, order, me_ref[0], weight_ref, weight_out, sems)
    for copy in copies:
        copy.start()
    squares[...] = add_squares(blocks, jnp.zeros(squares.shape, F32))
    for copy in copies:
        copy.wait()


def squares_beside(me, weight, blocks, n, order):
    part, columns = weight.shape[0] // n, weight.shape[1]
    vmem = pl.BlockSpec(memory_space=pltpu.VMEM)
    return pl.pallas_call(
        functools.partial(squares_kernel, n, order, len(blocks)),
        out_shape=(
            jax.ShapeDtypeStruct(blocks[0].shape[1:], F32),
            pltpu.VMEM((len(order), part, columns), BF16),
        ),
        in_specs=[
            pl.BlockSpec(memory_space=pltpu.SMEM),
            pl.BlockSpec(memory_space=pltpu.HBM),
        ]
        + [vmem] * len(blocks),
        out_specs=(vmem, vmem),
        scratch_shapes=[pltpu.SemaphoreType.DMA((len(order),))],
        compiler_params=pltpu.CompilerParams(vmem_limit_bytes=4 * 1024 * 1024),
        cost_estimate=hint(len(order) * 0.7),
    )(me, far(weight), *blocks)


def more_squares_kernel(positions_ref, length_ref, place_ref, before, *rest):
    *blocks, squares, cos_ref, sin_ref, allowed_ref = rest
    squares[...] = add_squares(blocks, before[...])
    steps = cos_ref.shape[0]
    lane = lax.broadcasted_iota(jnp.int32, (8, HD), 1)
    step = lax.broadcasted_iota(jnp.int32, (8, HD), 0)
    pair = lax.rem(lane, HD // 2).astype(F32)
    frequency = jnp.exp(-math.log(ROPE_BASE) * 2.0 * pair / HD)
    turns = (positions_ref[0] + step).astype(F32) * frequency
    cos = jnp.cos(turns)
    sin = jnp.where(lane < HD // 2, -1.0, 1.0) * jnp.sin(turns)
    for index in range(steps):
        cos_ref[index] = cos[index : index + 1]
        sin_ref[index] = sin[index : index + 1]
    allowed_ref[...] = jnp.where(place_ref[...] < length_ref[0], 1.0, 0.0)


def more_squares(blocks, before, positions, length, place, steps):
    vmem = pl.BlockSpec(memory_space=pltpu.VMEM)
    smem = pl.BlockSpec(memory_space=pltpu.SMEM)
    turns = jax.ShapeDtypeStruct((steps, 1, HD), F32)
    return pl.pallas_call(
        more_squares_kernel,
        out_shape=(
            jax.ShapeDtypeStruct(before.shape, F32),
            turns,
            turns,
            jax.ShapeDtypeStruct(place.shape, F32),
        ),
        in_specs=[smem, smem] + [vmem] * (len(blocks) + 2),
        out_specs=(vmem,) * 4,
        compiler_params=pltpu.CompilerParams(vmem_limit_bytes=4 * 1024 * 1024),
        cost_estimate=hint(1),
    )(positions, length, place, before, *blocks)


def project_kernel(n, order, me_ref, gain_ref, before_ref, mine_ref, other_ref, weight_ref, *rest):
    *helds, out_ref, last, spread, total, kept, sems = rest
    me = me_ref[0]
    rows, part = before_ref.shape
    copies = fetches(n, order, me, weight_ref, last, sems)
    for copy in copies:
        copy.start()
    places = [(held, slot) for held in helds for slot in range(held.shape[0])]
    early = len(places)
    places += [(last, slot) for slot in range(len(order))]
    blocks = list(zip(slots(n), places, strict=True))

    def products(picked, factor):
        summed = None
        for (entry, core), (held, slot) in picked:
            values = (mine_ref, other_ref)[core][entry].astype(F32)
            normed = (values * factor * gain_ref[owner(me, entry, core, n, True)]).astype(BF16)
            product = jnp.dot(normed, held[slot], preferred_element_type=F32)
            summed = product if summed is None else summed + product
        return summed

    def row_factor():
        square = add_squares([other_ref], before_ref[...])
        mean = jnp.sum(square, axis=1, keepdims=True) * (1.0 / (n * part))
        return lax.rsqrt(mean + EPS)

    @pl.when(me >= 0)
    def _():
        factor = row_factor()
        total[...] = products(blocks[:early], factor)
        kept[...] = jnp.broadcast_to(factor, kept.shape)

    for copy in copies:
        copy.wait()
    factor = kept[:, :1]
    summed = total[...] + products(blocks[early:], factor)
    columns = summed.shape[1] // 128
    steps = rows // n
    for block in range(columns):
        for step in range(steps):
            spread[:, step * columns + block, :] = summed[
                step * n : (step + 1) * n, block * 128 : (block + 1) * 128
            ]
    for target in range(n):
        out_ref[target] = spread[target, : steps * columns, :].astype(BF16)


def project(me, block, gain, weight, n, scalars, small, capacity):
    rows, part = block.shape
    columns = weight.shape[1]
    pieces = rows // n * (columns // 128)
    outer, middle = radices(n)
    order = slots(n)
    first, second = n // 4, 3 * n // 4

    arrived = [swap(block, n, o * 2 * middle) for o in range(outer - 1, 0, -1)]
    held, gain, weight_a, place, weights, head_gain = fetch(
        me, block, gain, weight, n, order[:first], small, capacity
    )
    row = jnp.stack([held] + arrived)
    later = [swap(row, n, m * 2) for m in range(1, middle)]
    squares, weight_b = squares_beside(me, weight, [row], n, order[first:second])
    later, squares = lax.optimization_barrier((later, squares))
    mine = jnp.concatenate([row] + later)
    other = swap(mine, n, 1)
    squares, cos, sin, allowed = more_squares(later, squares, *scalars, place, rows // n)
    vmem = pl.BlockSpec(memory_space=pltpu.VMEM)
    hbm = pl.BlockSpec(memory_space=pltpu.HBM)
    sent = pl.pallas_call(
        functools.partial(project_kernel, n, order[second:]),
        out_shape=jax.ShapeDtypeStruct((n, pieces, 128), BF16),
        in_specs=[pl.BlockSpec(memory_space=pltpu.SMEM)] + [vmem] * 4 + [hbm] + [vmem] * 2,
        out_specs=vmem,
        scratch_shapes=[
            pltpu.VMEM((n - second, part, columns), BF16),
            pltpu.VMEM((n, -(-pieces // 8) * 8, 128), F32),
            pltpu.VMEM((rows, columns), F32),
            pltpu.VMEM((rows, 128), F32),
            pltpu.SemaphoreType.DMA((n - second,)),
        ],
        compiler_params=pltpu.CompilerParams(vmem_limit_bytes=VMEM_LIMIT),
        cost_estimate=hint(6),
    )(me, gain, squares, mine, other, far(weight), near(weight_a), near(weight_b))
    return sent, (cos, sin, allowed, weights, head_gain)


def attend_kernel(
    received_ref, cos_ref, sin_ref, allowed_ref, lambda_ref, gain_ref,
    keys_one_ref, keys_two_ref, values_ref, out_ref, fresh,
):
    sources, pieces, _ = received_ref.shape
    steps = cos_ref.shape[0]
    blocks = pieces // steps
    pages, page, _ = keys_one_ref.shape
    capacity = pages * page
    for source in range(sources):
        piece = received_ref[source].astype(F32)
        for step in range(steps):
            fresh[step, source * blocks : (source + 1) * blocks, :] = piece[
                step * blocks : (step + 1) * blocks
            ]

    def heads(step, kind):
        return fresh[step, kind * H : (kind + 1) * H, :]

    def rotated(step, kind):
        values = heads(step, kind)
        turned = values * cos_ref[step] + pltpu.roll(values, HD // 2, 1) * sin_ref[step]
        return turned.astype(BF16).astype(F32)

    allowed = allowed_ref[...] > 0.0
    scale = 1.0 / math.sqrt(HD)
    head_row = lax.rem(lax.broadcasted_iota(jnp.int32, (steps * H, HD), 0), H)

    def softmax_map(kind, keys_ref):
        queries = [rotated(step, kind) for step in range(steps)]
        news = [rotated(step, kind + 2) for step in range(steps)]
        stacked = jnp.concatenate(queries, axis=0)
        apart = jnp.concatenate(
            [jnp.where(head_row == h, stacked, 0.0).astype(BF16) for h in range(H)], axis=1
        )
        older = lax.dot_general(
            apart, keys_ref[...].reshape(capacity, H * HD), (((1,), (1,)), ((), ())),
            preferred_element_type=F32,
        )
        older = jnp.where(allowed, older * scale, -1e38)
        parts = []
        for step in range(steps):
            cached = older[step * H : (step + 1) * H]
            newer = [
                jnp.sum(queries[step] * news[e], axis=1, keepdims=True) * scale
                for e in range(step + 1)
            ]
            top = jnp.max(cached, axis=1, keepdims=True)
            for value in newer:
                top = jnp.maximum(top, value)
            cached = jnp.exp(cached - top)
            newer = [jnp.exp(value - top) for value in newer]
            whole = jnp.sum(cached, axis=1, keepdims=True)
            for value in newer:
                whole = whole + value
            parts.append((cached / whole, [value / whole for value in newer]))
        return parts

    first = softmax_map(0, keys_one_ref)
    second = softmax_map(1, keys_two_ref)
    weight = lambda_ref[...]
    mix = jnp.concatenate(
        [first[step][0] - weight * second[step][0] for step in range(steps)], axis=0
    ).astype(BF16)
    spread = jnp.dot(mix, values_ref[...].reshape(capacity, -1), preferred_element_type=F32)
    wide_row = lax.broadcasted_iota(jnp.int32, (H, 2 * HD), 0)
    fresh_values = [
        jnp.concatenate(
            [fresh[e, pl.ds(4 * H + half, H, stride=2), :] for half in range(2)], axis=1
        )
        for e in range(steps)
    ]
    for step in range(steps):
        mixed = jnp.zeros((H, 2 * HD), F32)
        for h in range(H):
            block = spread[step * H : (step + 1) * H, h * 2 * HD : (h + 1) * 2 * HD]
            mixed = jnp.where(wide_row == h, block, mixed)
        for e in range(step + 1):
            share = first[step][1][e] - weight * second[step][1][e]
            mixed = mixed + share.astype(BF16).astype(F32) * fresh_values[e]
        norm = lax.rsqrt(jnp.mean(mixed * mixed, axis=1, keepdims=True) + EPS)
        out_ref[step * H : (step + 1) * H, :] = (mixed * norm * gain_ref[...]).astype(BF16)


def attend(received, cos, sin, allowed, weights, gain, keys_one, keys_two, values):
    steps = cos.shape[0]
    sources, pieces, _ = received.shape
    vmem = pl.BlockSpec(memory_space=pltpu.VMEM)
    held = [near(x) for x in (keys_one, keys_two, values)]
    return pl.pallas_call(
        attend_kernel,
        out_shape=jax.ShapeDtypeStruct((steps * H, 2 * HD), BF16),
        in_specs=[vmem] * 9,
        out_specs=vmem,
        scratch_shapes=[pltpu.VMEM((steps, sources * (pieces // steps), 128), F32)],
        compiler_params=pltpu.CompilerParams(vmem_limit_bytes=VMEM_LIMIT),
        cost_estimate=hint(10),
    )(received, cos, sin, allowed, weights, gain, *held)


def output_kernel(n, me_ref, mine_ref, other_ref, inputs_ref, *rest):
    *weights, out_ref, rows_ref = rest
    me = me_ref[0]
    half, heads, width = mine_ref.shape
    steps = heads // H
    lanes = width // 128
    for entry in range(half):
        for core, ref in ((0, mine_ref), (1, other_ref)):
            start = pl.multiple_of(owner(me, entry, core, n) * heads, 8)
            block = ref[entry].astype(F32)
            for lane in range(lanes):
                rows_ref[lane, pl.ds(start, heads), :] = block[:, lane * 128 : (lane + 1) * 128]
    total = None
    for h in range(H):
        left = jnp.concatenate(
            [
                jnp.concatenate(
                    [rows_ref[lane, pl.ds(step * H + h, n, stride=heads), :] for lane in range(lanes)],
                    axis=1,
                )
                for step in range(steps)
            ],
            axis=0,
        ).astype(BF16)
        held = weights[h * len(weights) // H]
        at = h * width % held.shape[0]
        product = jnp.dot(left, held[at : at + width, :], preferred_element_type=F32)
        total = product if total is None else total + product
    for step in range(steps):
        out_ref[step] = (
            inputs_ref[step].astype(F32) + total[step * n : (step + 1) * n]
        ).astype(BF16)


def keep_kernel(half, block_ref, from_ref, held, to_ref, sem):
    rows = to_ref.shape[0]
    copy = pltpu.make_async_copy(from_ref.at[pl.ds(half * rows, rows), :], to_ref, sem)
    copy.start()
    held[...] = block_ref[...]
    copy.wait()


def keep(block, weight, half, us):
    vmem = pl.BlockSpec(memory_space=pltpu.VMEM)
    return pl.pallas_call(
        functools.partial(keep_kernel, half),
        out_shape=(
            jax.ShapeDtypeStruct(block.shape, block.dtype),
            pltpu.VMEM((weight.shape[0] // 2, weight.shape[1]), weight.dtype),
        ),
        in_specs=[vmem, pl.BlockSpec(memory_space=pltpu.HBM)],
        out_specs=(vmem, vmem),
        scratch_shapes=[pltpu.SemaphoreType.DMA],
        compiler_params=pltpu.CompilerParams(vmem_limit_bytes=4 * 1024 * 1024),
        cost_estimate=hint(us),
    )(block, far(weight))


def output(me, attended, inputs, weight, n):
    kept = []

    def aside(half, block):
        block, part = keep(block, weight, half, 2)
        kept.append(near(part))
        return block

    mine, other = gather_blocks(
        attended, n, functools.partial(aside, 0), functools.partial(aside, 1)
    )
    half, heads, width = mine.shape
    vmem = pl.BlockSpec(memory_space=pltpu.VMEM)
    return pl.pallas_call(
        functools.partial(output_kernel, n),
        out_shape=jax.ShapeDtypeStruct(inputs.shape, BF16),
        in_specs=[pl.BlockSpec(memory_space=pltpu.SMEM)] + [vmem] * 5,
        out_specs=vmem,
        scratch_shapes=[pltpu.VMEM((width // 128, n * heads, 128), F32)],
        compiler_params=pltpu.CompilerParams(vmem_limit_bytes=VMEM_LIMIT),
    )(me, mine, other, inputs, *kept)


def angles(positions, steps):
    half = HD // 2
    frequency = jnp.exp(-math.log(ROPE_BASE) * 2.0 * jnp.arange(half, dtype=F32) / HD)
    places = (positions + jnp.arange(steps, dtype=jnp.int32)).astype(F32)
    turns = places[:, None] * frequency[None, :]
    cosine, sine = jnp.cos(turns), jnp.sin(turns)
    cos = jnp.concatenate([cosine, cosine], axis=-1)
    sin = jnp.concatenate([-sine, sine], axis=-1)
    return cos[:, None, :], sin[:, None, :]


def local(
    n, inputs, norm_gain, qkv_weight, head_lambda, head_gain, out_weight,
    key_one_pages, key_two_pages, value_pages, page_table, context_len, positions,
):
    steps, rows, part = inputs.shape
    me = lax.axis_index("gx").astype(jnp.int32).reshape(1)
    block = inputs.reshape(steps * rows, part)
    capacity = page_table.shape[1] * key_one_pages.shape[1]
    small = (page_table, head_lambda.reshape(1, H), head_gain.reshape(1, H * 2 * HD))
    sent, aside = project(
        me, block, norm_gain.reshape(n, 1, part), qkv_weight, n, (positions, context_len), small,
        capacity,
    )
    received = lax.all_to_all(sent, "gx", 0, 0)
    attended = attend(received, *aside, key_one_pages, key_two_pages, value_pages)
    return output(me, attended, inputs, out_weight, n)


def rotary(vectors, cos, sin):
    return vectors * cos + jnp.roll(vectors, HD // 2, axis=-1) * sin


def local_any(
    n, inputs, norm_gain, qkv_weight, head_lambda, head_gain, out_weight,
    key_one_pages, key_two_pages, value_pages, page_table, context_len, positions,
):
    steps = inputs.shape[0]
    own = page_table.shape[0]
    capacity = page_table.shape[1] * key_one_pages.shape[1]
    values = lax.all_gather(inputs, "gx", axis=2, tiled=True).astype(F32)
    factor = lax.rsqrt(jnp.mean(values * values, axis=-1, keepdims=True) + EPS)
    normed = (values * factor * norm_gain).astype(BF16)
    projected = jnp.einsum("sbd,dc->sbc", normed, qkv_weight, preferred_element_type=F32)
    received = lax.all_to_all(
        projected.astype(BF16), "gx", split_axis=1, concat_axis=2, tiled=True
    )
    cached = tuple(
        pool[page_table].reshape(own, capacity, H, -1)
        for pool in (key_one_pages, key_two_pages, value_pages)
    )
    both = received[..., : 4 * H * HD].reshape(steps, own, 4, H, HD).astype(F32)
    new_values = received[..., 4 * H * HD :].reshape(steps, own, H, 2 * HD)
    cos, sin = jax.vmap(lambda p: angles(p, steps))(positions.reshape(own, 1))
    cos, sin = (jnp.moveaxis(x, 0, 1)[:, :, None] for x in (cos, sin))
    turned = rotary(both, cos, sin).astype(BF16)
    place = jnp.arange(capacity, dtype=jnp.int32)
    allowed = (place[None, :] < context_len[:, None])[None, :, None, :]
    step = jnp.arange(steps)
    newer_allowed = (step[None, :] <= step[:, None])[:, None, None, :]

    def softmax_map(query, keys, news):
        older = jnp.einsum("tshd,sjhd->tshj", query, keys, preferred_element_type=F32)
        newer = jnp.einsum("tshd,eshd->tshe", query, news, preferred_element_type=F32)
        scores = jnp.concatenate(
            [jnp.where(allowed, older, -jnp.inf), jnp.where(newer_allowed, newer, -jnp.inf)], axis=-1
        )
        return jax.nn.softmax(scores * (1.0 / math.sqrt(HD)), axis=-1)

    first = softmax_map(turned[:, :, 0], cached[0], turned[:, :, 2])
    second = softmax_map(turned[:, :, 1], cached[1], turned[:, :, 3])
    mix = (first - head_lambda[:, None] * second).astype(BF16)
    mixed = jnp.einsum(
        "tshj,sjhf->tshf", mix[..., :capacity], cached[2], preferred_element_type=F32
    ) + jnp.einsum("tshe,eshf->tshf", mix[..., capacity:], new_values, preferred_element_type=F32)
    norm = lax.rsqrt(jnp.mean(mixed * mixed, axis=-1, keepdims=True) + EPS)
    grouped = (mixed * norm * head_gain.reshape(H, 2 * HD)).astype(BF16)
    whole = lax.all_gather(grouped.reshape(steps, own, -1), "gx", axis=1, tiled=True)
    branch = jnp.einsum("sbf,fd->sbd", whole, out_weight, preferred_element_type=F32)
    return (inputs.astype(F32) + branch).astype(BF16)


def solution(mesh):
    n = mesh.shape["gx"]
    placed = (
        P(None, "groups", "gx"),
        P(),
        P(None, "gx"),
        P(),
        P(),
        P(None, "gx"),
        P(("groups", "gx"), None, None),
        P(("groups", "gx"), None, None),
        P(("groups", "gx"), None, None),
        P(("groups", "gx"), None),
        P(("groups", "gx")),
        P(("groups", "gx")),
    )

    def chosen(inputs, norm_gain, qkv_weight, *rest):
        aligned = inputs.shape[2] % 128 == 0 and qkv_weight.shape[1] % 128 == 0
        single = rest[6].shape[0] == 1
        power = n >= 4 and n & (n - 1) == 0
        body = local if aligned and single and power else local_any
        return body(n, inputs, norm_gain, qkv_weight, *rest)

    return jax.shard_map(
        chosen, mesh=mesh, in_specs=placed, out_specs=P(None, "groups", "gx"), check_vma=False
    )
```

```python
import functools
import math

import jax
import jax.numpy as jnp
from jax import lax
from jax.experimental import pallas as pl
from jax.experimental.pallas import tpu as pltpu
from jax.sharding import PartitionSpec as P

H = 24
HD = 128
EPS = 1e-05
ROPE_BASE = 10000.0
F32 = jnp.float32
BF16 = jnp.bfloat16
VMEM_LIMIT = 16 * 1024 * 1024


def radices(n):
    rest = n // 2
    middle = 1
    while middle * middle * 4 <= rest:
        middle *= 2
    return rest // middle, middle


def swap(block, n, mask):
    return lax.ppermute(block, "gx", [(i, i ^ mask) for i in range(n)])


def gather_blocks(block, n, first_aside, second_aside):
    outer, middle = radices(n)
    arrived = [swap(block, n, o * 2 * middle) for o in range(1, outer)]
    rows = jnp.stack([first_aside(block)] + arrived)
    others = [swap(rows, n, m * 2) for m in range(1, middle)]
    rows, others = lax.optimization_barrier((second_aside(rows), others))
    mine = jnp.concatenate([rows] + others)
    return mine, swap(mine, n, 1)


def owner(me, entry, core, n):
    outer, middle = radices(n)
    mask = (entry % outer) * (2 * middle) + (entry // outer) * 2 + core
    return jnp.bitwise_xor(me, mask)


def far(x):
    return pltpu.with_memory_space_constraint(x, pltpu.HBM)


def hint(us):
    return pl.CostEstimate(flops=0, bytes_accessed=int(us * 3_000_000), transcendentals=0)


def slots(n):
    return [(entry, core) for core in range(2) for entry in range(n // 2)]


def fetches(n, order, me, from_ref, to_ref, sems):
    part = from_ref.shape[0] // n
    copies = []
    for slot, (entry, core) in enumerate(order):
        start = pl.multiple_of(owner(me, entry, core, n) * part, part)
        copies.append(
            pltpu.make_async_copy(
                from_ref.at[pl.ds(start, part), :], to_ref.at[slot], sems.at[slot]
            )
        )
    return copies


def fetch_kernel(n, order, *rest):
    (
        me_ref, block_ref, gain_ref, weight_ref, table_ref, lambda_ref, head_gain_ref,
        held, gain_out, weight_out, place_ref, lambda_out, head_gain_out,
        table, row_ref, wide_ref, sems, other_sems,
    ) = rest
    small = [
        pltpu.make_async_copy(start, end, other_sems.at[index])
        for index, (start, end) in enumerate(
            (
                (table_ref, table),
                (lambda_ref, row_ref),
                (head_gain_ref, wide_ref),
                (block_ref, held),
                (gain_ref, gain_out),
            )
        )
    ]
    large = fetches(n, order, me_ref[0], weight_ref, weight_out, sems)
    for copy in small + large:
        copy.start()
    for copy in small:
        copy.wait()

    capacity = place_ref.shape[1]
    pages = table_ref.shape[1]
    page = capacity // pages
    row = lax.broadcasted_iota(jnp.int32, (1, capacity), 1)
    place = jnp.zeros((1, capacity), jnp.int32)
    for index in range(pages):
        first = table[0, index] * page
        inside = (row >= first) & (row < first + page)
        place = jnp.where(inside, row - first + index * page, place)
    place_ref[...] = place
    across = lax.broadcasted_iota(jnp.int32, (H, H), 1) == lax.broadcasted_iota(jnp.int32, (H, H), 0)
    lambda_out[...] = jnp.sum(jnp.where(across, row_ref[...], 0.0), axis=1, keepdims=True)
    for h in range(H):
        head_gain_out[h : h + 1, :] = wide_ref[:, h * 2 * HD : (h + 1) * 2 * HD]

    for copy in large:
        copy.wait()


def fetch(me, block, gain, weight, n, order, small, capacity):
    part, columns = weight.shape[0] // n, weight.shape[1]
    vmem = pl.BlockSpec(memory_space=pltpu.VMEM)
    hbm = pl.BlockSpec(memory_space=pltpu.HBM)
    table, weights, head_gain = small
    return pl.pallas_call(
        functools.partial(fetch_kernel, n, order),
        out_shape=(
            pltpu.VMEM(block.shape, BF16),
            pltpu.VMEM(gain.shape, F32),
            pltpu.VMEM((len(order), part, columns), BF16),
            jax.ShapeDtypeStruct((1, capacity), jnp.int32),
            jax.ShapeDtypeStruct((H, 1), F32),
            jax.ShapeDtypeStruct((H, 2 * HD), F32),
        ),
        in_specs=[pl.BlockSpec(memory_space=pltpu.SMEM)] + [hbm] * 6,
        out_specs=(vmem,) * 6,
        scratch_shapes=[
            pltpu.SMEM(table.shape, table.dtype),
            pltpu.VMEM(weights.shape, F32),
            pltpu.VMEM(head_gain.shape, F32),
            pltpu.SemaphoreType.DMA((len(order),)),
            pltpu.SemaphoreType.DMA((5,)),
        ],
        compiler_params=pltpu.CompilerParams(vmem_limit_bytes=4 * 1024 * 1024),
        cost_estimate=hint(5),
    )(me, far(block), far(gain), far(weight), *map(far, small))


def near(x):
    return pltpu.with_memory_space_constraint(x, pltpu.VMEM)


def add_squares(refs, square):
    for ref in refs:
        for entry in range(ref.shape[0]):
            values = ref[entry].astype(F32)
            square = square + values * values
    return square


def squares_kernel(n, order, count, me_ref, weight_ref, *rest):
    blocks, (squares, weight_out, sems) = rest[:count], rest[count:]
    copies = fetches(n, order, me_ref[0], weight_ref, weight_out, sems)
    for copy in copies:
        copy.start()
    squares[...] = add_squares(blocks, jnp.zeros(squares.shape, F32))
    for copy in copies:
        copy.wait()


def squares_beside(me, weight, blocks, n, order):
    part, columns = weight.shape[0] // n, weight.shape[1]
    vmem = pl.BlockSpec(memory_space=pltpu.VMEM)
    return pl.pallas_call(
        functools.partial(squares_kernel, n, order, len(blocks)),
        out_shape=(
            jax.ShapeDtypeStruct(blocks[0].shape[1:], F32),
            pltpu.VMEM((len(order), part, columns), BF16),
        ),
        in_specs=[
            pl.BlockSpec(memory_space=pltpu.SMEM),
            pl.BlockSpec(memory_space=pltpu.HBM),
        ]
        + [vmem] * len(blocks),
        out_specs=(vmem, vmem),
        scratch_shapes=[pltpu.SemaphoreType.DMA((len(order),))],
        compiler_params=pltpu.CompilerParams(vmem_limit_bytes=4 * 1024 * 1024),
        cost_estimate=hint(len(order) * 0.7),
    )(me, far(weight), *blocks)


def more_squares_kernel(positions_ref, length_ref, place_ref, before, *rest):
    *blocks, squares, cos_ref, sin_ref, allowed_ref = rest
    squares[...] = add_squares(blocks, before[...])
    steps = cos_ref.shape[0]
    lane = lax.broadcasted_iota(jnp.int32, (8, HD), 1)
    step = lax.broadcasted_iota(jnp.int32, (8, HD), 0)
    pair = lax.rem(lane, HD // 2).astype(F32)
    frequency = jnp.exp(-math.log(ROPE_BASE) * 2.0 * pair / HD)
    turns = (positions_ref[0] + step).astype(F32) * frequency
    cos = jnp.cos(turns)
    sin = jnp.where(lane < HD // 2, -1.0, 1.0) * jnp.sin(turns)
    for index in range(steps):
        cos_ref[index] = cos[index : index + 1]
        sin_ref[index] = sin[index : index + 1]
    allowed_ref[...] = jnp.where(place_ref[...] < length_ref[0], 1.0, 0.0)


def more_squares(blocks, before, positions, length, place, steps):
    vmem = pl.BlockSpec(memory_space=pltpu.VMEM)
    smem = pl.BlockSpec(memory_space=pltpu.SMEM)
    turns = jax.ShapeDtypeStruct((steps, 1, HD), F32)
    return pl.pallas_call(
        more_squares_kernel,
        out_shape=(
            jax.ShapeDtypeStruct(before.shape, F32),
            turns,
            turns,
            jax.ShapeDtypeStruct(place.shape, F32),
        ),
        in_specs=[smem, smem] + [vmem] * (len(blocks) + 2),
        out_specs=(vmem,) * 4,
        compiler_params=pltpu.CompilerParams(vmem_limit_bytes=4 * 1024 * 1024),
        cost_estimate=hint(1),
    )(positions, length, place, before, *blocks)


def project_kernel(n, order, me_ref, gain_ref, before_ref, mine_ref, other_ref, weight_ref, *rest):
    *helds, out_ref, last, spread, total, kept, sems = rest
    me = me_ref[0]
    rows, part = before_ref.shape
    copies = fetches(n, order, me, weight_ref, last, sems)
    for copy in copies:
        copy.start()
    places = [(held, slot) for held in helds for slot in range(held.shape[0])]
    early = len(places)
    places += [(last, slot) for slot in range(len(order))]
    blocks = list(zip(slots(n), places, strict=True))

    def products(picked, factor):
        summed = None
        for (entry, core), (held, slot) in picked:
            values = (mine_ref, other_ref)[core][entry].astype(F32)
            normed = (values * factor * gain_ref[owner(me, entry, core, n)]).astype(BF16)
            product = jnp.dot(normed, held[slot], preferred_element_type=F32)
            summed = product if summed is None else summed + product
        return summed

    def row_factor():
        square = add_squares([other_ref], before_ref[...])
        mean = jnp.sum(square, axis=1, keepdims=True) * (1.0 / (n * part))
        return lax.rsqrt(mean + EPS)

    @pl.when(me >= 0)
    def _():
        factor = row_factor()
        total[...] = products(blocks[:early], factor)
        kept[...] = jnp.broadcast_to(factor, kept.shape)

    for copy in copies:
        copy.wait()
    factor = kept[:, :1]
    summed = total[...] + products(blocks[early:], factor)
    columns = summed.shape[1] // 128
    steps = rows // n
    for block in range(columns):
        for step in range(steps):
            spread[:, step * columns + block, :] = summed[
                step * n : (step + 1) * n, block * 128 : (block + 1) * 128
            ]
    for target in range(n):
        out_ref[target] = spread[target, : steps * columns, :].astype(BF16)


def project(me, block, gain, weight, n, scalars, small, capacity):
    rows, part = block.shape
    columns = weight.shape[1]
    pieces = rows // n * (columns // 128)
    outer, middle = radices(n)
    order = slots(n)
    first, second = n // 4, 3 * n // 4

    arrived = [swap(block, n, o * 2 * middle) for o in range(1, outer)]
    held, gain, weight_a, place, weights, head_gain = fetch(
        me, block, gain, weight, n, order[:first], small, capacity
    )
    row = jnp.stack([held] + arrived)
    later = [swap(row, n, m * 2) for m in range(1, middle)]
    squares, weight_b = squares_beside(me, weight, [row], n, order[first:second])
    later, squares = lax.optimization_barrier((later, squares))
    mine = jnp.concatenate([row] + later)
    other = swap(mine, n, 1)
    squares, cos, sin, allowed = more_squares(later, squares, *scalars, place, rows // n)
    vmem = pl.BlockSpec(memory_space=pltpu.VMEM)
    hbm = pl.BlockSpec(memory_space=pltpu.HBM)
    sent = pl.pallas_call(
        functools.partial(project_kernel, n, order[second:]),
        out_shape=jax.ShapeDtypeStruct((n, pieces, 128), BF16),
        in_specs=[pl.BlockSpec(memory_space=pltpu.SMEM)] + [vmem] * 4 + [hbm] + [vmem] * 2,
        out_specs=vmem,
        scratch_shapes=[
            pltpu.VMEM((n - second, part, columns), BF16),
            pltpu.VMEM((n, -(-pieces // 8) * 8, 128), F32),
            pltpu.VMEM((rows, columns), F32),
            pltpu.VMEM((rows, 128), F32),
            pltpu.SemaphoreType.DMA((n - second,)),
        ],
        compiler_params=pltpu.CompilerParams(vmem_limit_bytes=VMEM_LIMIT),
        cost_estimate=hint(6),
    )(me, gain, squares, mine, other, far(weight), near(weight_a), near(weight_b))
    return sent, (cos, sin, allowed, weights, head_gain)


def attend_kernel(
    received_ref, cos_ref, sin_ref, allowed_ref, lambda_ref, gain_ref,
    keys_one_ref, keys_two_ref, values_ref, out_ref, fresh,
):
    sources, pieces, _ = received_ref.shape
    steps = cos_ref.shape[0]
    blocks = pieces // steps
    pages, page, _ = keys_one_ref.shape
    capacity = pages * page
    for source in range(sources):
        piece = received_ref[source].astype(F32)
        for step in range(steps):
            fresh[step, source * blocks : (source + 1) * blocks, :] = piece[
                step * blocks : (step + 1) * blocks
            ]

    def heads(step, kind):
        return fresh[step, kind * H : (kind + 1) * H, :]

    def rotated(step, kind):
        values = heads(step, kind)
        turned = values * cos_ref[step] + pltpu.roll(values, HD // 2, 1) * sin_ref[step]
        return turned.astype(BF16).astype(F32)

    allowed = allowed_ref[...] > 0.0
    scale = 1.0 / math.sqrt(HD)
    head_row = lax.rem(lax.broadcasted_iota(jnp.int32, (steps * H, HD), 0), H)

    def softmax_map(kind, keys_ref):
        queries = [rotated(step, kind) for step in range(steps)]
        news = [rotated(step, kind + 2) for step in range(steps)]
        stacked = jnp.concatenate(queries, axis=0)
        apart = jnp.concatenate(
            [jnp.where(head_row == h, stacked, 0.0).astype(BF16) for h in range(H)], axis=1
        )
        older = lax.dot_general(
            apart, keys_ref[...].reshape(capacity, H * HD), (((1,), (1,)), ((), ())),
            preferred_element_type=F32,
        )
        older = jnp.where(allowed, older * scale, -1e38)
        parts = []
        for step in range(steps):
            cached = older[step * H : (step + 1) * H]
            newer = [
                jnp.sum(queries[step] * news[e], axis=1, keepdims=True) * scale
                for e in range(step + 1)
            ]
            top = jnp.max(cached, axis=1, keepdims=True)
            for value in newer:
                top = jnp.maximum(top, value)
            cached = jnp.exp(cached - top)
            newer = [jnp.exp(value - top) for value in newer]
            whole = jnp.sum(cached, axis=1, keepdims=True)
            for value in newer:
                whole = whole + value
            parts.append((cached / whole, [value / whole for value in newer]))
        return parts

    first = softmax_map(0, keys_one_ref)
    second = softmax_map(1, keys_two_ref)
    weight = lambda_ref[...]
    mix = jnp.concatenate(
        [first[step][0] - weight * second[step][0] for step in range(steps)], axis=0
    ).astype(BF16)
    spread = jnp.dot(mix, values_ref[...].reshape(capacity, -1), preferred_element_type=F32)
    wide_row = lax.broadcasted_iota(jnp.int32, (H, 2 * HD), 0)
    fresh_values = [
        jnp.concatenate(
            [fresh[e, pl.ds(4 * H + half, H, stride=2), :] for half in range(2)], axis=1
        )
        for e in range(steps)
    ]
    for step in range(steps):
        mixed = jnp.zeros((H, 2 * HD), F32)
        for h in range(H):
            block = spread[step * H : (step + 1) * H, h * 2 * HD : (h + 1) * 2 * HD]
            mixed = jnp.where(wide_row == h, block, mixed)
        for e in range(step + 1):
            share = first[step][1][e] - weight * second[step][1][e]
            mixed = mixed + share.astype(BF16).astype(F32) * fresh_values[e]
        norm = lax.rsqrt(jnp.mean(mixed * mixed, axis=1, keepdims=True) + EPS)
        out_ref[step * H : (step + 1) * H, :] = (mixed * norm * gain_ref[...]).astype(BF16)


def attend(received, cos, sin, allowed, weights, gain, keys_one, keys_two, values):
    steps = cos.shape[0]
    sources, pieces, _ = received.shape
    vmem = pl.BlockSpec(memory_space=pltpu.VMEM)
    held = [near(x) for x in (keys_one, keys_two, values)]
    return pl.pallas_call(
        attend_kernel,
        out_shape=jax.ShapeDtypeStruct((steps * H, 2 * HD), BF16),
        in_specs=[vmem] * 9,
        out_specs=vmem,
        scratch_shapes=[pltpu.VMEM((steps, sources * (pieces // steps), 128), F32)],
        compiler_params=pltpu.CompilerParams(vmem_limit_bytes=VMEM_LIMIT),
        cost_estimate=hint(10),
    )(received, cos, sin, allowed, weights, gain, *held)


def output_kernel(n, me_ref, mine_ref, other_ref, inputs_ref, *rest):
    *weights, out_ref, rows_ref = rest
    me = me_ref[0]
    half, heads, width = mine_ref.shape
    steps = heads // H
    lanes = width // 128
    for entry in range(half):
        for core, ref in ((0, mine_ref), (1, other_ref)):
            start = pl.multiple_of(owner(me, entry, core, n) * heads, 8)
            block = ref[entry].astype(F32)
            for lane in range(lanes):
                rows_ref[lane, pl.ds(start, heads), :] = block[:, lane * 128 : (lane + 1) * 128]
    total = None
    for h in range(H):
        left = jnp.concatenate(
            [
                jnp.concatenate(
                    [rows_ref[lane, pl.ds(step * H + h, n, stride=heads), :] for lane in range(lanes)],
                    axis=1,
                )
                for step in range(steps)
            ],
            axis=0,
        ).astype(BF16)
        held = weights[h * len(weights) // H]
        at = h * width % held.shape[0]
        product = jnp.dot(left, held[at : at + width, :], preferred_element_type=F32)
        total = product if total is None else total + product
    for step in range(steps):
        out_ref[step] = (
            inputs_ref[step].astype(F32) + total[step * n : (step + 1) * n]
        ).astype(BF16)


def keep_kernel(half, block_ref, from_ref, held, to_ref, sem):
    rows = to_ref.shape[0]
    copy = pltpu.make_async_copy(from_ref.at[pl.ds(half * rows, rows), :], to_ref, sem)
    copy.start()
    held[...] = block_ref[...]
    copy.wait()


def keep(block, weight, half, us):
    vmem = pl.BlockSpec(memory_space=pltpu.VMEM)
    return pl.pallas_call(
        functools.partial(keep_kernel, half),
        out_shape=(
            jax.ShapeDtypeStruct(block.shape, block.dtype),
            pltpu.VMEM((weight.shape[0] // 2, weight.shape[1]), weight.dtype),
        ),
        in_specs=[vmem, pl.BlockSpec(memory_space=pltpu.HBM)],
        out_specs=(vmem, vmem),
        scratch_shapes=[pltpu.SemaphoreType.DMA],
        compiler_params=pltpu.CompilerParams(vmem_limit_bytes=4 * 1024 * 1024),
        cost_estimate=hint(us),
    )(block, far(weight))


def output(me, attended, inputs, weight, n):
    kept = []

    def aside(half, block):
        block, part = keep(block, weight, half, 2)
        kept.append(near(part))
        return block

    mine, other = gather_blocks(
        attended, n, functools.partial(aside, 0), functools.partial(aside, 1)
    )
    half, heads, width = mine.shape
    vmem = pl.BlockSpec(memory_space=pltpu.VMEM)
    return pl.pallas_call(
        functools.partial(output_kernel, n),
        out_shape=jax.ShapeDtypeStruct(inputs.shape, BF16),
        in_specs=[pl.BlockSpec(memory_space=pltpu.SMEM)] + [vmem] * 5,
        out_specs=vmem,
        scratch_shapes=[pltpu.VMEM((width // 128, n * heads, 128), F32)],
        compiler_params=pltpu.CompilerParams(vmem_limit_bytes=VMEM_LIMIT),
    )(me, mine, other, inputs, *kept)


def angles(positions, steps):
    half = HD // 2
    frequency = jnp.exp(-math.log(ROPE_BASE) * 2.0 * jnp.arange(half, dtype=F32) / HD)
    places = (positions + jnp.arange(steps, dtype=jnp.int32)).astype(F32)
    turns = places[:, None] * frequency[None, :]
    cosine, sine = jnp.cos(turns), jnp.sin(turns)
    cos = jnp.concatenate([cosine, cosine], axis=-1)
    sin = jnp.concatenate([-sine, sine], axis=-1)
    return cos[:, None, :], sin[:, None, :]


def local(
    n, inputs, norm_gain, qkv_weight, head_lambda, head_gain, out_weight,
    key_one_pages, key_two_pages, value_pages, page_table, context_len, positions,
):
    steps, rows, part = inputs.shape
    me = lax.axis_index("gx").astype(jnp.int32).reshape(1)
    block = inputs.reshape(steps * rows, part)
    capacity = page_table.shape[1] * key_one_pages.shape[1]
    small = (page_table, head_lambda.reshape(1, H), head_gain.reshape(1, H * 2 * HD))
    sent, aside = project(
        me, block, norm_gain.reshape(n, 1, part), qkv_weight, n, (positions, context_len), small,
        capacity,
    )
    received = lax.all_to_all(sent, "gx", 0, 0)
    attended = attend(received, *aside, key_one_pages, key_two_pages, value_pages)
    return output(me, attended, inputs, out_weight, n)


def rotary(vectors, cos, sin):
    return vectors * cos + jnp.roll(vectors, HD // 2, axis=-1) * sin


def local_any(
    n, inputs, norm_gain, qkv_weight, head_lambda, head_gain, out_weight,
    key_one_pages, key_two_pages, value_pages, page_table, context_len, positions,
):
    steps = inputs.shape[0]
    own = page_table.shape[0]
    capacity = page_table.shape[1] * key_one_pages.shape[1]
    values = lax.all_gather(inputs, "gx", axis=2, tiled=True).astype(F32)
    factor = lax.rsqrt(jnp.mean(values * values, axis=-1, keepdims=True) + EPS)
    normed = (values * factor * norm_gain).astype(BF16)
    projected = jnp.einsum("sbd,dc->sbc", normed, qkv_weight, preferred_element_type=F32)
    received = lax.all_to_all(
        projected.astype(BF16), "gx", split_axis=1, concat_axis=2, tiled=True
    )
    cached = tuple(
        pool[page_table].reshape(own, capacity, H, -1)
        for pool in (key_one_pages, key_two_pages, value_pages)
    )
    both = received[..., : 4 * H * HD].reshape(steps, own, 4, H, HD).astype(F32)
    new_values = received[..., 4 * H * HD :].reshape(steps, own, H, 2 * HD)
    cos, sin = jax.vmap(lambda p: angles(p, steps))(positions.reshape(own, 1))
    cos, sin = (jnp.moveaxis(x, 0, 1)[:, :, None] for x in (cos, sin))
    turned = rotary(both, cos, sin).astype(BF16)
    place = jnp.arange(capacity, dtype=jnp.int32)
    allowed = (place[None, :] < context_len[:, None])[None, :, None, :]
    step = jnp.arange(steps)
    newer_allowed = (step[None, :] <= step[:, None])[:, None, None, :]

    def softmax_map(query, keys, news):
        older = jnp.einsum("tshd,sjhd->tshj", query, keys, preferred_element_type=F32)
        newer = jnp.einsum("tshd,eshd->tshe", query, news, preferred_element_type=F32)
        scores = jnp.concatenate(
            [jnp.where(allowed, older, -jnp.inf), jnp.where(newer_allowed, newer, -jnp.inf)], axis=-1
        )
        return jax.nn.softmax(scores * (1.0 / math.sqrt(HD)), axis=-1)

    first = softmax_map(turned[:, :, 0], cached[0], turned[:, :, 2])
    second = softmax_map(turned[:, :, 1], cached[1], turned[:, :, 3])
    mix = (first - head_lambda[:, None] * second).astype(BF16)
    mixed = jnp.einsum(
        "tshj,sjhf->tshf", mix[..., :capacity], cached[2], preferred_element_type=F32
    ) + jnp.einsum("tshe,eshf->tshf", mix[..., capacity:], new_values, preferred_element_type=F32)
    norm = lax.rsqrt(jnp.mean(mixed * mixed, axis=-1, keepdims=True) + EPS)
    grouped = (mixed * norm * head_gain.reshape(H, 2 * HD)).astype(BF16)
    whole = lax.all_gather(grouped.reshape(steps, own, -1), "gx", axis=1, tiled=True)
    branch = jnp.einsum("sbf,fd->sbd", whole, out_weight, preferred_element_type=F32)
    return (inputs.astype(F32) + branch).astype(BF16)


def solution(mesh):
    n = mesh.shape["gx"]
    placed = (
        P(None, "groups", "gx"),
        P(),
        P(None, "gx"),
        P(),
        P(),
        P(None, "gx"),
        P(("groups", "gx"), None, None),
        P(("groups", "gx"), None, None),
        P(("groups", "gx"), None, None),
        P(("groups", "gx"), None),
        P(("groups", "gx")),
        P(("groups", "gx")),
    )

    def chosen(inputs, norm_gain, qkv_weight, *rest):
        aligned = inputs.shape[2] % 128 == 0 and qkv_weight.shape[1] % 128 == 0
        single = rest[6].shape[0] == 1
        power = n >= 4 and n & (n - 1) == 0
        body = local if aligned and single and power else local_any
        return body(n, inputs, norm_gain, qkv_weight, *rest)

    return jax.shard_map(
        chosen, mesh=mesh, in_specs=placed, out_specs=P(None, "groups", "gx"), check_vma=False
    )
```

```python
import functools
import math

import jax
import jax.numpy as jnp
from jax import lax
from jax.experimental import pallas as pl
from jax.experimental.pallas import tpu as pltpu
from jax.sharding import PartitionSpec as P

H = 24
HD = 128
EPS = 1e-05
ROPE_BASE = 10000.0
F32 = jnp.float32
BF16 = jnp.bfloat16
VMEM_LIMIT = 16 * 1024 * 1024


def radices(n):
    rest = n // 2
    middle = 1
    while middle * middle * 4 <= rest:
        middle *= 2
    return rest // middle, middle


def swap(block, n, mask):
    return lax.ppermute(block, "gx", [(i, i ^ mask) for i in range(n)])


def gather_blocks(block, n, first_aside, second_aside):
    outer, middle = radices(n)
    arrived = [swap(block, n, o * 2 * middle) for o in range(1, outer)]
    rows = jnp.stack([first_aside(block)] + arrived)
    others = [swap(rows, n, m * 2) for m in range(1, middle)]
    rows, others = lax.optimization_barrier((second_aside(rows), others))
    mine = jnp.concatenate([rows] + others)
    return mine, swap(mine, n, 1)


def owner(me, entry, core, n):
    outer, middle = radices(n)
    mask = (entry % outer) * (2 * middle) + (entry // outer) * 2 + core
    return jnp.bitwise_xor(me, mask)


def far(x):
    return pltpu.with_memory_space_constraint(x, pltpu.HBM)


def hint(us):
    return pl.CostEstimate(flops=0, bytes_accessed=int(us * 3_000_000), transcendentals=0)


def slots(n):
    return [(entry, core) for core in range(2) for entry in range(n // 2)]


def fetches(n, order, me, from_ref, to_ref, sems):
    part = from_ref.shape[0] // n
    copies = []
    for slot, (entry, core) in enumerate(order):
        start = pl.multiple_of(owner(me, entry, core, n) * part, part)
        copies.append(
            pltpu.make_async_copy(
                from_ref.at[pl.ds(start, part), :], to_ref.at[slot], sems.at[slot]
            )
        )
    return copies


def fetch_kernel(n, order, *rest):
    (
        me_ref, block_ref, gain_ref, weight_ref, table_ref, lambda_ref, head_gain_ref,
        held, gain_out, weight_out, place_ref, lambda_out, head_gain_out,
        table, row_ref, wide_ref, sems, other_sems,
    ) = rest
    small = [
        pltpu.make_async_copy(start, end, other_sems.at[index])
        for index, (start, end) in enumerate(
            (
                (table_ref, table),
                (lambda_ref, row_ref),
                (head_gain_ref, wide_ref),
                (block_ref, held),
                (gain_ref, gain_out),
            )
        )
    ]
    large = fetches(n, order, me_ref[0], weight_ref, weight_out, sems)
    for copy in small + large:
        copy.start()
    for copy in small:
        copy.wait()

    capacity = place_ref.shape[1]
    pages = table_ref.shape[1]
    page = capacity // pages
    row = lax.broadcasted_iota(jnp.int32, (1, capacity), 1)
    place = jnp.zeros((1, capacity), jnp.int32)
    for index in range(pages):
        first = table[0, index] * page
        inside = (row >= first) & (row < first + page)
        place = jnp.where(inside, row - first + index * page, place)
    place_ref[...] = place
    across = lax.broadcasted_iota(jnp.int32, (H, H), 1) == lax.broadcasted_iota(jnp.int32, (H, H), 0)
    lambda_out[...] = jnp.sum(jnp.where(across, row_ref[...], 0.0), axis=1, keepdims=True)
    for h in range(H):
        head_gain_out[h : h + 1, :] = wide_ref[:, h * 2 * HD : (h + 1) * 2 * HD]

    for copy in large:
        copy.wait()


def fetch(me, block, gain, weight, n, order, small, capacity):
    part, columns = weight.shape[0] // n, weight.shape[1]
    vmem = pl.BlockSpec(memory_space=pltpu.VMEM)
    hbm = pl.BlockSpec(memory_space=pltpu.HBM)
    table, weights, head_gain = small
    return pl.pallas_call(
        functools.partial(fetch_kernel, n, order),
        out_shape=(
            pltpu.VMEM(block.shape, BF16),
            pltpu.VMEM(gain.shape, F32),
            pltpu.VMEM((len(order), part, columns), BF16),
            jax.ShapeDtypeStruct((1, capacity), jnp.int32),
            jax.ShapeDtypeStruct((H, 1), F32),
            jax.ShapeDtypeStruct((H, 2 * HD), F32),
        ),
        in_specs=[pl.BlockSpec(memory_space=pltpu.SMEM)] + [hbm] * 6,
        out_specs=(vmem,) * 6,
        scratch_shapes=[
            pltpu.SMEM(table.shape, table.dtype),
            pltpu.VMEM(weights.shape, F32),
            pltpu.VMEM(head_gain.shape, F32),
            pltpu.SemaphoreType.DMA((len(order),)),
            pltpu.SemaphoreType.DMA((5,)),
        ],
        compiler_params=pltpu.CompilerParams(vmem_limit_bytes=4 * 1024 * 1024),
        cost_estimate=hint(5),
    )(me, far(block), far(gain), far(weight), *map(far, small))


def near(x):
    return pltpu.with_memory_space_constraint(x, pltpu.VMEM)


def add_squares(refs, square):
    for ref in refs:
        for entry in range(ref.shape[0]):
            values = ref[entry].astype(F32)
            square = square + values * values
    return square


def squares_kernel(n, order, count, me_ref, weight_ref, *rest):
    blocks, (squares, weight_out, sems) = rest[:count], rest[count:]
    copies = fetches(n, order, me_ref[0], weight_ref, weight_out, sems)
    for copy in copies:
        copy.start()
    squares[...] = add_squares(blocks, jnp.zeros(squares.shape, F32))
    for copy in copies:
        copy.wait()


def squares_beside(me, weight, blocks, n, order):
    part, columns = weight.shape[0] // n, weight.shape[1]
    vmem = pl.BlockSpec(memory_space=pltpu.VMEM)
    return pl.pallas_call(
        functools.partial(squares_kernel, n, order, len(blocks)),
        out_shape=(
            jax.ShapeDtypeStruct(blocks[0].shape[1:], F32),
            pltpu.VMEM((len(order), part, columns), BF16),
        ),
        in_specs=[
            pl.BlockSpec(memory_space=pltpu.SMEM),
            pl.BlockSpec(memory_space=pltpu.HBM),
        ]
        + [vmem] * len(blocks),
        out_specs=(vmem, vmem),
        scratch_shapes=[pltpu.SemaphoreType.DMA((len(order),))],
        compiler_params=pltpu.CompilerParams(vmem_limit_bytes=4 * 1024 * 1024),
        cost_estimate=hint(len(order) * 0.7),
    )(me, far(weight), *blocks)


def more_squares_kernel(positions_ref, length_ref, place_ref, before, *rest):
    *blocks, squares, cos_ref, sin_ref, allowed_ref = rest
    squares[...] = add_squares(blocks, before[...])
    steps = cos_ref.shape[0]
    lane = lax.broadcasted_iota(jnp.int32, (8, HD), 1)
    step = lax.broadcasted_iota(jnp.int32, (8, HD), 0)
    pair = lax.rem(lane, HD // 2).astype(F32)
    frequency = jnp.exp(-math.log(ROPE_BASE) * 2.0 * pair / HD)
    turns = (positions_ref[0] + step).astype(F32) * frequency
    cos = jnp.cos(turns)
    sin = jnp.where(lane < HD // 2, -1.0, 1.0) * jnp.sin(turns)
    for index in range(steps):
        cos_ref[index] = cos[index : index + 1]
        sin_ref[index] = sin[index : index + 1]
    allowed_ref[...] = jnp.where(place_ref[...] < length_ref[0], 1.0, 0.0)


def more_squares(blocks, before, positions, length, place, steps):
    vmem = pl.BlockSpec(memory_space=pltpu.VMEM)
    smem = pl.BlockSpec(memory_space=pltpu.SMEM)
    turns = jax.ShapeDtypeStruct((steps, 1, HD), F32)
    return pl.pallas_call(
        more_squares_kernel,
        out_shape=(
            jax.ShapeDtypeStruct(before.shape, F32),
            turns,
            turns,
            jax.ShapeDtypeStruct(place.shape, F32),
        ),
        in_specs=[smem, smem] + [vmem] * (len(blocks) + 2),
        out_specs=(vmem,) * 4,
        compiler_params=pltpu.CompilerParams(vmem_limit_bytes=4 * 1024 * 1024),
        cost_estimate=hint(1),
    )(positions, length, place, before, *blocks)


def project_kernel(n, order, me_ref, gain_ref, before_ref, mine_ref, other_ref, weight_ref, *rest):
    *helds, out_ref, last, spread, total, kept, sems = rest
    me = me_ref[0]
    rows, part = before_ref.shape
    copies = fetches(n, order, me, weight_ref, last, sems)
    for copy in copies:
        copy.start()
    places = [(held, slot) for held in helds for slot in range(held.shape[0])]
    early = len(places)
    places += [(last, slot) for slot in range(len(order))]
    blocks = list(zip(slots(n), places, strict=True))

    def products(picked, factor):
        summed = None
        for (entry, core), (held, slot) in picked:
            values = (mine_ref, other_ref)[core][entry].astype(F32)
            normed = (values * factor * gain_ref[owner(me, entry, core, n)]).astype(BF16)
            product = jnp.dot(normed, held[slot], preferred_element_type=F32)
            summed = product if summed is None else summed + product
        return summed

    def row_factor():
        square = add_squares([other_ref], before_ref[...])
        mean = jnp.sum(square, axis=1, keepdims=True) * (1.0 / (n * part))
        return lax.rsqrt(mean + EPS)

    @pl.when(me >= 0)
    def _():
        factor = row_factor()
        total[...] = products(blocks[:early], factor)
        kept[...] = jnp.broadcast_to(factor, kept.shape)

    factor = kept[:, :1]
    summed = total[...]
    half = -(-len(copies) // 2)
    for group in (slice(0, half), slice(half, len(copies))):
        for copy in copies[group]:
            copy.wait()
        summed = summed + products(blocks[early:][group], factor)
    columns = summed.shape[1] // 128
    steps = rows // n
    for block in range(columns):
        for step in range(steps):
            spread[:, step * columns + block, :] = summed[
                step * n : (step + 1) * n, block * 128 : (block + 1) * 128
            ]
    for target in range(n):
        out_ref[target] = spread[target, : steps * columns, :].astype(BF16)


def project(me, block, gain, weight, n, scalars, small, capacity):
    rows, part = block.shape
    columns = weight.shape[1]
    pieces = rows // n * (columns // 128)
    outer, middle = radices(n)
    order = slots(n)
    first, second = n // 4, 5 * n // 8

    arrived = [swap(block, n, o * 2 * middle) for o in range(1, outer)]
    held, gain, weight_a, place, weights, head_gain = fetch(
        me, block, gain, weight, n, order[:first], small, capacity
    )
    row = jnp.stack([held] + arrived)
    later = [swap(row, n, m * 2) for m in range(1, middle)]
    squares, weight_b = squares_beside(me, weight, [row], n, order[first:second])
    later, squares = lax.optimization_barrier((later, squares))
    mine = jnp.concatenate([row] + later)
    other = swap(mine, n, 1)
    squares, cos, sin, allowed = more_squares(later, squares, *scalars, place, rows // n)
    vmem = pl.BlockSpec(memory_space=pltpu.VMEM)
    hbm = pl.BlockSpec(memory_space=pltpu.HBM)
    sent = pl.pallas_call(
        functools.partial(project_kernel, n, order[second:]),
        out_shape=jax.ShapeDtypeStruct((n, pieces, 128), BF16),
        in_specs=[pl.BlockSpec(memory_space=pltpu.SMEM)] + [vmem] * 4 + [hbm] + [vmem] * 2,
        out_specs=vmem,
        scratch_shapes=[
            pltpu.VMEM((n - second, part, columns), BF16),
            pltpu.VMEM((n, -(-pieces // 8) * 8, 128), F32),
            pltpu.VMEM((rows, columns), F32),
            pltpu.VMEM((rows, 128), F32),
            pltpu.SemaphoreType.DMA((n - second,)),
        ],
        compiler_params=pltpu.CompilerParams(vmem_limit_bytes=VMEM_LIMIT),
        cost_estimate=hint(6),
    )(me, gain, squares, mine, other, far(weight), near(weight_a), near(weight_b))
    return sent, (cos, sin, allowed, weights, head_gain)


def attend_kernel(
    received_ref, cos_ref, sin_ref, allowed_ref, lambda_ref, gain_ref,
    keys_one_ref, keys_two_ref, values_ref, out_ref, fresh,
):
    sources, pieces, _ = received_ref.shape
    steps = cos_ref.shape[0]
    blocks = pieces // steps
    pages, page, _ = keys_one_ref.shape
    capacity = pages * page
    for source in range(sources):
        piece = received_ref[source].astype(F32)
        for step in range(steps):
            fresh[step, source * blocks : (source + 1) * blocks, :] = piece[
                step * blocks : (step + 1) * blocks
            ]

    def heads(step, kind):
        return fresh[step, kind * H : (kind + 1) * H, :]

    def rotated(step, kind):
        values = heads(step, kind)
        turned = values * cos_ref[step] + pltpu.roll(values, HD // 2, 1) * sin_ref[step]
        return turned.astype(BF16).astype(F32)

    allowed = allowed_ref[...] > 0.0
    scale = 1.0 / math.sqrt(HD)
    head_row = lax.rem(lax.broadcasted_iota(jnp.int32, (steps * H, HD), 0), H)

    def softmax_map(kind, keys_ref):
        queries = [rotated(step, kind) for step in range(steps)]
        news = [rotated(step, kind + 2) for step in range(steps)]
        stacked = jnp.concatenate(queries, axis=0)
        apart = jnp.concatenate(
            [jnp.where(head_row == h, stacked, 0.0).astype(BF16) for h in range(H)], axis=1
        )
        older = lax.dot_general(
            apart, keys_ref[...].reshape(capacity, H * HD), (((1,), (1,)), ((), ())),
            preferred_element_type=F32,
        )
        older = jnp.where(allowed, older * scale, -1e38)
        parts = []
        for step in range(steps):
            cached = older[step * H : (step + 1) * H]
            newer = [
                jnp.sum(queries[step] * news[e], axis=1, keepdims=True) * scale
                for e in range(step + 1)
            ]
            top = jnp.max(cached, axis=1, keepdims=True)
            for value in newer:
                top = jnp.maximum(top, value)
            cached = jnp.exp(cached - top)
            newer = [jnp.exp(value - top) for value in newer]
            whole = jnp.sum(cached, axis=1, keepdims=True)
            for value in newer:
                whole = whole + value
            parts.append((cached / whole, [value / whole for value in newer]))
        return parts

    first = softmax_map(0, keys_one_ref)
    second = softmax_map(1, keys_two_ref)
    weight = lambda_ref[...]
    mix = jnp.concatenate(
        [first[step][0] - weight * second[step][0] for step in range(steps)], axis=0
    ).astype(BF16)
    spread = jnp.dot(mix, values_ref[...].reshape(capacity, -1), preferred_element_type=F32)
    wide_row = lax.broadcasted_iota(jnp.int32, (H, 2 * HD), 0)
    fresh_values = [
        jnp.concatenate(
            [fresh[e, pl.ds(4 * H + half, H, stride=2), :] for half in range(2)], axis=1
        )
        for e in range(steps)
    ]
    for step in range(steps):
        mixed = jnp.zeros((H, 2 * HD), F32)
        for h in range(H):
            block = spread[step * H : (step + 1) * H, h * 2 * HD : (h + 1) * 2 * HD]
            mixed = jnp.where(wide_row == h, block, mixed)
        for e in range(step + 1):
            share = first[step][1][e] - weight * second[step][1][e]
            mixed = mixed + share.astype(BF16).astype(F32) * fresh_values[e]
        norm = lax.rsqrt(jnp.mean(mixed * mixed, axis=1, keepdims=True) + EPS)
        out_ref[step * H : (step + 1) * H, :] = (mixed * norm * gain_ref[...]).astype(BF16)


def attend(received, cos, sin, allowed, weights, gain, keys_one, keys_two, values):
    steps = cos.shape[0]
    sources, pieces, _ = received.shape
    vmem = pl.BlockSpec(memory_space=pltpu.VMEM)
    held = [near(x) for x in (keys_one, keys_two, values)]
    return pl.pallas_call(
        attend_kernel,
        out_shape=jax.ShapeDtypeStruct((steps * H, 2 * HD), BF16),
        in_specs=[vmem] * 9,
        out_specs=vmem,
        scratch_shapes=[pltpu.VMEM((steps, sources * (pieces // steps), 128), F32)],
        compiler_params=pltpu.CompilerParams(vmem_limit_bytes=VMEM_LIMIT),
        cost_estimate=hint(10),
    )(received, cos, sin, allowed, weights, gain, *held)


def output_kernel(n, me_ref, mine_ref, other_ref, inputs_ref, *rest):
    *weights, out_ref, rows_ref = rest
    me = me_ref[0]
    half, heads, width = mine_ref.shape
    steps = heads // H
    lanes = width // 128
    for entry in range(half):
        for core, ref in ((0, mine_ref), (1, other_ref)):
            start = pl.multiple_of(owner(me, entry, core, n) * heads, 8)
            block = ref[entry].astype(F32)
            for lane in range(lanes):
                rows_ref[lane, pl.ds(start, heads), :] = block[:, lane * 128 : (lane + 1) * 128]
    total = None
    for h in range(H):
        left = jnp.concatenate(
            [
                jnp.concatenate(
                    [rows_ref[lane, pl.ds(step * H + h, n, stride=heads), :] for lane in range(lanes)],
                    axis=1,
                )
                for step in range(steps)
            ],
            axis=0,
        ).astype(BF16)
        held = weights[h * len(weights) // H]
        at = h * width % held.shape[0]
        product = jnp.dot(left, held[at : at + width, :], preferred_element_type=F32)
        total = product if total is None else total + product
    for step in range(steps):
        out_ref[step] = (
            inputs_ref[step].astype(F32) + total[step * n : (step + 1) * n]
        ).astype(BF16)


def keep_kernel(half, block_ref, from_ref, held, to_ref, sem):
    rows = to_ref.shape[0]
    copy = pltpu.make_async_copy(from_ref.at[pl.ds(half * rows, rows), :], to_ref, sem)
    copy.start()
    held[...] = block_ref[...]
    copy.wait()


def keep(block, weight, half, us):
    vmem = pl.BlockSpec(memory_space=pltpu.VMEM)
    return pl.pallas_call(
        functools.partial(keep_kernel, half),
        out_shape=(
            jax.ShapeDtypeStruct(block.shape, block.dtype),
            pltpu.VMEM((weight.shape[0] // 2, weight.shape[1]), weight.dtype),
        ),
        in_specs=[vmem, pl.BlockSpec(memory_space=pltpu.HBM)],
        out_specs=(vmem, vmem),
        scratch_shapes=[pltpu.SemaphoreType.DMA],
        compiler_params=pltpu.CompilerParams(vmem_limit_bytes=4 * 1024 * 1024),
        cost_estimate=hint(us),
    )(block, far(weight))


def output(me, attended, inputs, weight, n):
    kept = []

    def aside(half, block):
        block, part = keep(block, weight, half, 2)
        kept.append(near(part))
        return block

    mine, other = gather_blocks(
        attended, n, functools.partial(aside, 0), functools.partial(aside, 1)
    )
    half, heads, width = mine.shape
    vmem = pl.BlockSpec(memory_space=pltpu.VMEM)
    return pl.pallas_call(
        functools.partial(output_kernel, n),
        out_shape=jax.ShapeDtypeStruct(inputs.shape, BF16),
        in_specs=[pl.BlockSpec(memory_space=pltpu.SMEM)] + [vmem] * 5,
        out_specs=vmem,
        scratch_shapes=[pltpu.VMEM((width // 128, n * heads, 128), F32)],
        compiler_params=pltpu.CompilerParams(vmem_limit_bytes=VMEM_LIMIT),
    )(me, mine, other, inputs, *kept)


def angles(positions, steps):
    half = HD // 2
    frequency = jnp.exp(-math.log(ROPE_BASE) * 2.0 * jnp.arange(half, dtype=F32) / HD)
    places = (positions + jnp.arange(steps, dtype=jnp.int32)).astype(F32)
    turns = places[:, None] * frequency[None, :]
    cosine, sine = jnp.cos(turns), jnp.sin(turns)
    cos = jnp.concatenate([cosine, cosine], axis=-1)
    sin = jnp.concatenate([-sine, sine], axis=-1)
    return cos[:, None, :], sin[:, None, :]


def local(
    n, inputs, norm_gain, qkv_weight, head_lambda, head_gain, out_weight,
    key_one_pages, key_two_pages, value_pages, page_table, context_len, positions,
):
    steps, rows, part = inputs.shape
    me = lax.axis_index("gx").astype(jnp.int32).reshape(1)
    block = inputs.reshape(steps * rows, part)
    capacity = page_table.shape[1] * key_one_pages.shape[1]
    small = (page_table, head_lambda.reshape(1, H), head_gain.reshape(1, H * 2 * HD))
    sent, aside = project(
        me, block, norm_gain.reshape(n, 1, part), qkv_weight, n, (positions, context_len), small,
        capacity,
    )
    received = lax.all_to_all(sent, "gx", 0, 0)
    attended = attend(received, *aside, key_one_pages, key_two_pages, value_pages)
    return output(me, attended, inputs, out_weight, n)


def rotary(vectors, cos, sin):
    return vectors * cos + jnp.roll(vectors, HD // 2, axis=-1) * sin


def local_any(
    n, inputs, norm_gain, qkv_weight, head_lambda, head_gain, out_weight,
    key_one_pages, key_two_pages, value_pages, page_table, context_len, positions,
):
    steps = inputs.shape[0]
    own = page_table.shape[0]
    capacity = page_table.shape[1] * key_one_pages.shape[1]
    values = lax.all_gather(inputs, "gx", axis=2, tiled=True).astype(F32)
    factor = lax.rsqrt(jnp.mean(values * values, axis=-1, keepdims=True) + EPS)
    normed = (values * factor * norm_gain).astype(BF16)
    projected = jnp.einsum("sbd,dc->sbc", normed, qkv_weight, preferred_element_type=F32)
    received = lax.all_to_all(
        projected.astype(BF16), "gx", split_axis=1, concat_axis=2, tiled=True
    )
    cached = tuple(
        pool[page_table].reshape(own, capacity, H, -1)
        for pool in (key_one_pages, key_two_pages, value_pages)
    )
    both = received[..., : 4 * H * HD].reshape(steps, own, 4, H, HD).astype(F32)
    new_values = received[..., 4 * H * HD :].reshape(steps, own, H, 2 * HD)
    cos, sin = jax.vmap(lambda p: angles(p, steps))(positions.reshape(own, 1))
    cos, sin = (jnp.moveaxis(x, 0, 1)[:, :, None] for x in (cos, sin))
    turned = rotary(both, cos, sin).astype(BF16)
    place = jnp.arange(capacity, dtype=jnp.int32)
    allowed = (place[None, :] < context_len[:, None])[None, :, None, :]
    step = jnp.arange(steps)
    newer_allowed = (step[None, :] <= step[:, None])[:, None, None, :]

    def softmax_map(query, keys, news):
        older = jnp.einsum("tshd,sjhd->tshj", query, keys, preferred_element_type=F32)
        newer = jnp.einsum("tshd,eshd->tshe", query, news, preferred_element_type=F32)
        scores = jnp.concatenate(
            [jnp.where(allowed, older, -jnp.inf), jnp.where(newer_allowed, newer, -jnp.inf)], axis=-1
        )
        return jax.nn.softmax(scores * (1.0 / math.sqrt(HD)), axis=-1)

    first = softmax_map(turned[:, :, 0], cached[0], turned[:, :, 2])
    second = softmax_map(turned[:, :, 1], cached[1], turned[:, :, 3])
    mix = (first - head_lambda[:, None] * second).astype(BF16)
    mixed = jnp.einsum(
        "tshj,sjhf->tshf", mix[..., :capacity], cached[2], preferred_element_type=F32
    ) + jnp.einsum("tshe,eshf->tshf", mix[..., capacity:], new_values, preferred_element_type=F32)
    norm = lax.rsqrt(jnp.mean(mixed * mixed, axis=-1, keepdims=True) + EPS)
    grouped = (mixed * norm * head_gain.reshape(H, 2 * HD)).astype(BF16)
    whole = lax.all_gather(grouped.reshape(steps, own, -1), "gx", axis=1, tiled=True)
    branch = jnp.einsum("sbf,fd->sbd", whole, out_weight, preferred_element_type=F32)
    return (inputs.astype(F32) + branch).astype(BF16)


def solution(mesh):
    n = mesh.shape["gx"]
    placed = (
        P(None, "groups", "gx"),
        P(),
        P(None, "gx"),
        P(),
        P(),
        P(None, "gx"),
        P(("groups", "gx"), None, None),
        P(("groups", "gx"), None, None),
        P(("groups", "gx"), None, None),
        P(("groups", "gx"), None),
        P(("groups", "gx")),
        P(("groups", "gx")),
    )

    def chosen(inputs, norm_gain, qkv_weight, *rest):
        aligned = inputs.shape[2] % 128 == 0 and qkv_weight.shape[1] % 128 == 0
        single = rest[6].shape[0] == 1
        power = n >= 4 and n & (n - 1) == 0
        body = local if aligned and single and power else local_any
        return body(n, inputs, norm_gain, qkv_weight, *rest)

    return jax.shard_map(
        chosen, mesh=mesh, in_specs=placed, out_specs=P(None, "groups", "gx"), check_vma=False
    )
```

```python
import functools
import math

import jax
import jax.numpy as jnp
from jax import lax
from jax.experimental import pallas as pl
from jax.experimental.pallas import tpu as pltpu
from jax.sharding import PartitionSpec as P

H = 24
HD = 128
EPS = 1e-05
ROPE_BASE = 10000.0
F32 = jnp.float32
BF16 = jnp.bfloat16
VMEM_LIMIT = 16 * 1024 * 1024


def radices(n):
    rest = n // 2
    middle = 1
    while middle * middle * 4 <= rest:
        middle *= 2
    return rest // middle, middle


def swap(block, n, mask):
    return lax.ppermute(block, "gx", [(i, i ^ mask) for i in range(n)])


def gather_blocks(block, n, first_aside, second_aside):
    outer, middle = radices(n)
    arrived = [swap(block, n, o * 2 * middle) for o in range(outer - 1, 0, -1)]
    rows = jnp.stack([first_aside(block)] + arrived)
    others = [swap(rows, n, m * 2) for m in range(1, middle)]
    rows, others = lax.optimization_barrier((second_aside(rows), others))
    mine = jnp.concatenate([rows] + others)
    return mine, swap(mine, n, 1)


def owner(me, entry, core, n, reverse=False):
    outer, middle = radices(n)
    place = entry % outer
    if reverse:
        place = (outer - place) % outer
    mask = place * (2 * middle) + (entry // outer) * 2 + core
    return jnp.bitwise_xor(me, mask)


def far(x):
    return pltpu.with_memory_space_constraint(x, pltpu.HBM)


def hint(us):
    return pl.CostEstimate(flops=0, bytes_accessed=int(us * 3_000_000), transcendentals=0)


def slots(n):
    return [(entry, core) for core in range(2) for entry in range(n // 2)]


def fetches(n, order, me, from_ref, to_ref, sems):
    part = from_ref.shape[0] // n
    copies = []
    for slot, (entry, core) in enumerate(order):
        start = pl.multiple_of(owner(me, entry, core, n) * part, part)
        copies.append(
            pltpu.make_async_copy(
                from_ref.at[pl.ds(start, part), :], to_ref.at[slot], sems.at[slot]
            )
        )
    return copies


def fetch_kernel(n, order, *rest):
    (
        me_ref, block_ref, gain_ref, weight_ref, table_ref, lambda_ref, head_gain_ref,
        held, gain_out, weight_out, place_ref, lambda_out, head_gain_out,
        table, row_ref, wide_ref, sems, other_sems,
    ) = rest
    small = [
        pltpu.make_async_copy(start, end, other_sems.at[index])
        for index, (start, end) in enumerate(
            (
                (table_ref, table),
                (lambda_ref, row_ref),
                (head_gain_ref, wide_ref),
                (block_ref, held),
                (gain_ref, gain_out),
            )
        )
    ]
    large = fetches(n, order, me_ref[0], weight_ref, weight_out, sems)
    for copy in small + large:
        copy.start()
    for copy in small:
        copy.wait()

    capacity = place_ref.shape[1]
    pages = table_ref.shape[1]
    page = capacity // pages
    row = lax.broadcasted_iota(jnp.int32, (1, capacity), 1)
    place = jnp.zeros((1, capacity), jnp.int32)
    for index in range(pages):
        first = table[0, index] * page
        inside = (row >= first) & (row < first + page)
        place = jnp.where(inside, row - first + index * page, place)
    place_ref[...] = place
    across = lax.broadcasted_iota(jnp.int32, (H, H), 1) == lax.broadcasted_iota(jnp.int32, (H, H), 0)
    lambda_out[...] = jnp.sum(jnp.where(across, row_ref[...], 0.0), axis=1, keepdims=True)
    for h in range(H):
        head_gain_out[h : h + 1, :] = wide_ref[:, h * 2 * HD : (h + 1) * 2 * HD]

    for copy in large:
        copy.wait()


def fetch(me, block, gain, weight, n, order, small, capacity):
    part, columns = weight.shape[0] // n, weight.shape[1]
    vmem = pl.BlockSpec(memory_space=pltpu.VMEM)
    hbm = pl.BlockSpec(memory_space=pltpu.HBM)
    table, weights, head_gain = small
    return pl.pallas_call(
        functools.partial(fetch_kernel, n, order),
        out_shape=(
            pltpu.VMEM(block.shape, BF16),
            pltpu.VMEM(gain.shape, F32),
            pltpu.VMEM((len(order), part, columns), BF16),
            jax.ShapeDtypeStruct((1, capacity), jnp.int32),
            jax.ShapeDtypeStruct((H, 1), F32),
            jax.ShapeDtypeStruct((H, 2 * HD), F32),
        ),
        in_specs=[pl.BlockSpec(memory_space=pltpu.SMEM)] + [hbm] * 6,
        out_specs=(vmem,) * 6,
        scratch_shapes=[
            pltpu.SMEM(table.shape, table.dtype),
            pltpu.VMEM(weights.shape, F32),
            pltpu.VMEM(head_gain.shape, F32),
            pltpu.SemaphoreType.DMA((len(order),)),
            pltpu.SemaphoreType.DMA((5,)),
        ],
        compiler_params=pltpu.CompilerParams(vmem_limit_bytes=4 * 1024 * 1024),
        cost_estimate=hint(5),
    )(me, far(block), far(gain), far(weight), *map(far, small))


def near(x):
    return pltpu.with_memory_space_constraint(x, pltpu.VMEM)


def add_squares(refs, square):
    for ref in refs:
        for entry in range(ref.shape[0]):
            values = ref[entry].astype(F32)
            square = square + values * values
    return square


def squares_kernel(n, order, count, me_ref, weight_ref, *rest):
    blocks, (squares, weight_out, sems) = rest[:count], rest[count:]
    copies = fetches(n, order, me_ref[0], weight_ref, weight_out, sems)
    for copy in copies:
        copy.start()
    squares[...] = add_squares(blocks, jnp.zeros(squares.shape, F32))
    for copy in copies:
        copy.wait()


def squares_beside(me, weight, blocks, n, order):
    part, columns = weight.shape[0] // n, weight.shape[1]
    vmem = pl.BlockSpec(memory_space=pltpu.VMEM)
    return pl.pallas_call(
        functools.partial(squares_kernel, n, order, len(blocks)),
        out_shape=(
            jax.ShapeDtypeStruct(blocks[0].shape[1:], F32),
            pltpu.VMEM((len(order), part, columns), BF16),
        ),
        in_specs=[
            pl.BlockSpec(memory_space=pltpu.SMEM),
            pl.BlockSpec(memory_space=pltpu.HBM),
        ]
        + [vmem] * len(blocks),
        out_specs=(vmem, vmem),
        scratch_shapes=[pltpu.SemaphoreType.DMA((len(order),))],
        compiler_params=pltpu.CompilerParams(vmem_limit_bytes=4 * 1024 * 1024),
        cost_estimate=hint(len(order) * 0.7),
    )(me, far(weight), *blocks)


def more_squares_kernel(positions_ref, length_ref, place_ref, before, *rest):
    *blocks, squares, cos_ref, sin_ref, allowed_ref = rest
    squares[...] = add_squares(blocks, before[...])
    steps = cos_ref.shape[0]
    lane = lax.broadcasted_iota(jnp.int32, (8, HD), 1)
    step = lax.broadcasted_iota(jnp.int32, (8, HD), 0)
    pair = lax.rem(lane, HD // 2).astype(F32)
    frequency = jnp.exp(-math.log(ROPE_BASE) * 2.0 * pair / HD)
    turns = (positions_ref[0] + step).astype(F32) * frequency
    cos = jnp.cos(turns)
    sin = jnp.where(lane < HD // 2, -1.0, 1.0) * jnp.sin(turns)
    for index in range(steps):
        cos_ref[index] = cos[index : index + 1]
        sin_ref[index] = sin[index : index + 1]
    allowed_ref[...] = jnp.where(place_ref[...] < length_ref[0], 1.0, 0.0)


def more_squares(blocks, before, positions, length, place, steps):
    vmem = pl.BlockSpec(memory_space=pltpu.VMEM)
    smem = pl.BlockSpec(memory_space=pltpu.SMEM)
    turns = jax.ShapeDtypeStruct((steps, 1, HD), F32)
    return pl.pallas_call(
        more_squares_kernel,
        out_shape=(
            jax.ShapeDtypeStruct(before.shape, F32),
            turns,
            turns,
            jax.ShapeDtypeStruct(place.shape, F32),
        ),
        in_specs=[smem, smem] + [vmem] * (len(blocks) + 2),
        out_specs=(vmem,) * 4,
        compiler_params=pltpu.CompilerParams(vmem_limit_bytes=4 * 1024 * 1024),
        cost_estimate=hint(1),
    )(positions, length, place, before, *blocks)


def project_kernel(n, order, me_ref, gain_ref, before_ref, mine_ref, other_ref, weight_ref, *rest):
    *helds, out_ref, last, spread, total, kept, sems = rest
    me = me_ref[0]
    rows, part = before_ref.shape
    copies = fetches(n, order, me, weight_ref, last, sems)
    for copy in copies:
        copy.start()
    places = [(held, slot) for held in helds for slot in range(held.shape[0])]
    early = len(places)
    places += [(last, slot) for slot in range(len(order))]
    blocks = list(zip(slots(n), places, strict=True))

    def products(picked, factor):
        summed = None
        for (entry, core), (held, slot) in picked:
            values = (mine_ref, other_ref)[core][entry].astype(F32)
            normed = (values * factor * gain_ref[owner(me, entry, core, n)]).astype(BF16)
            product = jnp.dot(normed, held[slot], preferred_element_type=F32)
            summed = product if summed is None else summed + product
        return summed

    def row_factor():
        square = add_squares([other_ref], before_ref[...])
        mean = jnp.sum(square, axis=1, keepdims=True) * (1.0 / (n * part))
        return lax.rsqrt(mean + EPS)

    @pl.when(me >= 0)
    def _():
        factor = row_factor()
        total[...] = products(blocks[:early], factor)
        kept[...] = jnp.broadcast_to(factor, kept.shape)

    for copy in copies:
        copy.wait()
    factor = kept[:, :1]
    summed = total[...] + products(blocks[early:], factor)
    columns = summed.shape[1] // 128
    steps = rows // n
    for block in range(columns):
        for step in range(steps):
            spread[:, step * columns + block, :] = summed[
                step * n : (step + 1) * n, block * 128 : (block + 1) * 128
            ]
    for target in range(n):
        out_ref[target] = spread[target, : steps * columns, :].astype(BF16)


def project(me, block, gain, weight, n, scalars, small, capacity):
    rows, part = block.shape
    columns = weight.shape[1]
    pieces = rows // n * (columns // 128)
    outer, middle = radices(n)
    order = slots(n)
    first, second = n // 4, 3 * n // 4

    arrived = [swap(block, n, o * 2 * middle) for o in range(1, outer)]
    held, gain, weight_a, place, weights, head_gain = fetch(
        me, block, gain, weight, n, order[:first], small, capacity
    )
    row = jnp.stack([held] + arrived)
    later = [swap(row, n, m * 2) for m in range(1, middle)]
    squares, weight_b = squares_beside(me, weight, [row], n, order[first:second])
    later, squares = lax.optimization_barrier((later, squares))
    mine = jnp.concatenate([row] + later)
    other = swap(mine, n, 1)
    squares, cos, sin, allowed = more_squares(later, squares, *scalars, place, rows // n)
    vmem = pl.BlockSpec(memory_space=pltpu.VMEM)
    hbm = pl.BlockSpec(memory_space=pltpu.HBM)
    sent = pl.pallas_call(
        functools.partial(project_kernel, n, order[second:]),
        out_shape=jax.ShapeDtypeStruct((n, pieces, 128), BF16),
        in_specs=[pl.BlockSpec(memory_space=pltpu.SMEM)] + [vmem] * 4 + [hbm] + [vmem] * 2,
        out_specs=vmem,
        scratch_shapes=[
            pltpu.VMEM((n - second, part, columns), BF16),
            pltpu.VMEM((n, -(-pieces // 8) * 8, 128), F32),
            pltpu.VMEM((rows, columns), F32),
            pltpu.VMEM((rows, 128), F32),
            pltpu.SemaphoreType.DMA((n - second,)),
        ],
        compiler_params=pltpu.CompilerParams(vmem_limit_bytes=VMEM_LIMIT),
        cost_estimate=hint(6),
    )(me, gain, squares, mine, other, far(weight), near(weight_a), near(weight_b))
    return sent, (cos, sin, allowed, weights, head_gain)


def attend_kernel(
    received_ref, cos_ref, sin_ref, allowed_ref, lambda_ref, gain_ref,
    keys_one_ref, keys_two_ref, values_ref, out_ref, fresh,
):
    sources, pieces, _ = received_ref.shape
    steps = cos_ref.shape[0]
    blocks = pieces // steps
    pages, page, _ = keys_one_ref.shape
    capacity = pages * page
    for source in range(sources):
        piece = received_ref[source].astype(F32)
        for step in range(steps):
            fresh[step, source * blocks : (source + 1) * blocks, :] = piece[
                step * blocks : (step + 1) * blocks
            ]

    def heads(step, kind):
        return fresh[step, kind * H : (kind + 1) * H, :]

    def rotated(step, kind):
        values = heads(step, kind)
        turned = values * cos_ref[step] + pltpu.roll(values, HD // 2, 1) * sin_ref[step]
        return turned.astype(BF16).astype(F32)

    allowed = allowed_ref[...] > 0.0
    scale = 1.0 / math.sqrt(HD)
    head_row = lax.rem(lax.broadcasted_iota(jnp.int32, (steps * H, HD), 0), H)

    def softmax_map(kind, keys_ref):
        queries = [rotated(step, kind) for step in range(steps)]
        news = [rotated(step, kind + 2) for step in range(steps)]
        stacked = jnp.concatenate(queries, axis=0)
        apart = jnp.concatenate(
            [jnp.where(head_row == h, stacked, 0.0).astype(BF16) for h in range(H)], axis=1
        )
        older = lax.dot_general(
            apart, keys_ref[...].reshape(capacity, H * HD), (((1,), (1,)), ((), ())),
            preferred_element_type=F32,
        )
        older = jnp.where(allowed, older * scale, -1e38)
        parts = []
        for step in range(steps):
            cached = older[step * H : (step + 1) * H]
            newer = [
                jnp.sum(queries[step] * news[e], axis=1, keepdims=True) * scale
                for e in range(step + 1)
            ]
            top = jnp.max(cached, axis=1, keepdims=True)
            for value in newer:
                top = jnp.maximum(top, value)
            cached = jnp.exp(cached - top)
            newer = [jnp.exp(value - top) for value in newer]
            whole = jnp.sum(cached, axis=1, keepdims=True)
            for value in newer:
                whole = whole + value
            parts.append((cached / whole, [value / whole for value in newer]))
        return parts

    first = softmax_map(0, keys_one_ref)
    second = softmax_map(1, keys_two_ref)
    weight = lambda_ref[...]
    mix = jnp.concatenate(
        [first[step][0] - weight * second[step][0] for step in range(steps)], axis=0
    ).astype(BF16)
    spread = jnp.dot(mix, values_ref[...].reshape(capacity, -1), preferred_element_type=F32)
    wide_row = lax.broadcasted_iota(jnp.int32, (H, 2 * HD), 0)
    fresh_values = [
        jnp.concatenate(
            [fresh[e, pl.ds(4 * H + half, H, stride=2), :] for half in range(2)], axis=1
        )
        for e in range(steps)
    ]
    for step in range(steps):
        mixed = jnp.zeros((H, 2 * HD), F32)
        for h in range(H):
            block = spread[step * H : (step + 1) * H, h * 2 * HD : (h + 1) * 2 * HD]
            mixed = jnp.where(wide_row == h, block, mixed)
        for e in range(step + 1):
            share = first[step][1][e] - weight * second[step][1][e]
            mixed = mixed + share.astype(BF16).astype(F32) * fresh_values[e]
        norm = lax.rsqrt(jnp.mean(mixed * mixed, axis=1, keepdims=True) + EPS)
        out_ref[step * H : (step + 1) * H, :] = (mixed * norm * gain_ref[...]).astype(BF16)


def attend(received, cos, sin, allowed, weights, gain, keys_one, keys_two, values):
    steps = cos.shape[0]
    sources, pieces, _ = received.shape
    vmem = pl.BlockSpec(memory_space=pltpu.VMEM)
    held = [near(x) for x in (keys_one, keys_two, values)]
    return pl.pallas_call(
        attend_kernel,
        out_shape=jax.ShapeDtypeStruct((steps * H, 2 * HD), BF16),
        in_specs=[vmem] * 9,
        out_specs=vmem,
        scratch_shapes=[pltpu.VMEM((steps, sources * (pieces // steps), 128), F32)],
        compiler_params=pltpu.CompilerParams(vmem_limit_bytes=VMEM_LIMIT),
        cost_estimate=hint(10),
    )(received, cos, sin, allowed, weights, gain, *held)


def output_kernel(n, me_ref, mine_ref, other_ref, inputs_ref, *rest):
    *weights, out_ref, rows_ref = rest
    me = me_ref[0]
    half, heads, width = mine_ref.shape
    steps = heads // H
    lanes = width // 128
    for entry in range(half):
        for core, ref in ((0, mine_ref), (1, other_ref)):
            start = pl.multiple_of(owner(me, entry, core, n, True) * heads, 8)
            block = ref[entry].astype(F32)
            for lane in range(lanes):
                rows_ref[lane, pl.ds(start, heads), :] = block[:, lane * 128 : (lane + 1) * 128]
    total = None
    for h in range(H):
        left = jnp.concatenate(
            [
                jnp.concatenate(
                    [rows_ref[lane, pl.ds(step * H + h, n, stride=heads), :] for lane in range(lanes)],
                    axis=1,
                )
                for step in range(steps)
            ],
            axis=0,
        ).astype(BF16)
        held = weights[h * len(weights) // H]
        at = h * width % held.shape[0]
        product = jnp.dot(left, held[at : at + width, :], preferred_element_type=F32)
        total = product if total is None else total + product
    for step in range(steps):
        out_ref[step] = (
            inputs_ref[step].astype(F32) + total[step * n : (step + 1) * n]
        ).astype(BF16)


def keep_kernel(half, block_ref, from_ref, held, to_ref, sem):
    rows = to_ref.shape[0]
    copy = pltpu.make_async_copy(from_ref.at[pl.ds(half * rows, rows), :], to_ref, sem)
    copy.start()
    held[...] = block_ref[...]
    copy.wait()


def keep(block, weight, half, us):
    vmem = pl.BlockSpec(memory_space=pltpu.VMEM)
    return pl.pallas_call(
        functools.partial(keep_kernel, half),
        out_shape=(
            jax.ShapeDtypeStruct(block.shape, block.dtype),
            pltpu.VMEM((weight.shape[0] // 2, weight.shape[1]), weight.dtype),
        ),
        in_specs=[vmem, pl.BlockSpec(memory_space=pltpu.HBM)],
        out_specs=(vmem, vmem),
        scratch_shapes=[pltpu.SemaphoreType.DMA],
        compiler_params=pltpu.CompilerParams(vmem_limit_bytes=4 * 1024 * 1024),
        cost_estimate=hint(us),
    )(block, far(weight))


def output(me, attended, inputs, weight, n):
    kept = []

    def aside(half, block):
        block, part = keep(block, weight, half, 2)
        kept.append(near(part))
        return block

    mine, other = gather_blocks(
        attended, n, functools.partial(aside, 0), functools.partial(aside, 1)
    )
    half, heads, width = mine.shape
    vmem = pl.BlockSpec(memory_space=pltpu.VMEM)
    return pl.pallas_call(
        functools.partial(output_kernel, n),
        out_shape=jax.ShapeDtypeStruct(inputs.shape, BF16),
        in_specs=[pl.BlockSpec(memory_space=pltpu.SMEM)] + [vmem] * 5,
        out_specs=vmem,
        scratch_shapes=[pltpu.VMEM((width // 128, n * heads, 128), F32)],
        compiler_params=pltpu.CompilerParams(vmem_limit_bytes=VMEM_LIMIT),
    )(me, mine, other, inputs, *kept)


def angles(positions, steps):
    half = HD // 2
    frequency = jnp.exp(-math.log(ROPE_BASE) * 2.0 * jnp.arange(half, dtype=F32) / HD)
    places = (positions + jnp.arange(steps, dtype=jnp.int32)).astype(F32)
    turns = places[:, None] * frequency[None, :]
    cosine, sine = jnp.cos(turns), jnp.sin(turns)
    cos = jnp.concatenate([cosine, cosine], axis=-1)
    sin = jnp.concatenate([-sine, sine], axis=-1)
    return cos[:, None, :], sin[:, None, :]


def local(
    n, inputs, norm_gain, qkv_weight, head_lambda, head_gain, out_weight,
    key_one_pages, key_two_pages, value_pages, page_table, context_len, positions,
):
    steps, rows, part = inputs.shape
    me = lax.axis_index("gx").astype(jnp.int32).reshape(1)
    block = inputs.reshape(steps * rows, part)
    capacity = page_table.shape[1] * key_one_pages.shape[1]
    small = (page_table, head_lambda.reshape(1, H), head_gain.reshape(1, H * 2 * HD))
    sent, aside = project(
        me, block, norm_gain.reshape(n, 1, part), qkv_weight, n, (positions, context_len), small,
        capacity,
    )
    received = lax.all_to_all(sent, "gx", 0, 0)
    attended = attend(received, *aside, key_one_pages, key_two_pages, value_pages)
    return output(me, attended, inputs, out_weight, n)


def rotary(vectors, cos, sin):
    return vectors * cos + jnp.roll(vectors, HD // 2, axis=-1) * sin


def local_any(
    n, inputs, norm_gain, qkv_weight, head_lambda, head_gain, out_weight,
    key_one_pages, key_two_pages, value_pages, page_table, context_len, positions,
):
    steps = inputs.shape[0]
    own = page_table.shape[0]
    capacity = page_table.shape[1] * key_one_pages.shape[1]
    values = lax.all_gather(inputs, "gx", axis=2, tiled=True).astype(F32)
    factor = lax.rsqrt(jnp.mean(values * values, axis=-1, keepdims=True) + EPS)
    normed = (values * factor * norm_gain).astype(BF16)
    projected = jnp.einsum("sbd,dc->sbc", normed, qkv_weight, preferred_element_type=F32)
    received = lax.all_to_all(
        projected.astype(BF16), "gx", split_axis=1, concat_axis=2, tiled=True
    )
    cached = tuple(
        pool[page_table].reshape(own, capacity, H, -1)
        for pool in (key_one_pages, key_two_pages, value_pages)
    )
    both = received[..., : 4 * H * HD].reshape(steps, own, 4, H, HD).astype(F32)
    new_values = received[..., 4 * H * HD :].reshape(steps, own, H, 2 * HD)
    cos, sin = jax.vmap(lambda p: angles(p, steps))(positions.reshape(own, 1))
    cos, sin = (jnp.moveaxis(x, 0, 1)[:, :, None] for x in (cos, sin))
    turned = rotary(both, cos, sin).astype(BF16)
    place = jnp.arange(capacity, dtype=jnp.int32)
    allowed = (place[None, :] < context_len[:, None])[None, :, None, :]
    step = jnp.arange(steps)
    newer_allowed = (step[None, :] <= step[:, None])[:, None, None, :]

    def softmax_map(query, keys, news):
        older = jnp.einsum("tshd,sjhd->tshj", query, keys, preferred_element_type=F32)
        newer = jnp.einsum("tshd,eshd->tshe", query, news, preferred_element_type=F32)
        scores = jnp.concatenate(
            [jnp.where(allowed, older, -jnp.inf), jnp.where(newer_allowed, newer, -jnp.inf)], axis=-1
        )
        return jax.nn.softmax(scores * (1.0 / math.sqrt(HD)), axis=-1)

    first = softmax_map(turned[:, :, 0], cached[0], turned[:, :, 2])
    second = softmax_map(turned[:, :, 1], cached[1], turned[:, :, 3])
    mix = (first - head_lambda[:, None] * second).astype(BF16)
    mixed = jnp.einsum(
        "tshj,sjhf->tshf", mix[..., :capacity], cached[2], preferred_element_type=F32
    ) + jnp.einsum("tshe,eshf->tshf", mix[..., capacity:], new_values, preferred_element_type=F32)
    norm = lax.rsqrt(jnp.mean(mixed * mixed, axis=-1, keepdims=True) + EPS)
    grouped = (mixed * norm * head_gain.reshape(H, 2 * HD)).astype(BF16)
    whole = lax.all_gather(grouped.reshape(steps, own, -1), "gx", axis=1, tiled=True)
    branch = jnp.einsum("sbf,fd->sbd", whole, out_weight, preferred_element_type=F32)
    return (inputs.astype(F32) + branch).astype(BF16)


def solution(mesh):
    n = mesh.shape["gx"]
    placed = (
        P(None, "groups", "gx"),
        P(),
        P(None, "gx"),
        P(),
        P(),
        P(None, "gx"),
        P(("groups", "gx"), None, None),
        P(("groups", "gx"), None, None),
        P(("groups", "gx"), None, None),
        P(("groups", "gx"), None),
        P(("groups", "gx")),
        P(("groups", "gx")),
    )

    def chosen(inputs, norm_gain, qkv_weight, *rest):
        aligned = inputs.shape[2] % 128 == 0 and qkv_weight.shape[1] % 128 == 0
        single = rest[6].shape[0] == 1
        power = n >= 4 and n & (n - 1) == 0
        body = local if aligned and single and power else local_any
        return body(n, inputs, norm_gain, qkv_weight, *rest)

    return jax.shard_map(
        chosen, mesh=mesh, in_specs=placed, out_specs=P(None, "groups", "gx"), check_vma=False
    )
```

```python
import functools
import math

import jax
import jax.numpy as jnp
from jax import lax
from jax.experimental import pallas as pl
from jax.experimental.pallas import tpu as pltpu
from jax.sharding import PartitionSpec as P

H = 24
HD = 128
EPS = 1e-05
ROPE_BASE = 10000.0
F32 = jnp.float32
BF16 = jnp.bfloat16
VMEM_LIMIT = 16 * 1024 * 1024


def radices(n):
    rest = n // 2
    middle = 1
    while middle * middle * 4 <= rest:
        middle *= 2
    return rest // middle, middle


def swap(block, n, mask):
    return lax.ppermute(block, "gx", [(i, i ^ mask) for i in range(n)])


def gather_blocks(block, n, first_aside, second_aside):
    outer, middle = radices(n)
    arrived = [swap(block, n, m * 2) for m in range(1, middle)]
    rows = jnp.stack([first_aside(block)] + arrived)
    others = [swap(rows, n, o * 2 * middle) for o in range(1, outer)]
    rows, others = lax.optimization_barrier((second_aside(rows), others))
    mine = jnp.concatenate([rows] + others)
    return mine, swap(mine, n, 1)


def owner(me, entry, core, n):
    outer, middle = radices(n)
    mask = (entry % outer) * (2 * middle) + (entry // outer) * 2 + core
    return jnp.bitwise_xor(me, mask)


def far(x):
    return pltpu.with_memory_space_constraint(x, pltpu.HBM)


def hint(us):
    return pl.CostEstimate(flops=0, bytes_accessed=int(us * 3_000_000), transcendentals=0)


def slots(n):
    return [(entry, core) for core in range(2) for entry in range(n // 2)]


def fetches(n, order, me, from_ref, to_ref, sems):
    part = from_ref.shape[0] // n
    copies = []
    for slot, (entry, core) in enumerate(order):
        start = pl.multiple_of(owner(me, entry, core, n) * part, part)
        copies.append(
            pltpu.make_async_copy(
                from_ref.at[pl.ds(start, part), :], to_ref.at[slot], sems.at[slot]
            )
        )
    return copies


def fetch_kernel(n, order, *rest):
    (
        me_ref, block_ref, gain_ref, weight_ref, table_ref, lambda_ref, head_gain_ref,
        held, gain_out, weight_out, place_ref, lambda_out, head_gain_out,
        table, row_ref, wide_ref, sems, other_sems,
    ) = rest
    small = [
        pltpu.make_async_copy(start, end, other_sems.at[index])
        for index, (start, end) in enumerate(
            (
                (table_ref, table),
                (lambda_ref, row_ref),
                (head_gain_ref, wide_ref),
                (block_ref, held),
                (gain_ref, gain_out),
            )
        )
    ]
    large = fetches(n, order, me_ref[0], weight_ref, weight_out, sems)
    for copy in small + large:
        copy.start()
    for copy in small:
        copy.wait()

    capacity = place_ref.shape[1]
    pages = table_ref.shape[1]
    page = capacity // pages
    row = lax.broadcasted_iota(jnp.int32, (1, capacity), 1)
    place = jnp.zeros((1, capacity), jnp.int32)
    for index in range(pages):
        first = table[0, index] * page
        inside = (row >= first) & (row < first + page)
        place = jnp.where(inside, row - first + index * page, place)
    place_ref[...] = place
    across = lax.broadcasted_iota(jnp.int32, (H, H), 1) == lax.broadcasted_iota(jnp.int32, (H, H), 0)
    lambda_out[...] = jnp.sum(jnp.where(across, row_ref[...], 0.0), axis=1, keepdims=True)
    for h in range(H):
        head_gain_out[h : h + 1, :] = wide_ref[:, h * 2 * HD : (h + 1) * 2 * HD]

    for copy in large:
        copy.wait()


def fetch(me, block, gain, weight, n, order, small, capacity):
    part, columns = weight.shape[0] // n, weight.shape[1]
    vmem = pl.BlockSpec(memory_space=pltpu.VMEM)
    hbm = pl.BlockSpec(memory_space=pltpu.HBM)
    table, weights, head_gain = small
    return pl.pallas_call(
        functools.partial(fetch_kernel, n, order),
        out_shape=(
            pltpu.VMEM(block.shape, BF16),
            pltpu.VMEM(gain.shape, F32),
            pltpu.VMEM((len(order), part, columns), BF16),
            jax.ShapeDtypeStruct((1, capacity), jnp.int32),
            jax.ShapeDtypeStruct((H, 1), F32),
            jax.ShapeDtypeStruct((H, 2 * HD), F32),
        ),
        in_specs=[pl.BlockSpec(memory_space=pltpu.SMEM)] + [hbm] * 6,
        out_specs=(vmem,) * 6,
        scratch_shapes=[
            pltpu.SMEM(table.shape, table.dtype),
            pltpu.VMEM(weights.shape, F32),
            pltpu.VMEM(head_gain.shape, F32),
            pltpu.SemaphoreType.DMA((len(order),)),
            pltpu.SemaphoreType.DMA((5,)),
        ],
        compiler_params=pltpu.CompilerParams(vmem_limit_bytes=4 * 1024 * 1024),
        cost_estimate=hint(5),
    )(me, far(block), far(gain), far(weight), *map(far, small))


def near(x):
    return pltpu.with_memory_space_constraint(x, pltpu.VMEM)


def add_squares(refs, square):
    for ref in refs:
        for entry in range(ref.shape[0]):
            values = ref[entry].astype(F32)
            square = square + values * values
    return square


def squares_kernel(n, order, count, me_ref, weight_ref, *rest):
    blocks, (squares, weight_out, sems) = rest[:count], rest[count:]
    copies = fetches(n, order, me_ref[0], weight_ref, weight_out, sems)
    for copy in copies:
        copy.start()
    squares[...] = add_squares(blocks, jnp.zeros(squares.shape, F32))
    for copy in copies:
        copy.wait()


def squares_beside(me, weight, blocks, n, order):
    part, columns = weight.shape[0] // n, weight.shape[1]
    vmem = pl.BlockSpec(memory_space=pltpu.VMEM)
    return pl.pallas_call(
        functools.partial(squares_kernel, n, order, len(blocks)),
        out_shape=(
            jax.ShapeDtypeStruct(blocks[0].shape[1:], F32),
            pltpu.VMEM((len(order), part, columns), BF16),
        ),
        in_specs=[
            pl.BlockSpec(memory_space=pltpu.SMEM),
            pl.BlockSpec(memory_space=pltpu.HBM),
        ]
        + [vmem] * len(blocks),
        out_specs=(vmem, vmem),
        scratch_shapes=[pltpu.SemaphoreType.DMA((len(order),))],
        compiler_params=pltpu.CompilerParams(vmem_limit_bytes=4 * 1024 * 1024),
        cost_estimate=hint(len(order) * 0.7),
    )(me, far(weight), *blocks)


def more_squares_kernel(positions_ref, length_ref, place_ref, before, *rest):
    *blocks, squares, cos_ref, sin_ref, allowed_ref = rest
    squares[...] = add_squares(blocks, before[...])
    steps = cos_ref.shape[0]
    lane = lax.broadcasted_iota(jnp.int32, (8, HD), 1)
    step = lax.broadcasted_iota(jnp.int32, (8, HD), 0)
    pair = lax.rem(lane, HD // 2).astype(F32)
    frequency = jnp.exp(-math.log(ROPE_BASE) * 2.0 * pair / HD)
    turns = (positions_ref[0] + step).astype(F32) * frequency
    cos = jnp.cos(turns)
    sin = jnp.where(lane < HD // 2, -1.0, 1.0) * jnp.sin(turns)
    for index in range(steps):
        cos_ref[index] = cos[index : index + 1]
        sin_ref[index] = sin[index : index + 1]
    allowed_ref[...] = jnp.where(place_ref[...] < length_ref[0], 1.0, 0.0)


def more_squares(blocks, before, positions, length, place, steps):
    vmem = pl.BlockSpec(memory_space=pltpu.VMEM)
    smem = pl.BlockSpec(memory_space=pltpu.SMEM)
    turns = jax.ShapeDtypeStruct((steps, 1, HD), F32)
    return pl.pallas_call(
        more_squares_kernel,
        out_shape=(
            jax.ShapeDtypeStruct(before.shape, F32),
            turns,
            turns,
            jax.ShapeDtypeStruct(place.shape, F32),
        ),
        in_specs=[smem, smem] + [vmem] * (len(blocks) + 2),
        out_specs=(vmem,) * 4,
        compiler_params=pltpu.CompilerParams(vmem_limit_bytes=4 * 1024 * 1024),
        cost_estimate=hint(1),
    )(positions, length, place, before, *blocks)


def project_kernel(n, order, me_ref, gain_ref, before_ref, mine_ref, other_ref, weight_ref, *rest):
    *helds, out_ref, last, spread, total, kept, sems = rest
    me = me_ref[0]
    rows, part = before_ref.shape
    copies = fetches(n, order, me, weight_ref, last, sems)
    for copy in copies:
        copy.start()
    places = [(held, slot) for held in helds for slot in range(held.shape[0])]
    early = len(places)
    places += [(last, slot) for slot in range(len(order))]
    blocks = list(zip(slots(n), places, strict=True))

    def products(picked, factor):
        summed = None
        for (entry, core), (held, slot) in picked:
            values = (mine_ref, other_ref)[core][entry].astype(F32)
            normed = (values * factor * gain_ref[owner(me, entry, core, n)]).astype(BF16)
            product = jnp.dot(normed, held[slot], preferred_element_type=F32)
            summed = product if summed is None else summed + product
        return summed

    def row_factor():
        square = add_squares([other_ref], before_ref[...])
        mean = jnp.sum(square, axis=1, keepdims=True) * (1.0 / (n * part))
        return lax.rsqrt(mean + EPS)

    @pl.when(me >= 0)
    def _():
        factor = row_factor()
        total[...] = products(blocks[:early], factor)
        kept[...] = jnp.broadcast_to(factor, kept.shape)

    for copy in copies:
        copy.wait()
    factor = kept[:, :1]
    summed = total[...] + products(blocks[early:], factor)
    columns = summed.shape[1] // 128
    steps = rows // n
    for block in range(columns):
        for step in range(steps):
            spread[:, step * columns + block, :] = summed[
                step * n : (step + 1) * n, block * 128 : (block + 1) * 128
            ]
    for target in range(n):
        out_ref[target] = spread[target, : steps * columns, :].astype(BF16)


def project(me, block, gain, weight, n, scalars, small, capacity):
    rows, part = block.shape
    columns = weight.shape[1]
    pieces = rows // n * (columns // 128)
    outer, middle = radices(n)
    order = slots(n)
    first, second = n // 4, 3 * n // 4

    arrived = [swap(block, n, o * 2 * middle) for o in range(1, outer)]
    held, gain, weight_a, place, weights, head_gain = fetch(
        me, block, gain, weight, n, order[:first], small, capacity
    )
    row = jnp.stack([held] + arrived)
    later = [swap(row, n, m * 2) for m in range(1, middle)]
    squares, weight_b = squares_beside(me, weight, [row], n, order[first:second])
    later, squares = lax.optimization_barrier((later, squares))
    mine = jnp.concatenate([row] + later)
    other = swap(mine, n, 1)
    squares, cos, sin, allowed = more_squares(later, squares, *scalars, place, rows // n)
    vmem = pl.BlockSpec(memory_space=pltpu.VMEM)
    hbm = pl.BlockSpec(memory_space=pltpu.HBM)
    sent = pl.pallas_call(
        functools.partial(project_kernel, n, order[second:]),
        out_shape=jax.ShapeDtypeStruct((n, pieces, 128), BF16),
        in_specs=[pl.BlockSpec(memory_space=pltpu.SMEM)] + [vmem] * 4 + [hbm] + [vmem] * 2,
        out_specs=vmem,
        scratch_shapes=[
            pltpu.VMEM((n - second, part, columns), BF16),
            pltpu.VMEM((n, -(-pieces // 8) * 8, 128), F32),
            pltpu.VMEM((rows, columns), F32),
            pltpu.VMEM((rows, 128), F32),
            pltpu.SemaphoreType.DMA((n - second,)),
        ],
        compiler_params=pltpu.CompilerParams(vmem_limit_bytes=VMEM_LIMIT),
        cost_estimate=hint(6),
    )(me, gain, squares, mine, other, far(weight), near(weight_a), near(weight_b))
    return sent, (cos, sin, allowed, weights, head_gain)


def attend_kernel(
    received_ref, cos_ref, sin_ref, allowed_ref, lambda_ref, gain_ref,
    keys_one_ref, keys_two_ref, values_ref, out_ref, fresh,
):
    sources, pieces, _ = received_ref.shape
    steps = cos_ref.shape[0]
    blocks = pieces // steps
    pages, page, _ = keys_one_ref.shape
    capacity = pages * page
    for source in range(sources):
        piece = received_ref[source].astype(F32)
        for step in range(steps):
            fresh[step, source * blocks : (source + 1) * blocks, :] = piece[
                step * blocks : (step + 1) * blocks
            ]

    def heads(step, kind):
        return fresh[step, kind * H : (kind + 1) * H, :]

    def rotated(step, kind):
        values = heads(step, kind)
        turned = values * cos_ref[step] + pltpu.roll(values, HD // 2, 1) * sin_ref[step]
        return turned.astype(BF16).astype(F32)

    allowed = allowed_ref[...] > 0.0
    scale = 1.0 / math.sqrt(HD)
    head_row = lax.rem(lax.broadcasted_iota(jnp.int32, (steps * H, HD), 0), H)

    def softmax_map(kind, keys_ref):
        queries = [rotated(step, kind) for step in range(steps)]
        news = [rotated(step, kind + 2) for step in range(steps)]
        stacked = jnp.concatenate(queries, axis=0)
        apart = jnp.concatenate(
            [jnp.where(head_row == h, stacked, 0.0).astype(BF16) for h in range(H)], axis=1
        )
        older = lax.dot_general(
            apart, keys_ref[...].reshape(capacity, H * HD), (((1,), (1,)), ((), ())),
            preferred_element_type=F32,
        )
        older = jnp.where(allowed, older * scale, -1e38)
        parts = []
        for step in range(steps):
            cached = older[step * H : (step + 1) * H]
            newer = [
                jnp.sum(queries[step] * news[e], axis=1, keepdims=True) * scale
                for e in range(step + 1)
            ]
            top = jnp.max(cached, axis=1, keepdims=True)
            for value in newer:
                top = jnp.maximum(top, value)
            cached = jnp.exp(cached - top)
            newer = [jnp.exp(value - top) for value in newer]
            whole = jnp.sum(cached, axis=1, keepdims=True)
            for value in newer:
                whole = whole + value
            parts.append((cached / whole, [value / whole for value in newer]))
        return parts

    first = softmax_map(0, keys_one_ref)
    second = softmax_map(1, keys_two_ref)
    weight = lambda_ref[...]
    mix = jnp.concatenate(
        [first[step][0] - weight * second[step][0] for step in range(steps)], axis=0
    ).astype(BF16)
    spread = jnp.dot(mix, values_ref[...].reshape(capacity, -1), preferred_element_type=F32)
    wide_row = lax.broadcasted_iota(jnp.int32, (H, 2 * HD), 0)
    fresh_values = [
        jnp.concatenate(
            [fresh[e, pl.ds(4 * H + half, H, stride=2), :] for half in range(2)], axis=1
        )
        for e in range(steps)
    ]
    for step in range(steps):
        mixed = jnp.zeros((H, 2 * HD), F32)
        for h in range(H):
            block = spread[step * H : (step + 1) * H, h * 2 * HD : (h + 1) * 2 * HD]
            mixed = jnp.where(wide_row == h, block, mixed)
        for e in range(step + 1):
            share = first[step][1][e] - weight * second[step][1][e]
            mixed = mixed + share.astype(BF16).astype(F32) * fresh_values[e]
        norm = lax.rsqrt(jnp.mean(mixed * mixed, axis=1, keepdims=True) + EPS)
        out_ref[step * H : (step + 1) * H, :] = (mixed * norm * gain_ref[...]).astype(BF16)


def attend(received, cos, sin, allowed, weights, gain, keys_one, keys_two, values):
    steps = cos.shape[0]
    sources, pieces, _ = received.shape
    vmem = pl.BlockSpec(memory_space=pltpu.VMEM)
    held = [near(x) for x in (keys_one, keys_two, values)]
    return pl.pallas_call(
        attend_kernel,
        out_shape=jax.ShapeDtypeStruct((steps * H, 2 * HD), BF16),
        in_specs=[vmem] * 9,
        out_specs=vmem,
        scratch_shapes=[pltpu.VMEM((steps, sources * (pieces // steps), 128), F32)],
        compiler_params=pltpu.CompilerParams(vmem_limit_bytes=VMEM_LIMIT),
        cost_estimate=hint(10),
    )(received, cos, sin, allowed, weights, gain, *held)


def output_kernel(n, me_ref, mine_ref, other_ref, inputs_ref, *rest):
    *weights, out_ref, rows_ref = rest
    me = me_ref[0]
    half, heads, width = mine_ref.shape
    steps = heads // H
    lanes = width // 128
    for entry in range(half):
        for core, ref in ((0, mine_ref), (1, other_ref)):
            source = jnp.bitwise_xor(me, 2 * entry + core)
            start = pl.multiple_of(source * heads, 8)
            block = ref[entry].astype(F32)
            for lane in range(lanes):
                rows_ref[lane, pl.ds(start, heads), :] = block[:, lane * 128 : (lane + 1) * 128]
    total = None
    for h in range(H):
        left = jnp.concatenate(
            [
                jnp.concatenate(
                    [rows_ref[lane, pl.ds(step * H + h, n, stride=heads), :] for lane in range(lanes)],
                    axis=1,
                )
                for step in range(steps)
            ],
            axis=0,
        ).astype(BF16)
        held = weights[h * len(weights) // H]
        at = h * width % held.shape[0]
        product = jnp.dot(left, held[at : at + width, :], preferred_element_type=F32)
        total = product if total is None else total + product
    for step in range(steps):
        out_ref[step] = (
            inputs_ref[step].astype(F32) + total[step * n : (step + 1) * n]
        ).astype(BF16)


def keep_kernel(half, block_ref, from_ref, held, to_ref, sem):
    rows = to_ref.shape[0]
    copy = pltpu.make_async_copy(from_ref.at[pl.ds(half * rows, rows), :], to_ref, sem)
    copy.start()
    held[...] = block_ref[...]
    copy.wait()


def keep(block, weight, half, us):
    vmem = pl.BlockSpec(memory_space=pltpu.VMEM)
    return pl.pallas_call(
        functools.partial(keep_kernel, half),
        out_shape=(
            jax.ShapeDtypeStruct(block.shape, block.dtype),
            pltpu.VMEM((weight.shape[0] // 2, weight.shape[1]), weight.dtype),
        ),
        in_specs=[vmem, pl.BlockSpec(memory_space=pltpu.HBM)],
        out_specs=(vmem, vmem),
        scratch_shapes=[pltpu.SemaphoreType.DMA],
        compiler_params=pltpu.CompilerParams(vmem_limit_bytes=4 * 1024 * 1024),
        cost_estimate=hint(us),
    )(block, far(weight))


def output(me, attended, inputs, weight, n):
    kept = []

    def aside(half, block):
        block, part = keep(block, weight, half, 2)
        kept.append(near(part))
        return block

    mine, other = gather_blocks(
        attended, n, functools.partial(aside, 0), functools.partial(aside, 1)
    )
    half, heads, width = mine.shape
    vmem = pl.BlockSpec(memory_space=pltpu.VMEM)
    return pl.pallas_call(
        functools.partial(output_kernel, n),
        out_shape=jax.ShapeDtypeStruct(inputs.shape, BF16),
        in_specs=[pl.BlockSpec(memory_space=pltpu.SMEM)] + [vmem] * 5,
        out_specs=vmem,
        scratch_shapes=[pltpu.VMEM((width // 128, n * heads, 128), F32)],
        compiler_params=pltpu.CompilerParams(vmem_limit_bytes=VMEM_LIMIT),
    )(me, mine, other, inputs, *kept)


def angles(positions, steps):
    half = HD // 2
    frequency = jnp.exp(-math.log(ROPE_BASE) * 2.0 * jnp.arange(half, dtype=F32) / HD)
    places = (positions + jnp.arange(steps, dtype=jnp.int32)).astype(F32)
    turns = places[:, None] * frequency[None, :]
    cosine, sine = jnp.cos(turns), jnp.sin(turns)
    cos = jnp.concatenate([cosine, cosine], axis=-1)
    sin = jnp.concatenate([-sine, sine], axis=-1)
    return cos[:, None, :], sin[:, None, :]


def local(
    n, inputs, norm_gain, qkv_weight, head_lambda, head_gain, out_weight,
    key_one_pages, key_two_pages, value_pages, page_table, context_len, positions,
):
    steps, rows, part = inputs.shape
    me = lax.axis_index("gx").astype(jnp.int32).reshape(1)
    block = inputs.reshape(steps * rows, part)
    capacity = page_table.shape[1] * key_one_pages.shape[1]
    small = (page_table, head_lambda.reshape(1, H), head_gain.reshape(1, H * 2 * HD))
    sent, aside = project(
        me, block, norm_gain.reshape(n, 1, part), qkv_weight, n, (positions, context_len), small,
        capacity,
    )
    received = lax.all_to_all(sent, "gx", 0, 0)
    attended = attend(received, *aside, key_one_pages, key_two_pages, value_pages)
    return output(me, attended, inputs, out_weight, n)


def rotary(vectors, cos, sin):
    return vectors * cos + jnp.roll(vectors, HD // 2, axis=-1) * sin


def local_any(
    n, inputs, norm_gain, qkv_weight, head_lambda, head_gain, out_weight,
    key_one_pages, key_two_pages, value_pages, page_table, context_len, positions,
):
    steps = inputs.shape[0]
    own = page_table.shape[0]
    capacity = page_table.shape[1] * key_one_pages.shape[1]
    values = lax.all_gather(inputs, "gx", axis=2, tiled=True).astype(F32)
    factor = lax.rsqrt(jnp.mean(values * values, axis=-1, keepdims=True) + EPS)
    normed = (values * factor * norm_gain).astype(BF16)
    projected = jnp.einsum("sbd,dc->sbc", normed, qkv_weight, preferred_element_type=F32)
    received = lax.all_to_all(
        projected.astype(BF16), "gx", split_axis=1, concat_axis=2, tiled=True
    )
    cached = tuple(
        pool[page_table].reshape(own, capacity, H, -1)
        for pool in (key_one_pages, key_two_pages, value_pages)
    )
    both = received[..., : 4 * H * HD].reshape(steps, own, 4, H, HD).astype(F32)
    new_values = received[..., 4 * H * HD :].reshape(steps, own, H, 2 * HD)
    cos, sin = jax.vmap(lambda p: angles(p, steps))(positions.reshape(own, 1))
    cos, sin = (jnp.moveaxis(x, 0, 1)[:, :, None] for x in (cos, sin))
    turned = rotary(both, cos, sin).astype(BF16)
    place = jnp.arange(capacity, dtype=jnp.int32)
    allowed = (place[None, :] < context_len[:, None])[None, :, None, :]
    step = jnp.arange(steps)
    newer_allowed = (step[None, :] <= step[:, None])[:, None, None, :]

    def softmax_map(query, keys, news):
        older = jnp.einsum("tshd,sjhd->tshj", query, keys, preferred_element_type=F32)
        newer = jnp.einsum("tshd,eshd->tshe", query, news, preferred_element_type=F32)
        scores = jnp.concatenate(
            [jnp.where(allowed, older, -jnp.inf), jnp.where(newer_allowed, newer, -jnp.inf)], axis=-1
        )
        return jax.nn.softmax(scores * (1.0 / math.sqrt(HD)), axis=-1)

    first = softmax_map(turned[:, :, 0], cached[0], turned[:, :, 2])
    second = softmax_map(turned[:, :, 1], cached[1], turned[:, :, 3])
    mix = (first - head_lambda[:, None] * second).astype(BF16)
    mixed = jnp.einsum(
        "tshj,sjhf->tshf", mix[..., :capacity], cached[2], preferred_element_type=F32
    ) + jnp.einsum("tshe,eshf->tshf", mix[..., capacity:], new_values, preferred_element_type=F32)
    norm = lax.rsqrt(jnp.mean(mixed * mixed, axis=-1, keepdims=True) + EPS)
    grouped = (mixed * norm * head_gain.reshape(H, 2 * HD)).astype(BF16)
    whole = lax.all_gather(grouped.reshape(steps, own, -1), "gx", axis=1, tiled=True)
    branch = jnp.einsum("sbf,fd->sbd", whole, out_weight, preferred_element_type=F32)
    return (inputs.astype(F32) + branch).astype(BF16)


def solution(mesh):
    n = mesh.shape["gx"]
    placed = (
        P(None, "groups", "gx"),
        P(),
        P(None, "gx"),
        P(),
        P(),
        P(None, "gx"),
        P(("groups", "gx"), None, None),
        P(("groups", "gx"), None, None),
        P(("groups", "gx"), None, None),
        P(("groups", "gx"), None),
        P(("groups", "gx")),
        P(("groups", "gx")),
    )

    def chosen(inputs, norm_gain, qkv_weight, *rest):
        aligned = inputs.shape[2] % 128 == 0 and qkv_weight.shape[1] % 128 == 0
        single = rest[6].shape[0] == 1
        power = n >= 4 and n & (n - 1) == 0
        body = local if aligned and single and power else local_any
        return body(n, inputs, norm_gain, qkv_weight, *rest)

    return jax.shard_map(
        chosen, mesh=mesh, in_specs=placed, out_specs=P(None, "groups", "gx"), check_vma=False
    )
```

```python
import functools
import math

import jax
import jax.numpy as jnp
from jax import lax
from jax.experimental import pallas as pl
from jax.experimental.pallas import tpu as pltpu
from jax.sharding import PartitionSpec as P

H = 24
HD = 128
EPS = 1e-05
ROPE_BASE = 10000.0
F32 = jnp.float32
BF16 = jnp.bfloat16
VMEM_LIMIT = 16 * 1024 * 1024


def radices(n):
    rest = n // 2
    middle = 1
    while middle * middle * 4 <= rest:
        middle *= 2
    return rest // middle, middle


def swap(block, n, mask):
    return lax.ppermute(block, "gx", [(i, i ^ mask) for i in range(n)])


def gather_blocks(block, n, first_aside, second_aside):
    outer, middle = radices(n)
    arrived = [swap(block, n, m * 2) for m in range(1, middle)]
    rows = jnp.stack([first_aside(block)] + arrived)
    others = [swap(rows, n, o * 2 * middle) for o in range(outer - 1, 0, -1)]
    rows, others = lax.optimization_barrier((second_aside(rows), others))
    mine = jnp.concatenate([rows] + others)
    return mine, swap(mine, n, 1)


def owner(me, entry, core, n):
    outer, middle = radices(n)
    mask = (entry % outer) * (2 * middle) + (entry // outer) * 2 + core
    return jnp.bitwise_xor(me, mask)


def far(x):
    return pltpu.with_memory_space_constraint(x, pltpu.HBM)


def hint(us):
    return pl.CostEstimate(flops=0, bytes_accessed=int(us * 3_000_000), transcendentals=0)


def slots(n):
    return [(entry, core) for core in range(2) for entry in range(n // 2)]


def fetches(n, order, me, from_ref, to_ref, sems):
    part = from_ref.shape[0] // n
    copies = []
    for slot, (entry, core) in enumerate(order):
        start = pl.multiple_of(owner(me, entry, core, n) * part, part)
        copies.append(
            pltpu.make_async_copy(
                from_ref.at[pl.ds(start, part), :], to_ref.at[slot], sems.at[slot]
            )
        )
    return copies


def fetch_kernel(n, order, *rest):
    (
        me_ref, block_ref, gain_ref, weight_ref, table_ref, lambda_ref, head_gain_ref,
        held, gain_out, weight_out, place_ref, lambda_out, head_gain_out,
        table, row_ref, wide_ref, sems, other_sems,
    ) = rest
    small = [
        pltpu.make_async_copy(start, end, other_sems.at[index])
        for index, (start, end) in enumerate(
            (
                (table_ref, table),
                (lambda_ref, row_ref),
                (head_gain_ref, wide_ref),
                (block_ref, held),
                (gain_ref, gain_out),
            )
        )
    ]
    large = fetches(n, order, me_ref[0], weight_ref, weight_out, sems)
    for copy in small + large:
        copy.start()
    for copy in small:
        copy.wait()

    capacity = place_ref.shape[1]
    pages = table_ref.shape[1]
    page = capacity // pages
    row = lax.broadcasted_iota(jnp.int32, (1, capacity), 1)
    place = jnp.zeros((1, capacity), jnp.int32)
    for index in range(pages):
        first = table[0, index] * page
        inside = (row >= first) & (row < first + page)
        place = jnp.where(inside, row - first + index * page, place)
    place_ref[...] = place
    across = lax.broadcasted_iota(jnp.int32, (H, H), 1) == lax.broadcasted_iota(jnp.int32, (H, H), 0)
    lambda_out[...] = jnp.sum(jnp.where(across, row_ref[...], 0.0), axis=1, keepdims=True)
    for h in range(H):
        head_gain_out[h : h + 1, :] = wide_ref[:, h * 2 * HD : (h + 1) * 2 * HD]

    for copy in large:
        copy.wait()


def fetch(me, block, gain, weight, n, order, small, capacity):
    part, columns = weight.shape[0] // n, weight.shape[1]
    vmem = pl.BlockSpec(memory_space=pltpu.VMEM)
    hbm = pl.BlockSpec(memory_space=pltpu.HBM)
    table, weights, head_gain = small
    return pl.pallas_call(
        functools.partial(fetch_kernel, n, order),
        out_shape=(
            pltpu.VMEM(block.shape, BF16),
            pltpu.VMEM(gain.shape, F32),
            pltpu.VMEM((len(order), part, columns), BF16),
            jax.ShapeDtypeStruct((1, capacity), jnp.int32),
            jax.ShapeDtypeStruct((H, 1), F32),
            jax.ShapeDtypeStruct((H, 2 * HD), F32),
        ),
        in_specs=[pl.BlockSpec(memory_space=pltpu.SMEM)] + [hbm] * 6,
        out_specs=(vmem,) * 6,
        scratch_shapes=[
            pltpu.SMEM(table.shape, table.dtype),
            pltpu.VMEM(weights.shape, F32),
            pltpu.VMEM(head_gain.shape, F32),
            pltpu.SemaphoreType.DMA((len(order),)),
            pltpu.SemaphoreType.DMA((5,)),
        ],
        compiler_params=pltpu.CompilerParams(vmem_limit_bytes=4 * 1024 * 1024),
        cost_estimate=hint(5),
    )(me, far(block), far(gain), far(weight), *map(far, small))


def near(x):
    return pltpu.with_memory_space_constraint(x, pltpu.VMEM)


def add_squares(refs, square):
    for ref in refs:
        for entry in range(ref.shape[0]):
            values = ref[entry].astype(F32)
            square = square + values * values
    return square


def squares_kernel(n, order, count, me_ref, weight_ref, *rest):
    blocks, (squares, weight_out, sems) = rest[:count], rest[count:]
    copies = fetches(n, order, me_ref[0], weight_ref, weight_out, sems)
    for copy in copies:
        copy.start()
    squares[...] = add_squares(blocks, jnp.zeros(squares.shape, F32))
    for copy in copies:
        copy.wait()


def squares_beside(me, weight, blocks, n, order):
    part, columns = weight.shape[0] // n, weight.shape[1]
    vmem = pl.BlockSpec(memory_space=pltpu.VMEM)
    return pl.pallas_call(
        functools.partial(squares_kernel, n, order, len(blocks)),
        out_shape=(
            jax.ShapeDtypeStruct(blocks[0].shape[1:], F32),
            pltpu.VMEM((len(order), part, columns), BF16),
        ),
        in_specs=[
            pl.BlockSpec(memory_space=pltpu.SMEM),
            pl.BlockSpec(memory_space=pltpu.HBM),
        ]
        + [vmem] * len(blocks),
        out_specs=(vmem, vmem),
        scratch_shapes=[pltpu.SemaphoreType.DMA((len(order),))],
        compiler_params=pltpu.CompilerParams(vmem_limit_bytes=4 * 1024 * 1024),
        cost_estimate=hint(len(order) * 0.7),
    )(me, far(weight), *blocks)


def more_squares_kernel(positions_ref, length_ref, place_ref, before, *rest):
    *blocks, squares, cos_ref, sin_ref, allowed_ref = rest
    squares[...] = add_squares(blocks, before[...])
    steps = cos_ref.shape[0]
    lane = lax.broadcasted_iota(jnp.int32, (8, HD), 1)
    step = lax.broadcasted_iota(jnp.int32, (8, HD), 0)
    pair = lax.rem(lane, HD // 2).astype(F32)
    frequency = jnp.exp(-math.log(ROPE_BASE) * 2.0 * pair / HD)
    turns = (positions_ref[0] + step).astype(F32) * frequency
    cos = jnp.cos(turns)
    sin = jnp.where(lane < HD // 2, -1.0, 1.0) * jnp.sin(turns)
    for index in range(steps):
        cos_ref[index] = cos[index : index + 1]
        sin_ref[index] = sin[index : index + 1]
    allowed_ref[...] = jnp.where(place_ref[...] < length_ref[0], 1.0, 0.0)


def more_squares(blocks, before, positions, length, place, steps):
    vmem = pl.BlockSpec(memory_space=pltpu.VMEM)
    smem = pl.BlockSpec(memory_space=pltpu.SMEM)
    turns = jax.ShapeDtypeStruct((steps, 1, HD), F32)
    return pl.pallas_call(
        more_squares_kernel,
        out_shape=(
            jax.ShapeDtypeStruct(before.shape, F32),
            turns,
            turns,
            jax.ShapeDtypeStruct(place.shape, F32),
        ),
        in_specs=[smem, smem] + [vmem] * (len(blocks) + 2),
        out_specs=(vmem,) * 4,
        compiler_params=pltpu.CompilerParams(vmem_limit_bytes=4 * 1024 * 1024),
        cost_estimate=hint(1),
    )(positions, length, place, before, *blocks)


def project_kernel(n, order, me_ref, gain_ref, before_ref, mine_ref, other_ref, weight_ref, *rest):
    *helds, out_ref, last, spread, total, kept, sems = rest
    me = me_ref[0]
    rows, part = before_ref.shape
    copies = fetches(n, order, me, weight_ref, last, sems)
    for copy in copies:
        copy.start()
    places = [(held, slot) for held in helds for slot in range(held.shape[0])]
    early = len(places)
    places += [(last, slot) for slot in range(len(order))]
    blocks = list(zip(slots(n), places, strict=True))

    def products(picked, factor):
        summed = None
        for (entry, core), (held, slot) in picked:
            values = (mine_ref, other_ref)[core][entry].astype(F32)
            normed = (values * factor * gain_ref[owner(me, entry, core, n)]).astype(BF16)
            product = jnp.dot(normed, held[slot], preferred_element_type=F32)
            summed = product if summed is None else summed + product
        return summed

    def row_factor():
        square = add_squares([other_ref], before_ref[...])
        mean = jnp.sum(square, axis=1, keepdims=True) * (1.0 / (n * part))
        return lax.rsqrt(mean + EPS)

    @pl.when(me >= 0)
    def _():
        factor = row_factor()
        total[...] = products(blocks[:early], factor)
        kept[...] = jnp.broadcast_to(factor, kept.shape)

    for copy in copies:
        copy.wait()
    factor = kept[:, :1]
    summed = total[...] + products(blocks[early:], factor)
    columns = summed.shape[1] // 128
    steps = rows // n
    for block in range(columns):
        for step in range(steps):
            spread[:, step * columns + block, :] = summed[
                step * n : (step + 1) * n, block * 128 : (block + 1) * 128
            ]
    for target in range(n):
        out_ref[target] = spread[target, : steps * columns, :].astype(BF16)


def project(me, block, gain, weight, n, scalars, small, capacity):
    rows, part = block.shape
    columns = weight.shape[1]
    pieces = rows // n * (columns // 128)
    outer, middle = radices(n)
    order = slots(n)
    first, second = n // 4, 3 * n // 4

    arrived = [swap(block, n, o * 2 * middle) for o in range(1, outer)]
    held, gain, weight_a, place, weights, head_gain = fetch(
        me, block, gain, weight, n, order[:first], small, capacity
    )
    row = jnp.stack([held] + arrived)
    later = [swap(row, n, m * 2) for m in range(1, middle)]
    squares, weight_b = squares_beside(me, weight, [row], n, order[first:second])
    later, squares = lax.optimization_barrier((later, squares))
    mine = jnp.concatenate([row] + later)
    other = swap(mine, n, 1)
    squares, cos, sin, allowed = more_squares(later, squares, *scalars, place, rows // n)
    vmem = pl.BlockSpec(memory_space=pltpu.VMEM)
    hbm = pl.BlockSpec(memory_space=pltpu.HBM)
    sent = pl.pallas_call(
        functools.partial(project_kernel, n, order[second:]),
        out_shape=jax.ShapeDtypeStruct((n, pieces, 128), BF16),
        in_specs=[pl.BlockSpec(memory_space=pltpu.SMEM)] + [vmem] * 4 + [hbm] + [vmem] * 2,
        out_specs=vmem,
        scratch_shapes=[
            pltpu.VMEM((n - second, part, columns), BF16),
            pltpu.VMEM((n, -(-pieces // 8) * 8, 128), F32),
            pltpu.VMEM((rows, columns), F32),
            pltpu.VMEM((rows, 128), F32),
            pltpu.SemaphoreType.DMA((n - second,)),
        ],
        compiler_params=pltpu.CompilerParams(vmem_limit_bytes=VMEM_LIMIT),
        cost_estimate=hint(6),
    )(me, gain, squares, mine, other, far(weight), near(weight_a), near(weight_b))
    return sent, (cos, sin, allowed, weights, head_gain)


def attend_kernel(
    received_ref, cos_ref, sin_ref, allowed_ref, lambda_ref, gain_ref,
    keys_one_ref, keys_two_ref, values_ref, out_ref, fresh,
):
    sources, pieces, _ = received_ref.shape
    steps = cos_ref.shape[0]
    blocks = pieces // steps
    pages, page, _ = keys_one_ref.shape
    capacity = pages * page
    for source in range(sources):
        piece = received_ref[source].astype(F32)
        for step in range(steps):
            fresh[step, source * blocks : (source + 1) * blocks, :] = piece[
                step * blocks : (step + 1) * blocks
            ]

    def heads(step, kind):
        return fresh[step, kind * H : (kind + 1) * H, :]

    def rotated(step, kind):
        values = heads(step, kind)
        turned = values * cos_ref[step] + pltpu.roll(values, HD // 2, 1) * sin_ref[step]
        return turned.astype(BF16).astype(F32)

    allowed = allowed_ref[...] > 0.0
    scale = 1.0 / math.sqrt(HD)
    head_row = lax.rem(lax.broadcasted_iota(jnp.int32, (steps * H, HD), 0), H)

    def softmax_map(kind, keys_ref):
        queries = [rotated(step, kind) for step in range(steps)]
        news = [rotated(step, kind + 2) for step in range(steps)]
        stacked = jnp.concatenate(queries, axis=0)
        apart = jnp.concatenate(
            [jnp.where(head_row == h, stacked, 0.0).astype(BF16) for h in range(H)], axis=1
        )
        older = lax.dot_general(
            apart, keys_ref[...].reshape(capacity, H * HD), (((1,), (1,)), ((), ())),
            preferred_element_type=F32,
        )
        older = jnp.where(allowed, older * scale, -1e38)
        parts = []
        for step in range(steps):
            cached = older[step * H : (step + 1) * H]
            newer = [
                jnp.sum(queries[step] * news[e], axis=1, keepdims=True) * scale
                for e in range(step + 1)
            ]
            top = jnp.max(cached, axis=1, keepdims=True)
            for value in newer:
                top = jnp.maximum(top, value)
            cached = jnp.exp(cached - top)
            newer = [jnp.exp(value - top) for value in newer]
            whole = jnp.sum(cached, axis=1, keepdims=True)
            for value in newer:
                whole = whole + value
            parts.append((cached / whole, [value / whole for value in newer]))
        return parts

    first = softmax_map(0, keys_one_ref)
    second = softmax_map(1, keys_two_ref)
    weight = lambda_ref[...]
    mix = jnp.concatenate(
        [first[step][0] - weight * second[step][0] for step in range(steps)], axis=0
    ).astype(BF16)
    spread = jnp.dot(mix, values_ref[...].reshape(capacity, -1), preferred_element_type=F32)
    wide_row = lax.broadcasted_iota(jnp.int32, (H, 2 * HD), 0)
    fresh_values = [
        jnp.concatenate(
            [fresh[e, pl.ds(4 * H + half, H, stride=2), :] for half in range(2)], axis=1
        )
        for e in range(steps)
    ]
    for step in range(steps):
        mixed = jnp.zeros((H, 2 * HD), F32)
        for h in range(H):
            block = spread[step * H : (step + 1) * H, h * 2 * HD : (h + 1) * 2 * HD]
            mixed = jnp.where(wide_row == h, block, mixed)
        for e in range(step + 1):
            share = first[step][1][e] - weight * second[step][1][e]
            mixed = mixed + share.astype(BF16).astype(F32) * fresh_values[e]
        norm = lax.rsqrt(jnp.mean(mixed * mixed, axis=1, keepdims=True) + EPS)
        out_ref[step * H : (step + 1) * H, :] = (mixed * norm * gain_ref[...]).astype(BF16)


def attend(received, cos, sin, allowed, weights, gain, keys_one, keys_two, values):
    steps = cos.shape[0]
    sources, pieces, _ = received.shape
    vmem = pl.BlockSpec(memory_space=pltpu.VMEM)
    held = [near(x) for x in (keys_one, keys_two, values)]
    return pl.pallas_call(
        attend_kernel,
        out_shape=jax.ShapeDtypeStruct((steps * H, 2 * HD), BF16),
        in_specs=[vmem] * 9,
        out_specs=vmem,
        scratch_shapes=[pltpu.VMEM((steps, sources * (pieces // steps), 128), F32)],
        compiler_params=pltpu.CompilerParams(vmem_limit_bytes=VMEM_LIMIT),
        cost_estimate=hint(10),
    )(received, cos, sin, allowed, weights, gain, *held)


def output_kernel(n, me_ref, mine_ref, other_ref, inputs_ref, *rest):
    *weights, out_ref, rows_ref = rest
    me = me_ref[0]
    half, heads, width = mine_ref.shape
    steps = heads // H
    lanes = width // 128
    outer, middle = radices(n)
    for entry in range(half):
        for core, ref in ((0, mine_ref), (1, other_ref)):
            along = (outer - entry // middle) % outer
            source = jnp.bitwise_xor(me, 2 * (along * middle + entry % middle) + core)
            start = pl.multiple_of(source * heads, 8)
            block = ref[entry].astype(F32)
            for lane in range(lanes):
                rows_ref[lane, pl.ds(start, heads), :] = block[:, lane * 128 : (lane + 1) * 128]
    total = None
    for h in range(H):
        left = jnp.concatenate(
            [
                jnp.concatenate(
                    [rows_ref[lane, pl.ds(step * H + h, n, stride=heads), :] for lane in range(lanes)],
                    axis=1,
                )
                for step in range(steps)
            ],
            axis=0,
        ).astype(BF16)
        held = weights[h * len(weights) // H]
        at = h * width % held.shape[0]
        product = jnp.dot(left, held[at : at + width, :], preferred_element_type=F32)
        total = product if total is None else total + product
    for step in range(steps):
        out_ref[step] = (
            inputs_ref[step].astype(F32) + total[step * n : (step + 1) * n]
        ).astype(BF16)


def keep_kernel(half, block_ref, from_ref, held, to_ref, sem):
    rows = to_ref.shape[0]
    copy = pltpu.make_async_copy(from_ref.at[pl.ds(half * rows, rows), :], to_ref, sem)
    copy.start()
    held[...] = block_ref[...]
    copy.wait()


def keep(block, weight, half, us):
    vmem = pl.BlockSpec(memory_space=pltpu.VMEM)
    return pl.pallas_call(
        functools.partial(keep_kernel, half),
        out_shape=(
            jax.ShapeDtypeStruct(block.shape, block.dtype),
            pltpu.VMEM((weight.shape[0] // 2, weight.shape[1]), weight.dtype),
        ),
        in_specs=[vmem, pl.BlockSpec(memory_space=pltpu.HBM)],
        out_specs=(vmem, vmem),
        scratch_shapes=[pltpu.SemaphoreType.DMA],
        compiler_params=pltpu.CompilerParams(vmem_limit_bytes=4 * 1024 * 1024),
        cost_estimate=hint(us),
    )(block, far(weight))


def output(me, attended, inputs, weight, n):
    kept = []

    def aside(half, block):
        block, part = keep(block, weight, half, 2)
        kept.append(near(part))
        return block

    mine, other = gather_blocks(
        attended, n, functools.partial(aside, 0), functools.partial(aside, 1)
    )
    half, heads, width = mine.shape
    vmem = pl.BlockSpec(memory_space=pltpu.VMEM)
    return pl.pallas_call(
        functools.partial(output_kernel, n),
        out_shape=jax.ShapeDtypeStruct(inputs.shape, BF16),
        in_specs=[pl.BlockSpec(memory_space=pltpu.SMEM)] + [vmem] * 5,
        out_specs=vmem,
        scratch_shapes=[pltpu.VMEM((width // 128, n * heads, 128), F32)],
        compiler_params=pltpu.CompilerParams(vmem_limit_bytes=VMEM_LIMIT),
    )(me, mine, other, inputs, *kept)


def angles(positions, steps):
    half = HD // 2
    frequency = jnp.exp(-math.log(ROPE_BASE) * 2.0 * jnp.arange(half, dtype=F32) / HD)
    places = (positions + jnp.arange(steps, dtype=jnp.int32)).astype(F32)
    turns = places[:, None] * frequency[None, :]
    cosine, sine = jnp.cos(turns), jnp.sin(turns)
    cos = jnp.concatenate([cosine, cosine], axis=-1)
    sin = jnp.concatenate([-sine, sine], axis=-1)
    return cos[:, None, :], sin[:, None, :]


def local(
    n, inputs, norm_gain, qkv_weight, head_lambda, head_gain, out_weight,
    key_one_pages, key_two_pages, value_pages, page_table, context_len, positions,
):
    steps, rows, part = inputs.shape
    me = lax.axis_index("gx").astype(jnp.int32).reshape(1)
    block = inputs.reshape(steps * rows, part)
    capacity = page_table.shape[1] * key_one_pages.shape[1]
    small = (page_table, head_lambda.reshape(1, H), head_gain.reshape(1, H * 2 * HD))
    sent, aside = project(
        me, block, norm_gain.reshape(n, 1, part), qkv_weight, n, (positions, context_len), small,
        capacity,
    )
    received = lax.all_to_all(sent, "gx", 0, 0)
    attended = attend(received, *aside, key_one_pages, key_two_pages, value_pages)
    return output(me, attended, inputs, out_weight, n)


def rotary(vectors, cos, sin):
    return vectors * cos + jnp.roll(vectors, HD // 2, axis=-1) * sin


def local_any(
    n, inputs, norm_gain, qkv_weight, head_lambda, head_gain, out_weight,
    key_one_pages, key_two_pages, value_pages, page_table, context_len, positions,
):
    steps = inputs.shape[0]
    own = page_table.shape[0]
    capacity = page_table.shape[1] * key_one_pages.shape[1]
    values = lax.all_gather(inputs, "gx", axis=2, tiled=True).astype(F32)
    factor = lax.rsqrt(jnp.mean(values * values, axis=-1, keepdims=True) + EPS)
    normed = (values * factor * norm_gain).astype(BF16)
    projected = jnp.einsum("sbd,dc->sbc", normed, qkv_weight, preferred_element_type=F32)
    received = lax.all_to_all(
        projected.astype(BF16), "gx", split_axis=1, concat_axis=2, tiled=True
    )
    cached = tuple(
        pool[page_table].reshape(own, capacity, H, -1)
        for pool in (key_one_pages, key_two_pages, value_pages)
    )
    both = received[..., : 4 * H * HD].reshape(steps, own, 4, H, HD).astype(F32)
    new_values = received[..., 4 * H * HD :].reshape(steps, own, H, 2 * HD)
    cos, sin = jax.vmap(lambda p: angles(p, steps))(positions.reshape(own, 1))
    cos, sin = (jnp.moveaxis(x, 0, 1)[:, :, None] for x in (cos, sin))
    turned = rotary(both, cos, sin).astype(BF16)
    place = jnp.arange(capacity, dtype=jnp.int32)
    allowed = (place[None, :] < context_len[:, None])[None, :, None, :]
    step = jnp.arange(steps)
    newer_allowed = (step[None, :] <= step[:, None])[:, None, None, :]

    def softmax_map(query, keys, news):
        older = jnp.einsum("tshd,sjhd->tshj", query, keys, preferred_element_type=F32)
        newer = jnp.einsum("tshd,eshd->tshe", query, news, preferred_element_type=F32)
        scores = jnp.concatenate(
            [jnp.where(allowed, older, -jnp.inf), jnp.where(newer_allowed, newer, -jnp.inf)], axis=-1
        )
        return jax.nn.softmax(scores * (1.0 / math.sqrt(HD)), axis=-1)

    first = softmax_map(turned[:, :, 0], cached[0], turned[:, :, 2])
    second = softmax_map(turned[:, :, 1], cached[1], turned[:, :, 3])
    mix = (first - head_lambda[:, None] * second).astype(BF16)
    mixed = jnp.einsum(
        "tshj,sjhf->tshf", mix[..., :capacity], cached[2], preferred_element_type=F32
    ) + jnp.einsum("tshe,eshf->tshf", mix[..., capacity:], new_values, preferred_element_type=F32)
    norm = lax.rsqrt(jnp.mean(mixed * mixed, axis=-1, keepdims=True) + EPS)
    grouped = (mixed * norm * head_gain.reshape(H, 2 * HD)).astype(BF16)
    whole = lax.all_gather(grouped.reshape(steps, own, -1), "gx", axis=1, tiled=True)
    branch = jnp.einsum("sbf,fd->sbd", whole, out_weight, preferred_element_type=F32)
    return (inputs.astype(F32) + branch).astype(BF16)


def solution(mesh):
    n = mesh.shape["gx"]
    placed = (
        P(None, "groups", "gx"),
        P(),
        P(None, "gx"),
        P(),
        P(),
        P(None, "gx"),
        P(("groups", "gx"), None, None),
        P(("groups", "gx"), None, None),
        P(("groups", "gx"), None, None),
        P(("groups", "gx"), None),
        P(("groups", "gx")),
        P(("groups", "gx")),
    )

    def chosen(inputs, norm_gain, qkv_weight, *rest):
        aligned = inputs.shape[2] % 128 == 0 and qkv_weight.shape[1] % 128 == 0
        single = rest[6].shape[0] == 1
        power = n >= 4 and n & (n - 1) == 0
        body = local if aligned and single and power else local_any
        return body(n, inputs, norm_gain, qkv_weight, *rest)

    return jax.shard_map(
        chosen, mesh=mesh, in_specs=placed, out_specs=P(None, "groups", "gx"), check_vma=False
    )
```

```python
import functools
import math

import jax
import jax.numpy as jnp
from jax import lax
from jax.experimental import pallas as pl
from jax.experimental.pallas import tpu as pltpu
from jax.sharding import PartitionSpec as P

H = 24
HD = 128
EPS = 1e-05
ROPE_BASE = 10000.0
F32 = jnp.float32
BF16 = jnp.bfloat16
VMEM_LIMIT = 16 * 1024 * 1024


def radices(n):
    rest = n // 2
    middle = 1
    while middle * middle * 4 <= rest:
        middle *= 2
    return rest // middle, middle


def swap(block, n, mask):
    return lax.ppermute(block, "gx", [(i, i ^ mask) for i in range(n)])


def gather_blocks(block, n, first_aside, second_aside):
    outer, middle = radices(n)
    arrived = [swap(block, n, m * 2) for m in range(1, middle)]
    rows = jnp.stack([first_aside(block)] + arrived)
    others = [swap(rows, n, o * 2 * middle) for o in range(1, outer)]
    rows, others = lax.optimization_barrier((second_aside(rows), others))
    mine = jnp.concatenate([rows] + others)
    return mine, swap(mine, n, 1)


def owner(me, entry, core, n):
    outer, middle = radices(n)
    mask = (entry % outer) * (2 * middle) + (entry // outer) * 2 + core
    return jnp.bitwise_xor(me, mask)


def far(x):
    return pltpu.with_memory_space_constraint(x, pltpu.HBM)


def hint(us):
    return pl.CostEstimate(flops=0, bytes_accessed=int(us * 3_000_000), transcendentals=0)


def slots(n):
    return [(entry, core) for core in range(2) for entry in range(n // 2)]


def fetches(n, order, me, from_ref, to_ref, sems):
    part = from_ref.shape[0] // n
    copies = []
    for slot, (entry, core) in enumerate(order):
        start = pl.multiple_of(owner(me, entry, core, n) * part, part)
        copies.append(
            pltpu.make_async_copy(
                from_ref.at[pl.ds(start, part), :], to_ref.at[slot], sems.at[slot]
            )
        )
    return copies


def fetch_kernel(n, order, *rest):
    (
        me_ref, block_ref, gain_ref, weight_ref, table_ref, lambda_ref, head_gain_ref,
        held, gain_out, weight_out, place_ref, lambda_out, head_gain_out,
        table, row_ref, wide_ref, sems, other_sems,
    ) = rest
    small = [
        pltpu.make_async_copy(start, end, other_sems.at[index])
        for index, (start, end) in enumerate(
            (
                (table_ref, table),
                (lambda_ref, row_ref),
                (head_gain_ref, wide_ref),
                (block_ref, held),
                (gain_ref, gain_out),
            )
        )
    ]
    large = fetches(n, order, me_ref[0], weight_ref, weight_out, sems)
    for copy in small + large:
        copy.start()
    for copy in small:
        copy.wait()

    capacity = place_ref.shape[1]
    pages = table_ref.shape[1]
    page = capacity // pages
    row = lax.broadcasted_iota(jnp.int32, (1, capacity), 1)
    place = jnp.zeros((1, capacity), jnp.int32)
    for index in range(pages):
        first = table[0, index] * page
        inside = (row >= first) & (row < first + page)
        place = jnp.where(inside, row - first + index * page, place)
    place_ref[...] = place
    across = lax.broadcasted_iota(jnp.int32, (H, H), 1) == lax.broadcasted_iota(jnp.int32, (H, H), 0)
    lambda_out[...] = jnp.sum(jnp.where(across, row_ref[...], 0.0), axis=1, keepdims=True)
    for h in range(H):
        head_gain_out[h : h + 1, :] = wide_ref[:, h * 2 * HD : (h + 1) * 2 * HD]

    for copy in large:
        copy.wait()


def fetch(me, block, gain, weight, n, order, small, capacity):
    part, columns = weight.shape[0] // n, weight.shape[1]
    vmem = pl.BlockSpec(memory_space=pltpu.VMEM)
    hbm = pl.BlockSpec(memory_space=pltpu.HBM)
    table, weights, head_gain = small
    return pl.pallas_call(
        functools.partial(fetch_kernel, n, order),
        out_shape=(
            pltpu.VMEM(block.shape, BF16),
            pltpu.VMEM(gain.shape, F32),
            pltpu.VMEM((len(order), part, columns), BF16),
            jax.ShapeDtypeStruct((1, capacity), jnp.int32),
            jax.ShapeDtypeStruct((H, 1), F32),
            jax.ShapeDtypeStruct((H, 2 * HD), F32),
        ),
        in_specs=[pl.BlockSpec(memory_space=pltpu.SMEM)] + [hbm] * 6,
        out_specs=(vmem,) * 6,
        scratch_shapes=[
            pltpu.SMEM(table.shape, table.dtype),
            pltpu.VMEM(weights.shape, F32),
            pltpu.VMEM(head_gain.shape, F32),
            pltpu.SemaphoreType.DMA((len(order),)),
            pltpu.SemaphoreType.DMA((5,)),
        ],
        compiler_params=pltpu.CompilerParams(vmem_limit_bytes=4 * 1024 * 1024),
        cost_estimate=hint(5),
    )(me, far(block), far(gain), far(weight), *map(far, small))


def near(x):
    return pltpu.with_memory_space_constraint(x, pltpu.VMEM)


def add_squares(refs, square):
    for ref in refs:
        for entry in range(ref.shape[0]):
            values = ref[entry].astype(F32)
            square = square + values * values
    return square


def squares_kernel(n, order, count, me_ref, weight_ref, *rest):
    blocks, (squares, weight_out, sems) = rest[:count], rest[count:]
    copies = fetches(n, order, me_ref[0], weight_ref, weight_out, sems)
    for copy in copies:
        copy.start()
    squares[...] = add_squares(blocks, jnp.zeros(squares.shape, F32))
    for copy in copies:
        copy.wait()


def squares_beside(me, weight, blocks, n, order):
    part, columns = weight.shape[0] // n, weight.shape[1]
    vmem = pl.BlockSpec(memory_space=pltpu.VMEM)
    return pl.pallas_call(
        functools.partial(squares_kernel, n, order, len(blocks)),
        out_shape=(
            jax.ShapeDtypeStruct(blocks[0].shape[1:], F32),
            pltpu.VMEM((len(order), part, columns), BF16),
        ),
        in_specs=[
            pl.BlockSpec(memory_space=pltpu.SMEM),
            pl.BlockSpec(memory_space=pltpu.HBM),
        ]
        + [vmem] * len(blocks),
        out_specs=(vmem, vmem),
        scratch_shapes=[pltpu.SemaphoreType.DMA((len(order),))],
        compiler_params=pltpu.CompilerParams(vmem_limit_bytes=4 * 1024 * 1024),
        cost_estimate=hint(len(order) * 0.7),
    )(me, far(weight), *blocks)


def more_squares_kernel(positions_ref, length_ref, place_ref, before, *rest):
    *blocks, squares, cos_ref, sin_ref, allowed_ref = rest
    squares[...] = add_squares(blocks, before[...])
    steps = cos_ref.shape[0]
    lane = lax.broadcasted_iota(jnp.int32, (8, HD), 1)
    step = lax.broadcasted_iota(jnp.int32, (8, HD), 0)
    pair = lax.rem(lane, HD // 2).astype(F32)
    frequency = jnp.exp(-math.log(ROPE_BASE) * 2.0 * pair / HD)
    turns = (positions_ref[0] + step).astype(F32) * frequency
    cos = jnp.cos(turns)
    sin = jnp.where(lane < HD // 2, -1.0, 1.0) * jnp.sin(turns)
    for index in range(steps):
        cos_ref[index] = cos[index : index + 1]
        sin_ref[index] = sin[index : index + 1]
    allowed_ref[...] = jnp.where(place_ref[...] < length_ref[0], 1.0, 0.0)


def more_squares(blocks, before, positions, length, place, steps):
    vmem = pl.BlockSpec(memory_space=pltpu.VMEM)
    smem = pl.BlockSpec(memory_space=pltpu.SMEM)
    turns = jax.ShapeDtypeStruct((steps, 1, HD), F32)
    return pl.pallas_call(
        more_squares_kernel,
        out_shape=(
            jax.ShapeDtypeStruct(before.shape, F32),
            turns,
            turns,
            jax.ShapeDtypeStruct(place.shape, F32),
        ),
        in_specs=[smem, smem] + [vmem] * (len(blocks) + 2),
        out_specs=(vmem,) * 4,
        compiler_params=pltpu.CompilerParams(vmem_limit_bytes=4 * 1024 * 1024),
        cost_estimate=hint(1),
    )(positions, length, place, before, *blocks)


def project_kernel(n, order, me_ref, gain_ref, before_ref, mine_ref, other_ref, weight_ref, *rest):
    *helds, out_ref, last, spread, total, kept, sems = rest
    me = me_ref[0]
    rows, part = before_ref.shape
    copies = fetches(n, order, me, weight_ref, last, sems)
    for copy in copies:
        copy.start()
    places = [(held, slot) for held in helds for slot in range(held.shape[0])]
    early = len(places)
    places += [(last, slot) for slot in range(len(order))]
    blocks = list(zip(slots(n), places, strict=True))

    def products(picked, factor):
        summed = None
        for (entry, core), (held, slot) in picked:
            values = (mine_ref, other_ref)[core][entry].astype(F32)
            normed = (values * factor * gain_ref[owner(me, entry, core, n)]).astype(BF16)
            product = jnp.dot(normed, held[slot], preferred_element_type=F32)
            summed = product if summed is None else summed + product
        return summed

    def row_factor():
        square = add_squares([other_ref], before_ref[...])
        mean = jnp.sum(square, axis=1, keepdims=True) * (1.0 / (n * part))
        return lax.rsqrt(mean + EPS)

    @pl.when(me >= 0)
    def _():
        factor = row_factor()
        total[...] = products(blocks[:early], factor)
        kept[...] = jnp.broadcast_to(factor, kept.shape)

    for copy in copies:
        copy.wait()
    factor = kept[:, :1]
    summed = total[...] + products(blocks[early:], factor)
    columns = summed.shape[1] // 128
    steps = rows // n
    for block in range(columns):
        for step in range(steps):
            spread[:, step * columns + block, :] = summed[
                step * n : (step + 1) * n, block * 128 : (block + 1) * 128
            ]
    for target in range(n):
        out_ref[target] = spread[target, : steps * columns, :].astype(BF16)


def project(me, block, gain, weight, n, scalars, small, capacity):
    rows, part = block.shape
    columns = weight.shape[1]
    pieces = rows // n * (columns // 128)
    outer, middle = radices(n)
    order = slots(n)
    first, second = 5 * n // 16, 3 * n // 4

    arrived = [swap(block, n, o * 2 * middle) for o in range(1, outer)]
    held, gain, weight_a, place, weights, head_gain = fetch(
        me, block, gain, weight, n, order[:first], small, capacity
    )
    row = jnp.stack([held] + arrived)
    later = [swap(row, n, m * 2) for m in range(1, middle)]
    squares, weight_b = squares_beside(me, weight, [row], n, order[first:second])
    later, squares = lax.optimization_barrier((later, squares))
    mine = jnp.concatenate([row] + later)
    other = swap(mine, n, 1)
    squares, cos, sin, allowed = more_squares(later, squares, *scalars, place, rows // n)
    vmem = pl.BlockSpec(memory_space=pltpu.VMEM)
    hbm = pl.BlockSpec(memory_space=pltpu.HBM)
    sent = pl.pallas_call(
        functools.partial(project_kernel, n, order[second:]),
        out_shape=jax.ShapeDtypeStruct((n, pieces, 128), BF16),
        in_specs=[pl.BlockSpec(memory_space=pltpu.SMEM)] + [vmem] * 4 + [hbm] + [vmem] * 2,
        out_specs=vmem,
        scratch_shapes=[
            pltpu.VMEM((n - second, part, columns), BF16),
            pltpu.VMEM((n, -(-pieces // 8) * 8, 128), F32),
            pltpu.VMEM((rows, columns), F32),
            pltpu.VMEM((rows, 128), F32),
            pltpu.SemaphoreType.DMA((n - second,)),
        ],
        compiler_params=pltpu.CompilerParams(vmem_limit_bytes=VMEM_LIMIT),
        cost_estimate=hint(6),
    )(me, gain, squares, mine, other, far(weight), near(weight_a), near(weight_b))
    return sent, (cos, sin, allowed, weights, head_gain)


def attend_kernel(
    received_ref, cos_ref, sin_ref, allowed_ref, lambda_ref, gain_ref,
    keys_one_ref, keys_two_ref, values_ref, out_ref, fresh,
):
    sources, pieces, _ = received_ref.shape
    steps = cos_ref.shape[0]
    blocks = pieces // steps
    pages, page, _ = keys_one_ref.shape
    capacity = pages * page
    for source in range(sources):
        piece = received_ref[source].astype(F32)
        for step in range(steps):
            fresh[step, source * blocks : (source + 1) * blocks, :] = piece[
                step * blocks : (step + 1) * blocks
            ]

    def heads(step, kind):
        return fresh[step, kind * H : (kind + 1) * H, :]

    def rotated(step, kind):
        values = heads(step, kind)
        turned = values * cos_ref[step] + pltpu.roll(values, HD // 2, 1) * sin_ref[step]
        return turned.astype(BF16).astype(F32)

    allowed = allowed_ref[...] > 0.0
    scale = 1.0 / math.sqrt(HD)
    head_row = lax.rem(lax.broadcasted_iota(jnp.int32, (steps * H, HD), 0), H)

    def softmax_map(kind, keys_ref):
        queries = [rotated(step, kind) for step in range(steps)]
        news = [rotated(step, kind + 2) for step in range(steps)]
        stacked = jnp.concatenate(queries, axis=0)
        apart = jnp.concatenate(
            [jnp.where(head_row == h, stacked, 0.0).astype(BF16) for h in range(H)], axis=1
        )
        older = lax.dot_general(
            apart, keys_ref[...].reshape(capacity, H * HD), (((1,), (1,)), ((), ())),
            preferred_element_type=F32,
        )
        older = jnp.where(allowed, older * scale, -1e38)
        parts = []
        for step in range(steps):
            cached = older[step * H : (step + 1) * H]
            newer = [
                jnp.sum(queries[step] * news[e], axis=1, keepdims=True) * scale
                for e in range(step + 1)
            ]
            top = jnp.max(cached, axis=1, keepdims=True)
            for value in newer:
                top = jnp.maximum(top, value)
            cached = jnp.exp(cached - top)
            newer = [jnp.exp(value - top) for value in newer]
            whole = jnp.sum(cached, axis=1, keepdims=True)
            for value in newer:
                whole = whole + value
            parts.append((cached / whole, [value / whole for value in newer]))
        return parts

    first = softmax_map(0, keys_one_ref)
    second = softmax_map(1, keys_two_ref)
    weight = lambda_ref[...]
    mix = jnp.concatenate(
        [first[step][0] - weight * second[step][0] for step in range(steps)], axis=0
    ).astype(BF16)
    spread = jnp.dot(mix, values_ref[...].reshape(capacity, -1), preferred_element_type=F32)
    wide_row = lax.broadcasted_iota(jnp.int32, (H, 2 * HD), 0)
    fresh_values = [
        jnp.concatenate(
            [fresh[e, pl.ds(4 * H + half, H, stride=2), :] for half in range(2)], axis=1
        )
        for e in range(steps)
    ]
    for step in range(steps):
        mixed = jnp.zeros((H, 2 * HD), F32)
        for h in range(H):
            block = spread[step * H : (step + 1) * H, h * 2 * HD : (h + 1) * 2 * HD]
            mixed = jnp.where(wide_row == h, block, mixed)
        for e in range(step + 1):
            share = first[step][1][e] - weight * second[step][1][e]
            mixed = mixed + share.astype(BF16).astype(F32) * fresh_values[e]
        norm = lax.rsqrt(jnp.mean(mixed * mixed, axis=1, keepdims=True) + EPS)
        out_ref[step * H : (step + 1) * H, :] = (mixed * norm * gain_ref[...]).astype(BF16)


def attend(received, cos, sin, allowed, weights, gain, keys_one, keys_two, values):
    steps = cos.shape[0]
    sources, pieces, _ = received.shape
    vmem = pl.BlockSpec(memory_space=pltpu.VMEM)
    held = [near(x) for x in (keys_one, keys_two, values)]
    return pl.pallas_call(
        attend_kernel,
        out_shape=jax.ShapeDtypeStruct((steps * H, 2 * HD), BF16),
        in_specs=[vmem] * 9,
        out_specs=vmem,
        scratch_shapes=[pltpu.VMEM((steps, sources * (pieces // steps), 128), F32)],
        compiler_params=pltpu.CompilerParams(vmem_limit_bytes=VMEM_LIMIT),
        cost_estimate=hint(10),
    )(received, cos, sin, allowed, weights, gain, *held)


def output_kernel(n, me_ref, mine_ref, other_ref, inputs_ref, *rest):
    *weights, out_ref, rows_ref = rest
    me = me_ref[0]
    half, heads, width = mine_ref.shape
    steps = heads // H
    lanes = width // 128
    for entry in range(half):
        for core, ref in ((0, mine_ref), (1, other_ref)):
            source = jnp.bitwise_xor(me, 2 * entry + core)
            start = pl.multiple_of(source * heads, 8)
            block = ref[entry].astype(F32)
            for lane in range(lanes):
                rows_ref[lane, pl.ds(start, heads), :] = block[:, lane * 128 : (lane + 1) * 128]
    total = None
    for h in range(H):
        left = jnp.concatenate(
            [
                jnp.concatenate(
                    [rows_ref[lane, pl.ds(step * H + h, n, stride=heads), :] for lane in range(lanes)],
                    axis=1,
                )
                for step in range(steps)
            ],
            axis=0,
        ).astype(BF16)
        held = weights[h * len(weights) // H]
        at = h * width % held.shape[0]
        product = jnp.dot(left, held[at : at + width, :], preferred_element_type=F32)
        total = product if total is None else total + product
    for step in range(steps):
        out_ref[step] = (
            inputs_ref[step].astype(F32) + total[step * n : (step + 1) * n]
        ).astype(BF16)


def keep_kernel(half, block_ref, from_ref, held, to_ref, sem):
    rows = to_ref.shape[0]
    copy = pltpu.make_async_copy(from_ref.at[pl.ds(half * rows, rows), :], to_ref, sem)
    copy.start()
    held[...] = block_ref[...]
    copy.wait()


def keep(block, weight, half, us):
    vmem = pl.BlockSpec(memory_space=pltpu.VMEM)
    return pl.pallas_call(
        functools.partial(keep_kernel, half),
        out_shape=(
            jax.ShapeDtypeStruct(block.shape, block.dtype),
            pltpu.VMEM((weight.shape[0] // 2, weight.shape[1]), weight.dtype),
        ),
        in_specs=[vmem, pl.BlockSpec(memory_space=pltpu.HBM)],
        out_specs=(vmem, vmem),
        scratch_shapes=[pltpu.SemaphoreType.DMA],
        compiler_params=pltpu.CompilerParams(vmem_limit_bytes=4 * 1024 * 1024),
        cost_estimate=hint(us),
    )(block, far(weight))


def output(me, attended, inputs, weight, n):
    kept = []

    def aside(half, block):
        block, part = keep(block, weight, half, 2)
        kept.append(near(part))
        return block

    mine, other = gather_blocks(
        attended, n, functools.partial(aside, 0), functools.partial(aside, 1)
    )
    half, heads, width = mine.shape
    vmem = pl.BlockSpec(memory_space=pltpu.VMEM)
    return pl.pallas_call(
        functools.partial(output_kernel, n),
        out_shape=jax.ShapeDtypeStruct(inputs.shape, BF16),
        in_specs=[pl.BlockSpec(memory_space=pltpu.SMEM)] + [vmem] * 5,
        out_specs=vmem,
        scratch_shapes=[pltpu.VMEM((width // 128, n * heads, 128), F32)],
        compiler_params=pltpu.CompilerParams(vmem_limit_bytes=VMEM_LIMIT),
    )(me, mine, other, inputs, *kept)


def angles(positions, steps):
    half = HD // 2
    frequency = jnp.exp(-math.log(ROPE_BASE) * 2.0 * jnp.arange(half, dtype=F32) / HD)
    places = (positions + jnp.arange(steps, dtype=jnp.int32)).astype(F32)
    turns = places[:, None] * frequency[None, :]
    cosine, sine = jnp.cos(turns), jnp.sin(turns)
    cos = jnp.concatenate([cosine, cosine], axis=-1)
    sin = jnp.concatenate([-sine, sine], axis=-1)
    return cos[:, None, :], sin[:, None, :]


def local(
    n, inputs, norm_gain, qkv_weight, head_lambda, head_gain, out_weight,
    key_one_pages, key_two_pages, value_pages, page_table, context_len, positions,
):
    steps, rows, part = inputs.shape
    me = lax.axis_index("gx").astype(jnp.int32).reshape(1)
    block = inputs.reshape(steps * rows, part)
    capacity = page_table.shape[1] * key_one_pages.shape[1]
    small = (page_table, head_lambda.reshape(1, H), head_gain.reshape(1, H * 2 * HD))
    sent, aside = project(
        me, block, norm_gain.reshape(n, 1, part), qkv_weight, n, (positions, context_len), small,
        capacity,
    )
    received = lax.all_to_all(sent, "gx", 0, 0)
    attended = attend(received, *aside, key_one_pages, key_two_pages, value_pages)
    return output(me, attended, inputs, out_weight, n)


def rotary(vectors, cos, sin):
    return vectors * cos + jnp.roll(vectors, HD // 2, axis=-1) * sin


def local_any(
    n, inputs, norm_gain, qkv_weight, head_lambda, head_gain, out_weight,
    key_one_pages, key_two_pages, value_pages, page_table, context_len, positions,
):
    steps = inputs.shape[0]
    own = page_table.shape[0]
    capacity = page_table.shape[1] * key_one_pages.shape[1]
    values = lax.all_gather(inputs, "gx", axis=2, tiled=True).astype(F32)
    factor = lax.rsqrt(jnp.mean(values * values, axis=-1, keepdims=True) + EPS)
    normed = (values * factor * norm_gain).astype(BF16)
    projected = jnp.einsum("sbd,dc->sbc", normed, qkv_weight, preferred_element_type=F32)
    received = lax.all_to_all(
        projected.astype(BF16), "gx", split_axis=1, concat_axis=2, tiled=True
    )
    cached = tuple(
        pool[page_table].reshape(own, capacity, H, -1)
        for pool in (key_one_pages, key_two_pages, value_pages)
    )
    both = received[..., : 4 * H * HD].reshape(steps, own, 4, H, HD).astype(F32)
    new_values = received[..., 4 * H * HD :].reshape(steps, own, H, 2 * HD)
    cos, sin = jax.vmap(lambda p: angles(p, steps))(positions.reshape(own, 1))
    cos, sin = (jnp.moveaxis(x, 0, 1)[:, :, None] for x in (cos, sin))
    turned = rotary(both, cos, sin).astype(BF16)
    place = jnp.arange(capacity, dtype=jnp.int32)
    allowed = (place[None, :] < context_len[:, None])[None, :, None, :]
    step = jnp.arange(steps)
    newer_allowed = (step[None, :] <= step[:, None])[:, None, None, :]

    def softmax_map(query, keys, news):
        older = jnp.einsum("tshd,sjhd->tshj", query, keys, preferred_element_type=F32)
        newer = jnp.einsum("tshd,eshd->tshe", query, news, preferred_element_type=F32)
        scores = jnp.concatenate(
            [jnp.where(allowed, older, -jnp.inf), jnp.where(newer_allowed, newer, -jnp.inf)], axis=-1
        )
        return jax.nn.softmax(scores * (1.0 / math.sqrt(HD)), axis=-1)

    first = softmax_map(turned[:, :, 0], cached[0], turned[:, :, 2])
    second = softmax_map(turned[:, :, 1], cached[1], turned[:, :, 3])
    mix = (first - head_lambda[:, None] * second).astype(BF16)
    mixed = jnp.einsum(
        "tshj,sjhf->tshf", mix[..., :capacity], cached[2], preferred_element_type=F32
    ) + jnp.einsum("tshe,eshf->tshf", mix[..., capacity:], new_values, preferred_element_type=F32)
    norm = lax.rsqrt(jnp.mean(mixed * mixed, axis=-1, keepdims=True) + EPS)
    grouped = (mixed * norm * head_gain.reshape(H, 2 * HD)).astype(BF16)
    whole = lax.all_gather(grouped.reshape(steps, own, -1), "gx", axis=1, tiled=True)
    branch = jnp.einsum("sbf,fd->sbd", whole, out_weight, preferred_element_type=F32)
    return (inputs.astype(F32) + branch).astype(BF16)


def solution(mesh):
    n = mesh.shape["gx"]
    placed = (
        P(None, "groups", "gx"),
        P(),
        P(None, "gx"),
        P(),
        P(),
        P(None, "gx"),
        P(("groups", "gx"), None, None),
        P(("groups", "gx"), None, None),
        P(("groups", "gx"), None, None),
        P(("groups", "gx"), None),
        P(("groups", "gx")),
        P(("groups", "gx")),
    )

    def chosen(inputs, norm_gain, qkv_weight, *rest):
        aligned = inputs.shape[2] % 128 == 0 and qkv_weight.shape[1] % 128 == 0
        single = rest[6].shape[0] == 1
        power = n >= 4 and n & (n - 1) == 0
        body = local if aligned and single and power else local_any
        return body(n, inputs, norm_gain, qkv_weight, *rest)

    return jax.shard_map(
        chosen, mesh=mesh, in_specs=placed, out_specs=P(None, "groups", "gx"), check_vma=False
    )
```

```python
import functools
import math

import jax
import jax.numpy as jnp
from jax import lax
from jax.experimental import pallas as pl
from jax.experimental.pallas import tpu as pltpu
from jax.sharding import PartitionSpec as P

H = 24
HD = 128
EPS = 1e-05
ROPE_BASE = 10000.0
F32 = jnp.float32
BF16 = jnp.bfloat16
VMEM_LIMIT = 16 * 1024 * 1024


def radices(n):
    rest = n // 2
    middle = 1
    while middle * middle * 4 <= rest:
        middle *= 2
    return rest // middle, middle


def swap(block, n, mask):
    return lax.ppermute(block, "gx", [(i, i ^ mask) for i in range(n)])


def gather_blocks(block, n, first_aside, second_aside):
    outer, middle = radices(n)
    arrived = [swap(block, n, m * 2) for m in range(1, middle)]
    rows = jnp.stack([first_aside(block)] + arrived)
    others = [swap(rows, n, o * 2 * middle) for o in range(1, outer)]
    rows, others = lax.optimization_barrier((second_aside(rows), others))
    mine = jnp.concatenate([rows] + others)
    return mine, swap(mine, n, 1)


def owner(me, entry, core, n):
    outer, middle = radices(n)
    mask = (entry % outer) * (2 * middle) + (entry // outer) * 2 + core
    return jnp.bitwise_xor(me, mask)


def far(x):
    return pltpu.with_memory_space_constraint(x, pltpu.HBM)


def hint(us):
    return pl.CostEstimate(flops=0, bytes_accessed=int(us * 3_000_000), transcendentals=0)


def slots(n):
    return [(entry, core) for core in range(2) for entry in range(n // 2)]


def fetches(n, order, me, from_ref, to_ref, sems):
    part = from_ref.shape[0] // n
    copies = []
    for slot, (entry, core) in enumerate(order):
        start = pl.multiple_of(owner(me, entry, core, n) * part, part)
        copies.append(
            pltpu.make_async_copy(
                from_ref.at[pl.ds(start, part), :], to_ref.at[slot], sems.at[slot]
            )
        )
    return copies


def fetch_kernel(n, order, *rest):
    (
        me_ref, block_ref, gain_ref, weight_ref, table_ref, lambda_ref, head_gain_ref,
        held, gain_out, weight_out, place_ref, lambda_out, head_gain_out,
        table, row_ref, wide_ref, sems, other_sems,
    ) = rest
    small = [
        pltpu.make_async_copy(start, end, other_sems.at[index])
        for index, (start, end) in enumerate(
            (
                (table_ref, table),
                (lambda_ref, row_ref),
                (head_gain_ref, wide_ref),
                (block_ref, held),
                (gain_ref, gain_out),
            )
        )
    ]
    large = fetches(n, order, me_ref[0], weight_ref, weight_out, sems)
    for copy in small + large:
        copy.start()
    for copy in small:
        copy.wait()

    capacity = place_ref.shape[1]
    pages = table_ref.shape[1]
    page = capacity // pages
    row = lax.broadcasted_iota(jnp.int32, (1, capacity), 1)
    place = jnp.zeros((1, capacity), jnp.int32)
    for index in range(pages):
        first = table[0, index] * page
        inside = (row >= first) & (row < first + page)
        place = jnp.where(inside, row - first + index * page, place)
    place_ref[...] = place
    across = lax.broadcasted_iota(jnp.int32, (H, H), 1) == lax.broadcasted_iota(jnp.int32, (H, H), 0)
    lambda_out[...] = jnp.sum(jnp.where(across, row_ref[...], 0.0), axis=1, keepdims=True)
    for h in range(H):
        head_gain_out[h : h + 1, :] = wide_ref[:, h * 2 * HD : (h + 1) * 2 * HD]

    for copy in large:
        copy.wait()


def fetch(me, block, gain, weight, n, order, small, capacity):
    part, columns = weight.shape[0] // n, weight.shape[1]
    vmem = pl.BlockSpec(memory_space=pltpu.VMEM)
    hbm = pl.BlockSpec(memory_space=pltpu.HBM)
    table, weights, head_gain = small
    return pl.pallas_call(
        functools.partial(fetch_kernel, n, order),
        out_shape=(
            pltpu.VMEM(block.shape, BF16),
            pltpu.VMEM(gain.shape, F32),
            pltpu.VMEM((len(order), part, columns), BF16),
            jax.ShapeDtypeStruct((1, capacity), jnp.int32),
            jax.ShapeDtypeStruct((H, 1), F32),
            jax.ShapeDtypeStruct((H, 2 * HD), F32),
        ),
        in_specs=[pl.BlockSpec(memory_space=pltpu.SMEM)] + [hbm] * 6,
        out_specs=(vmem,) * 6,
        scratch_shapes=[
            pltpu.SMEM(table.shape, table.dtype),
            pltpu.VMEM(weights.shape, F32),
            pltpu.VMEM(head_gain.shape, F32),
            pltpu.SemaphoreType.DMA((len(order),)),
            pltpu.SemaphoreType.DMA((5,)),
        ],
        compiler_params=pltpu.CompilerParams(vmem_limit_bytes=4 * 1024 * 1024),
        cost_estimate=hint(5),
    )(me, far(block), far(gain), far(weight), *map(far, small))


def near(x):
    return pltpu.with_memory_space_constraint(x, pltpu.VMEM)


def add_squares(refs, square):
    for ref in refs:
        for entry in range(ref.shape[0]):
            values = ref[entry].astype(F32)
            square = square + values * values
    return square


def squares_kernel(n, order, count, me_ref, weight_ref, *rest):
    blocks, (squares, weight_out, sems) = rest[:count], rest[count:]
    copies = fetches(n, order, me_ref[0], weight_ref, weight_out, sems)
    for copy in copies:
        copy.start()
    squares[...] = add_squares(blocks, jnp.zeros(squares.shape, F32))
    for copy in copies:
        copy.wait()


def squares_beside(me, weight, blocks, n, order):
    part, columns = weight.shape[0] // n, weight.shape[1]
    vmem = pl.BlockSpec(memory_space=pltpu.VMEM)
    return pl.pallas_call(
        functools.partial(squares_kernel, n, order, len(blocks)),
        out_shape=(
            jax.ShapeDtypeStruct(blocks[0].shape[1:], F32),
            pltpu.VMEM((len(order), part, columns), BF16),
        ),
        in_specs=[
            pl.BlockSpec(memory_space=pltpu.SMEM),
            pl.BlockSpec(memory_space=pltpu.HBM),
        ]
        + [vmem] * len(blocks),
        out_specs=(vmem, vmem),
        scratch_shapes=[pltpu.SemaphoreType.DMA((len(order),))],
        compiler_params=pltpu.CompilerParams(vmem_limit_bytes=4 * 1024 * 1024),
        cost_estimate=hint(len(order) * 0.7),
    )(me, far(weight), *blocks)


def more_squares_kernel(positions_ref, length_ref, place_ref, before, *rest):
    *blocks, squares, cos_ref, sin_ref, allowed_ref = rest
    squares[...] = add_squares(blocks, before[...])
    steps = cos_ref.shape[0]
    lane = lax.broadcasted_iota(jnp.int32, (8, HD), 1)
    step = lax.broadcasted_iota(jnp.int32, (8, HD), 0)
    pair = lax.rem(lane, HD // 2).astype(F32)
    frequency = jnp.exp(-math.log(ROPE_BASE) * 2.0 * pair / HD)
    turns = (positions_ref[0] + step).astype(F32) * frequency
    cos = jnp.cos(turns)
    sin = jnp.where(lane < HD // 2, -1.0, 1.0) * jnp.sin(turns)
    for index in range(steps):
        cos_ref[index] = cos[index : index + 1]
        sin_ref[index] = sin[index : index + 1]
    allowed_ref[...] = jnp.where(place_ref[...] < length_ref[0], 1.0, 0.0)


def more_squares(blocks, before, positions, length, place, steps):
    vmem = pl.BlockSpec(memory_space=pltpu.VMEM)
    smem = pl.BlockSpec(memory_space=pltpu.SMEM)
    turns = jax.ShapeDtypeStruct((steps, 1, HD), F32)
    return pl.pallas_call(
        more_squares_kernel,
        out_shape=(
            jax.ShapeDtypeStruct(before.shape, F32),
            turns,
            turns,
            jax.ShapeDtypeStruct(place.shape, F32),
        ),
        in_specs=[smem, smem] + [vmem] * (len(blocks) + 2),
        out_specs=(vmem,) * 4,
        compiler_params=pltpu.CompilerParams(vmem_limit_bytes=4 * 1024 * 1024),
        cost_estimate=hint(1),
    )(positions, length, place, before, *blocks)


def project_kernel(n, order, me_ref, gain_ref, before_ref, mine_ref, other_ref, weight_ref, *rest):
    *helds, out_ref, last, spread, total, kept, sems = rest
    me = me_ref[0]
    rows, part = before_ref.shape
    copies = fetches(n, order, me, weight_ref, last, sems)
    for copy in copies:
        copy.start()
    places = [(held, slot) for held in helds for slot in range(held.shape[0])]
    early = len(places)
    places += [(last, slot) for slot in range(len(order))]
    blocks = list(zip(slots(n), places, strict=True))

    def products(picked, factor):
        summed = None
        for (entry, core), (held, slot) in picked:
            values = (mine_ref, other_ref)[core][entry].astype(F32)
            normed = (values * factor * gain_ref[owner(me, entry, core, n)]).astype(BF16)
            product = jnp.dot(normed, held[slot], preferred_element_type=F32)
            summed = product if summed is None else summed + product
        return summed

    def row_factor():
        square = add_squares([other_ref], before_ref[...])
        mean = jnp.sum(square, axis=1, keepdims=True) * (1.0 / (n * part))
        return lax.rsqrt(mean + EPS)

    @pl.when(me >= 0)
    def _():
        factor = row_factor()
        total[...] = products(blocks[:early], factor)
        kept[...] = jnp.broadcast_to(factor, kept.shape)

    factor = kept[:, :1]
    summed = total[...]
    half = -(-len(copies) // 2)
    for group in (slice(0, half), slice(half, len(copies))):
        for copy in copies[group]:
            copy.wait()
        summed = summed + products(blocks[early:][group], factor)
    columns = summed.shape[1] // 128
    steps = rows // n
    for block in range(columns):
        for step in range(steps):
            spread[:, step * columns + block, :] = summed[
                step * n : (step + 1) * n, block * 128 : (block + 1) * 128
            ]
    for target in range(n):
        out_ref[target] = spread[target, : steps * columns, :].astype(BF16)


def project(me, block, gain, weight, n, scalars, small, capacity):
    rows, part = block.shape
    columns = weight.shape[1]
    pieces = rows // n * (columns // 128)
    outer, middle = radices(n)
    order = slots(n)
    first, second = n // 4, 3 * n // 4

    arrived = [swap(block, n, o * 2 * middle) for o in range(1, outer)]
    held, gain, weight_a, place, weights, head_gain = fetch(
        me, block, gain, weight, n, order[:first], small, capacity
    )
    row = jnp.stack([held] + arrived)
    later = [swap(row, n, m * 2) for m in range(1, middle)]
    squares, weight_b = squares_beside(me, weight, [row], n, order[first:second])
    later, squares = lax.optimization_barrier((later, squares))
    mine = jnp.concatenate([row] + later)
    other = swap(mine, n, 1)
    squares, cos, sin, allowed = more_squares(later, squares, *scalars, place, rows // n)
    vmem = pl.BlockSpec(memory_space=pltpu.VMEM)
    hbm = pl.BlockSpec(memory_space=pltpu.HBM)
    sent = pl.pallas_call(
        functools.partial(project_kernel, n, order[second:]),
        out_shape=jax.ShapeDtypeStruct((n, pieces, 128), BF16),
        in_specs=[pl.BlockSpec(memory_space=pltpu.SMEM)] + [vmem] * 4 + [hbm] + [vmem] * 2,
        out_specs=vmem,
        scratch_shapes=[
            pltpu.VMEM((n - second, part, columns), BF16),
            pltpu.VMEM((n, -(-pieces // 8) * 8, 128), F32),
            pltpu.VMEM((rows, columns), F32),
            pltpu.VMEM((rows, 128), F32),
            pltpu.SemaphoreType.DMA((n - second,)),
        ],
        compiler_params=pltpu.CompilerParams(vmem_limit_bytes=VMEM_LIMIT),
        cost_estimate=hint(6),
    )(me, gain, squares, mine, other, far(weight), near(weight_a), near(weight_b))
    return sent, (cos, sin, allowed, weights, head_gain)


def attend_kernel(
    received_ref, cos_ref, sin_ref, allowed_ref, lambda_ref, gain_ref,
    keys_one_ref, keys_two_ref, values_ref, out_ref, fresh,
):
    sources, pieces, _ = received_ref.shape
    steps = cos_ref.shape[0]
    blocks = pieces // steps
    pages, page, _ = keys_one_ref.shape
    capacity = pages * page
    for source in range(sources):
        piece = received_ref[source].astype(F32)
        for step in range(steps):
            fresh[step, source * blocks : (source + 1) * blocks, :] = piece[
                step * blocks : (step + 1) * blocks
            ]

    def heads(step, kind):
        return fresh[step, kind * H : (kind + 1) * H, :]

    def rotated(step, kind):
        values = heads(step, kind)
        turned = values * cos_ref[step] + pltpu.roll(values, HD // 2, 1) * sin_ref[step]
        return turned.astype(BF16).astype(F32)

    allowed = allowed_ref[...] > 0.0
    scale = 1.0 / math.sqrt(HD)
    head_row = lax.rem(lax.broadcasted_iota(jnp.int32, (steps * H, HD), 0), H)

    def softmax_map(kind, keys_ref):
        queries = [rotated(step, kind) for step in range(steps)]
        news = [rotated(step, kind + 2) for step in range(steps)]
        stacked = jnp.concatenate(queries, axis=0)
        apart = jnp.concatenate(
            [jnp.where(head_row == h, stacked, 0.0).astype(BF16) for h in range(H)], axis=1
        )
        older = lax.dot_general(
            apart, keys_ref[...].reshape(capacity, H * HD), (((1,), (1,)), ((), ())),
            preferred_element_type=F32,
        )
        older = jnp.where(allowed, older * scale, -1e38)
        parts = []
        for step in range(steps):
            cached = older[step * H : (step + 1) * H]
            newer = [
                jnp.sum(queries[step] * news[e], axis=1, keepdims=True) * scale
                for e in range(step + 1)
            ]
            top = jnp.max(cached, axis=1, keepdims=True)
            for value in newer:
                top = jnp.maximum(top, value)
            cached = jnp.exp(cached - top)
            newer = [jnp.exp(value - top) for value in newer]
            whole = jnp.sum(cached, axis=1, keepdims=True)
            for value in newer:
                whole = whole + value
            parts.append((cached / whole, [value / whole for value in newer]))
        return parts

    first = softmax_map(0, keys_one_ref)
    second = softmax_map(1, keys_two_ref)
    weight = lambda_ref[...]
    mix = jnp.concatenate(
        [first[step][0] - weight * second[step][0] for step in range(steps)], axis=0
    ).astype(BF16)
    spread = jnp.dot(mix, values_ref[...].reshape(capacity, -1), preferred_element_type=F32)
    wide_row = lax.broadcasted_iota(jnp.int32, (H, 2 * HD), 0)
    fresh_values = [
        jnp.concatenate(
            [fresh[e, pl.ds(4 * H + half, H, stride=2), :] for half in range(2)], axis=1
        )
        for e in range(steps)
    ]
    for step in range(steps):
        mixed = jnp.zeros((H, 2 * HD), F32)
        for h in range(H):
            block = spread[step * H : (step + 1) * H, h * 2 * HD : (h + 1) * 2 * HD]
            mixed = jnp.where(wide_row == h, block, mixed)
        for e in range(step + 1):
            share = first[step][1][e] - weight * second[step][1][e]
            mixed = mixed + share.astype(BF16).astype(F32) * fresh_values[e]
        norm = lax.rsqrt(jnp.mean(mixed * mixed, axis=1, keepdims=True) + EPS)
        out_ref[step * H : (step + 1) * H, :] = (mixed * norm * gain_ref[...]).astype(BF16)


def attend(received, cos, sin, allowed, weights, gain, keys_one, keys_two, values):
    steps = cos.shape[0]
    sources, pieces, _ = received.shape
    vmem = pl.BlockSpec(memory_space=pltpu.VMEM)
    held = [near(x) for x in (keys_one, keys_two, values)]
    return pl.pallas_call(
        attend_kernel,
        out_shape=jax.ShapeDtypeStruct((steps * H, 2 * HD), BF16),
        in_specs=[vmem] * 9,
        out_specs=vmem,
        scratch_shapes=[pltpu.VMEM((steps, sources * (pieces // steps), 128), F32)],
        compiler_params=pltpu.CompilerParams(vmem_limit_bytes=VMEM_LIMIT),
        cost_estimate=hint(10),
    )(received, cos, sin, allowed, weights, gain, *held)


def output_kernel(n, me_ref, mine_ref, other_ref, inputs_ref, *rest):
    *weights, out_ref, rows_ref = rest
    me = me_ref[0]
    half, heads, width = mine_ref.shape
    steps = heads // H
    lanes = width // 128
    for entry in range(half):
        for core, ref in ((0, mine_ref), (1, other_ref)):
            source = jnp.bitwise_xor(me, 2 * entry + core)
            start = pl.multiple_of(source * heads, 8)
            block = ref[entry].astype(F32)
            for lane in range(lanes):
                rows_ref[lane, pl.ds(start, heads), :] = block[:, lane * 128 : (lane + 1) * 128]
    total = None
    for h in range(H):
        left = jnp.concatenate(
            [
                jnp.concatenate(
                    [rows_ref[lane, pl.ds(step * H + h, n, stride=heads), :] for lane in range(lanes)],
                    axis=1,
                )
                for step in range(steps)
            ],
            axis=0,
        ).astype(BF16)
        held = weights[h * len(weights) // H]
        at = h * width % held.shape[0]
        product = jnp.dot(left, held[at : at + width, :], preferred_element_type=F32)
        total = product if total is None else total + product
    for step in range(steps):
        out_ref[step] = (
            inputs_ref[step].astype(F32) + total[step * n : (step + 1) * n]
        ).astype(BF16)


def keep_kernel(half, block_ref, from_ref, held, to_ref, sem):
    rows = to_ref.shape[0]
    copy = pltpu.make_async_copy(from_ref.at[pl.ds(half * rows, rows), :], to_ref, sem)
    copy.start()
    held[...] = block_ref[...]
    copy.wait()


def keep(block, weight, half, us):
    vmem = pl.BlockSpec(memory_space=pltpu.VMEM)
    return pl.pallas_call(
        functools.partial(keep_kernel, half),
        out_shape=(
            jax.ShapeDtypeStruct(block.shape, block.dtype),
            pltpu.VMEM((weight.shape[0] // 2, weight.shape[1]), weight.dtype),
        ),
        in_specs=[vmem, pl.BlockSpec(memory_space=pltpu.HBM)],
        out_specs=(vmem, vmem),
        scratch_shapes=[pltpu.SemaphoreType.DMA],
        compiler_params=pltpu.CompilerParams(vmem_limit_bytes=4 * 1024 * 1024),
        cost_estimate=hint(us),
    )(block, far(weight))


def output(me, attended, inputs, weight, n):
    kept = []

    def aside(half, block):
        block, part = keep(block, weight, half, 2)
        kept.append(near(part))
        return block

    mine, other = gather_blocks(
        attended, n, functools.partial(aside, 0), functools.partial(aside, 1)
    )
    half, heads, width = mine.shape
    vmem = pl.BlockSpec(memory_space=pltpu.VMEM)
    return pl.pallas_call(
        functools.partial(output_kernel, n),
        out_shape=jax.ShapeDtypeStruct(inputs.shape, BF16),
        in_specs=[pl.BlockSpec(memory_space=pltpu.SMEM)] + [vmem] * 5,
        out_specs=vmem,
        scratch_shapes=[pltpu.VMEM((width // 128, n * heads, 128), F32)],
        compiler_params=pltpu.CompilerParams(vmem_limit_bytes=VMEM_LIMIT),
    )(me, mine, other, inputs, *kept)


def angles(positions, steps):
    half = HD // 2
    frequency = jnp.exp(-math.log(ROPE_BASE) * 2.0 * jnp.arange(half, dtype=F32) / HD)
    places = (positions + jnp.arange(steps, dtype=jnp.int32)).astype(F32)
    turns = places[:, None] * frequency[None, :]
    cosine, sine = jnp.cos(turns), jnp.sin(turns)
    cos = jnp.concatenate([cosine, cosine], axis=-1)
    sin = jnp.concatenate([-sine, sine], axis=-1)
    return cos[:, None, :], sin[:, None, :]


def local(
    n, inputs, norm_gain, qkv_weight, head_lambda, head_gain, out_weight,
    key_one_pages, key_two_pages, value_pages, page_table, context_len, positions,
):
    steps, rows, part = inputs.shape
    me = lax.axis_index("gx").astype(jnp.int32).reshape(1)
    block = inputs.reshape(steps * rows, part)
    capacity = page_table.shape[1] * key_one_pages.shape[1]
    small = (page_table, head_lambda.reshape(1, H), head_gain.reshape(1, H * 2 * HD))
    sent, aside = project(
        me, block, norm_gain.reshape(n, 1, part), qkv_weight, n, (positions, context_len), small,
        capacity,
    )
    received = lax.all_to_all(sent, "gx", 0, 0)
    attended = attend(received, *aside, key_one_pages, key_two_pages, value_pages)
    return output(me, attended, inputs, out_weight, n)


def rotary(vectors, cos, sin):
    return vectors * cos + jnp.roll(vectors, HD // 2, axis=-1) * sin


def local_any(
    n, inputs, norm_gain, qkv_weight, head_lambda, head_gain, out_weight,
    key_one_pages, key_two_pages, value_pages, page_table, context_len, positions,
):
    steps = inputs.shape[0]
    own = page_table.shape[0]
    capacity = page_table.shape[1] * key_one_pages.shape[1]
    values = lax.all_gather(inputs, "gx", axis=2, tiled=True).astype(F32)
    factor = lax.rsqrt(jnp.mean(values * values, axis=-1, keepdims=True) + EPS)
    normed = (values * factor * norm_gain).astype(BF16)
    projected = jnp.einsum("sbd,dc->sbc", normed, qkv_weight, preferred_element_type=F32)
    received = lax.all_to_all(
        projected.astype(BF16), "gx", split_axis=1, concat_axis=2, tiled=True
    )
    cached = tuple(
        pool[page_table].reshape(own, capacity, H, -1)
        for pool in (key_one_pages, key_two_pages, value_pages)
    )
    both = received[..., : 4 * H * HD].reshape(steps, own, 4, H, HD).astype(F32)
    new_values = received[..., 4 * H * HD :].reshape(steps, own, H, 2 * HD)
    cos, sin = jax.vmap(lambda p: angles(p, steps))(positions.reshape(own, 1))
    cos, sin = (jnp.moveaxis(x, 0, 1)[:, :, None] for x in (cos, sin))
    turned = rotary(both, cos, sin).astype(BF16)
    place = jnp.arange(capacity, dtype=jnp.int32)
    allowed = (place[None, :] < context_len[:, None])[None, :, None, :]
    step = jnp.arange(steps)
    newer_allowed = (step[None, :] <= step[:, None])[:, None, None, :]

    def softmax_map(query, keys, news):
        older = jnp.einsum("tshd,sjhd->tshj", query, keys, preferred_element_type=F32)
        newer = jnp.einsum("tshd,eshd->tshe", query, news, preferred_element_type=F32)
        scores = jnp.concatenate(
            [jnp.where(allowed, older, -jnp.inf), jnp.where(newer_allowed, newer, -jnp.inf)], axis=-1
        )
        return jax.nn.softmax(scores * (1.0 / math.sqrt(HD)), axis=-1)

    first = softmax_map(turned[:, :, 0], cached[0], turned[:, :, 2])
    second = softmax_map(turned[:, :, 1], cached[1], turned[:, :, 3])
    mix = (first - head_lambda[:, None] * second).astype(BF16)
    mixed = jnp.einsum(
        "tshj,sjhf->tshf", mix[..., :capacity], cached[2], preferred_element_type=F32
    ) + jnp.einsum("tshe,eshf->tshf", mix[..., capacity:], new_values, preferred_element_type=F32)
    norm = lax.rsqrt(jnp.mean(mixed * mixed, axis=-1, keepdims=True) + EPS)
    grouped = (mixed * norm * head_gain.reshape(H, 2 * HD)).astype(BF16)
    whole = lax.all_gather(grouped.reshape(steps, own, -1), "gx", axis=1, tiled=True)
    branch = jnp.einsum("sbf,fd->sbd", whole, out_weight, preferred_element_type=F32)
    return (inputs.astype(F32) + branch).astype(BF16)


def solution(mesh):
    n = mesh.shape["gx"]
    placed = (
        P(None, "groups", "gx"),
        P(),
        P(None, "gx"),
        P(),
        P(),
        P(None, "gx"),
        P(("groups", "gx"), None, None),
        P(("groups", "gx"), None, None),
        P(("groups", "gx"), None, None),
        P(("groups", "gx"), None),
        P(("groups", "gx")),
        P(("groups", "gx")),
    )

    def chosen(inputs, norm_gain, qkv_weight, *rest):
        aligned = inputs.shape[2] % 128 == 0 and qkv_weight.shape[1] % 128 == 0
        single = rest[6].shape[0] == 1
        power = n >= 4 and n & (n - 1) == 0
        body = local if aligned and single and power else local_any
        return body(n, inputs, norm_gain, qkv_weight, *rest)

    return jax.shard_map(
        chosen, mesh=mesh, in_specs=placed, out_specs=P(None, "groups", "gx"), check_vma=False
    )
```
